32 devices in a mesh: half: 2 (over core), dp: 2 (over x), expert: 8 (over z, y).
Axes of the slice: x: 2, y: 2, z: 4, core: 2. Of those that a mesh axis runs over, the one named last changes fastest.
Arguments:
- tokens: bfloat16 [2, 32, 128, 1024], P('half', ('dp', 'expert')), may hold values from -6 to 6
- cotangent: bfloat16 [2, 32, 128, 1024], P('half', ('dp', 'expert')), may hold values from -6 to 6
- lengths: int32 [2, 32], P(None, ('dp', 'expert')), may hold values from 64 to 128
- routes: int32 [2, 32, 128, 2], P('half', ('dp', 'expert')), may hold values from 0 to 7, all different within a row
- self_qkv: bfloat16 [2, 1024, 3072], P('half'), may hold values from -0.1875 to 0.1875
- self_out: bfloat16 [2, 1024, 1024], P('half'), may hold values from -1 to 1
- cross_weights: bfloat16 [2, 1024, 2048], P('half')
- router: bfloat16 [2, 1024, 8], P('half'), may hold values from -0.125 to 0.125
- gains: float32 [2, 3, 1024], P('half'), may hold values from 0.5 to 1.5
- bias_table: float32 [2, 512], P('half'), may hold values from -4 to 4
- expert_in: bfloat16 [2, 8, 2, 1024, 2816], P('half', 'expert'), may hold values from -0.1875 to 0.1875
- expert_out: bfloat16 [2, 8, 2816, 1024], P('half', 'expert'), may hold values from -0.21875 to 0.21875
Outputs:
- outputs: bfloat16 [2, 32, 128, 1024], P('half', ('dp', 'expert'))
- d_tokens: bfloat16 [2, 32, 128, 1024], P('half', ('dp', 'expert'))
- d_self_qkv: float32 [2, 1024, 3072], P('half', ('dp', 'expert'))
- d_self_out: float32 [2, 1024, 1024], P('half', ('dp', 'expert'))
- d_cross: float32 [2, 1024, 2048], P('half', ('dp', 'expert'))
- d_router: float32 [2, 1024, 8], P('half', ('dp', 'expert'))
- d_gains: float32 [2, 3, 1024], P('half', None, ('dp', 'expert'))
- d_bias_table: float32 [2, 512], P('half', ('dp', 'expert'))
- d_expert_in: float32 [2, 8, 2, 1024, 2816], P('half', 'expert', None, None, 'dp')
- d_expert_out: float32 [2, 8, 2816, 1024], P('half', 'expert', 'dp')
- counts: int32 [2, 2, 8], P('half', 'dp', 'expert')
The draws below stay inside these ranges and needn't reach their ends.
Inputs may be any that keep to these rules, and one draw needn't show every extreme that they name: `routes`: the 2 experts of a token differ.
All inputs are finite; a program needn't handle non-finite values.
Results may differ from the reference program's by a relative error of at most 0.023.
Values may be sent and summed in bfloat16 or wider, within the bound.
A program may use at most 640 MiB of HBM per device.

```python
import jax
import jax.numpy as jnp
from jax import lax

D = 1024
H = 16
HEAD = 64
FF = 2816
BUCKETS = 32
TOP = 2
EXPERTS = 8
LEN = 128
SEQS = 32
CAP = 40


def draw_cross_weights(key, part):
    key = jax.random.fold_in(key, 7)
    base = jax.random.truncated_normal(key, -4.0, 4.0, (2, D, 2 * D), jnp.float32)
    column = jnp.arange(2 * D)[None, None, :]
    stack_index = jnp.arange(2)[:, None, None]
    widened = (stack_index == 1) & (column >= D)
    scale = jnp.where(widened, (D // 32) ** (-0.5), D ** (-0.5))
    return (base * scale).astype(jnp.bfloat16)


def with_ends(result, rng, low, top_value):
    shape = result.shape
    spot = [jax.random.randint(jax.random.fold_in(rng, axis), (), 0, shape[axis]) for axis in range(len(shape))]
    result = result.at[tuple(spot)].set(low)
    longest = shape.index(max(shape))
    spot[longest] = (spot[longest] + 1) % shape[longest]
    return result.at[tuple(spot)].set(top_value)


def block_levels(key, shape, pieces, smallest, high):
    def one(dim, blocks):
        heights = jax.random.uniform(jax.random.fold_in(jax.random.fold_in(key, 6), dim), (blocks,), jnp.float32, smallest / len(pieces), high / len(pieces))
        return jnp.repeat(jnp.exp(heights), shape[dim] // blocks).reshape((-1,) + (1,) * (len(shape) - dim - 1))

    level = one(*pieces[0])
    for cut in pieces[1:]:
        level = level * one(*cut)
    return level


def picks_of(stream_key, rows, count, top, lift):
    order = jax.random.permutation(jax.random.fold_in(stream_key, 1), count)
    favour = order
    for power in range(3):
        favour = favour * favour // count
    favour = favour * lift // count
    lots = jax.random.randint(jax.random.fold_in(stream_key, 2), (rows, count), 0, 4096) + favour
    holders = jax.random.permutation(jax.random.fold_in(stream_key, 3), rows)[jnp.arange(count) % rows]
    lots = jnp.where(jnp.arange(rows)[:, None] == holders[None, :], 1 << 14, lots)
    priority = lots * count + jnp.arange(count)
    return lax.top_k(priority.astype(jnp.int32), top)[1].astype(jnp.int32)


def bell_draw(own_key, extent, scale, reach, cuts=(), kind=jnp.bfloat16):
    factor_of = block_levels(own_key, extent, cuts, -0.22, 0.18) if cuts else 1.0
    result = jax.random.normal(own_key, extent, jnp.float32) * scale * factor_of
    return jnp.minimum(jnp.maximum(result, -reach), reach).astype(kind)


def setup_inputs(seed: int = 0) -> dict:
    seeds = jax.random.split(jax.random.key(seed), 13)
    return {
        "tokens": bell_draw(seeds[0], (2, SEQS, LEN, D), 1.0, 6.0, ((0, 2), (1, 16))),
        "cotangent": bell_draw(seeds[1], (2, SEQS, LEN, D), 1.0, 6.0, ((0, 2), (1, 16))),
        "lengths": with_ends(jax.random.randint(seeds[2], (2, SEQS), LEN // 2, LEN + 1), jax.random.fold_in(seeds[2], 1), LEN // 2, LEN).astype(jnp.int32),
        "routes": picks_of(seeds[3], 2 * SEQS * LEN, EXPERTS, TOP, 2048).reshape((2, SEQS, LEN, TOP)),
        "self_qkv": bell_draw(seeds[4], (2, D, 3 * D), D ** -0.5, 0.1875, ((0, 2),)),
        "self_out": bell_draw(seeds[5], (2, D, D), (D // 32) ** -0.5, 1.0, ((0, 2),)),
        "cross_weights": draw_cross_weights(jax.random.fold_in(seeds[12], 71), 0),
        "router": bell_draw(seeds[7], (2, D, EXPERTS), (2 * D) ** -0.5, 0.125, ((0, 2),)),
        "gains": jnp.clip(1.0 + 0.1 * jax.random.normal(seeds[8], (2, 3, D), jnp.float32), 0.5, 1.5),
        "bias_table": bell_draw(seeds[9], (2, BUCKETS * H), 1.0, 4.0, ((0, 2),), jnp.float32),
        "expert_in": bell_draw(seeds[10], (2, EXPERTS, 2, D, FF), D ** -0.5, 0.1875, ((0, 2), (1, 8))),
        "expert_out": bell_draw(seeds[11], (2, EXPERTS, FF, D), (FF // 4) ** -0.5, 0.21875, ((0, 2), (1, 8))),
    }


EPS = 1e-06
UPPER_PRECISION = lax.Precision.HIGHEST
ENC_STEPS = (12, 16, 23, 32, 46, 64, 91)
DEC_STEPS = (19, 21, 24, 27, 31, 35, 40, 46, 52, 59, 67, 77, 87, 99, 113)

@jax.custom_vjp
def lower_precision(v):
    return lax.optimization_barrier(v.astype(jnp.bfloat16)).astype(jnp.float32)

@jax.custom_vjp
def lower_backward(v):
    return v

def low_keep(v):
    return (lower_precision(v), None)

def low_pass(kept, grad):
    return (grad,)

def back_keep(v):
    return (v, None)

def back_low(kept, grad):
    return (lower_precision(grad),)
lower_precision.defvjp(low_keep, low_pass)
lower_backward.defvjp(back_keep, back_low)

def positions(length):
    query_pos = jnp.arange(length).astype(jnp.int32)[:, None]
    key_pos = jnp.arange(length).astype(jnp.int32)[None, :]
    apart = jnp.abs(key_pos - query_pos)
    coarse = 8 + sum(((apart >= step).astype(jnp.int32) for step in ENC_STEPS))
    forward_bucket = jnp.where(apart < 8, apart, coarse) + 16 * (key_pos > query_pos).astype(jnp.int32)
    behind = jnp.maximum(query_pos - key_pos, 0)
    coarse = 16 + sum(((behind >= step).astype(jnp.int32) for step in DEC_STEPS))
    causal_bucket = jnp.where(behind < 16, behind, coarse)
    return (forward_bucket.astype(jnp.int32), causal_bucket.astype(jnp.int32))

def rms(values, gain):
    return values * lax.rsqrt(lax.optimization_barrier(jnp.mean(values * values, axis=-1, keepdims=True)) + EPS) * gain

def attend(query_rows, key_rows, values, bias, allowed):
    scores = jnp.einsum('qhd,khd->hqk', query_rows, key_rows, precision=UPPER_PRECISION) * 0.125 + bias
    scores = lower_backward(jnp.where(allowed, scores, -1000000000.0))
    weights = lower_precision(jax.nn.softmax(scores, axis=-1))
    return jnp.einsum('hqk,khd->qhd', weights, values, precision=UPPER_PRECISION)

def self_block(inputs, sizes, gain, query_key_value_weight, output_weight, table, bucket, causal):
    count, length, width = inputs.shape
    normed_rows = lower_precision(rms(inputs, gain))
    projected_rows = lower_backward(lower_precision(jnp.einsum('ayb,bx->ayx', normed_rows, query_key_value_weight, precision=UPPER_PRECISION)))
    split = projected_rows.reshape(count, length, 3, H, HEAD)
    bias = jnp.transpose(table.reshape(BUCKETS, H)[bucket], (2, 0, 1))
    query_pos = jnp.arange(length).astype(jnp.int32)[:, None]
    key_pos = jnp.arange(length).astype(jnp.int32)[None, :]

    def single(item):
        rows, size = item
        allowed = key_pos < size
        if causal:
            allowed = allowed & (key_pos <= query_pos)
        return attend(rows[:, 0], rows[:, 1], rows[:, 2], bias, allowed)
    mixed_heads = lax.map(jax.checkpoint(single), (split, sizes))
    mixed_heads = lower_backward(lower_precision(mixed_heads.reshape(count, length, width)))
    branch_output = lower_backward(jnp.einsum('iap,po->iao', mixed_heads, output_weight, precision=UPPER_PRECISION))
    return inputs + branch_output

def cross_block(inputs, memory, sizes, gain, query_weight, output_weight):
    count, length, width = inputs.shape
    normed_rows = lower_precision(rms(inputs, gain))
    query_rows = lower_backward(lower_precision(jnp.einsum('ayb,bx->ayx', normed_rows, query_weight, precision=UPPER_PRECISION)))
    query_rows = query_rows.reshape(count, length, H, HEAD)
    pairs = memory.reshape(count, length, 2, H, HEAD)
    key_pos = jnp.arange(length).astype(jnp.int32)[None, :]

    def single(item):
        rows, kv_rows, size = item
        return attend(rows, kv_rows[:, 0], kv_rows[:, 1], 0.0, key_pos < size)
    mixed_heads = lax.map(jax.checkpoint(single), (query_rows, pairs, sizes))
    mixed_heads = lower_backward(lower_precision(mixed_heads.reshape(count, length, width)))
    branch_output = lower_backward(jnp.einsum('iap,po->iao', mixed_heads, output_weight, precision=UPPER_PRECISION))
    return inputs + branch_output

def memory_block(encoded, gain, key_value_weight):
    normed_rows = lower_precision(rms(encoded, gain))
    return lower_backward(lower_precision(jnp.einsum('ayb,bx->ayx', normed_rows, key_value_weight, precision=UPPER_PRECISION)))

def slots(route_rows):
    count, length, top = route_rows.shape
    order = jnp.transpose(route_rows, (0, 2, 1)).reshape(count, top * length)
    picked = (order[:, :, None] == jnp.arange(EXPERTS).astype(jnp.int32)[None, None, :]).astype(jnp.int32)
    place = (lax.optimization_barrier(jnp.sum(jnp.cumsum(picked, axis=1) * picked, axis=2)) - 1).astype(jnp.int32)
    return jnp.transpose(place.reshape(count, top, length), (0, 2, 1))

def expert(item):
    rows, w_in, w_down = item
    mixed_heads = lower_backward(jnp.einsum('rd,gdf->grf', rows, w_in, precision=UPPER_PRECISION))
    hidden = lower_precision(jax.nn.gelu(mixed_heads[0]) * mixed_heads[1])
    return lower_backward(lower_precision(jnp.einsum('rf,fd->rd', hidden, w_down, precision=UPPER_PRECISION)))

def moe_block(inputs, route_rows, gain, router_weight, w_in, w_down):
    count, length, width = inputs.shape
    normed_rows = rms(inputs, gain)
    normed_low = lower_precision(normed_rows)
    router_logits = jnp.einsum('ayb,bx->ayx', normed_rows, router_weight, precision=UPPER_PRECISION)
    probs = jax.nn.softmax(router_logits, axis=-1)
    chosen = jnp.take_along_axis(probs, route_rows, axis=-1)
    gates = chosen / lax.optimization_barrier(jnp.sum(chosen, axis=-1, keepdims=True))
    place = slots(route_rows)
    kept = place < CAP
    seq_index = jnp.arange(count).astype(jnp.int32)[:, None, None]
    rows_all = EXPERTS * count * CAP
    target = jnp.where(kept, (route_rows * count + seq_index) * CAP + place, rows_all).astype(jnp.int32)
    source = jnp.broadcast_to(normed_low[:, :, None, :], (count, length, TOP, width))
    buffer = jnp.zeros((rows_all, width), jnp.float32).at[target.reshape(-1)].set(source.reshape(-1, width), mode='drop')
    buffer = lower_backward(buffer.reshape(EXPERTS, count * CAP, width))
    results = lax.map(jax.checkpoint(expert), (buffer, w_in, w_down))
    fetch = jnp.minimum(target, rows_all - 1).reshape(-1)
    rows = jnp.take(results.reshape(rows_all, width), fetch, axis=0).reshape(count, length, TOP, width)
    weight = jnp.where(kept, gates, 0.0)
    return inputs + lax.optimization_barrier(jnp.sum(weight[..., None] * rows, axis=2))

def tally(route_rows):
    kept = slots(route_rows) < CAP
    hot = route_rows[..., None] == jnp.arange(EXPERTS).astype(jnp.int32)
    kept_count = lax.optimization_barrier(jnp.sum((hot & kept[..., None]).astype(jnp.int32), axis=(0, 1, 2)))
    whole = lax.optimization_barrier(jnp.sum(hot.astype(jnp.int32), axis=(0, 1, 2)))
    return jnp.stack([kept_count, whole - kept_count]).astype(jnp.int32)

def reference(tokens, cotangent, lengths, routes, self_qkv, self_out, cross_weights, router, gains, bias_table, expert_in, expert_out):
    enc_bucket, dec_bucket = positions(LEN)

    def forward(inputs, query_key_value_weight, output_weight, w_cross, router_weight, gain, table, w_in, w_down):
        first = self_block(inputs[0], lengths[0], gain[0, 0], query_key_value_weight[0], output_weight[0], table[0], enc_bucket, False)
        encoded = moe_block(first, routes[0], gain[0, 1], router_weight[0], w_in[0], w_down[0])
        memory = memory_block(encoded, gain[0, 2], w_cross[0])
        first = self_block(inputs[1], lengths[1], gain[1, 0], query_key_value_weight[1], output_weight[1], table[1], dec_bucket, True)
        second = cross_block(first, memory, lengths[0], gain[1, 2], w_cross[1][:, :D], w_cross[1][:, D:])
        decoded = moe_block(second, routes[1], gain[1, 1], router_weight[1], w_in[1], w_down[1])
        return jnp.stack([encoded, decoded])
    outputs, pull = jax.vjp(forward, tokens.astype(jnp.float32), self_qkv.astype(jnp.float32), self_out.astype(jnp.float32), cross_weights.astype(jnp.float32), router.astype(jnp.float32), gains.astype(jnp.float32), bias_table.astype(jnp.float32), expert_in.astype(jnp.float32), expert_out.astype(jnp.float32))
    grads = pull(cotangent.astype(jnp.float32))
    counts = jnp.stack([tally(routes[0]), tally(routes[1])])
    return (outputs.astype(jnp.bfloat16), grads[0].astype(jnp.bfloat16), grads[1], grads[2], grads[3], grads[4], grads[5], grads[6], grads[7], grads[8], counts)
```

```python
import functools

import jax
import jax.numpy as jnp
import numpy as np
from jax import lax
from jax.experimental import pallas as pl
from jax.experimental.pallas import tpu as pltpu
from jax.sharding import PartitionSpec as P

H = 16
BUCKETS = 32
EPS = 1e-06
ENC_STEPS = (12, 16, 23, 32, 46, 64, 91)
DEC_STEPS = (19, 21, 24, 27, 31, 35, 40, 46, 52, 59, 67, 77, 87, 99, 113)
F32 = jnp.float32
BF16 = jnp.bfloat16
MESH = pl.DeviceIdType.MESH
NT = (((1,), (1,)), ((), ()))
TN = (((0,), (0,)), ((), ()))


def dot(a, b, dims=(((1,), (0,)), ((), ()))):
    return lax.dot_general(a, b, dims, preferred_element_type=F32)


def diagonal_buckets(diff):
    apart = np.abs(diff)
    coarse = 8 + sum((apart >= step).astype(np.int32) for step in ENC_STEPS)
    enc = np.where(apart < 8, apart, coarse) + 16 * (diff > 0)
    behind = np.maximum(-diff, 0)
    coarse = 16 + sum((behind >= step).astype(np.int32) for step in DEC_STEPS)
    dec = np.where(behind < 16, behind, coarse)
    return enc.astype(np.int32), dec.astype(np.int32)


def masked_scores(info, seq, bias_ref, query, key_rows, head, lane_mask, length):
    part = jnp.where(lane_mask, query, jnp.zeros_like(query))
    scores = dot(part, key_rows, NT) * 0.125
    if bias_ref is not None:
        row = jnp.broadcast_to(bias_ref[pl.ds(head, 1), :], (length, 2 * length))
        scores = scores + pltpu.roll(row, 0, 1, stride=1, stride_axis=0)[:, :length]
    row_id = lax.broadcasted_iota(jnp.int32, (length, length), 0)
    col_id = lax.broadcasted_iota(jnp.int32, (length, length), 1)
    reach = jnp.where(info[2] > 0, row_id, length)
    return jnp.where((col_id < info[seq]) & (col_id <= reach), scores, -1000000000.0)


def softmax_parts(scores):
    peak = jnp.max(scores, axis=-1, keepdims=True)
    spread = jnp.exp(scores - peak)
    return spread / jnp.sum(spread, axis=-1, keepdims=True)


def attend_kernel(has_bias, info, *refs):
    bias_ref, (q_ref, k_ref, v_ref, out_ref) = (refs[0], refs[1:]) if has_bias else (None, refs)
    length, width = q_ref.shape
    seq = pl.program_id(0)
    low = lax.broadcasted_iota(jnp.int32, (length, 128), 1) < 64

    @pl.loop(0, width // 128)
    def _(pair):
        cols = pl.ds(pl.multiple_of(pair * 128, 128), 128)
        q, k, v = q_ref[:, cols], k_ref[:, cols], v_ref[:, cols]
        mixed = []
        for side in range(2):
            mask = low if side == 0 else jnp.logical_not(low)
            scores = masked_scores(info, seq, bias_ref, q, k, 2 * pair + side, mask, length)
            mixed.append(dot(softmax_parts(scores).astype(BF16), v))
        out_ref[:, cols] = jnp.where(low, mixed[0], mixed[1]).astype(BF16)


def attend_back_kernel(has_bias, info, *refs):
    if has_bias:
        bias_ref, q_ref, k_ref, v_ref, g_ref, dq_ref, dkv_ref, diag_ref = refs
    else:
        bias_ref = diag_ref = None
        q_ref, k_ref, v_ref, g_ref, dq_ref, dkv_ref = refs
    length, width = q_ref.shape
    seq = pl.program_id(0)
    low = lax.broadcasted_iota(jnp.int32, (length, 128), 1) < 64
    if has_bias:
        row_id = lax.broadcasted_iota(jnp.int32, (length, length), 0)
        col_id = lax.broadcasted_iota(jnp.int32, (length, length), 1)
        flip = (row_id + col_id == length - 1).astype(F32).astype(BF16)

        @pl.when(seq == 0)
        def _():
            diag_ref[...] = jnp.zeros_like(diag_ref)

    @pl.loop(0, width // 128)
    def _(pair):
        cols = pl.ds(pl.multiple_of(pair * 128, 128), 128)
        q, k, v, g = q_ref[:, cols], k_ref[:, cols], v_ref[:, cols], g_ref[:, cols]
        dqs, dks, dvs = [], [], []
        for side in range(2):
            mask = low if side == 0 else jnp.logical_not(low)
            head = 2 * pair + side
            probs = softmax_parts(masked_scores(info, seq, bias_ref, q, k, head, mask, length))
            part = jnp.where(mask, g, jnp.zeros_like(g))
            dweights = dot(part, v, NT)
            dvs.append(dot(probs.astype(BF16), g, TN))
            dscores = probs * (dweights - jnp.sum(dweights * probs, axis=-1, keepdims=True))
            dlow = dscores.astype(BF16)
            dqs.append(dot(dlow, k))
            dks.append(dot(dlow, q, TN))
            if has_bias:
                upside = dot(flip, dlow)
                wide = jnp.concatenate([upside, jnp.zeros((length, length), F32)], axis=1)
                turned = pltpu.roll(wide, 0, 1, stride=1, stride_axis=0)
                diag_ref[pl.ds(head, 1), :] += jnp.sum(turned, axis=0, keepdims=True)
        dq_ref[:, cols] = (jnp.where(low, dqs[0], dqs[1]) * 0.125).astype(BF16)
        dkv_ref[:, cols] = (jnp.where(low, dks[0], dks[1]) * 0.125).astype(BF16)
        vcols = pl.ds(pl.multiple_of(width + pair * 128, 128), 128)
        dkv_ref[:, vcols] = jnp.where(low, dvs[0], dvs[1]).astype(BF16)


def attend(info, bias, q, kv, blocks, length, width):
    rows = q.shape[0]
    seqs = rows // length
    specs = [
        pl.BlockSpec((length, width), lambda s, b=b: (s, b)) for b in blocks
    ]
    lead = [] if bias is None else [pl.BlockSpec(bias.shape, lambda s: (0, 0))]
    args = [] if bias is None else [bias]
    return pl.pallas_call(
        functools.partial(attend_kernel, bias is not None),
        grid=(seqs,),
        in_specs=[pl.BlockSpec(memory_space=pltpu.SMEM)] + lead + specs,
        out_specs=pl.BlockSpec((length, width), lambda s: (s, 0)),
        out_shape=jax.ShapeDtypeStruct((rows, width), BF16),
        name="attend",
    )(info, *args, q, kv, kv)


def attend_back(info, bias, q, kv, blocks, grad, length, width):
    rows = q.shape[0]
    seqs = rows // length
    specs = [
        pl.BlockSpec((length, width), lambda s, b=b: (s, b)) for b in (*blocks, 0)
    ]
    lead = [] if bias is None else [pl.BlockSpec(bias.shape, lambda s: (0, 0))]
    args = [] if bias is None else [bias]
    out_specs = [
        pl.BlockSpec((length, width), lambda s: (s, 0)),
        pl.BlockSpec((length, 2 * width), lambda s: (s, 0)),
    ]
    out_shape = [
        jax.ShapeDtypeStruct((rows, width), BF16),
        jax.ShapeDtypeStruct((rows, 2 * width), BF16),
    ]
    if bias is not None:
        out_specs.append(pl.BlockSpec(bias.shape, lambda s: (0, 0)))
        out_shape.append(jax.ShapeDtypeStruct(bias.shape, F32))
    return pl.pallas_call(
        functools.partial(attend_back_kernel, bias is not None),
        grid=(seqs,),
        in_specs=[pl.BlockSpec(memory_space=pltpu.SMEM)] + lead + specs,
        out_specs=out_specs,
        out_shape=out_shape,
        name="attend_back",
    )(info, *args, q, kv, kv, grad)


def norm_parts(values, gain):
    scale = lax.rsqrt(jnp.mean(values * values, axis=-1, keepdims=True) + EPS)
    return values * scale * gain, scale


def norm_back(values, scale, gain, grad):
    unit = values * scale
    gain_grad = jnp.sum(grad * unit, axis=0)
    pushed = grad * gain
    back = scale * (pushed - unit * jnp.mean(pushed * unit, axis=-1, keepdims=True))
    return back, gain_grad


def gelu_parts(gate):
    c = 0.7978845608028654
    inner = c * (gate + 0.044715 * gate * gate * gate)
    t = jnp.tanh(inner)
    value = 0.5 * gate * (1.0 + t)
    slope = 0.5 * (1.0 + t) + 0.5 * gate * (1.0 - t * t) * c * (1.0 + 3.0 * 0.044715 * gate * gate)
    return value, slope


def moe_forward(send, w_in, w_down, turn, kept_from):
    experts, rows, width = send.shape
    arrived = lax.all_to_all(send, "expert", split_axis=0, concat_axis=0, tiled=True)
    flat = arrived.reshape(-1, width)
    value, _ = gelu_parts(dot(flat, w_in[0]))
    hidden = (value * dot(flat, w_in[1])).astype(BF16)
    result = dot(hidden, w_down).astype(BF16).reshape(send.shape)
    back = lax.all_to_all(result, "expert", split_axis=0, concat_axis=0, tiled=True)
    if kept_from is None:
        return back, arrived
    mine = lax.axis_index("half") == turn
    return jnp.where(mine, back, kept_from[0]), jnp.where(mine, arrived, kept_from[1])


def moe_backward(grad_send, received, w_in, w_down, turn, kept_from):
    width = grad_send.shape[2]
    arrived = lax.all_to_all(grad_send, "expert", split_axis=0, concat_axis=0, tiled=True)
    flat_grad = arrived.reshape(-1, width)
    flat = received.reshape(-1, width)
    up = dot(flat, w_in[1])
    value, slope = gelu_parts(dot(flat, w_in[0]))
    hidden = (value * up).astype(BF16)
    dhidden = dot(flat_grad, w_down, NT)
    dgate = (dhidden * up * slope).astype(BF16)
    dup = (dhidden * value).astype(BF16)
    drows = (dot(dgate, w_in[0], NT) + dot(dup, w_in[1], NT)).astype(BF16)
    back = lax.all_to_all(
        drows.reshape(arrived.shape), "expert", split_axis=0, concat_axis=0, tiled=True
    )
    out = (back, dgate, dup, hidden, flat_grad)
    if kept_from is None:
        return out
    mine = lax.axis_index("half") == turn
    return tuple(jnp.where(mine, a, b) for a, b in zip(out, kept_from))


def body(
    tokens,
    cotangent,
    lengths,
    routes,
    self_qkv,
    self_out,
    cross_weights,
    router,
    gains,
    bias_table,
    expert_in,
    expert_out,
):
    _, seqs, length, width = tokens.shape
    heads = H
    experts = router.shape[2]
    top = routes.shape[3]
    capacity = (5 * top * length + 4 * experts - 1) // (4 * experts)
    block_rows = -(-seqs * capacity // 16) * 16
    rows = seqs * length
    slots = experts * block_rows
    half_index = lax.axis_index("half")
    decoder = half_index == 1
    wqkv, wout, wcross, wrouter, gain = (
        self_qkv[0],
        self_out[0],
        cross_weights[0],
        router[0],
        gains[0],
    )
    w_in, w_down = expert_in[0, 0], expert_out[0, 0]

    column = np.arange(2 * length)
    hot, hot_back = (
        (
            jnp.where(decoder, *reversed(diagonal_buckets(diff)))[:, None]
            == jnp.arange(BUCKETS)[None, :]
        ).astype(F32)
        for diff in (np.where(column < length, column, column - 2 * length), column - length + 1)
    )
    bias = lax.dot_general(
        bias_table[0].reshape(BUCKETS, heads),
        hot,
        (((0,), (1,)), ((), ())),
        precision=lax.Precision.HIGHEST,
        preferred_element_type=F32,
    )
    own_lengths = jnp.where(decoder, lengths[1], lengths[0])
    self_info = jnp.concatenate([own_lengths, half_index[None]]).astype(jnp.int32)
    cross_info = jnp.concatenate([lengths[0], jnp.zeros((1,), jnp.int32)]).astype(jnp.int32)

    order = jnp.transpose(routes[0], (0, 2, 1)).reshape(seqs, top * length)
    expert_ids = jnp.arange(experts, dtype=jnp.int32)
    picked = (order[:, :, None] == expert_ids).astype(BF16)
    earlier = np.tril(np.ones((top * length, top * length), np.float32), -1).astype(BF16)
    before = jnp.einsum("pq,sqe->spe", earlier, picked, preferred_element_type=F32)
    place = jnp.sum(before * picked.astype(F32), axis=2).astype(jnp.int32)
    kept = place < capacity
    base = order * block_rows + jnp.arange(seqs, dtype=jnp.int32)[:, None] * capacity
    target = jnp.where(kept, base + place, -1).reshape(seqs, top, length)
    target = jnp.transpose(target, (1, 0, 2)).reshape(top, rows)
    slot_ids = jnp.arange(slots, dtype=jnp.int32)
    spots = (target[:, :, None] == slot_ids).astype(BF16)
    both = jnp.sum(spots.astype(F32), axis=0).astype(BF16)
    stacked = spots.reshape(top * rows, slots)
    kept_hot = picked.astype(F32) * kept[:, :, None].astype(F32)
    kept_count = jnp.sum(kept_hot, axis=(0, 1))
    all_count = jnp.sum(picked.astype(F32), axis=(0, 1))
    tallies = jnp.concatenate([kept_count, all_count - kept_count])
    route_hot = (routes[0].reshape(rows, top, 1) == expert_ids).astype(F32)

    def route(values):
        normed, scale = norm_parts(values, gain[1])
        low = normed.astype(BF16)
        rest = (normed - low.astype(F32)).astype(BF16)
        logits = dot(low, wrouter) + dot(rest, wrouter)
        probs = jax.nn.softmax(logits, axis=-1)
        chosen = jnp.sum(probs[:, None, :] * route_hot, axis=-1)
        total = jnp.sum(chosen, axis=-1, keepdims=True)
        gates = chosen / total
        send = dot(both, low, TN).astype(BF16).reshape(experts, block_rows, width)
        return dict(scale=scale, low=low, probs=probs, gates=gates, total=total, send=send)

    def fetch(returned):
        flat = returned.reshape(slots, width)
        return dot(stacked, flat).reshape(top, rows, width)

    def combine(values, gates, results):
        return values + jnp.sum(jnp.transpose(gates)[:, :, None] * results, axis=0)

    values = tokens[0].reshape(rows, width).astype(F32)
    normed, scale0 = norm_parts(values, gain[0])
    low0 = normed.astype(BF16)
    qkv = dot(low0, wqkv).astype(BF16)
    mixed0 = attend(self_info, bias, qkv, qkv, (0, 1, 2), length, width)
    first = values + dot(mixed0, wout)

    state = route(first)
    returned, received = moe_forward(state["send"], w_in, w_down, 0, None)
    final_enc = combine(first, state["gates"], fetch(returned))
    normed, scale_m = norm_parts(final_enc, gain[2])
    low_m = normed.astype(BF16)
    memory = dot(low_m, wcross).astype(BF16)
    names = ("half", "dp", "expert")
    forward_pairs, back_pairs = half_pairs(lax.axis_size("dp") * lax.axis_size("expert"))
    memory = lax.ppermute(memory, names, forward_pairs)

    normed, scale_c = norm_parts(first, gain[2])
    low_c = normed.astype(BF16)
    query = dot(low_c, wcross[:, :width]).astype(BF16)
    mixed_c = attend(cross_info, None, query, memory, (0, 0, 1), length, width)
    second = jnp.where(decoder, first + dot(mixed_c, wcross[:, width:]), first)

    state = route(second)
    returned, received = moe_forward(state["send"], w_in, w_down, 1, (returned, received))
    results = fetch(returned)
    final = combine(second, state["gates"], results)
    outputs = final.astype(BF16)

    def moe_gradient(grad):
        dgates = jnp.transpose(jnp.sum(grad[None] * results, axis=-1))
        spread = (jnp.transpose(state["gates"])[:, :, None] * grad[None]).astype(BF16)
        send = dot(stacked, spread.reshape(top * rows, width), TN)
        return dgates, send.astype(BF16).reshape(experts, block_rows, width)

    def moe_input_gradient(grad, dgates, back):
        gates, total, probs = state["gates"], state["total"], state["probs"]
        dchosen = (dgates - jnp.sum(dgates * gates, axis=-1, keepdims=True)) / total
        dprobs = jnp.sum(dchosen[:, :, None] * route_hot, axis=1)
        dlogits = probs * (dprobs - jnp.sum(dprobs * probs, axis=-1, keepdims=True))
        dnormed = dot(both, back.reshape(slots, width)) + lax.dot_general(
            dlogits, wrouter.astype(F32), NT, preferred_element_type=F32
        )
        dvalues, dgain = norm_back(second, state["scale"], gain[1], dnormed)
        normed = second * state["scale"] * gain[1]
        drouter = lax.dot_general(
            normed, dlogits, TN, precision=lax.Precision.HIGHEST, preferred_element_type=F32
        )
        return grad + dvalues, dgain, drouter

    grad_dec = cotangent[0].reshape(rows, width).astype(F32)
    dgates, grad_send = moe_gradient(grad_dec)
    kept_from = moe_backward(grad_send, received, w_in, w_down, 1, None)
    grad_second, _, _ = moe_input_gradient(grad_dec, dgates, kept_from[0])

    dbranch_c = grad_second.astype(BF16)
    dmixed_c = dot(dbranch_c, wcross[:, width:], NT).astype(BF16)
    dquery, dmemory = attend_back(
        cross_info, None, query, memory, (0, 0, 1), dmixed_c, length, width
    )
    dmemory = lax.ppermute(dmemory, names, back_pairs)
    dnormed = dot(dquery, wcross[:, :width], NT)
    dvalues, dgain_c = norm_back(first, scale_c, gain[2], dnormed)
    grad_first_dec = grad_second + dvalues

    dnormed = dot(dmemory, wcross, NT)
    dvalues, dgain_m = norm_back(final_enc, scale_m, gain[2], dnormed)
    grad = jnp.where(decoder, grad_dec, grad_dec + dvalues)
    dgates, grad_send = moe_gradient(grad)
    back, dgate, dup, hidden, flat_grad = moe_backward(
        grad_send, received, w_in, w_down, 0, kept_from
    )
    grad_second, dgain_moe, drouter = moe_input_gradient(grad, dgates, back)
    grad_first = jnp.where(decoder, grad_first_dec, grad_second)

    dbranch = grad_first.astype(BF16)
    dmixed = dot(dbranch, wout, NT).astype(BF16)
    dq, dkv, diag = attend_back(self_info, bias, qkv, qkv, (0, 1, 2), dmixed, length, width)
    dnormed = dot(dq, wqkv[:, :width], NT) + dot(dkv, wqkv[:, width:], NT)
    dvalues, dgain_self = norm_back(values, scale0, gain[0], dnormed)
    d_tokens = (grad_first + dvalues).astype(BF16)
    dtable = lax.dot_general(
        hot_back, diag, (((0,), (1,)), ((), ())), precision=lax.Precision.HIGHEST,
        preferred_element_type=F32,
    ).reshape(-1)

    left = jnp.where(decoder, low_c, low_m)
    right_enc = dot(left, jnp.where(decoder, jnp.concatenate([dquery, dquery], 1), dmemory), TN)
    dcross_out = dot(mixed_c, dbranch_c, TN)
    dcross = jnp.where(
        decoder, jnp.concatenate([right_enc[:, :width], dcross_out], axis=1), right_enc
    )
    dqkv = jnp.concatenate([dot(low0, dq, TN), dot(low0, dkv, TN)], axis=1)
    dout = dot(mixed0, dbranch, TN)
    flat = received.reshape(-1, width)
    din = jnp.stack([dot(flat, dgate, TN), dot(flat, dup, TN)])
    ddown = dot(hidden, flat_grad, TN)
    dgains = jnp.stack([dgain_self, dgain_moe, jnp.where(decoder, dgain_c, dgain_m)])

    axes = ("dp", "expert")

    def scattered(array, dim, over=axes):
        return lax.psum_scatter(array, over, scatter_dimension=dim, tiled=True).astype(F32)

    counts = scattered(tallies, 0).astype(jnp.int32).reshape(1, 1, 1)
    return (
        outputs.reshape(1, seqs, length, width),
        d_tokens.reshape(1, seqs, length, width),
        scattered(dqkv.astype(BF16), 0)[None],
        scattered(dout.astype(BF16), 0)[None],
        scattered(dcross.astype(BF16), 0)[None],
        scattered(drouter, 0)[None],
        scattered(dgains, 1)[None],
        scattered(dtable, 0)[None],
        scattered(din.astype(BF16), 2, "dp")[None, None],
        scattered(ddown.astype(BF16), 0, "dp")[None, None],
        counts,
    )


def half_pairs(count):
    return (
        [(i, count + i) for i in range(count)],
        [(count + i, i) for i in range(count)],
    )


def solution(mesh):
    placed = (
        P("half", ("dp", "expert"), None, None),
        P("half", ("dp", "expert"), None, None),
        P(None, ("dp", "expert")),
        P("half", ("dp", "expert"), None, None),
        P("half", None, None),
        P("half", None, None),
        P("half", None, None),
        P("half", None, None),
        P("half", None, None),
        P("half", None),
        P("half", "expert", None, None, None),
        P("half", "expert", None, None),
    )
    return jax.shard_map(
        body,
        mesh=mesh,
        in_specs=placed,
        out_specs=(
            P("half", ("dp", "expert"), None, None),
            P("half", ("dp", "expert"), None, None),
            P("half", ("dp", "expert"), None),
            P("half", ("dp", "expert"), None),
            P("half", ("dp", "expert"), None),
            P("half", ("dp", "expert"), None),
            P("half", None, ("dp", "expert")),
            P("half", ("dp", "expert")),
            P("half", "expert", None, None, "dp"),
            P("half", "expert", "dp", None),
            P("half", "dp", "expert"),
        ),
        check_vma=False,
    )
```

```python
import functools

import jax
import jax.numpy as jnp
import numpy as np
from jax import lax
from jax.experimental import pallas as pl
from jax.experimental.pallas import tpu as pltpu
from jax.sharding import PartitionSpec as P

H = 16
BUCKETS = 32
EPS = 1e-06
ENC_STEPS = (12, 16, 23, 32, 46, 64, 91)
DEC_STEPS = (19, 21, 24, 27, 31, 35, 40, 46, 52, 59, 67, 77, 87, 99, 113)
F32 = jnp.float32
BF16 = jnp.bfloat16
MESH = pl.DeviceIdType.MESH
NT = (((1,), (1,)), ((), ()))
TN = (((0,), (0,)), ((), ()))


def dot(a, b, dims=(((1,), (0,)), ((), ()))):
    return lax.dot_general(a, b, dims, preferred_element_type=F32)


def diagonal_buckets(diff):
    apart = np.abs(diff)
    coarse = 8 + sum((apart >= step).astype(np.int32) for step in ENC_STEPS)
    enc = np.where(apart < 8, apart, coarse) + 16 * (diff > 0)
    behind = np.maximum(-diff, 0)
    coarse = 16 + sum((behind >= step).astype(np.int32) for step in DEC_STEPS)
    dec = np.where(behind < 16, behind, coarse)
    return enc.astype(np.int32), dec.astype(np.int32)


def masked_scores(info, seq, bias_ref, query, key_rows, head, lane_mask, length):
    part = jnp.where(lane_mask, query, jnp.zeros_like(query))
    scores = dot(part, key_rows, NT) * 0.125
    if bias_ref is not None:
        row = jnp.broadcast_to(bias_ref[pl.ds(head, 1), :], (length, 2 * length))
        scores = scores + pltpu.roll(row, 0, 1, stride=1, stride_axis=0)[:, :length]
    row_id = lax.broadcasted_iota(jnp.int32, (length, length), 0)
    col_id = lax.broadcasted_iota(jnp.int32, (length, length), 1)
    reach = jnp.where(info[2] > 0, row_id, length)
    return jnp.where((col_id < info[seq]) & (col_id <= reach), scores, -1000000000.0)


def softmax_parts(scores):
    peak = jnp.max(scores, axis=-1, keepdims=True)
    spread = jnp.exp(scores - peak)
    return spread / jnp.sum(spread, axis=-1, keepdims=True)


def attend_kernel(has_bias, info, *refs):
    bias_ref, (q_ref, k_ref, v_ref, out_ref) = (refs[0], refs[1:]) if has_bias else (None, refs)
    length, width = q_ref.shape
    seq = pl.program_id(0)
    low = lax.broadcasted_iota(jnp.int32, (length, 128), 1) < 64

    @pl.loop(0, width // 128)
    def _(pair):
        cols = pl.ds(pl.multiple_of(pair * 128, 128), 128)
        q, k, v = q_ref[:, cols], k_ref[:, cols], v_ref[:, cols]
        mixed = []
        for side in range(2):
            mask = low if side == 0 else jnp.logical_not(low)
            scores = masked_scores(info, seq, bias_ref, q, k, 2 * pair + side, mask, length)
            mixed.append(dot(softmax_parts(scores).astype(BF16), v))
        out_ref[:, cols] = jnp.where(low, mixed[0], mixed[1]).astype(BF16)


def attend_back_kernel(has_bias, info, *refs):
    if has_bias:
        bias_ref, q_ref, k_ref, v_ref, g_ref, dq_ref, dkv_ref, diag_ref = refs
    else:
        bias_ref = diag_ref = None
        q_ref, k_ref, v_ref, g_ref, dq_ref, dkv_ref = refs
    length, width = q_ref.shape
    seq = pl.program_id(0)
    low = lax.broadcasted_iota(jnp.int32, (length, 128), 1) < 64
    if has_bias:
        row_id = lax.broadcasted_iota(jnp.int32, (length, length), 0)
        col_id = lax.broadcasted_iota(jnp.int32, (length, length), 1)
        flip = (row_id + col_id == length - 1).astype(F32).astype(BF16)

        @pl.when(seq == 0)
        def _():
            diag_ref[...] = jnp.zeros_like(diag_ref)

    @pl.loop(0, width // 128)
    def _(pair):
        cols = pl.ds(pl.multiple_of(pair * 128, 128), 128)
        q, k, v, g = q_ref[:, cols], k_ref[:, cols], v_ref[:, cols], g_ref[:, cols]
        dqs, dks, dvs = [], [], []
        for side in range(2):
            mask = low if side == 0 else jnp.logical_not(low)
            head = 2 * pair + side
            probs = softmax_parts(masked_scores(info, seq, bias_ref, q, k, head, mask, length))
            part = jnp.where(mask, g, jnp.zeros_like(g))
            dweights = dot(part, v, NT)
            dvs.append(dot(probs.astype(BF16), g, TN))
            dscores = probs * (dweights - jnp.sum(dweights * probs, axis=-1, keepdims=True))
            dlow = dscores.astype(BF16)
            dqs.append(dot(dlow, k))
            dks.append(dot(dlow, q, TN))
            if has_bias:
                upside = dot(flip, dlow)
                wide = jnp.concatenate([upside, jnp.zeros((length, length), F32)], axis=1)
                turned = pltpu.roll(wide, 0, 1, stride=1, stride_axis=0)
                diag_ref[pl.ds(head, 1), :] += jnp.sum(turned, axis=0, keepdims=True)
        dq_ref[:, cols] = (jnp.where(low, dqs[0], dqs[1]) * 0.125).astype(BF16)
        dkv_ref[:, cols] = (jnp.where(low, dks[0], dks[1]) * 0.125).astype(BF16)
        vcols = pl.ds(pl.multiple_of(width + pair * 128, 128), 128)
        dkv_ref[:, vcols] = jnp.where(low, dvs[0], dvs[1]).astype(BF16)


def attend(info, bias, q, kv, blocks, length, width):
    rows = q.shape[0]
    seqs = rows // length
    specs = [
        pl.BlockSpec((length, width), lambda s, b=b: (s, b)) for b in blocks
    ]
    lead = [] if bias is None else [pl.BlockSpec(bias.shape, lambda s: (0, 0))]
    args = [] if bias is None else [bias]
    return pl.pallas_call(
        functools.partial(attend_kernel, bias is not None),
        grid=(seqs,),
        in_specs=[pl.BlockSpec(memory_space=pltpu.SMEM)] + lead + specs,
        out_specs=pl.BlockSpec((length, width), lambda s: (s, 0)),
        out_shape=jax.ShapeDtypeStruct((rows, width), BF16),
        name="attend",
    )(info, *args, q, kv, kv)


def attend_back(info, bias, q, kv, blocks, grad, length, width):
    rows = q.shape[0]
    seqs = rows // length
    specs = [
        pl.BlockSpec((length, width), lambda s, b=b: (s, b)) for b in (*blocks, 0)
    ]
    lead = [] if bias is None else [pl.BlockSpec(bias.shape, lambda s: (0, 0))]
    args = [] if bias is None else [bias]
    out_specs = [
        pl.BlockSpec((length, width), lambda s: (s, 0)),
        pl.BlockSpec((length, 2 * width), lambda s: (s, 0)),
    ]
    out_shape = [
        jax.ShapeDtypeStruct((rows, width), BF16),
        jax.ShapeDtypeStruct((rows, 2 * width), BF16),
    ]
    if bias is not None:
        out_specs.append(pl.BlockSpec(bias.shape, lambda s: (0, 0)))
        out_shape.append(jax.ShapeDtypeStruct(bias.shape, F32))
    return pl.pallas_call(
        functools.partial(attend_back_kernel, bias is not None),
        grid=(seqs,),
        in_specs=[pl.BlockSpec(memory_space=pltpu.SMEM)] + lead + specs,
        out_specs=out_specs,
        out_shape=out_shape,
        name="attend_back",
    )(info, *args, q, kv, kv, grad)


def norm_parts(values, gain):
    scale = lax.rsqrt(jnp.mean(values * values, axis=-1, keepdims=True) + EPS)
    return values * scale * gain, scale


def norm_back(values, scale, gain, grad):
    unit = values * scale
    gain_grad = jnp.sum(grad * unit, axis=0)
    pushed = grad * gain
    back = scale * (pushed - unit * jnp.mean(pushed * unit, axis=-1, keepdims=True))
    return back, gain_grad


def gelu_parts(gate):
    c = 0.7978845608028654
    inner = c * (gate + 0.044715 * gate * gate * gate)
    t = jnp.tanh(inner)
    value = 0.5 * gate * (1.0 + t)
    slope = 0.5 * (1.0 + t) + 0.5 * gate * (1.0 - t * t) * c * (1.0 + 3.0 * 0.044715 * gate * gate)
    return value, slope


def moe_forward(send, w_in, w_down, turn, kept_from):
    experts, rows, width = send.shape
    arrived = lax.all_to_all(send, "expert", split_axis=0, concat_axis=0, tiled=True)
    flat = arrived.reshape(-1, width)
    value, _ = gelu_parts(dot(flat, w_in[0]))
    hidden = (value * dot(flat, w_in[1])).astype(BF16)
    result = dot(hidden, w_down).astype(BF16).reshape(send.shape)
    back = lax.all_to_all(result, "expert", split_axis=0, concat_axis=0, tiled=True)
    if kept_from is None:
        return back, arrived
    mine = lax.axis_index("half") == turn
    return jnp.where(mine, back, kept_from[0]), jnp.where(mine, arrived, kept_from[1])


def expert_parts(flat, flat_grad, w_in, w_down):
    up = dot(flat, w_in[1])
    value, slope = gelu_parts(dot(flat, w_in[0]))
    hidden = (value * up).astype(BF16)
    dhidden = dot(flat_grad, w_down, NT)
    return (dhidden * up * slope).astype(BF16), (dhidden * value).astype(BF16), hidden


def moe_backward(grad_send, received, w_in, w_down, turn, kept_from):
    width = grad_send.shape[2]
    arrived = lax.all_to_all(grad_send, "expert", split_axis=0, concat_axis=0, tiled=True)
    flat_grad = arrived.reshape(-1, width)
    flat = received.reshape(-1, width)
    dgate, dup, hidden = expert_parts(flat, flat_grad, w_in, w_down)
    drows = (dot(dgate, w_in[0], NT) + dot(dup, w_in[1], NT)).astype(BF16)
    back = lax.all_to_all(
        drows.reshape(arrived.shape), "expert", split_axis=0, concat_axis=0, tiled=True
    )
    out = (back, dgate, dup, hidden, flat_grad)
    if kept_from is None:
        return out
    mine = lax.axis_index("half") == turn
    return tuple(jnp.where(mine, a, b) for a, b in zip(out, kept_from))


def flipped(value, bit):
    step = 1 << bit
    return value + step * (1 - 2 * (value // step % 2))


def greet(partners):
    barrier = pltpu.get_barrier_semaphore()
    for partner in partners:
        pl.semaphore_signal(barrier, inc=1, device_id=partner, device_id_type=MESH)
    pl.semaphore_wait(barrier, len(partners))


def dense_kernel(starts, stages, ahead, *refs):
    xt_ref, dy_ref, small_ref, out_ref, small_out = refs[:5]
    xp, dyp, small_in = refs[5:8]
    sums = refs[8 : 8 + stages]
    parts = refs[8 + stages : 8 + 2 * stages]
    sx, rx, sy, ry, ss, rs, sk, rk = refs[8 + 2 * stages :]
    chunks = dy_ref.shape[0]
    half_rows = xp.shape[1]
    dp, me = lax.axis_index("dp"), lax.axis_index("expert")
    peer = {"dp": 1 - dp}
    partners = [{"expert": flipped(me, k)} for k in range(stages)]
    bits = [me // (1 << k) % 2 for k in range(stages)]
    greet([peer] + partners)

    def send(src, dst, out_sem, in_sem, device):
        return pltpu.make_async_remote_copy(
            src_ref=src,
            dst_ref=dst,
            send_sem=out_sem,
            recv_sem=in_sem,
            device_id=device,
            device_id_type=MESH,
        )

    def send_x(g):
        rows = pl.ds(pl.multiple_of((1 - dp) * half_rows, half_rows), half_rows)
        return send(xt_ref.at[g, rows], xp.at[g], sx.at[g], rx.at[g], peer)

    def send_dy(c):
        return send(dy_ref.at[c], dyp.at[c], sy.at[c], ry.at[c], peer)

    def send_small(step):
        src = small_ref if step == 0 else small_out.at[step - 1]
        device = peer if step == 0 else partners[step - 1]
        return send(src, small_in.at[step], ss.at[step], rs.at[step], device)

    def send_part(k, c):
        return send(
            sums[k].at[c, :, 1 - bits[k]], parts[k].at[c], sk.at[k, c], rk.at[k, c], partners[k]
        )

    send_small(0).start()
    for g in range(len(starts)):
        send_x(g).start()
        if g == 0:
            for c in range(ahead):
                send_dy(c).start()

    def step(i, carry):
        @pl.when(i < chunks)
        def _():
            @pl.when(i + ahead < chunks)
            def _():
                send_dy(i + ahead).start()

            group = jnp.int32(0)
            for g, first in enumerate(starts):
                if g:
                    group = group + (i >= first).astype(jnp.int32)

                @pl.when(i == first)
                def _(g=g):
                    send_x(g).wait_recv()

            send_dy(i).wait_recv()
            rows = pl.ds(pl.multiple_of(dp * half_rows, half_rows), half_rows)
            total = dot(xt_ref[group, rows], dy_ref[i]) + dot(xp[group], dyp[i])
            sums[0][i] = total.astype(BF16).reshape(sums[0].shape[1:])
            send_part(0, i).start()

        for k in range(stages):
            c = i - 1 - k

            @pl.when((c >= 0) & (c < chunks))
            def _(k=k, c=c):
                send_part(k, c).wait_recv()
                total = sums[k][c, :, bits[k]].astype(F32) + parts[k][c].astype(F32)
                if k + 1 < stages:
                    sums[k + 1][c] = total.astype(BF16).reshape(sums[k + 1].shape[1:])
                    send_part(k + 1, c).start()
                else:
                    out_ref[c] = total[0]

        for j in range(stages + 1):

            @pl.when(i == j)
            def _(j=j):
                send_small(j).wait_recv()
                own = small_ref[...] if j == 0 else small_out[j - 1]
                small_out[j] = own + small_in[j]
                if j < stages:
                    send_small(j + 1).start()

        return carry

    lax.fori_loop(0, chunks + stages, step, 0)

    def finish(c, carry):
        send_dy(c).wait_send()
        for k in range(stages):
            send_part(k, c).wait_send()
        return carry

    lax.fori_loop(0, chunks, finish, 0)
    for g in range(len(starts)):
        send_x(g).wait_send()
    for j in range(stages + 1):
        send_small(j).wait_send()


def dense_gradients(pairs, small, experts):
    chunk = 512
    rows, width = pairs[0][0].shape
    xt = jnp.stack([jnp.transpose(x) for x, _ in pairs])
    dy = jnp.concatenate([y for _, y in pairs], axis=1)
    chunks = dy.shape[1] // chunk
    dy = jnp.transpose(dy.reshape(rows, chunks, chunk), (1, 0, 2))
    starts, at = [], 0
    for _, y in pairs:
        starts.append(at)
        at += y.shape[1] // chunk
    stages = experts.bit_length() - 1
    own = width // (2 * experts)
    vmem = pl.BlockSpec(memory_space=pltpu.VMEM)
    dma = pltpu.SemaphoreType.DMA
    scratch = [
        pltpu.VMEM((len(pairs), width // 2, rows), BF16),
        pltpu.VMEM(dy.shape, BF16),
        pltpu.VMEM((stages + 1, *small.shape), F32),
    ]
    scratch += [
        pltpu.VMEM((chunks, experts >> (k + 1), 2, own, chunk), BF16) for k in range(stages)
    ]
    scratch += [pltpu.VMEM((chunks, experts >> (k + 1), own, chunk), BF16) for k in range(stages)]
    scratch += [
        dma((len(pairs),)),
        dma((len(pairs),)),
        dma((chunks,)),
        dma((chunks,)),
        dma((stages + 1,)),
        dma((stages + 1,)),
        dma((stages, chunks)),
        dma((stages, chunks)),
    ]
    out, sums = pl.pallas_call(
        functools.partial(dense_kernel, tuple(starts), stages, 4),
        in_specs=[vmem] * 3,
        out_specs=[vmem] * 2,
        out_shape=[
            jax.ShapeDtypeStruct((chunks, own, chunk), F32),
            jax.ShapeDtypeStruct((stages + 1, *small.shape), F32),
        ],
        scratch_shapes=scratch,
        compiler_params=pltpu.CompilerParams(
            collective_id=0, has_side_effects=True, vmem_limit_bytes=56 << 20
        ),
        name="dense_gradients",
    )(xt, dy, small)
    results = []
    for (_, y), first in zip(pairs, starts):
        count = y.shape[1] // chunk
        part = jnp.transpose(out[first : first + count], (1, 0, 2))
        results.append(part.reshape(own, count * chunk))
    return results, sums[stages]


def body(
    tokens,
    cotangent,
    lengths,
    routes,
    self_qkv,
    self_out,
    cross_weights,
    router,
    gains,
    bias_table,
    expert_in,
    expert_out,
):
    _, seqs, length, width = tokens.shape
    heads = H
    experts = router.shape[2]
    top = routes.shape[3]
    capacity = (5 * top * length + 4 * experts - 1) // (4 * experts)
    block_rows = -(-seqs * capacity // 16) * 16
    rows = seqs * length
    slots = experts * block_rows
    half_index = lax.axis_index("half")
    decoder = half_index == 1
    wqkv, wout, wcross, wrouter, gain = (
        self_qkv[0],
        self_out[0],
        cross_weights[0],
        router[0],
        gains[0],
    )
    w_in, w_down = expert_in[0, 0], expert_out[0, 0]

    column = np.arange(2 * length)
    hot, hot_back = (
        (
            jnp.where(decoder, *reversed(diagonal_buckets(diff)))[:, None]
            == jnp.arange(BUCKETS)[None, :]
        ).astype(F32)
        for diff in (np.where(column < length, column, column - 2 * length), column - length + 1)
    )
    bias = lax.dot_general(
        bias_table[0].reshape(BUCKETS, heads),
        hot,
        (((0,), (1,)), ((), ())),
        precision=lax.Precision.HIGHEST,
        preferred_element_type=F32,
    )
    own_lengths = jnp.where(decoder, lengths[1], lengths[0])
    self_info = jnp.concatenate([own_lengths, half_index[None]]).astype(jnp.int32)
    cross_info = jnp.concatenate([lengths[0], jnp.zeros((1,), jnp.int32)]).astype(jnp.int32)

    order = jnp.transpose(routes[0], (0, 2, 1)).reshape(seqs, top * length)
    expert_ids = jnp.arange(experts, dtype=jnp.int32)
    picked = (order[:, :, None] == expert_ids).astype(BF16)
    earlier = np.tril(np.ones((top * length, top * length), np.float32), -1).astype(BF16)
    before = jnp.einsum("pq,sqe->spe", earlier, picked, preferred_element_type=F32)
    place = jnp.sum(before * picked.astype(F32), axis=2).astype(jnp.int32)
    kept = place < capacity
    base = order * block_rows + jnp.arange(seqs, dtype=jnp.int32)[:, None] * capacity
    target = jnp.where(kept, base + place, -1).reshape(seqs, top, length)
    target = jnp.transpose(target, (1, 0, 2)).reshape(top, rows)
    slot_ids = jnp.arange(slots, dtype=jnp.int32)
    spots = (target[:, :, None] == slot_ids).astype(BF16)
    both = jnp.sum(spots.astype(F32), axis=0).astype(BF16)
    stacked = spots.reshape(top * rows, slots)
    kept_hot = picked.astype(F32) * kept[:, :, None].astype(F32)
    kept_count = jnp.sum(kept_hot, axis=(0, 1))
    all_count = jnp.sum(picked.astype(F32), axis=(0, 1))
    tallies = jnp.concatenate([kept_count, all_count - kept_count])
    route_hot = (routes[0].reshape(rows, top, 1) == expert_ids).astype(F32)

    def route(values):
        normed, scale = norm_parts(values, gain[1])
        low = normed.astype(BF16)
        rest = (normed - low.astype(F32)).astype(BF16)
        logits = dot(low, wrouter) + dot(rest, wrouter)
        probs = jax.nn.softmax(logits, axis=-1)
        chosen = jnp.sum(probs[:, None, :] * route_hot, axis=-1)
        total = jnp.sum(chosen, axis=-1, keepdims=True)
        gates = chosen / total
        send = dot(both, low, TN).astype(BF16).reshape(experts, block_rows, width)
        return dict(scale=scale, low=low, probs=probs, gates=gates, total=total, send=send)

    def fetch(returned):
        flat = returned.reshape(slots, width)
        return dot(stacked, flat).reshape(top, rows, width)

    def combine(values, gates, results):
        return values + jnp.sum(jnp.transpose(gates)[:, :, None] * results, axis=0)

    values = tokens[0].reshape(rows, width).astype(F32)
    normed, scale0 = norm_parts(values, gain[0])
    low0 = normed.astype(BF16)
    qkv = dot(low0, wqkv).astype(BF16)
    mixed0 = attend(self_info, bias, qkv, qkv, (0, 1, 2), length, width)
    first = values + dot(mixed0, wout)

    state = route(first)
    returned, received = moe_forward(state["send"], w_in, w_down, 0, None)
    final_enc = combine(first, state["gates"], fetch(returned))
    normed, scale_m = norm_parts(final_enc, gain[2])
    low_m = normed.astype(BF16)
    memory = dot(low_m, wcross).astype(BF16)
    names = ("half", "dp", "expert")
    forward_pairs, back_pairs = half_pairs(lax.axis_size("dp") * lax.axis_size("expert"))
    memory = lax.ppermute(memory, names, forward_pairs)

    normed, scale_c = norm_parts(first, gain[2])
    low_c = normed.astype(BF16)
    query = dot(low_c, wcross[:, :width]).astype(BF16)
    mixed_c = attend(cross_info, None, query, memory, (0, 0, 1), length, width)
    second = jnp.where(decoder, first + dot(mixed_c, wcross[:, width:]), first)

    state = route(second)
    returned, received = moe_forward(state["send"], w_in, w_down, 1, (returned, received))
    results = fetch(returned)
    final = combine(second, state["gates"], results)
    outputs = final.astype(BF16)

    def moe_gradient(grad):
        dgates = jnp.transpose(jnp.sum(grad[None] * results, axis=-1))
        spread = (jnp.transpose(state["gates"])[:, :, None] * grad[None]).astype(BF16)
        send = dot(stacked, spread.reshape(top * rows, width), TN)
        return dgates, send.astype(BF16).reshape(experts, block_rows, width)

    def moe_input_gradient(grad, dgates, back):
        gates, total, probs = state["gates"], state["total"], state["probs"]
        dchosen = (dgates - jnp.sum(dgates * gates, axis=-1, keepdims=True)) / total
        dprobs = jnp.sum(dchosen[:, :, None] * route_hot, axis=1)
        dlogits = probs * (dprobs - jnp.sum(dprobs * probs, axis=-1, keepdims=True))
        dnormed = dot(both, back.reshape(slots, width)) + lax.dot_general(
            dlogits, wrouter.astype(F32), NT, preferred_element_type=F32
        )
        dvalues, dgain = norm_back(second, state["scale"], gain[1], dnormed)
        normed = second * state["scale"] * gain[1]
        drouter = lax.dot_general(
            normed, dlogits, TN, precision=lax.Precision.HIGHEST, preferred_element_type=F32
        )
        return grad + dvalues, dgain, drouter

    grad_dec = cotangent[0].reshape(rows, width).astype(F32)
    dgates, grad_send = moe_gradient(grad_dec)
    kept_from = moe_backward(grad_send, received, w_in, w_down, 1, None)
    grad_second, _, _ = moe_input_gradient(grad_dec, dgates, kept_from[0])

    dbranch_c = grad_second.astype(BF16)
    dmixed_c = dot(dbranch_c, wcross[:, width:], NT).astype(BF16)
    dquery, dmemory = attend_back(
        cross_info, None, query, memory, (0, 0, 1), dmixed_c, length, width
    )
    dmemory = lax.ppermute(dmemory, names, back_pairs)
    dnormed = dot(dquery, wcross[:, :width], NT)
    dvalues, dgain_c = norm_back(first, scale_c, gain[2], dnormed)
    grad_first_dec = grad_second + dvalues

    dnormed = dot(dmemory, wcross, NT)
    dvalues, dgain_m = norm_back(final_enc, scale_m, gain[2], dnormed)
    grad = jnp.where(decoder, grad_dec, grad_dec + dvalues)
    dgates, grad_send = moe_gradient(grad)
    back, dgate, dup, hidden, flat_grad = moe_backward(
        grad_send, received, w_in, w_down, 0, kept_from
    )
    grad_second, dgain_moe, drouter = moe_input_gradient(grad, dgates, back)
    grad_first = jnp.where(decoder, grad_first_dec, grad_second)

    dbranch = grad_first.astype(BF16)
    dmixed = dot(dbranch, wout, NT).astype(BF16)
    dq, dkv, diag = attend_back(self_info, bias, qkv, qkv, (0, 1, 2), dmixed, length, width)
    dnormed = dot(dq, wqkv[:, :width], NT) + dot(dkv, wqkv[:, width:], NT)
    dvalues, dgain_self = norm_back(values, scale0, gain[0], dnormed)
    d_tokens = (grad_first + dvalues).astype(BF16)
    dtable = lax.dot_general(
        hot_back, diag, (((0,), (1,)), ((), ())), precision=lax.Precision.HIGHEST,
        preferred_element_type=F32,
    ).reshape(-1)

    left = jnp.where(decoder, low_c, low_m)
    right = jnp.where(decoder, dquery, dmemory[:, :width])
    left_out = jnp.where(decoder, mixed_c, low_m)
    right_out = jnp.where(decoder, dbranch_c, dmemory[:, width:])
    pairs = [
        (low0, jnp.concatenate([dq, dkv], axis=1)),
        (mixed0, dbranch),
        (left, right),
        (left_out, right_out),
    ]
    extra = jnp.concatenate([dtable, tallies, jnp.zeros((width - dtable.shape[0] - tallies.shape[0],), F32)])
    small = jnp.concatenate(
        [
            jnp.transpose(drouter),
            dgain_self[None],
            dgain_moe[None],
            jnp.where(decoder, dgain_c, dgain_m)[None],
            extra[None],
        ]
    )
    small = jnp.pad(small, ((0, -small.shape[0] % 8), (0, 0)))
    (dqkv, dout, dcross_a, dcross_b), small = dense_gradients(pairs, small, experts)
    dp_index = lax.axis_index("dp")
    place = dp_index * experts + lax.axis_index("expert")
    own = width // (2 * experts)
    mine = lax.dynamic_slice_in_dim(small[: experts + 3], place * own, own, 1)
    tail = small[experts + 3]
    own_table = dtable.shape[0] // (2 * experts)
    d_table = lax.dynamic_slice_in_dim(tail, place * own_table, own_table)
    counts = lax.dynamic_slice_in_dim(tail, dtable.shape[0] + place, 1).astype(jnp.int32)

    swap = [(0, 1), (1, 0)]
    ff = w_down.shape[0]
    span = ff // 2
    rows_own = received.reshape(-1, width)
    rows_peer = lax.ppermute(rows_own, "dp", swap)
    grad_peer = lax.ppermute(flat_grad, "dp", swap)
    in_half = lax.dynamic_slice_in_dim(w_in, dp_index * span, span, 2)
    down_half = lax.dynamic_slice_in_dim(w_down, dp_index * span, span, 0)
    peer_parts = expert_parts(rows_peer, grad_peer, in_half, down_half)
    own_parts = [
        lax.dynamic_slice_in_dim(a, dp_index * span, span, 1) for a in (dgate, dup, hidden)
    ]
    dgate, dup, hidden = [jnp.concatenate(p) for p in zip(own_parts, peer_parts)]
    all_rows = jnp.concatenate([rows_own, rows_peer])
    all_grad = jnp.concatenate([flat_grad, grad_peer])
    din = jnp.stack([dot(all_rows, dgate, TN), dot(all_rows, dup, TN)])
    ddown = dot(hidden, all_grad, TN)
    return (
        outputs.reshape(1, seqs, length, width),
        d_tokens.reshape(1, seqs, length, width),
        dqkv[None],
        dout[None],
        jnp.concatenate([dcross_a, dcross_b], axis=1)[None],
        jnp.transpose(mine[:experts])[None],
        mine[experts:][None],
        d_table[None],
        din[None, None],
        ddown[None, None],
        counts.reshape(1, 1, 1),
    )


def half_pairs(count):
    return (
        [(i, count + i) for i in range(count)],
        [(count + i, i) for i in range(count)],
    )


def solution(mesh):
    placed = (
        P("half", ("dp", "expert"), None, None),
        P("half", ("dp", "expert"), None, None),
        P(None, ("dp", "expert")),
        P("half", ("dp", "expert"), None, None),
        P("half", None, None),
        P("half", None, None),
        P("half", None, None),
        P("half", None, None),
        P("half", None, None),
        P("half", None),
        P("half", "expert", None, None, None),
        P("half", "expert", None, None),
    )
    return jax.shard_map(
        body,
        mesh=mesh,
        in_specs=placed,
        out_specs=(
            P("half", ("dp", "expert"), None, None),
            P("half", ("dp", "expert"), None, None),
            P("half", ("dp", "expert"), None),
            P("half", ("dp", "expert"), None),
            P("half", ("dp", "expert"), None),
            P("half", ("dp", "expert"), None),
            P("half", None, ("dp", "expert")),
            P("half", ("dp", "expert")),
            P("half", "expert", None, None, "dp"),
            P("half", "expert", "dp", None),
            P("half", "dp", "expert"),
        ),
        check_vma=False,
    )
```

```python
import functools

import jax
import jax.numpy as jnp
import numpy as np
from jax import lax
from jax.experimental import pallas as pl
from jax.experimental.pallas import tpu as pltpu
from jax.sharding import PartitionSpec as P

H = 16
BUCKETS = 32
EPS = 1e-06
ENC_STEPS = (12, 16, 23, 32, 46, 64, 91)
DEC_STEPS = (19, 21, 24, 27, 31, 35, 40, 46, 52, 59, 67, 77, 87, 99, 113)
F32 = jnp.float32
BF16 = jnp.bfloat16
MESH = pl.DeviceIdType.MESH
NT = (((1,), (1,)), ((), ()))
TN = (((0,), (0,)), ((), ()))


def dot(a, b, dims=(((1,), (0,)), ((), ()))):
    return lax.dot_general(a, b, dims, preferred_element_type=F32)


def diagonal_buckets(diff):
    apart = np.abs(diff)
    coarse = 8 + sum((apart >= step).astype(np.int32) for step in ENC_STEPS)
    enc = np.where(apart < 8, apart, coarse) + 16 * (diff > 0)
    behind = np.maximum(-diff, 0)
    coarse = 16 + sum((behind >= step).astype(np.int32) for step in DEC_STEPS)
    dec = np.where(behind < 16, behind, coarse)
    return enc.astype(np.int32), dec.astype(np.int32)


def masked_scores(info, seq, bias_ref, query, key_rows, head, lane_mask, length):
    part = jnp.where(lane_mask, query, jnp.zeros_like(query))
    scores = dot(part, key_rows, NT) * 0.125
    if bias_ref is not None:
        row = jnp.broadcast_to(bias_ref[pl.ds(head, 1), :], (length, 2 * length))
        scores = scores + pltpu.roll(row, 0, 1, stride=1, stride_axis=0)[:, :length]
    row_id = lax.broadcasted_iota(jnp.int32, (length, length), 0)
    col_id = lax.broadcasted_iota(jnp.int32, (length, length), 1)
    reach = jnp.where(info[2] > 0, row_id, length)
    return jnp.where((col_id < info[seq]) & (col_id <= reach), scores, -1000000000.0)


def softmax_parts(scores):
    peak = jnp.max(scores, axis=-1, keepdims=True)
    spread = jnp.exp(scores - peak)
    return spread / jnp.sum(spread, axis=-1, keepdims=True)


def attend_kernel(has_bias, info, *refs):
    bias_ref, (q_ref, k_ref, v_ref, out_ref) = (refs[0], refs[1:]) if has_bias else (None, refs)
    length, width = q_ref.shape
    seq = pl.program_id(0)
    low = lax.broadcasted_iota(jnp.int32, (length, 128), 1) < 64

    @pl.loop(0, width // 128)
    def _(pair):
        cols = pl.ds(pl.multiple_of(pair * 128, 128), 128)
        q, k, v = q_ref[:, cols], k_ref[:, cols], v_ref[:, cols]
        mixed = []
        for side in range(2):
            mask = low if side == 0 else jnp.logical_not(low)
            scores = masked_scores(info, seq, bias_ref, q, k, 2 * pair + side, mask, length)
            mixed.append(dot(softmax_parts(scores).astype(BF16), v))
        out_ref[:, cols] = jnp.where(low, mixed[0], mixed[1]).astype(BF16)


def attend_back_kernel(has_bias, info, *refs):
    if has_bias:
        bias_ref, q_ref, k_ref, v_ref, g_ref, dq_ref, dkv_ref, diag_ref = refs
    else:
        bias_ref = diag_ref = None
        q_ref, k_ref, v_ref, g_ref, dq_ref, dkv_ref = refs
    length, width = q_ref.shape
    seq = pl.program_id(0)
    low = lax.broadcasted_iota(jnp.int32, (length, 128), 1) < 64
    if has_bias:
        row_id = lax.broadcasted_iota(jnp.int32, (length, length), 0)
        col_id = lax.broadcasted_iota(jnp.int32, (length, length), 1)
        flip = (row_id + col_id == length - 1).astype(F32).astype(BF16)

        @pl.when(seq == 0)
        def _():
            diag_ref[...] = jnp.zeros_like(diag_ref)

    @pl.loop(0, width // 128)
    def _(pair):
        cols = pl.ds(pl.multiple_of(pair * 128, 128), 128)
        q, k, v, g = q_ref[:, cols], k_ref[:, cols], v_ref[:, cols], g_ref[:, cols]
        dqs, dks, dvs = [], [], []
        for side in range(2):
            mask = low if side == 0 else jnp.logical_not(low)
            head = 2 * pair + side
            probs = softmax_parts(masked_scores(info, seq, bias_ref, q, k, head, mask, length))
            part = jnp.where(mask, g, jnp.zeros_like(g))
            dweights = dot(part, v, NT)
            dvs.append(dot(probs.astype(BF16), g, TN))
            dscores = probs * (dweights - jnp.sum(dweights * probs, axis=-1, keepdims=True))
            dlow = dscores.astype(BF16)
            dqs.append(dot(dlow, k))
            dks.append(dot(dlow, q, TN))
            if has_bias:
                upside = dot(flip, dlow)
                wide = jnp.concatenate([upside, jnp.zeros((length, length), F32)], axis=1)
                turned = pltpu.roll(wide, 0, 1, stride=1, stride_axis=0)
                diag_ref[pl.ds(head, 1), :] += jnp.sum(turned, axis=0, keepdims=True)
        dq_ref[:, cols] = (jnp.where(low, dqs[0], dqs[1]) * 0.125).astype(BF16)
        dkv_ref[:, cols] = (jnp.where(low, dks[0], dks[1]) * 0.125).astype(BF16)
        vcols = pl.ds(pl.multiple_of(width + pair * 128, 128), 128)
        dkv_ref[:, vcols] = jnp.where(low, dvs[0], dvs[1]).astype(BF16)


def attend(info, bias, q, kv, blocks, length, width):
    rows = q.shape[0]
    seqs = rows // length
    specs = [
        pl.BlockSpec((length, width), lambda s, b=b: (s, b)) for b in blocks
    ]
    lead = [] if bias is None else [pl.BlockSpec(bias.shape, lambda s: (0, 0))]
    args = [] if bias is None else [bias]
    return pl.pallas_call(
        functools.partial(attend_kernel, bias is not None),
        grid=(seqs,),
        in_specs=[pl.BlockSpec(memory_space=pltpu.SMEM)] + lead + specs,
        out_specs=pl.BlockSpec((length, width), lambda s: (s, 0)),
        out_shape=jax.ShapeDtypeStruct((rows, width), BF16),
        name="attend",
    )(info, *args, q, kv, kv)


def attend_back(info, bias, q, kv, blocks, grad, length, width):
    rows = q.shape[0]
    seqs = rows // length
    specs = [
        pl.BlockSpec((length, width), lambda s, b=b: (s, b)) for b in (*blocks, 0)
    ]
    lead = [] if bias is None else [pl.BlockSpec(bias.shape, lambda s: (0, 0))]
    args = [] if bias is None else [bias]
    out_specs = [
        pl.BlockSpec((length, width), lambda s: (s, 0)),
        pl.BlockSpec((length, 2 * width), lambda s: (s, 0)),
    ]
    out_shape = [
        jax.ShapeDtypeStruct((rows, width), BF16),
        jax.ShapeDtypeStruct((rows, 2 * width), BF16),
    ]
    if bias is not None:
        out_specs.append(pl.BlockSpec(bias.shape, lambda s: (0, 0)))
        out_shape.append(jax.ShapeDtypeStruct(bias.shape, F32))
    return pl.pallas_call(
        functools.partial(attend_back_kernel, bias is not None),
        grid=(seqs,),
        in_specs=[pl.BlockSpec(memory_space=pltpu.SMEM)] + lead + specs,
        out_specs=out_specs,
        out_shape=out_shape,
        name="attend_back",
    )(info, *args, q, kv, kv, grad)


def norm_parts(values, gain):
    scale = lax.rsqrt(jnp.mean(values * values, axis=-1, keepdims=True) + EPS)
    return values * scale * gain, scale


def norm_back(values, scale, gain, grad):
    unit = values * scale
    gain_grad = jnp.sum(grad * unit, axis=0)
    pushed = grad * gain
    back = scale * (pushed - unit * jnp.mean(pushed * unit, axis=-1, keepdims=True))
    return back, gain_grad


def gelu_parts(gate):
    c = 0.7978845608028654
    inner = c * (gate + 0.044715 * gate * gate * gate)
    t = jnp.tanh(inner)
    value = 0.5 * gate * (1.0 + t)
    slope = 0.5 * (1.0 + t) + 0.5 * gate * (1.0 - t * t) * c * (1.0 + 3.0 * 0.044715 * gate * gate)
    return value, slope


def moe_forward(send, w_in, w_down, turn, kept_from):
    experts, rows, width = send.shape
    arrived = lax.all_to_all(send, "expert", split_axis=0, concat_axis=0, tiled=True)
    flat = arrived.reshape(-1, width)
    value, _ = gelu_parts(dot(flat, w_in[0]))
    hidden = (value * dot(flat, w_in[1])).astype(BF16)
    result = dot(hidden, w_down).astype(BF16).reshape(send.shape)
    back = lax.all_to_all(result, "expert", split_axis=0, concat_axis=0, tiled=True)
    if kept_from is None:
        return back, arrived
    mine = lax.axis_index("half") == turn
    return jnp.where(mine, back, kept_from[0]), jnp.where(mine, arrived, kept_from[1])


def flipped(value, bit):
    step = 1 << bit
    return value + step * (1 - 2 * (value // step % 2))


def crossed(value, other):
    for bit in range(other.bit_length()):
        if other >> bit & 1:
            value = flipped(value, bit)
    return value


def greet(partners):
    barrier = pltpu.get_barrier_semaphore()
    for partner in partners:
        pl.semaphore_signal(barrier, inc=1, device_id=partner, device_id_type=MESH)
    pl.semaphore_wait(barrier, len(partners))


def remote(src, dst, out_sem, in_sem, device):
    return pltpu.make_async_remote_copy(
        src_ref=src,
        dst_ref=dst,
        send_sem=out_sem,
        recv_sem=in_sem,
        device_id=device,
        device_id_type=MESH,
    )


def tile_loop(count, step, body):
    @pl.loop(0, count // step)
    def _(i):
        body(pl.multiple_of(i * step, step), step)

    if count % step:
        body(count // step * step, count % step)


def far_first(experts, group):
    return [*range(group, experts), *range(1, group)]


def expert_forward_kernel(turn, group, has_prev, *refs):
    send_ref, w_in, w_down = refs[:3]
    refs = refs[3 + 2 * has_prev :]
    back_out, rows_out, wg, wu, wd, rows, back, made, hidden = refs[:9]
    wsem, s1, r1, s2, r2, osem = refs[9:]
    experts, block, width = send_ref.shape
    ff = wd.shape[0]

    @pl.when(lax.axis_index("half") == turn)
    def _():
        me = lax.axis_index("expert")
        greet([{"expert": crossed(me, k)} for k in range(1, experts)])

        def there(k):
            partner = crossed(me, k)
            return remote(send_ref.at[partner], rows.at[me], s1.at[k], r1.at[k], {"expert": partner})

        def home(k):
            partner = crossed(me, k)
            return remote(made.at[partner], back.at[me], s2.at[k], r2.at[k], {"expert": partner})

        for k in far_first(experts, group):
            there(k).start()
        loads = [
            pltpu.make_async_copy(src, dst, wsem.at[i])
            for i, (src, dst) in enumerate(((w_in.at[0], wg), (w_in.at[1], wu), (w_down, wd)))
        ]
        for load in loads:
            load.start()
        rows[me] = send_ref[me]
        for part in range(experts // group):
            for k in range(part * group, part * group + group):
                if k:
                    there(k).wait_recv()
            base = crossed(me // group, part) * group
            if part == 0:
                loads[0].wait()
                loads[1].wait()

            def up_tile(start, size, base=base):
                x = rows[pl.ds(base, group)].reshape(group * block, width)
                cols = pl.ds(start, size)
                value, _ = gelu_parts(dot(x, wg[:, cols]))
                hidden[:, cols] = (value * dot(x, wu[:, cols])).astype(BF16)

            tile_loop(ff, 256, up_tile)
            if part == 0:
                loads[2].wait()

            def down_tile(start, size, base=base):
                cols = pl.ds(start, size)
                y = dot(hidden[...], wd[:, cols]).astype(BF16)
                made[pl.ds(base, group), :, cols] = y.reshape(group, block, size)

            tile_loop(width, 256, down_tile)
            for k in range(part * group, part * group + group):
                if k:
                    home(k).start()
        rows_copy = pltpu.make_async_copy(rows, rows_out, osem.at[0])
        rows_copy.start()
        back[me] = made[me]
        for k in range(1, experts):
            home(k).wait_recv()
        back_copy = pltpu.make_async_copy(back, back_out, osem.at[1])
        back_copy.start()
        for k in range(1, experts):
            there(k).wait_send()
            home(k).wait_send()
        rows_copy.wait()
        back_copy.wait()


def expert_backward_kernel(turn, group, has_prev, *refs):
    send_ref, own_rows, w_in, w_down = refs[:4]
    refs = refs[4 + 5 * has_prev :]
    back_out, mixed_out, hidden_out, rows_out, grad_out = refs[:5]
    wg, wu, wd, grads, back, made, rows_peer, grads_peer = refs[5:13]
    hidden, dgate, dup = refs[13:16]
    wsem, s1, r1, s2, r2, sx, rx, osem = refs[16:]
    experts, block, width = send_ref.shape
    ff = wd.shape[0]
    span = ff // 2
    total = experts * block
    parts = experts // group

    @pl.when(lax.axis_index("half") == turn)
    def _():
        me, dp = lax.axis_index("expert"), lax.axis_index("dp")
        peer = {"dp": 1 - dp}
        greet([{"expert": crossed(me, k)} for k in range(1, experts)] + [peer])

        def there(k):
            partner = crossed(me, k)
            return remote(send_ref.at[partner], grads.at[me], s1.at[k], r1.at[k], {"expert": partner})

        def home(k):
            partner = crossed(me, k)
            return remote(made.at[partner], back.at[me], s2.at[k], r2.at[k], {"expert": partner})

        def base_of(part):
            return crossed(me // group, part) * group

        rows_over = remote(own_rows, rows_peer, sx.at[parts], rx.at[parts], peer)

        def grads_over(part):
            blocks = pl.ds(base_of(part), group)
            return remote(grads.at[blocks], grads_peer.at[blocks], sx.at[part], rx.at[part], peer)

        for k in far_first(experts, group):
            there(k).start()
        loads = [
            pltpu.make_async_copy(src, dst, wsem.at[i])
            for i, (src, dst) in enumerate(((w_in.at[0], wg), (w_in.at[1], wu), (w_down, wd)))
        ]
        for load in loads:
            load.start()
        rows_over.start()
        grads[me] = send_ref[me]
        loads[0].wait()
        loads[1].wait()

        def up_tile(start, size):
            x = own_rows[...].reshape(total, width)
            cols = pl.ds(start, size)
            value, slope = gelu_parts(dot(x, wg[:, cols]))
            up = dot(x, wu[:, cols])
            hidden[:, cols] = (value * up).astype(BF16)
            dup[:, cols] = value.astype(BF16)
            dgate[:, cols] = (up * slope).astype(BF16)

        tile_loop(ff, 256, up_tile)
        loads[2].wait()
        for part in range(parts):
            for k in range(part * group, part * group + group):
                if k:
                    there(k).wait_recv()
            grads_over(part).start()
            base = base_of(part)
            span_rows = pl.ds(pl.multiple_of(base * block, group * block), group * block)

            def hidden_tile(start, size, base=base, span_rows=span_rows):
                dy = grads[pl.ds(base, group)].reshape(group * block, width)
                cols = pl.ds(start, size)
                dhidden = dot(dy, wd[cols, :], NT)
                dgate[span_rows, cols] = (dhidden * dgate[span_rows, cols].astype(F32)).astype(BF16)
                dup[span_rows, cols] = (dhidden * dup[span_rows, cols].astype(F32)).astype(BF16)

            tile_loop(ff, 256, hidden_tile)

            def rows_tile(start, size, base=base, span_rows=span_rows):
                cols = pl.ds(start, size)
                dr = dot(dgate[span_rows, :], wg[cols, :], NT) + dot(dup[span_rows, :], wu[cols, :], NT)
                made[pl.ds(base, group), :, cols] = dr.astype(BF16).reshape(group, block, size)

            tile_loop(width, 256, rows_tile)
            for k in range(part * group, part * group + group):
                if k:
                    home(k).start()
        back[me] = made[me]
        half_cols = pl.ds(pl.multiple_of(dp * span, 128), span)
        outs = [
            (dgate.at[:, half_cols], mixed_out.at[0, 0]),
            (dup.at[:, half_cols], mixed_out.at[1, 0]),
            (hidden.at[:, half_cols], hidden_out.at[0]),
            (own_rows, rows_out.at[0]),
            (grads, grad_out.at[0]),
        ]
        outs = [pltpu.make_async_copy(src, dst, osem.at[i]) for i, (src, dst) in enumerate(outs)]
        for out in outs:
            out.start()

        rows_over.wait_recv()
        for part in range(parts):
            grads_over(part).wait_recv()

        def peer_tile(start, size):
            x = rows_peer[...].reshape(total, width)
            dy = grads_peer[...].reshape(total, width)
            here = pl.ds(pl.multiple_of((1 - dp) * span + start, 128), size)
            cols = pl.ds(pl.multiple_of(dp * span + start, 128), size)
            value, slope = gelu_parts(dot(x, wg[:, cols]))
            up = dot(x, wu[:, cols])
            dhidden = dot(dy, wd[cols, :], NT)
            hidden[:, here] = (value * up).astype(BF16)
            dgate[:, here] = (dhidden * up * slope).astype(BF16)
            dup[:, here] = (dhidden * value).astype(BF16)

        tile_loop(span, 256, peer_tile)
        other_cols = pl.ds(pl.multiple_of((1 - dp) * span, 128), span)
        peers = [
            (dgate.at[:, other_cols], mixed_out.at[0, 1]),
            (dup.at[:, other_cols], mixed_out.at[1, 1]),
            (hidden.at[:, other_cols], hidden_out.at[1]),
            (rows_peer, rows_out.at[1]),
            (grads_peer, grad_out.at[1]),
        ]
        peers = [pltpu.make_async_copy(src, dst, osem.at[5 + i]) for i, (src, dst) in enumerate(peers)]
        for out in peers:
            out.start()
        for k in range(1, experts):
            home(k).wait_recv()
        back_copy = pltpu.make_async_copy(back, back_out, osem.at[10])
        back_copy.start()
        for k in range(1, experts):
            there(k).wait_send()
            home(k).wait_send()
        rows_over.wait_send()
        for part in range(parts):
            grads_over(part).wait_send()
        for out in [*outs, *peers, back_copy]:
            out.wait()


def group_of(experts, block):
    group = 1
    while group * 2 * block <= 320 and group * 2 <= experts:
        group *= 2
    return group


def expert_call(kernel, turn, inputs, weights, prev, out_shape, scratch, name):
    experts, block, _ = inputs[0].shape
    vmem, hbm = pl.BlockSpec(memory_space=pltpu.VMEM), pl.BlockSpec(memory_space=pl.ANY)
    prev = list(prev or [])
    first = len(inputs) + len(weights)
    return pl.pallas_call(
        functools.partial(kernel, turn, group_of(experts, block), bool(prev)),
        in_specs=[vmem] * len(inputs) + [hbm] * (len(weights) + len(prev)),
        out_specs=[hbm] * len(out_shape),
        out_shape=out_shape,
        input_output_aliases={first + i: i for i in range(len(prev))},
        scratch_shapes=scratch,
        compiler_params=pltpu.CompilerParams(
            collective_id=1 + turn + 2 * (len(inputs) - 1),
            has_side_effects=True,
            vmem_limit_bytes=60 << 20,
        ),
        name=name,
    )(*inputs, *weights, *prev)


def moe_forward(send, w_in, w_down, turn, prev):
    experts, block, width = send.shape
    ff = w_down.shape[0]
    group = group_of(experts, block)
    dma = pltpu.SemaphoreType.DMA
    scratch = [
        pltpu.VMEM((width, ff), BF16),
        pltpu.VMEM((width, ff), BF16),
        pltpu.VMEM((ff, width), BF16),
        *[pltpu.VMEM(send.shape, BF16)] * 3,
        pltpu.VMEM((group * block, ff), BF16),
        dma((3,)),
        *[dma((experts,))] * 4,
        dma((2,)),
    ]
    out_shape = [jax.ShapeDtypeStruct(send.shape, BF16)] * 2
    return expert_call(
        expert_forward_kernel, turn, [send], [w_in, w_down], prev, out_shape, scratch, "moe_forward"
    )


def moe_backward(grad_send, received, w_in, w_down, turn, prev):
    experts, block, width = grad_send.shape
    ff = w_down.shape[0]
    total = experts * block
    parts = experts // group_of(experts, block)
    dma = pltpu.SemaphoreType.DMA
    scratch = [
        pltpu.VMEM((width, ff), BF16),
        pltpu.VMEM((width, ff), BF16),
        pltpu.VMEM((ff, width), BF16),
        *[pltpu.VMEM(grad_send.shape, BF16)] * 5,
        *[pltpu.VMEM((total, ff), BF16)] * 3,
        dma((3,)),
        *[dma((experts,))] * 4,
        dma((parts + 1,)),
        dma((parts + 1,)),
        dma((11,)),
    ]
    out_shape = [
        jax.ShapeDtypeStruct(grad_send.shape, BF16),
        jax.ShapeDtypeStruct((2, 2, total, ff // 2), BF16),
        jax.ShapeDtypeStruct((2, total, ff // 2), BF16),
        jax.ShapeDtypeStruct((2, *grad_send.shape), BF16),
        jax.ShapeDtypeStruct((2, *grad_send.shape), BF16),
    ]
    return expert_call(
        expert_backward_kernel,
        turn,
        [grad_send, received],
        [w_in, w_down],
        prev,
        out_shape,
        scratch,
        "moe_backward",
    )


def dense_kernel(starts, stages, ahead, *refs):
    xt_ref, dy_ref, small_ref, out_ref, small_out = refs[:5]
    xp, dyp, small_in = refs[5:8]
    sums = refs[8 : 8 + stages]
    parts = refs[8 + stages : 8 + 2 * stages]
    sx, rx, sy, ry, ss, rs, sk, rk = refs[8 + 2 * stages :]
    chunks = dy_ref.shape[0]
    half_rows = xp.shape[1]
    dp, me = lax.axis_index("dp"), lax.axis_index("expert")
    peer = {"dp": 1 - dp}
    partners = [{"expert": flipped(me, k)} for k in range(stages)]
    bits = [me // (1 << k) % 2 for k in range(stages)]
    greet([peer] + partners)

    def send_x(g):
        rows = pl.ds(pl.multiple_of((1 - dp) * half_rows, half_rows), half_rows)
        return remote(xt_ref.at[g, rows], xp.at[g], sx.at[g], rx.at[g], peer)

    def send_dy(c):
        return remote(dy_ref.at[c], dyp.at[c], sy.at[c], ry.at[c], peer)

    def send_small(step):
        src = small_ref if step == 0 else small_out.at[step - 1]
        device = peer if step == 0 else partners[step - 1]
        return remote(src, small_in.at[step], ss.at[step], rs.at[step], device)

    def send_part(k, c):
        return remote(
            sums[k].at[c, :, 1 - bits[k]], parts[k].at[c], sk.at[k, c], rk.at[k, c], partners[k]
        )

    send_small(0).start()
    for g in range(len(starts)):
        send_x(g).start()
        if g == 0:
            for c in range(ahead):
                send_dy(c).start()

    def step(i, carry):
        @pl.when(i < chunks)
        def _():
            @pl.when(i + ahead < chunks)
            def _():
                send_dy(i + ahead).start()

            group = jnp.int32(0)
            for g, first in enumerate(starts):
                if g:
                    group = group + (i >= first).astype(jnp.int32)

                @pl.when(i == first)
                def _(g=g):
                    send_x(g).wait_recv()

            send_dy(i).wait_recv()
            rows = pl.ds(pl.multiple_of(dp * half_rows, half_rows), half_rows)
            total = dot(xt_ref[group, rows], dy_ref[i]) + dot(xp[group], dyp[i])
            sums[0][i] = total.astype(BF16).reshape(sums[0].shape[1:])
            send_part(0, i).start()

        for k in range(stages):
            c = i - 1 - k

            @pl.when((c >= 0) & (c < chunks))
            def _(k=k, c=c):
                send_part(k, c).wait_recv()
                total = sums[k][c, :, bits[k]].astype(F32) + parts[k][c].astype(F32)
                if k + 1 < stages:
                    sums[k + 1][c] = total.astype(BF16).reshape(sums[k + 1].shape[1:])
                    send_part(k + 1, c).start()
                else:
                    out_ref[c] = total[0]

        for j in range(stages + 1):

            @pl.when(i == j)
            def _(j=j):
                send_small(j).wait_recv()
                own = small_ref[...] if j == 0 else small_out[j - 1]
                small_out[j] = own + small_in[j]
                if j < stages:
                    send_small(j + 1).start()

        return carry

    lax.fori_loop(0, chunks + stages, step, 0)

    def finish(c, carry):
        send_dy(c).wait_send()
        for k in range(stages):
            send_part(k, c).wait_send()
        return carry

    lax.fori_loop(0, chunks, finish, 0)
    for g in range(len(starts)):
        send_x(g).wait_send()
    for j in range(stages + 1):
        send_small(j).wait_send()


def dense_gradients(pairs, small, experts):
    chunk = 512
    rows, width = pairs[0][0].shape
    xt = jnp.stack([jnp.transpose(x) for x, _ in pairs])
    dy = jnp.concatenate([y for _, y in pairs], axis=1)
    chunks = dy.shape[1] // chunk
    dy = jnp.transpose(dy.reshape(rows, chunks, chunk), (1, 0, 2))
    starts, at = [], 0
    for _, y in pairs:
        starts.append(at)
        at += y.shape[1] // chunk
    stages = experts.bit_length() - 1
    own = width // (2 * experts)
    vmem = pl.BlockSpec(memory_space=pltpu.VMEM)
    dma = pltpu.SemaphoreType.DMA
    scratch = [
        pltpu.VMEM((len(pairs), width // 2, rows), BF16),
        pltpu.VMEM(dy.shape, BF16),
        pltpu.VMEM((stages + 1, *small.shape), F32),
    ]
    scratch += [
        pltpu.VMEM((chunks, experts >> (k + 1), 2, own, chunk), BF16) for k in range(stages)
    ]
    scratch += [pltpu.VMEM((chunks, experts >> (k + 1), own, chunk), BF16) for k in range(stages)]
    scratch += [
        dma((len(pairs),)),
        dma((len(pairs),)),
        dma((chunks,)),
        dma((chunks,)),
        dma((stages + 1,)),
        dma((stages + 1,)),
        dma((stages, chunks)),
        dma((stages, chunks)),
    ]
    out, sums = pl.pallas_call(
        functools.partial(dense_kernel, tuple(starts), stages, 4),
        in_specs=[vmem] * 3,
        out_specs=[vmem] * 2,
        out_shape=[
            jax.ShapeDtypeStruct((chunks, own, chunk), F32),
            jax.ShapeDtypeStruct((stages + 1, *small.shape), F32),
        ],
        scratch_shapes=scratch,
        compiler_params=pltpu.CompilerParams(
            collective_id=0, has_side_effects=True, vmem_limit_bytes=56 << 20
        ),
        name="dense_gradients",
    )(xt, dy, small)
    results = []
    for (_, y), first in zip(pairs, starts):
        count = y.shape[1] // chunk
        part = jnp.transpose(out[first : first + count], (1, 0, 2))
        results.append(part.reshape(own, count * chunk))
    return results, sums[stages]


def body(
    tokens,
    cotangent,
    lengths,
    routes,
    self_qkv,
    self_out,
    cross_weights,
    router,
    gains,
    bias_table,
    expert_in,
    expert_out,
):
    _, seqs, length, width = tokens.shape
    heads = H
    experts = router.shape[2]
    top = routes.shape[3]
    capacity = (5 * top * length + 4 * experts - 1) // (4 * experts)
    block_rows = -(-seqs * capacity // 16) * 16
    rows = seqs * length
    slots = experts * block_rows
    half_index = lax.axis_index("half")
    decoder = half_index == 1
    wqkv, wout, wcross, wrouter, gain = (
        self_qkv[0],
        self_out[0],
        cross_weights[0],
        router[0],
        gains[0],
    )
    w_in, w_down = expert_in[0, 0], expert_out[0, 0]

    column = np.arange(2 * length)
    hot, hot_back = (
        (
            jnp.where(decoder, *reversed(diagonal_buckets(diff)))[:, None]
            == jnp.arange(BUCKETS)[None, :]
        ).astype(F32)
        for diff in (np.where(column < length, column, column - 2 * length), column - length + 1)
    )
    bias = lax.dot_general(
        bias_table[0].reshape(BUCKETS, heads),
        hot,
        (((0,), (1,)), ((), ())),
        precision=lax.Precision.HIGHEST,
        preferred_element_type=F32,
    )
    own_lengths = jnp.where(decoder, lengths[1], lengths[0])
    self_info = jnp.concatenate([own_lengths, half_index[None]]).astype(jnp.int32)
    cross_info = jnp.concatenate([lengths[0], jnp.zeros((1,), jnp.int32)]).astype(jnp.int32)

    order = jnp.transpose(routes[0], (0, 2, 1)).reshape(seqs, top * length)
    expert_ids = jnp.arange(experts, dtype=jnp.int32)
    picked = (order[:, :, None] == expert_ids).astype(BF16)
    earlier = np.tril(np.ones((top * length, top * length), np.float32), -1).astype(BF16)
    before = jnp.einsum("pq,sqe->spe", earlier, picked, preferred_element_type=F32)
    place = jnp.sum(before * picked.astype(F32), axis=2).astype(jnp.int32)
    kept = place < capacity
    base = order * block_rows + jnp.arange(seqs, dtype=jnp.int32)[:, None] * capacity
    target = jnp.where(kept, base + place, -1).reshape(seqs, top, length)
    target = jnp.transpose(target, (1, 0, 2)).reshape(top, rows)
    slot_ids = jnp.arange(slots, dtype=jnp.int32)
    spots = (target[:, :, None] == slot_ids).astype(BF16)
    both = jnp.sum(spots.astype(F32), axis=0).astype(BF16)
    stacked = spots.reshape(top * rows, slots)
    kept_hot = picked.astype(F32) * kept[:, :, None].astype(F32)
    kept_count = jnp.sum(kept_hot, axis=(0, 1))
    all_count = jnp.sum(picked.astype(F32), axis=(0, 1))
    tallies = jnp.concatenate([kept_count, all_count - kept_count])
    route_hot = (routes[0].reshape(rows, top, 1) == expert_ids).astype(F32)

    def route(values):
        normed, scale = norm_parts(values, gain[1])
        low = normed.astype(BF16)
        rest = (normed - low.astype(F32)).astype(BF16)
        logits = dot(low, wrouter) + dot(rest, wrouter)
        probs = jax.nn.softmax(logits, axis=-1)
        chosen = jnp.sum(probs[:, None, :] * route_hot, axis=-1)
        total = jnp.sum(chosen, axis=-1, keepdims=True)
        gates = chosen / total
        send = dot(both, low, TN).astype(BF16).reshape(experts, block_rows, width)
        return dict(scale=scale, low=low, probs=probs, gates=gates, total=total, send=send)

    def fetch(returned):
        flat = returned.reshape(slots, width)
        return dot(stacked, flat).reshape(top, rows, width)

    def combine(values, gates, results):
        return values + jnp.sum(jnp.transpose(gates)[:, :, None] * results, axis=0)

    values = tokens[0].reshape(rows, width).astype(F32)
    normed, scale0 = norm_parts(values, gain[0])
    low0 = normed.astype(BF16)
    qkv = dot(low0, wqkv).astype(BF16)
    mixed0 = attend(self_info, bias, qkv, qkv, (0, 1, 2), length, width)
    first = values + dot(mixed0, wout)

    state = route(first)
    returned, received = moe_forward(state["send"], w_in, w_down, 0, None)
    final_enc = combine(first, state["gates"], fetch(returned))
    normed, scale_m = norm_parts(final_enc, gain[2])
    low_m = normed.astype(BF16)
    memory = dot(low_m, wcross).astype(BF16)
    names = ("half", "dp", "expert")
    forward_pairs, back_pairs = half_pairs(lax.axis_size("dp") * lax.axis_size("expert"))
    memory = lax.ppermute(memory, names, forward_pairs)

    normed, scale_c = norm_parts(first, gain[2])
    low_c = normed.astype(BF16)
    query = dot(low_c, wcross[:, :width]).astype(BF16)
    mixed_c = attend(cross_info, None, query, memory, (0, 0, 1), length, width)
    second = jnp.where(decoder, first + dot(mixed_c, wcross[:, width:]), first)

    state = route(second)
    returned, received = moe_forward(state["send"], w_in, w_down, 1, (returned, received))
    results = fetch(returned)
    final = combine(second, state["gates"], results)
    outputs = final.astype(BF16)

    def moe_gradient(grad):
        dgates = jnp.transpose(jnp.sum(grad[None] * results, axis=-1))
        spread = (jnp.transpose(state["gates"])[:, :, None] * grad[None]).astype(BF16)
        send = dot(stacked, spread.reshape(top * rows, width), TN)
        return dgates, send.astype(BF16).reshape(experts, block_rows, width)

    def moe_input_gradient(grad, dgates, back):
        gates, total, probs = state["gates"], state["total"], state["probs"]
        dchosen = (dgates - jnp.sum(dgates * gates, axis=-1, keepdims=True)) / total
        dprobs = jnp.sum(dchosen[:, :, None] * route_hot, axis=1)
        dlogits = probs * (dprobs - jnp.sum(dprobs * probs, axis=-1, keepdims=True))
        dnormed = dot(both, back.reshape(slots, width)) + lax.dot_general(
            dlogits, wrouter.astype(F32), NT, preferred_element_type=F32
        )
        dvalues, dgain = norm_back(second, state["scale"], gain[1], dnormed)
        normed = second * state["scale"] * gain[1]
        drouter = lax.dot_general(
            normed, dlogits, TN, precision=lax.Precision.HIGHEST, preferred_element_type=F32
        )
        return grad + dvalues, dgain, drouter

    grad_dec = cotangent[0].reshape(rows, width).astype(F32)
    dgates, grad_send = moe_gradient(grad_dec)
    kept_from = moe_backward(grad_send, received, w_in, w_down, 1, None)
    grad_second, _, _ = moe_input_gradient(grad_dec, dgates, kept_from[0])

    dbranch_c = grad_second.astype(BF16)
    dmixed_c = dot(dbranch_c, wcross[:, width:], NT).astype(BF16)
    dquery, dmemory = attend_back(
        cross_info, None, query, memory, (0, 0, 1), dmixed_c, length, width
    )
    dmemory = lax.ppermute(dmemory, names, back_pairs)
    dnormed = dot(dquery, wcross[:, :width], NT)
    dvalues, dgain_c = norm_back(first, scale_c, gain[2], dnormed)
    grad_first_dec = grad_second + dvalues

    dnormed = dot(dmemory, wcross, NT)
    dvalues, dgain_m = norm_back(final_enc, scale_m, gain[2], dnormed)
    grad = jnp.where(decoder, grad_dec, grad_dec + dvalues)
    dgates, grad_send = moe_gradient(grad)
    back, mixed_grads, hidden, all_rows, all_grad = moe_backward(
        grad_send, received, w_in, w_down, 0, kept_from
    )
    grad_second, dgain_moe, drouter = moe_input_gradient(grad, dgates, back)
    grad_first = jnp.where(decoder, grad_first_dec, grad_second)

    dbranch = grad_first.astype(BF16)
    dmixed = dot(dbranch, wout, NT).astype(BF16)
    dq, dkv, diag = attend_back(self_info, bias, qkv, qkv, (0, 1, 2), dmixed, length, width)
    dnormed = dot(dq, wqkv[:, :width], NT) + dot(dkv, wqkv[:, width:], NT)
    dvalues, dgain_self = norm_back(values, scale0, gain[0], dnormed)
    d_tokens = (grad_first + dvalues).astype(BF16)
    dtable = lax.dot_general(
        hot_back, diag, (((0,), (1,)), ((), ())), precision=lax.Precision.HIGHEST,
        preferred_element_type=F32,
    ).reshape(-1)

    left = jnp.where(decoder, low_c, low_m)
    right = jnp.where(decoder, dquery, dmemory[:, :width])
    left_out = jnp.where(decoder, mixed_c, low_m)
    right_out = jnp.where(decoder, dbranch_c, dmemory[:, width:])
    pairs = [
        (low0, jnp.concatenate([dq, dkv], axis=1)),
        (mixed0, dbranch),
        (left, right),
        (left_out, right_out),
    ]
    extra = jnp.concatenate([dtable, tallies, jnp.zeros((width - dtable.shape[0] - tallies.shape[0],), F32)])
    small = jnp.concatenate(
        [
            jnp.transpose(drouter),
            dgain_self[None],
            dgain_moe[None],
            jnp.where(decoder, dgain_c, dgain_m)[None],
            extra[None],
        ]
    )
    small = jnp.pad(small, ((0, -small.shape[0] % 8), (0, 0)))
    (dqkv, dout, dcross_a, dcross_b), small = dense_gradients(pairs, small, experts)
    place = lax.axis_index("dp") * experts + lax.axis_index("expert")
    own = width // (2 * experts)
    mine = lax.dynamic_slice_in_dim(small[: experts + 3], place * own, own, 1)
    tail = small[experts + 3]
    own_table = dtable.shape[0] // (2 * experts)
    d_table = lax.dynamic_slice_in_dim(tail, place * own_table, own_table)
    counts = lax.dynamic_slice_in_dim(tail, dtable.shape[0] + place, 1).astype(jnp.int32)

    flat = all_rows.reshape(-1, width)
    ff_half = hidden.shape[-1]
    din = jnp.einsum(
        "rd,grf->gdf", flat, mixed_grads.reshape(2, -1, ff_half), preferred_element_type=F32
    )
    ddown = dot(hidden.reshape(-1, ff_half), all_grad.reshape(-1, width), TN)
    return (
        outputs.reshape(1, seqs, length, width),
        d_tokens.reshape(1, seqs, length, width),
        dqkv[None],
        dout[None],
        jnp.concatenate([dcross_a, dcross_b], axis=1)[None],
        jnp.transpose(mine[:experts])[None],
        mine[experts:][None],
        d_table[None],
        din[None, None],
        ddown[None, None],
        counts.reshape(1, 1, 1),
    )


def half_pairs(count):
    return (
        [(i, count + i) for i in range(count)],
        [(count + i, i) for i in range(count)],
    )


def solution(mesh):
    placed = (
        P("half", ("dp", "expert"), None, None),
        P("half", ("dp", "expert"), None, None),
        P(None, ("dp", "expert")),
        P("half", ("dp", "expert"), None, None),
        P("half", None, None),
        P("half", None, None),
        P("half", None, None),
        P("half", None, None),
        P("half", None, None),
        P("half", None),
        P("half", "expert", None, None, None),
        P("half", "expert", None, None),
    )
    return jax.shard_map(
        body,
        mesh=mesh,
        in_specs=placed,
        out_specs=(
            P("half", ("dp", "expert"), None, None),
            P("half", ("dp", "expert"), None, None),
            P("half", ("dp", "expert"), None),
            P("half", ("dp", "expert"), None),
            P("half", ("dp", "expert"), None),
            P("half", ("dp", "expert"), None),
            P("half", None, ("dp", "expert")),
            P("half", ("dp", "expert")),
            P("half", "expert", None, None, "dp"),
            P("half", "expert", "dp", None),
            P("half", "dp", "expert"),
        ),
        check_vma=False,
    )
```

```python
import functools

import jax
import jax.numpy as jnp
import numpy as np
from jax import lax
from jax.experimental import pallas as pl
from jax.experimental.pallas import tpu as pltpu
from jax.sharding import PartitionSpec as P

H = 16
BUCKETS = 32
EPS = 1e-06
ENC_STEPS = (12, 16, 23, 32, 46, 64, 91)
DEC_STEPS = (19, 21, 24, 27, 31, 35, 40, 46, 52, 59, 67, 77, 87, 99, 113)
F32 = jnp.float32
BF16 = jnp.bfloat16
MESH = pl.DeviceIdType.MESH
NT = (((1,), (1,)), ((), ()))
TN = (((0,), (0,)), ((), ()))


def dot(a, b, dims=(((1,), (0,)), ((), ()))):
    return lax.dot_general(a, b, dims, preferred_element_type=F32)


def diagonal_buckets(diff):
    apart = np.abs(diff)
    coarse = 8 + sum((apart >= step).astype(np.int32) for step in ENC_STEPS)
    enc = np.where(apart < 8, apart, coarse) + 16 * (diff > 0)
    behind = np.maximum(-diff, 0)
    coarse = 16 + sum((behind >= step).astype(np.int32) for step in DEC_STEPS)
    dec = np.where(behind < 16, behind, coarse)
    return enc.astype(np.int32), dec.astype(np.int32)


def masked_scores(info, seq, bias_ref, query, key_rows, head, lane_mask, length):
    part = jnp.where(lane_mask, query, jnp.zeros_like(query))
    scores = dot(part, key_rows, NT) * 0.125
    if bias_ref is not None:
        row = jnp.broadcast_to(bias_ref[pl.ds(head, 1), :], (length, 2 * length))
        scores = scores + pltpu.roll(row, 0, 1, stride=1, stride_axis=0)[:, :length]
    row_id = lax.broadcasted_iota(jnp.int32, (length, length), 0)
    col_id = lax.broadcasted_iota(jnp.int32, (length, length), 1)
    reach = jnp.where(info[2] > 0, row_id, length)
    return jnp.where((col_id < info[seq]) & (col_id <= reach), scores, -1000000000.0)


def softmax_parts(scores):
    peak = jnp.max(scores, axis=-1, keepdims=True)
    spread = jnp.exp(scores - peak)
    return spread / jnp.sum(spread, axis=-1, keepdims=True)


def attend_kernel(has_bias, info, *refs):
    bias_ref, (q_ref, k_ref, v_ref, out_ref) = (refs[0], refs[1:]) if has_bias else (None, refs)
    length, width = q_ref.shape
    seq = pl.program_id(0)
    low = lax.broadcasted_iota(jnp.int32, (length, 128), 1) < 64

    @pl.loop(0, width // 128, unroll=True)
    def _(pair):
        cols = pl.ds(pl.multiple_of(pair * 128, 128), 128)
        q, k, v = q_ref[:, cols], k_ref[:, cols], v_ref[:, cols]
        mixed = []
        for side in range(2):
            mask = low if side == 0 else jnp.logical_not(low)
            scores = masked_scores(info, seq, bias_ref, q, k, 2 * pair + side, mask, length)
            mixed.append(dot(softmax_parts(scores).astype(BF16), v))
        out_ref[:, cols] = jnp.where(low, mixed[0], mixed[1]).astype(BF16)


def attend_back_kernel(has_bias, info, *refs):
    if has_bias:
        bias_ref, q_ref, k_ref, v_ref, g_ref, dq_ref, diag_ref = refs
        dkv_ref, shift = dq_ref, q_ref.shape[1]
    else:
        bias_ref = diag_ref = None
        q_ref, k_ref, v_ref, g_ref, dq_ref, dkv_ref = refs
        shift = 0
    length, width = q_ref.shape
    seq = pl.program_id(0)
    low = lax.broadcasted_iota(jnp.int32, (length, 128), 1) < 64
    if has_bias:
        row_id = lax.broadcasted_iota(jnp.int32, (length, length), 0)
        col_id = lax.broadcasted_iota(jnp.int32, (length, length), 1)
        flip = (row_id + col_id == length - 1).astype(F32).astype(BF16)

        @pl.when(seq == 0)
        def _():
            diag_ref[...] = jnp.zeros_like(diag_ref)

    @pl.loop(0, width // 128, unroll=True)
    def _(pair):
        cols = pl.ds(pl.multiple_of(pair * 128, 128), 128)
        q, k, v, g = q_ref[:, cols], k_ref[:, cols], v_ref[:, cols], g_ref[:, cols]
        dqs, dks, dvs = [], [], []
        for side in range(2):
            mask = low if side == 0 else jnp.logical_not(low)
            head = 2 * pair + side
            probs = softmax_parts(masked_scores(info, seq, bias_ref, q, k, head, mask, length))
            part = jnp.where(mask, g, jnp.zeros_like(g))
            dweights = dot(part, v, NT)
            dvs.append(dot(probs.astype(BF16), g, TN))
            dscores = probs * (dweights - jnp.sum(dweights * probs, axis=-1, keepdims=True))
            dlow = dscores.astype(BF16)
            dqs.append(dot(dlow, k))
            dks.append(dot(dlow, q, TN))
            if has_bias:
                upside = dot(flip, dlow)
                wide = jnp.concatenate([upside, jnp.zeros((length, length), F32)], axis=1)
                turned = pltpu.roll(wide, 0, 1, stride=1, stride_axis=0)
                diag_ref[pl.ds(head, 1), :] += jnp.sum(turned, axis=0, keepdims=True)
        dq_ref[:, cols] = (jnp.where(low, dqs[0], dqs[1]) * 0.125).astype(BF16)
        kcols = pl.ds(pl.multiple_of(shift + pair * 128, 128), 128)
        dkv_ref[:, kcols] = (jnp.where(low, dks[0], dks[1]) * 0.125).astype(BF16)
        vcols = pl.ds(pl.multiple_of(shift + width + pair * 128, 128), 128)
        dkv_ref[:, vcols] = jnp.where(low, dvs[0], dvs[1]).astype(BF16)


def attend(info, bias, q, kv, blocks, length, width):
    rows = q.shape[0]
    seqs = rows // length
    specs = [
        pl.BlockSpec((length, width), lambda s, b=b: (s, b)) for b in blocks
    ]
    lead = [] if bias is None else [pl.BlockSpec(bias.shape, lambda s: (0, 0))]
    args = [] if bias is None else [bias]
    return pl.pallas_call(
        functools.partial(attend_kernel, bias is not None),
        grid=(seqs,),
        in_specs=[pl.BlockSpec(memory_space=pltpu.SMEM)] + lead + specs,
        out_specs=pl.BlockSpec((length, width), lambda s: (s, 0)),
        out_shape=jax.ShapeDtypeStruct((rows, width), BF16),
        name="attend",
    )(info, *args, q, kv, kv)


def attend_back(info, bias, q, kv, blocks, grad, length, width):
    rows = q.shape[0]
    seqs = rows // length
    specs = [
        pl.BlockSpec((length, width), lambda s, b=b: (s, b)) for b in (*blocks, 0)
    ]
    lead = [] if bias is None else [pl.BlockSpec(bias.shape, lambda s: (0, 0))]
    args = [] if bias is None else [bias]
    widths = (width, 2 * width) if bias is None else (3 * width,)
    out_specs = [pl.BlockSpec((length, w), lambda s: (s, 0)) for w in widths]
    out_shape = [jax.ShapeDtypeStruct((rows, w), BF16) for w in widths]
    if bias is not None:
        out_specs.append(pl.BlockSpec(bias.shape, lambda s: (0, 0)))
        out_shape.append(jax.ShapeDtypeStruct(bias.shape, F32))
    return pl.pallas_call(
        functools.partial(attend_back_kernel, bias is not None),
        grid=(seqs,),
        in_specs=[pl.BlockSpec(memory_space=pltpu.SMEM)] + lead + specs,
        out_specs=out_specs,
        out_shape=out_shape,
        name="attend_back",
    )(info, *args, q, kv, kv, grad)


def norm_parts(values, gain):
    scale = lax.rsqrt(jnp.mean(values * values, axis=-1, keepdims=True) + EPS)
    return values * scale * gain, scale


def norm_back(values, scale, gain, grad):
    unit = values * scale
    gain_grad = jnp.sum(grad * unit, axis=0)
    pushed = grad * gain
    back = scale * (pushed - unit * jnp.mean(pushed * unit, axis=-1, keepdims=True))
    return back, gain_grad


def gelu_parts(gate):
    c = 0.7978845608028654
    inner = c * (gate + 0.044715 * gate * gate * gate)
    t = jnp.tanh(inner)
    value = 0.5 * gate * (1.0 + t)
    slope = 0.5 * (1.0 + t) + 0.5 * gate * (1.0 - t * t) * c * (1.0 + 3.0 * 0.044715 * gate * gate)
    return value, slope


def moe_forward(send, w_in, w_down, turn, kept_from):
    experts, rows, width = send.shape
    arrived = lax.all_to_all(send, "expert", split_axis=0, concat_axis=0, tiled=True)
    flat = arrived.reshape(-1, width)
    value, _ = gelu_parts(dot(flat, w_in[0]))
    hidden = (value * dot(flat, w_in[1])).astype(BF16)
    result = dot(hidden, w_down).astype(BF16).reshape(send.shape)
    back = lax.all_to_all(result, "expert", split_axis=0, concat_axis=0, tiled=True)
    if kept_from is None:
        return back, arrived
    mine = lax.axis_index("half") == turn
    return jnp.where(mine, back, kept_from[0]), jnp.where(mine, arrived, kept_from[1])


def flipped(value, bit):
    step = 1 << bit
    return value + step * (1 - 2 * (value // step % 2))


def crossed(value, other):
    for bit in range(other.bit_length()):
        if other >> bit & 1:
            value = flipped(value, bit)
    return value


def greet(partners):
    barrier = pltpu.get_barrier_semaphore()
    for partner in partners:
        pl.semaphore_signal(barrier, inc=1, device_id=partner, device_id_type=MESH)
    pl.semaphore_wait(barrier, len(partners))


def remote(src, dst, out_sem, in_sem, device):
    return pltpu.make_async_remote_copy(
        src_ref=src,
        dst_ref=dst,
        send_sem=out_sem,
        recv_sem=in_sem,
        device_id=device,
        device_id_type=MESH,
    )


def tile_loop(count, step, body):
    @pl.loop(0, count // step)
    def _(i):
        body(pl.multiple_of(i * step, step), step)

    if count % step:
        body(count // step * step, count % step)


def far_first(experts, group):
    return [*range(group, experts), *range(1, group)]


def expert_forward_kernel(turn, group, has_prev, *refs):
    send_ref, w_in, w_down = refs[:3]
    refs = refs[3 + 2 * has_prev :]
    back_out, rows_out, wg, wu, wd, rows, back, made, hidden = refs[:9]
    wsem, s1, r1, s2, r2, osem = refs[9:]
    experts, block, width = send_ref.shape
    ff = wd.shape[0]

    @pl.when(lax.axis_index("half") == turn)
    def _():
        me = lax.axis_index("expert")
        greet([{"expert": crossed(me, k)} for k in range(1, experts)])

        def there(k):
            partner = crossed(me, k)
            return remote(send_ref.at[partner], rows.at[me], s1.at[k], r1.at[k], {"expert": partner})

        def home(k):
            partner = crossed(me, k)
            return remote(made.at[partner], back.at[me], s2.at[k], r2.at[k], {"expert": partner})

        for k in far_first(experts, group):
            there(k).start()
        loads = [
            pltpu.make_async_copy(src, dst, wsem.at[i])
            for i, (src, dst) in enumerate(((w_in.at[0], wg), (w_in.at[1], wu), (w_down, wd)))
        ]
        for load in loads:
            load.start()
        rows[me] = send_ref[me]
        for part in range(experts // group):
            for k in range(part * group, part * group + group):
                if k:
                    there(k).wait_recv()
            base = crossed(me // group, part) * group
            if part == 0:
                loads[0].wait()
                loads[1].wait()

            def up_tile(start, size, base=base):
                x = rows[pl.ds(base, group)].reshape(group * block, width)
                cols = pl.ds(start, size)
                value, _ = gelu_parts(dot(x, wg[:, cols]))
                hidden[:, cols] = (value * dot(x, wu[:, cols])).astype(BF16)

            tile_loop(ff, 512, up_tile)
            if part == 0:
                loads[2].wait()

            def down_tile(start, size, base=base):
                cols = pl.ds(start, size)
                y = dot(hidden[...], wd[:, cols]).astype(BF16)
                made[pl.ds(base, group), :, cols] = y.reshape(group, block, size)

            tile_loop(width, 512, down_tile)
            for k in range(part * group, part * group + group):
                if k:
                    home(k).start()
        rows_copy = pltpu.make_async_copy(rows, rows_out, osem.at[0])
        rows_copy.start()
        back[me] = made[me]
        for k in range(1, experts):
            home(k).wait_recv()
        back_copy = pltpu.make_async_copy(back, back_out, osem.at[1])
        back_copy.start()
        for k in range(1, experts):
            there(k).wait_send()
            home(k).wait_send()
        rows_copy.wait()
        back_copy.wait()


def expert_backward_kernel(turn, group, has_prev, *refs):
    send_ref, own_rows, w_in, w_down = refs[:4]
    refs = refs[4 + 5 * has_prev :]
    back_out, mixed_out, hidden_out, rows_out, grad_out = refs[:5]
    wg, wu, wd, grads, back, made, rows_peer, grads_peer = refs[5:13]
    hidden, dgate, dup = refs[13:16]
    wsem, s1, r1, s2, r2, sx, rx, osem = refs[16:]
    experts, block, width = send_ref.shape
    ff = wd.shape[0]
    span = ff // 2
    total = experts * block
    parts = experts // group

    @pl.when(lax.axis_index("half") == turn)
    def _():
        me, dp = lax.axis_index("expert"), lax.axis_index("dp")
        peer = {"dp": 1 - dp}
        greet([{"expert": crossed(me, k)} for k in range(1, experts)] + [peer])

        def there(k):
            partner = crossed(me, k)
            return remote(send_ref.at[partner], grads.at[me], s1.at[k], r1.at[k], {"expert": partner})

        def home(k):
            partner = crossed(me, k)
            return remote(made.at[partner], back.at[me], s2.at[k], r2.at[k], {"expert": partner})

        def base_of(part):
            return crossed(me // group, part) * group

        rows_over = remote(own_rows, rows_peer, sx.at[parts], rx.at[parts], peer)

        def grads_over(part):
            blocks = pl.ds(base_of(part), group)
            return remote(grads.at[blocks], grads_peer.at[blocks], sx.at[part], rx.at[part], peer)

        for k in far_first(experts, group):
            there(k).start()
        loads = [
            pltpu.make_async_copy(src, dst, wsem.at[i])
            for i, (src, dst) in enumerate(((w_in.at[0], wg), (w_in.at[1], wu), (w_down, wd)))
        ]
        for load in loads:
            load.start()
        rows_over.start()
        grads[me] = send_ref[me]
        loads[0].wait()
        loads[1].wait()

        def up_tile(start, size):
            x = own_rows[...].reshape(total, width)
            cols = pl.ds(start, size)
            value, slope = gelu_parts(dot(x, wg[:, cols]))
            up = dot(x, wu[:, cols])
            hidden[:, cols] = (value * up).astype(BF16)
            dup[:, cols] = value.astype(BF16)
            dgate[:, cols] = (up * slope).astype(BF16)

        tile_loop(ff, 512, up_tile)
        loads[2].wait()
        for part in range(parts):
            for k in range(part * group, part * group + group):
                if k:
                    there(k).wait_recv()
            grads_over(part).start()
            base = base_of(part)
            span_rows = pl.ds(pl.multiple_of(base * block, group * block), group * block)

            def hidden_tile(start, size, base=base, span_rows=span_rows):
                dy = grads[pl.ds(base, group)].reshape(group * block, width)
                cols = pl.ds(start, size)
                dhidden = dot(dy, wd[cols, :], NT)
                dgate[span_rows, cols] = (dhidden * dgate[span_rows, cols].astype(F32)).astype(BF16)
                dup[span_rows, cols] = (dhidden * dup[span_rows, cols].astype(F32)).astype(BF16)

            tile_loop(ff, 512, hidden_tile)

            def rows_tile(start, size, base=base, span_rows=span_rows):
                cols = pl.ds(start, size)
                dr = dot(dgate[span_rows, :], wg[cols, :], NT) + dot(dup[span_rows, :], wu[cols, :], NT)
                made[pl.ds(base, group), :, cols] = dr.astype(BF16).reshape(group, block, size)

            tile_loop(width, 512, rows_tile)
            for k in range(part * group, part * group + group):
                if k:
                    home(k).start()
        back[me] = made[me]
        half_cols = pl.ds(pl.multiple_of(dp * span, 128), span)
        outs = [
            (dgate.at[:, half_cols], mixed_out.at[0, 0]),
            (dup.at[:, half_cols], mixed_out.at[1, 0]),
            (hidden.at[:, half_cols], hidden_out.at[0]),
            (own_rows, rows_out.at[0]),
            (grads, grad_out.at[0]),
        ]
        outs = [pltpu.make_async_copy(src, dst, osem.at[i]) for i, (src, dst) in enumerate(outs)]
        for out in outs:
            out.start()

        rows_over.wait_recv()
        for part in range(parts):
            grads_over(part).wait_recv()

        def peer_tile(start, size):
            x = rows_peer[...].reshape(total, width)
            dy = grads_peer[...].reshape(total, width)
            here = pl.ds(pl.multiple_of((1 - dp) * span + start, 128), size)
            cols = pl.ds(pl.multiple_of(dp * span + start, 128), size)
            value, slope = gelu_parts(dot(x, wg[:, cols]))
            up = dot(x, wu[:, cols])
            dhidden = dot(dy, wd[cols, :], NT)
            hidden[:, here] = (value * up).astype(BF16)
            dgate[:, here] = (dhidden * up * slope).astype(BF16)
            dup[:, here] = (dhidden * value).astype(BF16)

        tile_loop(span, 512, peer_tile)
        other_cols = pl.ds(pl.multiple_of((1 - dp) * span, 128), span)
        peers = [
            (dgate.at[:, other_cols], mixed_out.at[0, 1]),
            (dup.at[:, other_cols], mixed_out.at[1, 1]),
            (hidden.at[:, other_cols], hidden_out.at[1]),
            (rows_peer, rows_out.at[1]),
            (grads_peer, grad_out.at[1]),
        ]
        peers = [pltpu.make_async_copy(src, dst, osem.at[5 + i]) for i, (src, dst) in enumerate(peers)]
        for out in peers:
            out.start()
        for k in range(1, experts):
            home(k).wait_recv()
        back_copy = pltpu.make_async_copy(back, back_out, osem.at[10])
        back_copy.start()
        for k in range(1, experts):
            there(k).wait_send()
            home(k).wait_send()
        rows_over.wait_send()
        for part in range(parts):
            grads_over(part).wait_send()
        for out in [*outs, *peers, back_copy]:
            out.wait()


def group_of(experts, block):
    group = 1
    while group * 2 * block <= 320 and group * 2 <= experts:
        group *= 2
    return group


def expert_call(kernel, turn, inputs, weights, prev, out_shape, scratch, name):
    experts, block, _ = inputs[0].shape
    vmem, hbm = pl.BlockSpec(memory_space=pltpu.VMEM), pl.BlockSpec(memory_space=pl.ANY)
    prev = list(prev or [])
    first = len(inputs) + len(weights)
    return pl.pallas_call(
        functools.partial(kernel, turn, group_of(experts, block), bool(prev)),
        in_specs=[vmem] * len(inputs) + [hbm] * (len(weights) + len(prev)),
        out_specs=[hbm] * len(out_shape),
        out_shape=out_shape,
        input_output_aliases={first + i: i for i in range(len(prev))},
        scratch_shapes=scratch,
        compiler_params=pltpu.CompilerParams(
            collective_id=1 + turn + 2 * (len(inputs) - 1),
            has_side_effects=True,
            vmem_limit_bytes=60 << 20,
        ),
        name=name,
    )(*inputs, *weights, *prev)


def moe_forward(send, w_in, w_down, turn, prev):
    experts, block, width = send.shape
    ff = w_down.shape[0]
    group = group_of(experts, block)
    dma = pltpu.SemaphoreType.DMA
    scratch = [
        pltpu.VMEM((width, ff), BF16),
        pltpu.VMEM((width, ff), BF16),
        pltpu.VMEM((ff, width), BF16),
        *[pltpu.VMEM(send.shape, BF16)] * 3,
        pltpu.VMEM((group * block, ff), BF16),
        dma((3,)),
        *[dma((experts,))] * 4,
        dma((2,)),
    ]
    out_shape = [jax.ShapeDtypeStruct(send.shape, BF16)] * 2
    return expert_call(
        expert_forward_kernel, turn, [send], [w_in, w_down], prev, out_shape, scratch, "moe_forward"
    )


def moe_backward(grad_send, received, w_in, w_down, turn, prev):
    experts, block, width = grad_send.shape
    ff = w_down.shape[0]
    total = experts * block
    parts = experts // group_of(experts, block)
    dma = pltpu.SemaphoreType.DMA
    scratch = [
        pltpu.VMEM((width, ff), BF16),
        pltpu.VMEM((width, ff), BF16),
        pltpu.VMEM((ff, width), BF16),
        *[pltpu.VMEM(grad_send.shape, BF16)] * 5,
        *[pltpu.VMEM((total, ff), BF16)] * 3,
        dma((3,)),
        *[dma((experts,))] * 4,
        dma((parts + 1,)),
        dma((parts + 1,)),
        dma((11,)),
    ]
    out_shape = [
        jax.ShapeDtypeStruct(grad_send.shape, BF16),
        jax.ShapeDtypeStruct((2, 2, total, ff // 2), BF16),
        jax.ShapeDtypeStruct((2, total, ff // 2), BF16),
        jax.ShapeDtypeStruct((2, *grad_send.shape), BF16),
        jax.ShapeDtypeStruct((2, *grad_send.shape), BF16),
    ]
    return expert_call(
        expert_backward_kernel,
        turn,
        [grad_send, received],
        [w_in, w_down],
        prev,
        out_shape,
        scratch,
        "moe_backward",
    )


def dense_kernel(stages, chunk, *refs):
    xt_ref, own_refs, peer_refs, small_ref, out_ref, small_out, small_in = (
        refs[0], refs[1:4], refs[4:7], refs[7], refs[8], refs[9], refs[10],
    )
    sums = refs[11 : 11 + stages]
    parts = refs[11 + stages : 11 + 2 * stages]
    ss, rs, sk, rk = refs[11 + 2 * stages :]
    counts = [ref.shape[1] // chunk for ref in own_refs]
    starts = [sum(counts[:i]) for i in range(3)]
    chunks = sum(counts)
    per_cross = counts[2] // 2
    half = xt_ref.shape[2] // 2
    dp, me = lax.axis_index("dp"), lax.axis_index("expert")
    peer = {"dp": 1 - dp}
    partners = [flipped(me, k) for k in range(stages)]
    bits = [me // (1 << k) % 2 for k in range(stages)]
    greet([peer] + [{"expert": p} for p in partners])

    def send_small(step):
        src = small_ref if step == 0 else small_out.at[step - 1]
        device = peer if step == 0 else {"expert": partners[step - 1]}
        return remote(src, small_in.at[step], ss.at[step], rs.at[step], device)

    def picked(k, c, values):
        if k > 1:
            return values[k]
        odd = lax.rem(c, 2)
        return values[k] + odd * (values[1 - k] - values[k])

    def send_first(c, odd):
        src = sums[0].at[c, :, 1 - bits[1]] if odd else sums[0].at[c, :, :, 1 - bits[0]]
        return remote(src, parts[0].at[c], sk.at[0, c], rk.at[0, c], {"expert": partners[odd]})

    def send_part(k, c):
        src = sums[k].at[c, :, 1 - picked(k, c, bits)]
        return remote(src, parts[k].at[c], sk.at[k, c], rk.at[k, c], {"expert": picked(k, c, partners)})

    def by_parity(c, body):
        for odd in range(2):

            @pl.when(lax.rem(c, 2) == odd)
            def _(odd=odd):
                body(odd)

    send_small(0).start()

    def step(i, carry):
        for g in range(3):

            @pl.when((i >= starts[g]) & (i < starts[g] + counts[g]))
            def _(g=g):
                c = i - starts[g]
                cols = pl.ds(pl.multiple_of(c * chunk, chunk), chunk)
                which = g if g < 2 else 2 + c // per_cross
                total = dot(xt_ref[which, :, :half], own_refs[g][:, cols])
                total += dot(xt_ref[which, :, half:], peer_refs[g][:, cols])
                sums[0][i] = total.astype(BF16).reshape(sums[0].shape[1:])
                by_parity(i, lambda odd: send_first(i, odd).start())

        for k in range(stages):
            c = i - 1 - k

            @pl.when((c >= 0) & (c < chunks))
            def _(k=k, c=c):
                def add(mine):
                    total = mine.astype(F32) + parts[k][c].astype(F32)
                    if k + 1 < stages:
                        sums[k + 1][c] = total.astype(BF16).reshape(sums[k + 1].shape[1:])
                        send_part(k + 1, c).start()
                    else:
                        out_ref[c] = total.reshape(out_ref.shape[1:])

                if k == 0:

                    def first(odd):
                        send_first(c, odd).wait_recv()
                        add(sums[0][c, :, bits[1]] if odd else sums[0][c, :, :, bits[0]])

                    by_parity(c, first)
                else:
                    send_part(k, c).wait_recv()
                    add(sums[k][c, :, picked(k, c, bits)])

        for j in range(stages + 1):

            @pl.when(i == j)
            def _(j=j):
                send_small(j).wait_recv()
                own = small_ref[...] if j == 0 else small_out[j - 1]
                small_out[j] = own + small_in[j]
                if j < stages:
                    send_small(j + 1).start()

        return carry

    lax.fori_loop(0, chunks + stages, step, 0)

    def finish(c, carry):
        by_parity(c, lambda odd: send_first(c, odd).wait_send())
        for k in range(1, stages):
            send_part(k, c).wait_send()
        return carry

    lax.fori_loop(0, chunks, finish, 0)
    for j in range(stages + 1):
        send_small(j).wait_send()


def over_dp(array):
    return lax.ppermute(array, "dp", [(0, 1), (1, 0)])


def both_halves(x):
    half = x.shape[1] // 2
    dp = lax.axis_index("dp")
    own = lax.dynamic_slice_in_dim(x, dp * half, half, 1)
    other = lax.dynamic_slice_in_dim(x, (1 - dp) * half, half, 1)
    return own, other


def dense_gradients(xt, own, peer, small, experts):
    chunk = 512
    half_rows = xt.shape[1]
    chunks = sum(y.shape[1] for y in own) // chunk
    stages = experts.bit_length() - 1
    keep = half_rows // experts
    vmem = pl.BlockSpec(memory_space=pltpu.VMEM)
    dma = pltpu.SemaphoreType.DMA
    blocks = [(experts // 4, 2, 2)] + [(experts >> (k + 1), 2) for k in range(1, stages)]
    scratch = [pltpu.VMEM((stages + 1, *small.shape), F32)]
    scratch += [pltpu.VMEM((chunks, *b, keep, chunk), BF16) for b in blocks]
    halved = [(experts // 4, 2)] + [(experts >> (k + 1),) for k in range(1, stages)]
    scratch += [pltpu.VMEM((chunks, *b, keep, chunk), BF16) for b in halved]
    scratch += [dma((stages + 1,)), dma((stages + 1,)), dma((stages, chunks)), dma((stages, chunks))]
    out, sums = pl.pallas_call(
        functools.partial(dense_kernel, stages, chunk),
        in_specs=[vmem] * 8,
        out_specs=[vmem] * 2,
        out_shape=[
            jax.ShapeDtypeStruct((chunks, keep, chunk), F32),
            jax.ShapeDtypeStruct((stages + 1, *small.shape), F32),
        ],
        scratch_shapes=scratch,
        compiler_params=pltpu.CompilerParams(
            collective_id=0, has_side_effects=True, vmem_limit_bytes=56 << 20
        ),
        name="dense_gradients",
    )(xt, *own, *peer, small)
    results, at = [], 0
    for y in own:
        count = y.shape[1] // chunk
        part = jnp.transpose(out[at : at + count], (1, 0, 2))
        results.append(part.reshape(keep, count * chunk))
        at += count
    return results, sums[stages]


def product_kernel(x_ref, y_ref, out_ref):
    out_ref[...] = dot(x_ref[...], y_ref[...].reshape(y_ref.shape[-2:]), TN).reshape(out_ref.shape)


def expert_gradients(rows, mixed, hidden, grads):
    total, width = rows.shape
    span = hidden.shape[1]
    tile = 256
    params = pltpu.CompilerParams(vmem_limit_bytes=40 << 20)
    din = pl.pallas_call(
        product_kernel,
        grid=(2, width // tile),
        in_specs=[
            pl.BlockSpec((total, tile), lambda g, i: (0, i)),
            pl.BlockSpec((1, total, span), lambda g, i: (g, 0, 0)),
        ],
        out_specs=pl.BlockSpec((1, tile, span), lambda g, i: (g, i, 0)),
        out_shape=jax.ShapeDtypeStruct((2, width, span), F32),
        compiler_params=params,
        name="expert_in_gradient",
    )(rows, mixed)
    ddown = pl.pallas_call(
        product_kernel,
        grid=(pl.cdiv(span, tile),),
        in_specs=[
            pl.BlockSpec((total, tile), lambda i: (0, i)),
            pl.BlockSpec((total, width), lambda i: (0, 0)),
        ],
        out_specs=pl.BlockSpec((tile, width), lambda i: (i, 0)),
        out_shape=jax.ShapeDtypeStruct((span, width), F32),
        compiler_params=params,
        name="expert_out_gradient",
    )(hidden, grads)
    return din, ddown


def body(
    tokens,
    cotangent,
    lengths,
    routes,
    self_qkv,
    self_out,
    cross_weights,
    router,
    gains,
    bias_table,
    expert_in,
    expert_out,
):
    _, seqs, length, width = tokens.shape
    heads = H
    experts = router.shape[2]
    top = routes.shape[3]
    capacity = (5 * top * length + 4 * experts - 1) // (4 * experts)
    block_rows = -(-seqs * capacity // 16) * 16
    rows = seqs * length
    slots = experts * block_rows
    half_index = lax.axis_index("half")
    decoder = half_index == 1
    wqkv, wout, wcross, wrouter, gain = (
        self_qkv[0],
        self_out[0],
        cross_weights[0],
        router[0],
        gains[0],
    )
    w_in, w_down = expert_in[0, 0], expert_out[0, 0]

    column = np.arange(2 * length)
    hot, hot_back = (
        (
            jnp.where(decoder, *reversed(diagonal_buckets(diff)))[:, None]
            == jnp.arange(BUCKETS)[None, :]
        ).astype(F32)
        for diff in (np.where(column < length, column, column - 2 * length), column - length + 1)
    )
    bias = lax.dot_general(
        bias_table[0].reshape(BUCKETS, heads),
        hot,
        (((0,), (1,)), ((), ())),
        precision=lax.Precision.HIGHEST,
        preferred_element_type=F32,
    )
    own_lengths = jnp.where(decoder, lengths[1], lengths[0])
    self_info = jnp.concatenate([own_lengths, half_index[None]]).astype(jnp.int32)
    cross_info = jnp.concatenate([lengths[0], jnp.zeros((1,), jnp.int32)]).astype(jnp.int32)

    order = jnp.transpose(routes[0], (0, 2, 1)).reshape(seqs, top * length)
    expert_ids = jnp.arange(experts, dtype=jnp.int32)
    picked = (order[:, :, None] == expert_ids).astype(BF16)
    earlier = np.tril(np.ones((top * length, top * length), np.float32), -1).astype(BF16)
    before = jnp.einsum("pq,sqe->spe", earlier, picked, preferred_element_type=F32)
    place = jnp.sum(before * picked.astype(F32), axis=2).astype(jnp.int32)
    kept = place < capacity
    base = order * block_rows + jnp.arange(seqs, dtype=jnp.int32)[:, None] * capacity
    target = jnp.where(kept, base + place, -1).reshape(seqs, top, length)
    target = jnp.transpose(target, (1, 0, 2)).reshape(top, rows)
    slot_ids = jnp.arange(slots, dtype=jnp.int32)
    spots = (target[:, :, None] == slot_ids).astype(BF16)
    both = jnp.sum(spots.astype(F32), axis=0).astype(BF16)
    stacked = spots.reshape(top * rows, slots)
    kept_hot = picked.astype(F32) * kept[:, :, None].astype(F32)
    kept_count = jnp.sum(kept_hot, axis=(0, 1))
    all_count = jnp.sum(picked.astype(F32), axis=(0, 1))
    tallies = jnp.concatenate([kept_count, all_count - kept_count])
    route_hot = (routes[0].reshape(rows, top, 1) == expert_ids).astype(F32)

    def route(values):
        normed, scale = norm_parts(values, gain[1])
        low = normed.astype(BF16)
        rest = (normed - low.astype(F32)).astype(BF16)
        logits = dot(low, wrouter) + dot(rest, wrouter)
        probs = jax.nn.softmax(logits, axis=-1)
        chosen = jnp.sum(probs[:, None, :] * route_hot, axis=-1)
        total = jnp.sum(chosen, axis=-1, keepdims=True)
        gates = chosen / total
        send = dot(both, low, TN).astype(BF16).reshape(experts, block_rows, width)
        return dict(scale=scale, low=low, probs=probs, gates=gates, total=total, send=send)

    def fetch(returned):
        flat = returned.reshape(slots, width)
        return dot(stacked, flat).reshape(top, rows, width)

    def combine(values, gates, results):
        return values + jnp.sum(jnp.transpose(gates)[:, :, None] * results, axis=0)

    values = tokens[0].reshape(rows, width).astype(F32)
    normed, scale0 = norm_parts(values, gain[0])
    low0 = normed.astype(BF16)
    qkv = dot(low0, wqkv).astype(BF16)
    mixed0 = attend(self_info, bias, qkv, qkv, (0, 1, 2), length, width)
    first = values + dot(mixed0, wout)

    state = route(first)
    returned, received = moe_forward(state["send"], w_in, w_down, 0, None)
    final_enc = combine(first, state["gates"], fetch(returned))
    normed, scale_m = norm_parts(final_enc, gain[2])
    low_m = normed.astype(BF16)
    memory = dot(low_m, wcross).astype(BF16)
    names = ("half", "dp", "expert")
    forward_pairs, back_pairs = half_pairs(lax.axis_size("dp") * lax.axis_size("expert"))
    memory = lax.ppermute(memory, names, forward_pairs)

    normed, scale_c = norm_parts(first, gain[2])
    low_c = normed.astype(BF16)
    query = dot(low_c, wcross[:, :width]).astype(BF16)
    mixed_c = attend(cross_info, None, query, memory, (0, 0, 1), length, width)
    second = jnp.where(decoder, first + dot(mixed_c, wcross[:, width:]), first)

    state = route(second)
    returned, received = moe_forward(state["send"], w_in, w_down, 1, (returned, received))
    results = fetch(returned)
    final = combine(second, state["gates"], results)
    outputs = final.astype(BF16)

    def moe_gradient(grad):
        dgates = jnp.transpose(jnp.sum(grad[None] * results, axis=-1))
        spread = (jnp.transpose(state["gates"])[:, :, None] * grad[None]).astype(BF16)
        send = dot(stacked, spread.reshape(top * rows, width), TN)
        return dgates, send.astype(BF16).reshape(experts, block_rows, width)

    def moe_input_gradient(grad, dgates, back):
        gates, total, probs = state["gates"], state["total"], state["probs"]
        dchosen = (dgates - jnp.sum(dgates * gates, axis=-1, keepdims=True)) / total
        dprobs = jnp.sum(dchosen[:, :, None] * route_hot, axis=1)
        dlogits = probs * (dprobs - jnp.sum(dprobs * probs, axis=-1, keepdims=True))
        dnormed = dot(both, back.reshape(slots, width)) + lax.dot_general(
            dlogits, wrouter.astype(F32), NT, preferred_element_type=F32
        )
        dvalues, dgain = norm_back(second, state["scale"], gain[1], dnormed)
        normed = second * state["scale"] * gain[1]
        drouter = lax.dot_general(
            normed, dlogits, TN, precision=lax.Precision.HIGHEST, preferred_element_type=F32
        )
        return grad + dvalues, dgain, drouter

    grad_dec = cotangent[0].reshape(rows, width).astype(F32)
    dgates, grad_send = moe_gradient(grad_dec)
    kept_from = moe_backward(grad_send, received, w_in, w_down, 1, None)
    grad_second, _, _ = moe_input_gradient(grad_dec, dgates, kept_from[0])

    dbranch_c = grad_second.astype(BF16)
    dmixed_c = dot(dbranch_c, wcross[:, width:], NT).astype(BF16)
    dquery, dmemory = attend_back(
        cross_info, None, query, memory, (0, 0, 1), dmixed_c, length, width
    )
    dmemory = lax.ppermute(dmemory, names, back_pairs)
    dnormed = dot(dquery, wcross[:, :width], NT)
    dvalues, dgain_c = norm_back(first, scale_c, gain[2], dnormed)
    grad_first_dec = grad_second + dvalues

    dnormed = dot(dmemory, wcross, NT)
    dvalues, dgain_m = norm_back(final_enc, scale_m, gain[2], dnormed)
    grad = jnp.where(decoder, grad_dec, grad_dec + dvalues)
    dgates, grad_send = moe_gradient(grad)
    back, mixed_grads, hidden, all_rows, all_grad = moe_backward(
        grad_send, received, w_in, w_down, 0, kept_from
    )
    grad_second, dgain_moe, drouter = moe_input_gradient(grad, dgates, back)
    grad_first = jnp.where(decoder, grad_first_dec, grad_second)

    dbranch = grad_first.astype(BF16)
    dmixed = dot(dbranch, wout, NT).astype(BF16)
    dqkv_rows, diag = attend_back(self_info, bias, qkv, qkv, (0, 1, 2), dmixed, length, width)
    dnormed = dot(dqkv_rows, wqkv, NT)
    dvalues, dgain_self = norm_back(values, scale0, gain[0], dnormed)
    d_tokens = (grad_first + dvalues).astype(BF16)
    dtable = lax.dot_general(
        hot_back, diag, (((0,), (1,)), ((), ())), precision=lax.Precision.HIGHEST,
        preferred_element_type=F32,
    ).reshape(-1)

    cross_grad = jnp.where(decoder, jnp.concatenate([dquery, dbranch_c], axis=1), dmemory)
    owns, others = zip(
        *map(
            both_halves,
            (low0, mixed0, jnp.where(decoder, low_c, low_m), jnp.where(decoder, mixed_c, low_m)),
        )
    )
    lefts = jnp.concatenate([jnp.stack(owns), over_dp(jnp.stack(others))], axis=1)
    xt = jnp.transpose(lefts, (0, 2, 1))
    own_grads = (dqkv_rows, dbranch, cross_grad)
    peer_grads = tuple(map(over_dp, own_grads))
    extra = jnp.concatenate([dtable, tallies, jnp.zeros((width - dtable.shape[0] - tallies.shape[0],), F32)])
    small = jnp.concatenate(
        [
            jnp.transpose(drouter),
            dgain_self[None],
            dgain_moe[None],
            jnp.where(decoder, dgain_c, dgain_m)[None],
            extra[None],
        ]
    )
    small = jnp.pad(small, ((0, -small.shape[0] % 8), (0, 0)))
    (dqkv, dout, dcross), small = dense_gradients(xt, own_grads, peer_grads, small, experts)
    place = lax.axis_index("dp") * experts + lax.axis_index("expert")
    own = width // (2 * experts)
    mine = lax.dynamic_slice_in_dim(small[: experts + 3], place * own, own, 1)
    tail = small[experts + 3]
    own_table = dtable.shape[0] // (2 * experts)
    d_table = lax.dynamic_slice_in_dim(tail, place * own_table, own_table)
    counts = lax.dynamic_slice_in_dim(tail, dtable.shape[0] + place, 1).astype(jnp.int32)

    ff_half = hidden.shape[-1]
    din, ddown = expert_gradients(
        all_rows.reshape(-1, width),
        mixed_grads.reshape(2, -1, ff_half),
        hidden.reshape(-1, ff_half),
        all_grad.reshape(-1, width),
    )
    return (
        outputs.reshape(1, seqs, length, width),
        d_tokens.reshape(1, seqs, length, width),
        dqkv[None],
        dout[None],
        dcross[None],
        jnp.transpose(mine[:experts])[None],
        mine[experts:][None],
        d_table[None],
        din[None, None],
        ddown[None, None],
        counts.reshape(1, 1, 1),
    )


def half_pairs(count):
    return (
        [(i, count + i) for i in range(count)],
        [(count + i, i) for i in range(count)],
    )


def solution(mesh):
    placed = (
        P("half", ("dp", "expert"), None, None),
        P("half", ("dp", "expert"), None, None),
        P(None, ("dp", "expert")),
        P("half", ("dp", "expert"), None, None),
        P("half", None, None),
        P("half", None, None),
        P("half", None, None),
        P("half", None, None),
        P("half", None, None),
        P("half", None),
        P("half", "expert", None, None, None),
        P("half", "expert", None, None),
    )
    return jax.shard_map(
        body,
        mesh=mesh,
        in_specs=placed,
        out_specs=(
            P("half", ("dp", "expert"), None, None),
            P("half", ("dp", "expert"), None, None),
            P("half", ("dp", "expert"), None),
            P("half", ("dp", "expert"), None),
            P("half", ("dp", "expert"), None),
            P("half", ("dp", "expert"), None),
            P("half", None, ("dp", "expert")),
            P("half", ("dp", "expert")),
            P("half", "expert", None, None, "dp"),
            P("half", "expert", "dp", None),
            P("half", "dp", "expert"),
        ),
        check_vma=False,
    )
```

```python
import functools

import jax
import jax.numpy as jnp
import numpy as np
from jax import lax
from jax.experimental import pallas as pl
from jax.experimental.pallas import tpu as pltpu
from jax.sharding import PartitionSpec as P

H = 16
BUCKETS = 32
EPS = 1e-06
ENC_STEPS = (12, 16, 23, 32, 46, 64, 91)
DEC_STEPS = (19, 21, 24, 27, 31, 35, 40, 46, 52, 59, 67, 77, 87, 99, 113)
F32 = jnp.float32
BF16 = jnp.bfloat16
MESH = pl.DeviceIdType.MESH
NT = (((1,), (1,)), ((), ()))
TN = (((0,), (0,)), ((), ()))


def dot(a, b, dims=(((1,), (0,)), ((), ()))):
    return lax.dot_general(a, b, dims, preferred_element_type=F32)


def diagonal_buckets(diff):
    apart = np.abs(diff)
    coarse = 8 + sum((apart >= step).astype(np.int32) for step in ENC_STEPS)
    enc = np.where(apart < 8, apart, coarse) + 16 * (diff > 0)
    behind = np.maximum(-diff, 0)
    coarse = 16 + sum((behind >= step).astype(np.int32) for step in DEC_STEPS)
    dec = np.where(behind < 16, behind, coarse)
    return enc.astype(np.int32), dec.astype(np.int32)


def diagonals(bias_ref, head, length):
    row = jnp.broadcast_to(bias_ref[pl.ds(head, 1), :], (length, 2 * length))
    return pltpu.roll(row, 0, 1, stride=1, stride_axis=0)[:, :length]


def fill_masks(info, mask_ref):
    seqs, length, _ = mask_ref.shape
    row_id = lax.broadcasted_iota(jnp.int32, (length, length), 0)
    col_id = lax.broadcasted_iota(jnp.int32, (length, length), 1)
    reach = jnp.where(info[seqs] > 0, row_id, length)
    for seq in range(seqs):
        allowed = (col_id < info[seq]) & (col_id <= reach)
        mask_ref[seq] = jnp.where(allowed, 0.0, -1000000000.0)


def attend_kernel(has_bias, info, *refs):
    bias_ref, refs = (refs[0], refs[1:]) if has_bias else (None, refs)
    q_ref, k_ref, v_ref, out_ref, log_ref, mask_ref = refs
    seqs, length, _ = mask_ref.shape
    low = lax.broadcasted_iota(jnp.int32, (length, 128), 1) < 64
    fill_masks(info, mask_ref)

    @pl.loop(0, q_ref.shape[1] // 128, unroll=True)
    def _(pair):
        cols = pl.ds(pl.multiple_of(pair * 128, 128), 128)
        biases = [diagonals(bias_ref, 2 * pair + side, length) if has_bias else 0.0 for side in range(2)]
        for seq in range(seqs):
            rows = pl.ds(seq * length, length)
            q, k, v = q_ref[rows, cols] * 0.125, k_ref[rows, cols], v_ref[rows, cols]
            mixed, peaks = [], []
            for side in range(2):
                mine = low if side == 0 else jnp.logical_not(low)
                part = jnp.where(mine, q, jnp.zeros_like(q))
                scores = dot(part, k, NT) + (mask_ref[seq] + biases[side])
                peak = jnp.max(scores, axis=-1, keepdims=True)
                spread = jnp.exp(scores - peak).astype(BF16)
                mixed.append(dot(spread, jnp.where(mine, v, jnp.ones_like(v))))
                peaks.append(peak)
            total = pltpu.roll(jnp.where(low, mixed[1], mixed[0]), 64, 1)
            out_ref[rows, cols] = (jnp.where(low, mixed[0], mixed[1]) / total).astype(BF16)
            log_ref[rows, cols] = jnp.where(low, peaks[0], peaks[1]) + jnp.log(total)


def attend_back_kernel(has_bias, info, *refs):
    if has_bias:
        bias_ref, q_ref, k_ref, v_ref, a_ref, log_ref, g_ref, dq_ref, diag_ref, mask_ref = refs
        dkv_ref, shift = dq_ref, q_ref.shape[1]
    else:
        q_ref, k_ref, v_ref, a_ref, log_ref, g_ref, dq_ref, dkv_ref, mask_ref = refs
        shift = 0
    seqs, length, _ = mask_ref.shape
    width = q_ref.shape[1]
    low = lax.broadcasted_iota(jnp.int32, (length, 128), 1) < 64
    fill_masks(info, mask_ref)
    if has_bias:
        row_id = lax.broadcasted_iota(jnp.int32, (length, length), 0)
        col_id = lax.broadcasted_iota(jnp.int32, (length, length), 1)
        flip = (row_id + col_id == length - 1).astype(F32).astype(BF16)

    @pl.loop(0, width // 128, unroll=True)
    def _(pair):
        cols = pl.ds(pl.multiple_of(pair * 128, 128), 128)
        kcols = pl.ds(pl.multiple_of(shift + pair * 128, 128), 128)
        vcols = pl.ds(pl.multiple_of(shift + width + pair * 128, 128), 128)
        biases = [diagonals(bias_ref, 2 * pair + side, length) if has_bias else 0.0 for side in range(2)]
        sums = [0.0, 0.0]
        for seq in range(seqs):
            rows = pl.ds(seq * length, length)
            q, k, v, g = q_ref[rows, cols] * 0.125, k_ref[rows, cols], v_ref[rows, cols], g_ref[rows, cols]
            logs = log_ref[rows, cols]
            turned = pltpu.roll(logs, 64, 1)
            product = g.astype(F32) * a_ref[rows, cols].astype(F32)
            minus = (-pltpu.roll(product, 64, 1)).astype(BF16)
            scaled = k * 0.125
            dqs, dks, dvs = [], [], []
            for side in range(2):
                mine = low if side == 0 else jnp.logical_not(low)
                part = jnp.where(mine, q, jnp.zeros_like(q))
                scores = dot(part, k, NT) + (mask_ref[seq] + biases[side])
                probs = jnp.exp(scores - jnp.where(mine, logs, turned))
                dvs.append(dot(probs.astype(BF16), g, TN))
                centred = dot(jnp.where(mine, g, minus), jnp.where(mine, v, jnp.ones_like(v)), NT)
                dlow = (probs * centred).astype(BF16)
                dqs.append(dot(dlow, scaled))
                dks.append(dot(dlow, q, TN))
                if has_bias:
                    sums[side] = sums[side] + dlow.astype(F32)
            dq_ref[rows, cols] = jnp.where(low, dqs[0], dqs[1]).astype(BF16)
            dkv_ref[rows, kcols] = jnp.where(low, dks[0], dks[1]).astype(BF16)
            dkv_ref[rows, vcols] = jnp.where(low, dvs[0], dvs[1]).astype(BF16)
        if has_bias:
            for side in range(2):
                upside = dot(flip, sums[side].astype(BF16))
                wide = jnp.concatenate([upside, jnp.zeros((length, length), F32)], axis=1)
                turned = pltpu.roll(wide, 0, 1, stride=1, stride_axis=0)
                diag_ref[pl.ds(2 * pair + side, 1), :] = jnp.sum(turned, axis=0, keepdims=True)


def attend_call(kernel, info, bias, q, kv, blocks, more, out_shape, length, name):
    rows = q.shape[0]
    seqs = rows // length
    width = more[0].shape[1] if more else out_shape[0].shape[1]
    lead = [] if bias is None else [bias]
    whole = [pl.BlockSpec(a.shape, lambda i: (0, 0)) for a in lead]
    picked = [pl.BlockSpec((rows, width), lambda i, b=b: (0, b)) for b in blocks]
    rest = [pl.BlockSpec(a.shape, lambda i: (0, 0)) for a in more]
    return pl.pallas_call(
        functools.partial(kernel, bias is not None),
        grid=(1,),
        in_specs=[pl.BlockSpec(memory_space=pltpu.SMEM)] + whole + picked + rest,
        out_specs=[pl.BlockSpec(o.shape, lambda i: (0, 0)) for o in out_shape],
        out_shape=out_shape,
        scratch_shapes=[pltpu.VMEM((seqs, length, length), F32)],
        compiler_params=pltpu.CompilerParams(vmem_limit_bytes=40 << 20),
        name=name,
    )(info, *lead, q, kv, kv, *more)


def attend(info, bias, q, kv, blocks, length, width):
    rows = q.shape[0]
    out_shape = [
        jax.ShapeDtypeStruct((rows, width), BF16),
        jax.ShapeDtypeStruct((rows, width), F32),
    ]
    return attend_call(attend_kernel, info, bias, q, kv, blocks, [], out_shape, length, "attend")


def attend_back(info, bias, q, kv, blocks, saved, grad, length, width):
    rows = q.shape[0]
    widths = (width, 2 * width) if bias is None else (3 * width,)
    out_shape = [jax.ShapeDtypeStruct((rows, w), BF16) for w in widths]
    if bias is not None:
        out_shape.append(jax.ShapeDtypeStruct(bias.shape, F32))
    more = [*saved, grad]
    return attend_call(attend_back_kernel, info, bias, q, kv, blocks, more, out_shape, length, "attend_back")


def norm_parts(values, gain):
    scale = lax.rsqrt(jnp.mean(values * values, axis=-1, keepdims=True) + EPS)
    return values * scale * gain, scale


def norm_back(values, scale, gain, grad):
    unit = values * scale
    gain_grad = jnp.sum(grad * unit, axis=0)
    pushed = grad * gain
    back = scale * (pushed - unit * jnp.mean(pushed * unit, axis=-1, keepdims=True))
    return back, gain_grad


def gelu_parts(gate):
    c = 0.7978845608028654
    inner = c * (gate + 0.044715 * gate * gate * gate)
    t = jnp.tanh(inner)
    value = 0.5 * gate * (1.0 + t)
    slope = 0.5 * (1.0 + t) + 0.5 * gate * (1.0 - t * t) * c * (1.0 + 3.0 * 0.044715 * gate * gate)
    return value, slope


def moe_forward(send, w_in, w_down, turn, kept_from):
    experts, rows, width = send.shape
    arrived = lax.all_to_all(send, "expert", split_axis=0, concat_axis=0, tiled=True)
    flat = arrived.reshape(-1, width)
    value, _ = gelu_parts(dot(flat, w_in[0]))
    hidden = (value * dot(flat, w_in[1])).astype(BF16)
    result = dot(hidden, w_down).astype(BF16).reshape(send.shape)
    back = lax.all_to_all(result, "expert", split_axis=0, concat_axis=0, tiled=True)
    if kept_from is None:
        return back, arrived
    mine = lax.axis_index("half") == turn
    return jnp.where(mine, back, kept_from[0]), jnp.where(mine, arrived, kept_from[1])


def flipped(value, bit):
    step = 1 << bit
    return value + step * (1 - 2 * (value // step % 2))


def crossed(value, other):
    for bit in range(other.bit_length()):
        if other >> bit & 1:
            value = flipped(value, bit)
    return value


def greet(partners):
    barrier = pltpu.get_barrier_semaphore()
    for partner in partners:
        pl.semaphore_signal(barrier, inc=1, device_id=partner, device_id_type=MESH)
    pl.semaphore_wait(barrier, len(partners))


def remote(src, dst, out_sem, in_sem, device):
    return pltpu.make_async_remote_copy(
        src_ref=src,
        dst_ref=dst,
        send_sem=out_sem,
        recv_sem=in_sem,
        device_id=device,
        device_id_type=MESH,
    )


def tile_loop(count, step, body):
    @pl.loop(0, count // step)
    def _(i):
        body(pl.multiple_of(i * step, step), step)

    if count % step:
        body(count // step * step, count % step)


def far_first(experts, group):
    return [*range(group, experts), *range(1, group)]


def expert_forward_kernel(turn, group, has_prev, *refs):
    send_ref, w_in, w_down = refs[:3]
    refs = refs[3 + 2 * has_prev :]
    back_out, rows_out, wg, wu, wd, rows, back, made, hidden = refs[:9]
    wsem, s1, r1, s2, r2, osem = refs[9:]
    experts, block, width = send_ref.shape
    ff = wd.shape[0]

    @pl.when(lax.axis_index("half") == turn)
    def _():
        me = lax.axis_index("expert")
        greet([{"expert": crossed(me, k)} for k in range(1, experts)])

        def there(k):
            partner = crossed(me, k)
            return remote(send_ref.at[partner], rows.at[me], s1.at[k], r1.at[k], {"expert": partner})

        def home(k):
            partner = crossed(me, k)
            return remote(made.at[partner], back.at[me], s2.at[k], r2.at[k], {"expert": partner})

        for k in far_first(experts, group):
            there(k).start()
        loads = [
            pltpu.make_async_copy(src, dst, wsem.at[i])
            for i, (src, dst) in enumerate(((w_in.at[0], wg), (w_in.at[1], wu), (w_down, wd)))
        ]
        for load in loads:
            load.start()
        rows[me] = send_ref[me]
        for part in range(experts // group):
            for k in range(part * group, part * group + group):
                if k:
                    there(k).wait_recv()
            base = crossed(me // group, part) * group
            if part == 0:
                loads[0].wait()
                loads[1].wait()

            def up_tile(start, size, base=base):
                x = rows[pl.ds(base, group)].reshape(group * block, width)
                cols = pl.ds(start, size)
                value, _ = gelu_parts(dot(x, wg[:, cols]))
                hidden[:, cols] = (value * dot(x, wu[:, cols])).astype(BF16)

            tile_loop(ff, 512, up_tile)
            if part == 0:
                loads[2].wait()

            def down_tile(start, size, base=base):
                cols = pl.ds(start, size)
                y = dot(hidden[...], wd[:, cols]).astype(BF16)
                made[pl.ds(base, group), :, cols] = y.reshape(group, block, size)

            tile_loop(width, 512, down_tile)
            for k in range(part * group, part * group + group):
                if k:
                    home(k).start()
        rows_copy = pltpu.make_async_copy(rows, rows_out, osem.at[0])
        rows_copy.start()
        back[me] = made[me]
        for k in range(1, experts):
            home(k).wait_recv()
        back_copy = pltpu.make_async_copy(back, back_out, osem.at[1])
        back_copy.start()
        for k in range(1, experts):
            there(k).wait_send()
            home(k).wait_send()
        rows_copy.wait()
        back_copy.wait()


def expert_backward_kernel(turn, group, has_prev, *refs):
    send_ref, own_rows, w_in, w_down = refs[:4]
    refs = refs[4 + 5 * has_prev :]
    back_out, mixed_out, hidden_out, rows_out, grad_out = refs[:5]
    wg, wu, wd, grads, back, made, rows_peer, grads_peer = refs[5:13]
    hidden, dgate, dup = refs[13:16]
    wsem, s1, r1, s2, r2, sx, rx, osem = refs[16:]
    experts, block, width = send_ref.shape
    ff = wd.shape[0]
    span = ff // 2
    total = experts * block
    parts = experts // group

    @pl.when(lax.axis_index("half") == turn)
    def _():
        me, dp = lax.axis_index("expert"), lax.axis_index("dp")
        peer = {"dp": 1 - dp}
        greet([{"expert": crossed(me, k)} for k in range(1, experts)] + [peer])

        def there(k):
            partner = crossed(me, k)
            return remote(send_ref.at[partner], grads.at[me], s1.at[k], r1.at[k], {"expert": partner})

        def home(k):
            partner = crossed(me, k)
            return remote(made.at[partner], back.at[me], s2.at[k], r2.at[k], {"expert": partner})

        def base_of(part):
            return crossed(me // group, part) * group

        rows_over = remote(own_rows, rows_peer, sx.at[parts], rx.at[parts], peer)

        def grads_over(part):
            blocks = pl.ds(base_of(part), group)
            return remote(grads.at[blocks], grads_peer.at[blocks], sx.at[part], rx.at[part], peer)

        for k in far_first(experts, group):
            there(k).start()
        loads = [
            pltpu.make_async_copy(src, dst, wsem.at[i])
            for i, (src, dst) in enumerate(((w_in.at[0], wg), (w_in.at[1], wu), (w_down, wd)))
        ]
        for load in loads:
            load.start()
        rows_over.start()
        grads[me] = send_ref[me]
        loads[0].wait()
        loads[1].wait()

        def up_tile(start, size):
            x = own_rows[...].reshape(total, width)
            cols = pl.ds(start, size)
            value, slope = gelu_parts(dot(x, wg[:, cols]))
            up = dot(x, wu[:, cols])
            hidden[:, cols] = (value * up).astype(BF16)
            dup[:, cols] = value.astype(BF16)
            dgate[:, cols] = (up * slope).astype(BF16)

        tile_loop(ff, 512, up_tile)
        loads[2].wait()
        for part in range(parts):
            for k in range(part * group, part * group + group):
                if k:
                    there(k).wait_recv()
            grads_over(part).start()
            base = base_of(part)
            span_rows = pl.ds(pl.multiple_of(base * block, group * block), group * block)

            def hidden_tile(start, size, base=base, span_rows=span_rows):
                dy = grads[pl.ds(base, group)].reshape(group * block, width)
                cols = pl.ds(start, size)
                dhidden = dot(dy, wd[cols, :], NT)
                dgate[span_rows, cols] = (dhidden * dgate[span_rows, cols].astype(F32)).astype(BF16)
                dup[span_rows, cols] = (dhidden * dup[span_rows, cols].astype(F32)).astype(BF16)

            tile_loop(ff, 512, hidden_tile)

            def rows_tile(start, size, base=base, span_rows=span_rows):
                cols = pl.ds(start, size)
                dr = dot(dgate[span_rows, :], wg[cols, :], NT) + dot(dup[span_rows, :], wu[cols, :], NT)
                made[pl.ds(base, group), :, cols] = dr.astype(BF16).reshape(group, block, size)

            tile_loop(width, 512, rows_tile)
            for k in range(part * group, part * group + group):
                if k:
                    home(k).start()
        back[me] = made[me]
        half_cols = pl.ds(pl.multiple_of(dp * span, 128), span)
        outs = [
            (dgate.at[:, half_cols], mixed_out.at[0, 0]),
            (dup.at[:, half_cols], mixed_out.at[1, 0]),
            (hidden.at[:, half_cols], hidden_out.at[0]),
            (own_rows, rows_out.at[0]),
            (grads, grad_out.at[0]),
        ]
        outs = [pltpu.make_async_copy(src, dst, osem.at[i]) for i, (src, dst) in enumerate(outs)]
        for out in outs:
            out.start()

        rows_over.wait_recv()
        for part in range(parts):
            grads_over(part).wait_recv()

        def peer_tile(start, size):
            x = rows_peer[...].reshape(total, width)
            dy = grads_peer[...].reshape(total, width)
            here = pl.ds(pl.multiple_of((1 - dp) * span + start, 128), size)
            cols = pl.ds(pl.multiple_of(dp * span + start, 128), size)
            value, slope = gelu_parts(dot(x, wg[:, cols]))
            up = dot(x, wu[:, cols])
            dhidden = dot(dy, wd[cols, :], NT)
            hidden[:, here] = (value * up).astype(BF16)
            dgate[:, here] = (dhidden * up * slope).astype(BF16)
            dup[:, here] = (dhidden * value).astype(BF16)

        tile_loop(span, 512, peer_tile)
        other_cols = pl.ds(pl.multiple_of((1 - dp) * span, 128), span)
        peers = [
            (dgate.at[:, other_cols], mixed_out.at[0, 1]),
            (dup.at[:, other_cols], mixed_out.at[1, 1]),
            (hidden.at[:, other_cols], hidden_out.at[1]),
            (rows_peer, rows_out.at[1]),
            (grads_peer, grad_out.at[1]),
        ]
        peers = [pltpu.make_async_copy(src, dst, osem.at[5 + i]) for i, (src, dst) in enumerate(peers)]
        for out in peers:
            out.start()
        for k in range(1, experts):
            home(k).wait_recv()
        back_copy = pltpu.make_async_copy(back, back_out, osem.at[10])
        back_copy.start()
        for k in range(1, experts):
            there(k).wait_send()
            home(k).wait_send()
        rows_over.wait_send()
        for part in range(parts):
            grads_over(part).wait_send()
        for out in [*outs, *peers, back_copy]:
            out.wait()


def group_of(experts, block):
    group = 1
    while group * 2 * block <= 320 and group * 2 <= experts:
        group *= 2
    return group


def expert_call(kernel, turn, inputs, weights, prev, out_shape, scratch, name):
    experts, block, _ = inputs[0].shape
    vmem, hbm = pl.BlockSpec(memory_space=pltpu.VMEM), pl.BlockSpec(memory_space=pl.ANY)
    prev = list(prev or [])
    first = len(inputs) + len(weights)
    return pl.pallas_call(
        functools.partial(kernel, turn, group_of(experts, block), bool(prev)),
        in_specs=[vmem] * len(inputs) + [hbm] * (len(weights) + len(prev)),
        out_specs=[hbm] * len(out_shape),
        out_shape=out_shape,
        input_output_aliases={first + i: i for i in range(len(prev))},
        scratch_shapes=scratch,
        compiler_params=pltpu.CompilerParams(
            collective_id=1 + turn + 2 * (len(inputs) - 1),
            has_side_effects=True,
            vmem_limit_bytes=60 << 20,
        ),
        name=name,
    )(*inputs, *weights, *prev)


def moe_forward(send, w_in, w_down, turn, prev):
    experts, block, width = send.shape
    ff = w_down.shape[0]
    group = group_of(experts, block)
    dma = pltpu.SemaphoreType.DMA
    scratch = [
        pltpu.VMEM((width, ff), BF16),
        pltpu.VMEM((width, ff), BF16),
        pltpu.VMEM((ff, width), BF16),
        *[pltpu.VMEM(send.shape, BF16)] * 3,
        pltpu.VMEM((group * block, ff), BF16),
        dma((3,)),
        *[dma((experts,))] * 4,
        dma((2,)),
    ]
    out_shape = [jax.ShapeDtypeStruct(send.shape, BF16)] * 2
    return expert_call(
        expert_forward_kernel, turn, [send], [w_in, w_down], prev, out_shape, scratch, "moe_forward"
    )


def moe_backward(grad_send, received, w_in, w_down, turn, prev):
    experts, block, width = grad_send.shape
    ff = w_down.shape[0]
    total = experts * block
    parts = experts // group_of(experts, block)
    dma = pltpu.SemaphoreType.DMA
    scratch = [
        pltpu.VMEM((width, ff), BF16),
        pltpu.VMEM((width, ff), BF16),
        pltpu.VMEM((ff, width), BF16),
        *[pltpu.VMEM(grad_send.shape, BF16)] * 5,
        *[pltpu.VMEM((total, ff), BF16)] * 3,
        dma((3,)),
        *[dma((experts,))] * 4,
        dma((parts + 1,)),
        dma((parts + 1,)),
        dma((11,)),
    ]
    out_shape = [
        jax.ShapeDtypeStruct(grad_send.shape, BF16),
        jax.ShapeDtypeStruct((2, 2, total, ff // 2), BF16),
        jax.ShapeDtypeStruct((2, total, ff // 2), BF16),
        jax.ShapeDtypeStruct((2, *grad_send.shape), BF16),
        jax.ShapeDtypeStruct((2, *grad_send.shape), BF16),
    ]
    return expert_call(
        expert_backward_kernel,
        turn,
        [grad_send, received],
        [w_in, w_down],
        prev,
        out_shape,
        scratch,
        "moe_backward",
    )


def dense_kernel(stages, chunk, lag, *refs):
    sources, small_ref = refs[:7], refs[7]
    out_refs, small_out, small_in = refs[8:11], refs[11], refs[12]
    held, refs = refs[13:20], refs[20:]
    xt_ref, own_refs, peer_refs = held[0], held[1:4], held[4:7]
    sums, parts = refs[:stages], refs[stages : 2 * stages]
    ss, rs, sk, rk, sl = refs[2 * stages :]
    counts = [ref.shape[1] // chunk for ref in own_refs]
    starts = [sum(counts[:i]) for i in range(3)]
    chunks = sum(counts)
    per_cross = counts[2] // 2
    half = xt_ref.shape[2] // 2
    dp, me = lax.axis_index("dp"), lax.axis_index("expert")
    peer = {"dp": 1 - dp}
    partners = [flipped(me, k) for k in range(stages)]
    bits = [me // (1 << k) % 2 for k in range(stages)]
    loads = [
        pltpu.make_async_copy(sources[i], held[i], sl.at[i]) for i in (0, 1, 4, 2, 5, 3, 6)
    ]
    for load in loads:
        load.start()
    greet([peer] + [{"expert": p} for p in partners])

    def send_small(step):
        src = small_ref if step == 0 else small_out.at[step - 1]
        device = peer if step == 0 else {"expert": partners[step - 1]}
        return remote(src, small_in.at[step], ss.at[step], rs.at[step], device)

    def picked(k, c, values):
        if k > 1:
            return values[k]
        odd = lax.rem(c, 2)
        return values[k] + odd * (values[1 - k] - values[k])

    def send_first(c, odd):
        src = sums[0].at[c, :, 1 - bits[1]] if odd else sums[0].at[c, :, :, 1 - bits[0]]
        return remote(src, parts[0].at[c], sk.at[0, c], rk.at[0, c], {"expert": partners[odd]})

    def send_part(k, c):
        src = sums[k].at[c, :, 1 - picked(k, c, bits)]
        return remote(src, parts[k].at[c], sk.at[k, c], rk.at[k, c], {"expert": picked(k, c, partners)})

    def by_parity(c, body):
        for odd in range(2):

            @pl.when(lax.rem(c, 2) == odd)
            def _(odd=odd):
                body(odd)

    send_small(0).start()

    def step(i, carry):
        for g in range(3):

            @pl.when(i == starts[g])
            def _(g=g):
                for load in loads[2 * g + (g > 0) : 2 * g + 3]:
                    load.wait()

            @pl.when((i >= starts[g]) & (i < starts[g] + counts[g]))
            def _(g=g):
                c = i - starts[g]
                cols = pl.ds(pl.multiple_of(c * chunk, chunk), chunk)
                which = g if g < 2 else 2 + c // per_cross
                total = dot(xt_ref[which, :, :half], own_refs[g][:, cols])
                total += dot(xt_ref[which, :, half:], peer_refs[g][:, cols])
                sums[0][i] = total.astype(BF16).reshape(sums[0].shape[1:])
                by_parity(i, lambda odd: send_first(i, odd).start())

        for k in range(stages):
            c = i - lag * (k + 1)

            @pl.when((c >= 0) & (c < chunks))
            def _(k=k, c=c):
                def add(mine):
                    total = mine.astype(F32) + parts[k][c].astype(F32)
                    if k + 1 < stages:
                        sums[k + 1][c] = total.astype(BF16).reshape(sums[k + 1].shape[1:])
                        send_part(k + 1, c).start()
                    else:
                        total = total.reshape(total.shape[-2:])
                        for g in range(3):

                            @pl.when((c >= starts[g]) & (c < starts[g] + counts[g]))
                            def _(g=g):
                                at = pl.multiple_of((c - starts[g]) * chunk, chunk)
                                out_refs[g][:, pl.ds(at, chunk)] = total

                if k == 0:

                    def first(odd):
                        send_first(c, odd).wait_recv()
                        add(sums[0][c, :, bits[1]] if odd else sums[0][c, :, :, bits[0]])

                    by_parity(c, first)
                else:
                    send_part(k, c).wait_recv()
                    add(sums[k][c, :, picked(k, c, bits)])

        for j in range(stages + 1):

            @pl.when(i == j)
            def _(j=j):
                send_small(j).wait_recv()
                own = small_ref[...] if j == 0 else small_out[j - 1]
                small_out[j] = own + small_in[j]
                if j < stages:
                    send_small(j + 1).start()

        return carry

    lax.fori_loop(0, chunks + lag * stages, step, 0)

    def finish(c, carry):
        by_parity(c, lambda odd: send_first(c, odd).wait_send())
        for k in range(1, stages):
            send_part(k, c).wait_send()
        return carry

    lax.fori_loop(0, chunks, finish, 0)
    for j in range(stages + 1):
        send_small(j).wait_send()


def over_dp(array):
    return lax.ppermute(array, "dp", [(0, 1), (1, 0)])


def both_halves(x):
    half = x.shape[1] // 2
    dp = lax.axis_index("dp")
    own = lax.dynamic_slice_in_dim(x, dp * half, half, 1)
    other = lax.dynamic_slice_in_dim(x, (1 - dp) * half, half, 1)
    return own, other


def dense_gradients(xt, own, peer, small, experts):
    chunk = 512
    half_rows = xt.shape[1]
    chunks = sum(y.shape[1] for y in own) // chunk
    stages = experts.bit_length() - 1
    keep = half_rows // experts
    vmem, hbm = pl.BlockSpec(memory_space=pltpu.VMEM), pl.BlockSpec(memory_space=pl.ANY)
    dma = pltpu.SemaphoreType.DMA
    sources = [xt, *own, *peer]
    blocks = [(experts // 4, 2, 2)] + [(experts >> (k + 1), 2) for k in range(1, stages)]
    halved = [(experts // 4, 2)] + [(experts >> (k + 1),) for k in range(1, stages)]
    scratch = [pltpu.VMEM((stages + 1, *small.shape), F32)]
    scratch += [pltpu.VMEM(a.shape, BF16) for a in sources]
    scratch += [pltpu.VMEM((chunks, *b, keep, chunk), BF16) for b in blocks + halved]
    scratch += [dma((stages + 1,)), dma((stages + 1,)), dma((stages, chunks)), dma((stages, chunks))]
    scratch += [dma((len(sources),))]
    *outs, sums = pl.pallas_call(
        functools.partial(dense_kernel, stages, chunk, 3),
        in_specs=[hbm] * len(sources) + [vmem],
        out_specs=[vmem] * 4,
        out_shape=[
            *(jax.ShapeDtypeStruct((keep, y.shape[1]), F32) for y in own),
            jax.ShapeDtypeStruct((stages + 1, *small.shape), F32),
        ],
        scratch_shapes=scratch,
        compiler_params=pltpu.CompilerParams(
            collective_id=0, has_side_effects=True, vmem_limit_bytes=56 << 20
        ),
        name="dense_gradients",
    )(*sources, small)
    return outs, sums[stages]


def product_kernel(x_ref, y_ref, out_ref):
    out_ref[...] = dot(x_ref[...], y_ref[...].reshape(y_ref.shape[-2:]), TN).reshape(out_ref.shape)


def expert_gradients(rows, mixed, hidden, grads):
    total, width = rows.shape
    span = hidden.shape[1]
    tile = 256
    params = pltpu.CompilerParams(vmem_limit_bytes=40 << 20)
    din = pl.pallas_call(
        product_kernel,
        grid=(2, width // tile),
        in_specs=[
            pl.BlockSpec((total, tile), lambda g, i: (0, i)),
            pl.BlockSpec((1, total, span), lambda g, i: (g, 0, 0)),
        ],
        out_specs=pl.BlockSpec((1, tile, span), lambda g, i: (g, i, 0)),
        out_shape=jax.ShapeDtypeStruct((2, width, span), F32),
        compiler_params=params,
        name="expert_in_gradient",
    )(rows, mixed)
    ddown = pl.pallas_call(
        product_kernel,
        grid=(pl.cdiv(span, tile),),
        in_specs=[
            pl.BlockSpec((total, tile), lambda i: (0, i)),
            pl.BlockSpec((total, width), lambda i: (0, 0)),
        ],
        out_specs=pl.BlockSpec((tile, width), lambda i: (i, 0)),
        out_shape=jax.ShapeDtypeStruct((span, width), F32),
        compiler_params=params,
        name="expert_out_gradient",
    )(hidden, grads)
    return din, ddown


def body(
    tokens,
    cotangent,
    lengths,
    routes,
    self_qkv,
    self_out,
    cross_weights,
    router,
    gains,
    bias_table,
    expert_in,
    expert_out,
):
    _, seqs, length, width = tokens.shape
    heads = H
    experts = router.shape[2]
    top = routes.shape[3]
    capacity = (5 * top * length + 4 * experts - 1) // (4 * experts)
    block_rows = -(-seqs * capacity // 16) * 16
    rows = seqs * length
    slots = experts * block_rows
    half_index = lax.axis_index("half")
    decoder = half_index == 1
    wqkv, wout, wcross, wrouter, gain = (
        self_qkv[0],
        self_out[0],
        cross_weights[0],
        router[0],
        gains[0],
    )
    w_in, w_down = expert_in[0, 0], expert_out[0, 0]

    column = np.arange(2 * length)
    hot, hot_back = (
        (
            jnp.where(decoder, *reversed(diagonal_buckets(diff)))[:, None]
            == jnp.arange(BUCKETS)[None, :]
        ).astype(F32)
        for diff in (np.where(column < length, column, column - 2 * length), column - length + 1)
    )
    bias = lax.dot_general(
        bias_table[0].reshape(BUCKETS, heads),
        hot,
        (((0,), (1,)), ((), ())),
        precision=lax.Precision.HIGHEST,
        preferred_element_type=F32,
    )
    own_lengths = jnp.where(decoder, lengths[1], lengths[0])
    self_info = jnp.concatenate([own_lengths, half_index[None]]).astype(jnp.int32)
    cross_info = jnp.concatenate([lengths[0], jnp.zeros((1,), jnp.int32)]).astype(jnp.int32)

    order = jnp.transpose(routes[0], (0, 2, 1)).reshape(seqs, top * length)
    expert_ids = jnp.arange(experts, dtype=jnp.int32)
    picked = (order[:, :, None] == expert_ids).astype(BF16)
    earlier = np.tril(np.ones((top * length, top * length), np.float32), -1).astype(BF16)
    before = jnp.einsum("pq,sqe->spe", earlier, picked, preferred_element_type=F32)
    place = jnp.sum(before * picked.astype(F32), axis=2).astype(jnp.int32)
    kept = place < capacity
    base = order * block_rows + jnp.arange(seqs, dtype=jnp.int32)[:, None] * capacity
    target = jnp.where(kept, base + place, -1).reshape(seqs, top, length)
    target = jnp.transpose(target, (1, 0, 2)).reshape(top, rows)
    slot_ids = jnp.arange(slots, dtype=jnp.int32)
    spots = (target[:, :, None] == slot_ids).astype(BF16)
    both = jnp.sum(spots.astype(F32), axis=0).astype(BF16)
    stacked = spots.reshape(top * rows, slots)
    kept_hot = picked.astype(F32) * kept[:, :, None].astype(F32)
    kept_count = jnp.sum(kept_hot, axis=(0, 1))
    all_count = jnp.sum(picked.astype(F32), axis=(0, 1))
    tallies = jnp.concatenate([kept_count, all_count - kept_count])
    route_hot = (routes[0].reshape(rows, top, 1) == expert_ids).astype(F32)

    def route(values):
        normed, scale = norm_parts(values, gain[1])
        low = normed.astype(BF16)
        rest = (normed - low.astype(F32)).astype(BF16)
        logits = dot(low, wrouter) + dot(rest, wrouter)
        probs = jax.nn.softmax(logits, axis=-1)
        chosen = jnp.sum(probs[:, None, :] * route_hot, axis=-1)
        total = jnp.sum(chosen, axis=-1, keepdims=True)
        gates = chosen / total
        send = dot(both, low, TN).astype(BF16).reshape(experts, block_rows, width)
        return dict(scale=scale, low=low, probs=probs, gates=gates, total=total, send=send)

    def fetch(returned):
        flat = returned.reshape(slots, width)
        return dot(stacked, flat).reshape(top, rows, width)

    def combine(values, gates, results):
        return values + jnp.sum(jnp.transpose(gates)[:, :, None] * results, axis=0)

    values = tokens[0].reshape(rows, width).astype(F32)
    normed, scale0 = norm_parts(values, gain[0])
    low0 = normed.astype(BF16)
    qkv = dot(low0, wqkv).astype(BF16)
    mixed0, log0 = attend(self_info, bias, qkv, qkv, (0, 1, 2), length, width)
    first = values + dot(mixed0, wout)

    state = route(first)
    returned, received = moe_forward(state["send"], w_in, w_down, 0, None)
    final_enc = combine(first, state["gates"], fetch(returned))
    normed, scale_m = norm_parts(final_enc, gain[2])
    low_m = normed.astype(BF16)
    memory = dot(low_m, wcross).astype(BF16)
    names = ("half", "dp", "expert")
    forward_pairs, back_pairs = half_pairs(lax.axis_size("dp") * lax.axis_size("expert"))
    memory = lax.ppermute(memory, names, forward_pairs)

    normed, scale_c = norm_parts(first, gain[2])
    low_c = normed.astype(BF16)
    query = dot(low_c, wcross[:, :width]).astype(BF16)
    mixed_c, log_c = attend(cross_info, None, query, memory, (0, 0, 1), length, width)
    second = jnp.where(decoder, first + dot(mixed_c, wcross[:, width:]), first)

    state = route(second)
    returned, received = moe_forward(state["send"], w_in, w_down, 1, (returned, received))
    results = fetch(returned)
    final = combine(second, state["gates"], results)
    outputs = final.astype(BF16)

    def moe_gradient(grad):
        dgates = jnp.transpose(jnp.sum(grad[None] * results, axis=-1))
        spread = (jnp.transpose(state["gates"])[:, :, None] * grad[None]).astype(BF16)
        send = dot(stacked, spread.reshape(top * rows, width), TN)
        return dgates, send.astype(BF16).reshape(experts, block_rows, width)

    def moe_input_gradient(grad, dgates, back):
        gates, total, probs = state["gates"], state["total"], state["probs"]
        dchosen = (dgates - jnp.sum(dgates * gates, axis=-1, keepdims=True)) / total
        dprobs = jnp.sum(dchosen[:, :, None] * route_hot, axis=1)
        dlogits = probs * (dprobs - jnp.sum(dprobs * probs, axis=-1, keepdims=True))
        dnormed = dot(both, back.reshape(slots, width)) + lax.dot_general(
            dlogits, wrouter.astype(F32), NT, preferred_element_type=F32
        )
        dvalues, dgain = norm_back(second, state["scale"], gain[1], dnormed)
        normed = second * state["scale"] * gain[1]
        drouter = lax.dot_general(
            normed, dlogits, TN, precision=lax.Precision.HIGHEST, preferred_element_type=F32
        )
        return grad + dvalues, dgain, drouter

    grad_dec = cotangent[0].reshape(rows, width).astype(F32)
    dgates, grad_send = moe_gradient(grad_dec)
    kept_from = moe_backward(grad_send, received, w_in, w_down, 1, None)
    grad_second, _, _ = moe_input_gradient(grad_dec, dgates, kept_from[0])

    dbranch_c = grad_second.astype(BF16)
    dmixed_c = dot(dbranch_c, wcross[:, width:], NT).astype(BF16)
    dquery, dmemory = attend_back(
        cross_info, None, query, memory, (0, 0, 1), (mixed_c, log_c), dmixed_c, length, width
    )
    dmemory = lax.ppermute(dmemory, names, back_pairs)
    dnormed = dot(dquery, wcross[:, :width], NT)
    dvalues, dgain_c = norm_back(first, scale_c, gain[2], dnormed)
    grad_first_dec = grad_second + dvalues

    dnormed = dot(dmemory, wcross, NT)
    dvalues, dgain_m = norm_back(final_enc, scale_m, gain[2], dnormed)
    grad = jnp.where(decoder, grad_dec, grad_dec + dvalues)
    dgates, grad_send = moe_gradient(grad)
    owns, others = zip(
        *map(
            both_halves,
            (low0, mixed0, jnp.where(decoder, low_c, low_m), jnp.where(decoder, mixed_c, low_m)),
        )
    )
    lefts = jnp.concatenate([jnp.stack(owns), over_dp(jnp.stack(others))], axis=1)
    xt = jnp.transpose(lefts, (0, 2, 1))
    grad_send, xt = lax.optimization_barrier((grad_send, xt))
    back, mixed_grads, hidden, all_rows, all_grad = moe_backward(
        grad_send, received, w_in, w_down, 0, kept_from
    )
    grad_second, dgain_moe, drouter = moe_input_gradient(grad, dgates, back)
    grad_first = jnp.where(decoder, grad_first_dec, grad_second)

    dbranch = grad_first.astype(BF16)
    dmixed = dot(dbranch, wout, NT).astype(BF16)
    dqkv_rows, diag = attend_back(
        self_info, bias, qkv, qkv, (0, 1, 2), (mixed0, log0), dmixed, length, width
    )
    dnormed = dot(dqkv_rows, wqkv, NT)
    dvalues, dgain_self = norm_back(values, scale0, gain[0], dnormed)
    d_tokens = (grad_first + dvalues).astype(BF16)
    dtable = lax.dot_general(
        hot_back, diag, (((0,), (1,)), ((), ())), precision=lax.Precision.HIGHEST,
        preferred_element_type=F32,
    ).reshape(-1)

    cross_grad = jnp.where(decoder, jnp.concatenate([dquery, dbranch_c], axis=1), dmemory)
    own_grads = (dqkv_rows, dbranch, cross_grad)
    peer_grads = tuple(map(over_dp, own_grads))
    places = 2 * experts
    own = width // places
    extra = jnp.concatenate([dtable.reshape(places, -1), tallies.reshape(places, 1)], axis=1)
    extra = jnp.pad(extra, ((0, 0), (0, -extra.shape[1] % own)))
    small = jnp.concatenate(
        [
            jnp.transpose(drouter),
            jnp.stack([dgain_self, dgain_moe, jnp.where(decoder, dgain_c, dgain_m)]),
            jnp.swapaxes(extra.reshape(places, -1, own), 0, 1).reshape(-1, width),
        ]
    )
    small = jnp.pad(small, ((0, -small.shape[0] % 8), (0, 0)))
    (dqkv, dout, dcross), small = dense_gradients(xt, own_grads, peer_grads, small, experts)
    place = lax.axis_index("dp") * experts + lax.axis_index("expert")
    mine = lax.dynamic_slice_in_dim(small, place * own, own, 1)
    tail = mine[experts + 3 :].reshape(-1)
    own_table = dtable.shape[0] // places
    d_table = tail[:own_table]
    counts = tail[own_table].astype(jnp.int32)

    ff_half = hidden.shape[-1]
    din, ddown = expert_gradients(
        all_rows.reshape(-1, width),
        mixed_grads.reshape(2, -1, ff_half),
        hidden.reshape(-1, ff_half),
        all_grad.reshape(-1, width),
    )
    return (
        outputs.reshape(1, seqs, length, width),
        d_tokens.reshape(1, seqs, length, width),
        dqkv[None],
        dout[None],
        dcross[None],
        jnp.transpose(mine[:experts])[None],
        mine[experts : experts + 3][None],
        d_table[None],
        din[None, None],
        ddown[None, None],
        counts.reshape(1, 1, 1),
    )


def half_pairs(count):
    return (
        [(i, count + i) for i in range(count)],
        [(count + i, i) for i in range(count)],
    )


def solution(mesh):
    placed = (
        P("half", ("dp", "expert"), None, None),
        P("half", ("dp", "expert"), None, None),
        P(None, ("dp", "expert")),
        P("half", ("dp", "expert"), None, None),
        P("half", None, None),
        P("half", None, None),
        P("half", None, None),
        P("half", None, None),
        P("half", None, None),
        P("half", None),
        P("half", "expert", None, None, None),
        P("half", "expert", None, None),
    )
    return jax.shard_map(
        body,
        mesh=mesh,
        in_specs=placed,
        out_specs=(
            P("half", ("dp", "expert"), None, None),
            P("half", ("dp", "expert"), None, None),
            P("half", ("dp", "expert"), None),
            P("half", ("dp", "expert"), None),
            P("half", ("dp", "expert"), None),
            P("half", ("dp", "expert"), None),
            P("half", None, ("dp", "expert")),
            P("half", ("dp", "expert")),
            P("half", "expert", None, None, "dp"),
            P("half", "expert", "dp", None),
            P("half", "dp", "expert"),
        ),
        check_vma=False,
    )
```

```python
import functools

import jax
import jax.numpy as jnp
import numpy as np
from jax import lax
from jax.experimental import pallas as pl
from jax.experimental.pallas import tpu as pltpu
from jax.sharding import PartitionSpec as P

H = 16
BUCKETS = 32
EPS = 1e-06
ENC_STEPS = (12, 16, 23, 32, 46, 64, 91)
DEC_STEPS = (19, 21, 24, 27, 31, 35, 40, 46, 52, 59, 67, 77, 87, 99, 113)
F32 = jnp.float32
BF16 = jnp.bfloat16
MESH = pl.DeviceIdType.MESH
NT = (((1,), (1,)), ((), ()))
TN = (((0,), (0,)), ((), ()))


def dot(a, b, dims=(((1,), (0,)), ((), ()))):
    return lax.dot_general(a, b, dims, preferred_element_type=F32)


def diagonal_buckets(diff):
    apart = np.abs(diff)
    coarse = 8 + sum((apart >= step).astype(np.int32) for step in ENC_STEPS)
    enc = np.where(apart < 8, apart, coarse) + 16 * (diff > 0)
    behind = np.maximum(-diff, 0)
    coarse = 16 + sum((behind >= step).astype(np.int32) for step in DEC_STEPS)
    dec = np.where(behind < 16, behind, coarse)
    return enc.astype(np.int32), dec.astype(np.int32)


def diagonals(bias_ref, head, length):
    row = jnp.broadcast_to(bias_ref[pl.ds(head, 1), :], (length, 2 * length))
    return pltpu.roll(row, 0, 1, stride=1, stride_axis=0)[:, :length]


def fill_masks(info, mask_ref):
    seqs, length, _ = mask_ref.shape
    row_id = lax.broadcasted_iota(jnp.int32, (length, length), 0)
    col_id = lax.broadcasted_iota(jnp.int32, (length, length), 1)
    reach = jnp.where(info[seqs] > 0, row_id, length)
    for seq in range(seqs):
        allowed = (col_id < info[seq]) & (col_id <= reach)
        mask_ref[seq] = jnp.where(allowed, 0.0, -1000000000.0)


def attend_kernel(has_bias, info, *refs):
    bias_ref, refs = (refs[0], refs[1:]) if has_bias else (None, refs)
    q_ref, k_ref, v_ref, out_ref, log_ref, mask_ref = refs
    seqs, length, _ = mask_ref.shape
    low = lax.broadcasted_iota(jnp.int32, (length, 128), 1) < 64
    fill_masks(info, mask_ref)

    @pl.loop(0, q_ref.shape[1] // 128, unroll=True)
    def _(pair):
        cols = pl.ds(pl.multiple_of(pair * 128, 128), 128)
        biases = [diagonals(bias_ref, 2 * pair + side, length) if has_bias else 0.0 for side in range(2)]
        for seq in range(seqs):
            rows = pl.ds(seq * length, length)
            q, k, v = q_ref[rows, cols] * 0.125, k_ref[rows, cols], v_ref[rows, cols]
            mixed, peaks = [], []
            for side in range(2):
                mine = low if side == 0 else jnp.logical_not(low)
                part = jnp.where(mine, q, jnp.zeros_like(q))
                scores = dot(part, k, NT) + (mask_ref[seq] + biases[side])
                peak = jnp.max(scores, axis=-1, keepdims=True)
                spread = jnp.exp(scores - peak).astype(BF16)
                mixed.append(dot(spread, jnp.where(mine, v, jnp.ones_like(v))))
                peaks.append(peak)
            total = pltpu.roll(jnp.where(low, mixed[1], mixed[0]), 64, 1)
            out_ref[rows, cols] = (jnp.where(low, mixed[0], mixed[1]) / total).astype(BF16)
            log_ref[rows, cols] = jnp.where(low, peaks[0], peaks[1]) + jnp.log(total)


def attend_back_kernel(has_bias, info, *refs):
    if has_bias:
        bias_ref, q_ref, k_ref, v_ref, a_ref, log_ref, g_ref, dq_ref, diag_ref, mask_ref = refs
        dkv_ref, shift = dq_ref, q_ref.shape[1]
    else:
        q_ref, k_ref, v_ref, a_ref, log_ref, g_ref, dq_ref, dkv_ref, mask_ref = refs
        shift = 0
    seqs, length, _ = mask_ref.shape
    width = q_ref.shape[1]
    low = lax.broadcasted_iota(jnp.int32, (length, 128), 1) < 64
    fill_masks(info, mask_ref)
    if has_bias:
        row_id = lax.broadcasted_iota(jnp.int32, (length, length), 0)
        col_id = lax.broadcasted_iota(jnp.int32, (length, length), 1)
        flip = (row_id + col_id == length - 1).astype(F32).astype(BF16)

    @pl.loop(0, width // 128, unroll=True)
    def _(pair):
        cols = pl.ds(pl.multiple_of(pair * 128, 128), 128)
        kcols = pl.ds(pl.multiple_of(shift + pair * 128, 128), 128)
        vcols = pl.ds(pl.multiple_of(shift + width + pair * 128, 128), 128)
        biases = [diagonals(bias_ref, 2 * pair + side, length) if has_bias else 0.0 for side in range(2)]
        sums = [0.0, 0.0]
        for seq in range(seqs):
            rows = pl.ds(seq * length, length)
            q, k, v, g = q_ref[rows, cols] * 0.125, k_ref[rows, cols], v_ref[rows, cols], g_ref[rows, cols]
            logs = log_ref[rows, cols]
            turned = pltpu.roll(logs, 64, 1)
            product = g.astype(F32) * a_ref[rows, cols].astype(F32)
            minus = (-pltpu.roll(product, 64, 1)).astype(BF16)
            scaled = k * 0.125
            dqs, dks, dvs = [], [], []
            for side in range(2):
                mine = low if side == 0 else jnp.logical_not(low)
                part = jnp.where(mine, q, jnp.zeros_like(q))
                scores = dot(part, k, NT) + (mask_ref[seq] + biases[side])
                probs = jnp.exp(scores - jnp.where(mine, logs, turned))
                dvs.append(dot(probs.astype(BF16), g, TN))
                centred = dot(jnp.where(mine, g, minus), jnp.where(mine, v, jnp.ones_like(v)), NT)
                dlow = (probs * centred).astype(BF16)
                dqs.append(dot(dlow, scaled))
                dks.append(dot(dlow, q, TN))
                if has_bias:
                    sums[side] = sums[side] + dlow.astype(F32)
            dq_ref[rows, cols] = jnp.where(low, dqs[0], dqs[1]).astype(BF16)
            dkv_ref[rows, kcols] = jnp.where(low, dks[0], dks[1]).astype(BF16)
            dkv_ref[rows, vcols] = jnp.where(low, dvs[0], dvs[1]).astype(BF16)
        if has_bias:
            for side in range(2):
                upside = dot(flip, sums[side].astype(BF16))
                wide = jnp.concatenate([upside, jnp.zeros((length, length), F32)], axis=1)
                turned = pltpu.roll(wide, 0, 1, stride=1, stride_axis=0)
                diag_ref[pl.ds(2 * pair + side, 1), :] = jnp.sum(turned, axis=0, keepdims=True)


def attend_call(kernel, info, bias, q, kv, blocks, more, out_shape, length, name):
    rows = q.shape[0]
    seqs = rows // length
    width = more[0].shape[1] if more else out_shape[0].shape[1]
    lead = [] if bias is None else [bias]
    whole = [pl.BlockSpec(a.shape, lambda i: (0, 0)) for a in lead]
    picked = [pl.BlockSpec((rows, width), lambda i, b=b: (0, b)) for b in blocks]
    rest = [pl.BlockSpec(a.shape, lambda i: (0, 0)) for a in more]
    return pl.pallas_call(
        functools.partial(kernel, bias is not None),
        grid=(1,),
        in_specs=[pl.BlockSpec(memory_space=pltpu.SMEM)] + whole + picked + rest,
        out_specs=[pl.BlockSpec(o.shape, lambda i: (0, 0)) for o in out_shape],
        out_shape=out_shape,
        scratch_shapes=[pltpu.VMEM((seqs, length, length), F32)],
        compiler_params=pltpu.CompilerParams(vmem_limit_bytes=40 << 20),
        name=name,
    )(info, *lead, q, kv, kv, *more)


def attend(info, bias, q, kv, blocks, length, width):
    rows = q.shape[0]
    out_shape = [
        jax.ShapeDtypeStruct((rows, width), BF16),
        jax.ShapeDtypeStruct((rows, width), F32),
    ]
    return attend_call(attend_kernel, info, bias, q, kv, blocks, [], out_shape, length, "attend")


def attend_back(info, bias, q, kv, blocks, saved, grad, length, width):
    rows = q.shape[0]
    widths = (width, 2 * width) if bias is None else (3 * width,)
    out_shape = [jax.ShapeDtypeStruct((rows, w), BF16) for w in widths]
    if bias is not None:
        out_shape.append(jax.ShapeDtypeStruct(bias.shape, F32))
    more = [*saved, grad]
    return attend_call(attend_back_kernel, info, bias, q, kv, blocks, more, out_shape, length, "attend_back")


def norm_parts(values, gain):
    scale = lax.rsqrt(jnp.mean(values * values, axis=-1, keepdims=True) + EPS)
    return values * scale * gain, scale


def norm_back(values, scale, gain, grad):
    unit = values * scale
    gain_grad = jnp.sum(grad * unit, axis=0)
    pushed = grad * gain
    back = scale * (pushed - unit * jnp.mean(pushed * unit, axis=-1, keepdims=True))
    return back, gain_grad


def gelu_parts(gate):
    c = 0.7978845608028654
    inner = c * (gate + 0.044715 * gate * gate * gate)
    t = jnp.tanh(inner)
    value = 0.5 * gate * (1.0 + t)
    slope = 0.5 * (1.0 + t) + 0.5 * gate * (1.0 - t * t) * c * (1.0 + 3.0 * 0.044715 * gate * gate)
    return value, slope


def moe_forward(send, w_in, w_down, turn, kept_from):
    experts, rows, width = send.shape
    arrived = lax.all_to_all(send, "expert", split_axis=0, concat_axis=0, tiled=True)
    flat = arrived.reshape(-1, width)
    value, _ = gelu_parts(dot(flat, w_in[0]))
    hidden = (value * dot(flat, w_in[1])).astype(BF16)
    result = dot(hidden, w_down).astype(BF16).reshape(send.shape)
    back = lax.all_to_all(result, "expert", split_axis=0, concat_axis=0, tiled=True)
    if kept_from is None:
        return back, arrived
    mine = lax.axis_index("half") == turn
    return jnp.where(mine, back, kept_from[0]), jnp.where(mine, arrived, kept_from[1])


def flipped(value, bit):
    step = 1 << bit
    return value + step * (1 - 2 * (value // step % 2))


def crossed(value, other):
    for bit in range(other.bit_length()):
        if other >> bit & 1:
            value = flipped(value, bit)
    return value


def greet(partners):
    barrier = pltpu.get_barrier_semaphore()
    for partner in partners:
        pl.semaphore_signal(barrier, inc=1, device_id=partner, device_id_type=MESH)
    pl.semaphore_wait(barrier, len(partners))


def remote(src, dst, out_sem, in_sem, device):
    return pltpu.make_async_remote_copy(
        src_ref=src,
        dst_ref=dst,
        send_sem=out_sem,
        recv_sem=in_sem,
        device_id=device,
        device_id_type=MESH,
    )


def tile_loop(count, step, body):
    @pl.loop(0, count // step)
    def _(i):
        body(pl.multiple_of(i * step, step), step)

    if count % step:
        body(count // step * step, count % step)


def far_first(experts, group):
    return [*range(group, experts), *range(1, group)]


def expert_forward_kernel(turn, group, has_prev, *refs):
    send_ref, w_in, w_down = refs[:3]
    refs = refs[3 + 2 * has_prev :]
    back_out, rows_out, wg, wu, wd, rows, back, made, hidden = refs[:9]
    wsem, s1, r1, s2, r2, osem = refs[9:]
    experts, block, width = send_ref.shape
    ff = wd.shape[0]

    @pl.when(lax.axis_index("half") == turn)
    def _():
        me = lax.axis_index("expert")
        greet([{"expert": crossed(me, k)} for k in range(1, experts)])

        def there(k):
            partner = crossed(me, k)
            return remote(send_ref.at[partner], rows.at[me], s1.at[k], r1.at[k], {"expert": partner})

        def home(k):
            partner = crossed(me, k)
            return remote(made.at[partner], back.at[me], s2.at[k], r2.at[k], {"expert": partner})

        for k in far_first(experts, group):
            there(k).start()
        loads = [
            pltpu.make_async_copy(src, dst, wsem.at[i])
            for i, (src, dst) in enumerate(((w_in.at[0], wg), (w_in.at[1], wu), (w_down, wd)))
        ]
        for load in loads:
            load.start()
        rows[me] = send_ref[me]
        for part in range(experts // group):
            for k in range(part * group, part * group + group):
                if k:
                    there(k).wait_recv()
            base = crossed(me // group, part) * group
            if part == 0:
                loads[0].wait()
                loads[1].wait()

            def up_tile(start, size, base=base):
                x = rows[pl.ds(base, group)].reshape(group * block, width)
                cols = pl.ds(start, size)
                value, _ = gelu_parts(dot(x, wg[:, cols]))
                hidden[:, cols] = (value * dot(x, wu[:, cols])).astype(BF16)

            tile_loop(ff, 512, up_tile)
            if part == 0:
                loads[2].wait()

            def down_tile(start, size, base=base):
                cols = pl.ds(start, size)
                y = dot(hidden[...], wd[:, cols]).astype(BF16)
                made[pl.ds(base, group), :, cols] = y.reshape(group, block, size)

            tile_loop(width, 512, down_tile)
            for k in range(part * group, part * group + group):
                if k:
                    home(k).start()
        rows_copy = pltpu.make_async_copy(rows, rows_out, osem.at[0])
        rows_copy.start()
        back[me] = made[me]
        for k in range(1, experts):
            home(k).wait_recv()
        back_copy = pltpu.make_async_copy(back, back_out, osem.at[1])
        back_copy.start()
        for k in range(1, experts):
            there(k).wait_send()
            home(k).wait_send()
        rows_copy.wait()
        back_copy.wait()


def expert_backward_kernel(turn, group, has_prev, *refs):
    send_ref, own_rows, w_in, w_down = refs[:4]
    lefts, refs = refs[4 + 5 * has_prev : 4 + 9 * has_prev], refs[4 + 9 * has_prev :]
    back_out, mixed_out, hidden_out, rows_out, grad_out = refs[:5]
    lefts_out, refs = refs[5 : 5 + has_prev], refs[5 + has_prev :]
    wg, wu, wd, grads, back, made, rows_peer, grads_peer = refs[:8]
    hidden, dgate, dup = refs[8:11]
    wsem, s1, r1, s2, r2, sx, rx, osem, sl, rl = refs[11:]
    experts, block, width = send_ref.shape
    ff = wd.shape[0]
    span = ff // 2
    total = experts * block
    parts = experts // group
    me, dp = lax.axis_index("expert"), lax.axis_index("dp")
    peer = {"dp": 1 - dp}

    def left_over(i):
        cols = pl.ds(pl.multiple_of((1 - dp) * (width // 2), 128), width // 2)
        return remote(lefts[i].at[:, cols], lefts_out[0].at[i], sl.at[i], rl.at[i], peer)

    if has_prev:

        @pl.when(lax.axis_index("half") != turn)
        def _():
            greet([peer])
            for i in range(4):
                left_over(i).start()
            for i in range(4):
                left_over(i).wait()

    @pl.when(lax.axis_index("half") == turn)
    def _():
        greet([{"expert": crossed(me, k)} for k in range(1, experts)] + [peer])

        def there(k):
            partner = crossed(me, k)
            return remote(send_ref.at[partner], grads.at[me], s1.at[k], r1.at[k], {"expert": partner})

        def home(k):
            partner = crossed(me, k)
            return remote(made.at[partner], back.at[me], s2.at[k], r2.at[k], {"expert": partner})

        def base_of(part):
            return crossed(me // group, part) * group

        rows_over = remote(own_rows, rows_peer, sx.at[parts], rx.at[parts], peer)

        def grads_over(part):
            blocks = pl.ds(base_of(part), group)
            return remote(grads.at[blocks], grads_peer.at[blocks], sx.at[part], rx.at[part], peer)

        for k in far_first(experts, group):
            there(k).start()
        loads = [
            pltpu.make_async_copy(src, dst, wsem.at[i])
            for i, (src, dst) in enumerate(((w_in.at[0], wg), (w_in.at[1], wu), (w_down, wd)))
        ]
        for load in loads:
            load.start()
        rows_over.start()
        if has_prev:
            for i in range(4):
                left_over(i).start()
        grads[me] = send_ref[me]
        loads[0].wait()
        loads[1].wait()

        def up_tile(start, size):
            x = own_rows[...].reshape(total, width)
            cols = pl.ds(start, size)
            value, slope = gelu_parts(dot(x, wg[:, cols]))
            up = dot(x, wu[:, cols])
            hidden[:, cols] = (value * up).astype(BF16)
            dup[:, cols] = value.astype(BF16)
            dgate[:, cols] = (up * slope).astype(BF16)

        tile_loop(ff, 512, up_tile)
        loads[2].wait()
        for part in range(parts):
            for k in range(part * group, part * group + group):
                if k:
                    there(k).wait_recv()
            grads_over(part).start()
            base = base_of(part)
            span_rows = pl.ds(pl.multiple_of(base * block, group * block), group * block)

            def hidden_tile(start, size, base=base, span_rows=span_rows):
                dy = grads[pl.ds(base, group)].reshape(group * block, width)
                cols = pl.ds(start, size)
                dhidden = dot(dy, wd[cols, :], NT)
                dgate[span_rows, cols] = (dhidden * dgate[span_rows, cols].astype(F32)).astype(BF16)
                dup[span_rows, cols] = (dhidden * dup[span_rows, cols].astype(F32)).astype(BF16)

            tile_loop(ff, 512, hidden_tile)

            def rows_tile(start, size, base=base, span_rows=span_rows):
                cols = pl.ds(start, size)
                dr = dot(dgate[span_rows, :], wg[cols, :], NT) + dot(dup[span_rows, :], wu[cols, :], NT)
                made[pl.ds(base, group), :, cols] = dr.astype(BF16).reshape(group, block, size)

            tile_loop(width, 512, rows_tile)
            for k in range(part * group, part * group + group):
                if k:
                    home(k).start()
        back[me] = made[me]
        half_cols = pl.ds(pl.multiple_of(dp * span, 128), span)
        outs = [
            (dgate.at[:, half_cols], mixed_out.at[0, 0]),
            (dup.at[:, half_cols], mixed_out.at[1, 0]),
            (hidden.at[:, half_cols], hidden_out.at[0]),
            (own_rows, rows_out.at[0]),
            (grads, grad_out.at[0]),
        ]
        outs = [pltpu.make_async_copy(src, dst, osem.at[i]) for i, (src, dst) in enumerate(outs)]
        for out in outs:
            out.start()

        rows_over.wait_recv()
        for part in range(parts):
            grads_over(part).wait_recv()

        def peer_tile(start, size):
            x = rows_peer[...].reshape(total, width)
            dy = grads_peer[...].reshape(total, width)
            here = pl.ds(pl.multiple_of((1 - dp) * span + start, 128), size)
            cols = pl.ds(pl.multiple_of(dp * span + start, 128), size)
            value, slope = gelu_parts(dot(x, wg[:, cols]))
            up = dot(x, wu[:, cols])
            dhidden = dot(dy, wd[cols, :], NT)
            hidden[:, here] = (value * up).astype(BF16)
            dgate[:, here] = (dhidden * up * slope).astype(BF16)
            dup[:, here] = (dhidden * value).astype(BF16)

        tile_loop(span, 512, peer_tile)
        other_cols = pl.ds(pl.multiple_of((1 - dp) * span, 128), span)
        peers = [
            (dgate.at[:, other_cols], mixed_out.at[0, 1]),
            (dup.at[:, other_cols], mixed_out.at[1, 1]),
            (hidden.at[:, other_cols], hidden_out.at[1]),
            (rows_peer, rows_out.at[1]),
            (grads_peer, grad_out.at[1]),
        ]
        peers = [pltpu.make_async_copy(src, dst, osem.at[5 + i]) for i, (src, dst) in enumerate(peers)]
        for out in peers:
            out.start()
        for k in range(1, experts):
            home(k).wait_recv()
        back_copy = pltpu.make_async_copy(back, back_out, osem.at[10])
        back_copy.start()
        for k in range(1, experts):
            there(k).wait_send()
            home(k).wait_send()
        rows_over.wait_send()
        for part in range(parts):
            grads_over(part).wait_send()
        if has_prev:
            for i in range(4):
                left_over(i).wait()
        for out in [*outs, *peers, back_copy]:
            out.wait()


def group_of(experts, block):
    group = 1
    while group * 2 * block <= 320 and group * 2 <= experts:
        group *= 2
    return group


def expert_call(kernel, turn, inputs, weights, prev, more, out_shape, scratch, name):
    experts, block, _ = inputs[0].shape
    vmem, hbm = pl.BlockSpec(memory_space=pltpu.VMEM), pl.BlockSpec(memory_space=pl.ANY)
    prev = list(prev or [])
    first = len(inputs) + len(weights)
    return pl.pallas_call(
        functools.partial(kernel, turn, group_of(experts, block), bool(prev)),
        in_specs=[vmem] * len(inputs) + [hbm] * (len(weights) + len(prev) + len(more)),
        out_specs=[hbm] * len(out_shape),
        out_shape=out_shape,
        input_output_aliases={first + i: i for i in range(len(prev))},
        scratch_shapes=scratch,
        compiler_params=pltpu.CompilerParams(
            collective_id=1 + turn + 2 * (len(inputs) - 1),
            has_side_effects=True,
            vmem_limit_bytes=60 << 20,
        ),
        name=name,
    )(*inputs, *weights, *prev, *more)


def moe_forward(send, w_in, w_down, turn, prev):
    experts, block, width = send.shape
    ff = w_down.shape[0]
    group = group_of(experts, block)
    dma = pltpu.SemaphoreType.DMA
    scratch = [
        pltpu.VMEM((width, ff), BF16),
        pltpu.VMEM((width, ff), BF16),
        pltpu.VMEM((ff, width), BF16),
        *[pltpu.VMEM(send.shape, BF16)] * 3,
        pltpu.VMEM((group * block, ff), BF16),
        dma((3,)),
        *[dma((experts,))] * 4,
        dma((2,)),
    ]
    out_shape = [jax.ShapeDtypeStruct(send.shape, BF16)] * 2
    return expert_call(
        expert_forward_kernel, turn, [send], [w_in, w_down], prev, [], out_shape, scratch, "moe_forward"
    )


def moe_backward(grad_send, received, w_in, w_down, turn, prev, lefts):
    experts, block, width = grad_send.shape
    ff = w_down.shape[0]
    total = experts * block
    parts = experts // group_of(experts, block)
    dma = pltpu.SemaphoreType.DMA
    scratch = [
        pltpu.VMEM((width, ff), BF16),
        pltpu.VMEM((width, ff), BF16),
        pltpu.VMEM((ff, width), BF16),
        *[pltpu.VMEM(grad_send.shape, BF16)] * 5,
        *[pltpu.VMEM((total, ff), BF16)] * 3,
        dma((3,)),
        *[dma((experts,))] * 4,
        dma((parts + 1,)),
        dma((parts + 1,)),
        dma((11,)),
        dma((4,)),
        dma((4,)),
    ]
    out_shape = [
        jax.ShapeDtypeStruct(grad_send.shape, BF16),
        jax.ShapeDtypeStruct((2, 2, total, ff // 2), BF16),
        jax.ShapeDtypeStruct((2, total, ff // 2), BF16),
        jax.ShapeDtypeStruct((2, *grad_send.shape), BF16),
        jax.ShapeDtypeStruct((2, *grad_send.shape), BF16),
    ]
    if lefts:
        out_shape.append(jax.ShapeDtypeStruct((4, lefts[0].shape[0], width // 2), BF16))
    return expert_call(
        expert_backward_kernel,
        turn,
        [grad_send, received],
        [w_in, w_down],
        prev,
        lefts,
        out_shape,
        scratch,
        "moe_backward",
    )


def dense_kernel(stages, chunk, lag, *refs):
    sources, small_ref = refs[:11], refs[11]
    out_refs, small_out, small_in = refs[12:15], refs[15], refs[16]
    held, xt_ref, refs = refs[17:28], refs[28], refs[29:]
    x_refs, own_refs, peer_refs, xp = held[:4], held[4:7], held[7:10], held[10]
    sums, parts = refs[:stages], refs[stages : 2 * stages]
    ss, rs, sk, rk, sl = refs[2 * stages :]
    counts = [ref.shape[1] // chunk for ref in own_refs]
    starts = [sum(counts[:i]) for i in range(3)]
    chunks = sum(counts)
    per_cross = counts[2] // 2
    rows, half = xp.shape[1:]
    dp, me = lax.axis_index("dp"), lax.axis_index("expert")
    peer = {"dp": 1 - dp}
    partners = [flipped(me, k) for k in range(stages)]
    bits = [me // (1 << k) % 2 for k in range(stages)]
    load = [pltpu.make_async_copy(sources[i], held[i], sl.at[i]) for i in range(11)]
    for i in (10, 2, 3, 6, 9, 0, 4, 7, 1, 5, 8):
        load[i].start()
    greet([peer] + [{"expert": p} for p in partners])

    def send_small(step):
        src = small_ref if step == 0 else small_out.at[step - 1]
        device = peer if step == 0 else {"expert": partners[stages - step]}
        return remote(src, small_in.at[step], ss.at[step], rs.at[step], device)

    def order(k, odd):
        return 1 - k if odd and k < 2 else k

    def send_part(k, c, odd):
        bit = order(k, odd)
        other = 1 - bits[bit]
        src = sums[0].at[c, :, :, other] if k == 0 and not odd else sums[k].at[c, :, other]
        return remote(src, parts[k].at[c], sk.at[k, c], rk.at[k, c], {"expert": partners[bit]})

    def turn_x(g):
        load[g].wait()
        cols = pl.ds(pl.multiple_of(dp * half, half), half)
        xt_ref[g, :, :rows] = jnp.transpose(x_refs[g][:, cols])
        xt_ref[g, :, rows:] = jnp.transpose(xp[g])

    def small_step(j):
        send_small(j).wait_recv()
        own = small_ref[...] if j == 0 else small_out[j - 1]
        small_out[j] = own + small_in[j]
        if j < stages:
            send_small(j + 1).start()

    send_small(0).start()
    load[10].wait()
    last = counts[2]
    early = chunks - last
    per = chunks // last

    def produce(i, carry):
        c = jnp.where(lax.rem(i, per) == 0, early + i // per, i - i // per - 1)
        for g in range(3):

            @pl.when(c == starts[g])
            def _(g=g):
                load[4 + g].wait()
                load[7 + g].wait()
                for x in (g,) if g < 2 else (2, 3):
                    turn_x(x)

            @pl.when((c >= starts[g]) & (c < starts[g] + counts[g]))
            def _(g=g):
                at = c - starts[g]
                cols = pl.ds(pl.multiple_of(at * chunk, chunk), chunk)
                which = g if g < 2 else 2 + at // per_cross
                total = dot(xt_ref[which, :, :rows], own_refs[g][:, cols])
                total += dot(xt_ref[which, :, rows:], peer_refs[g][:, cols])
                sums[0][c] = total.astype(BF16).reshape(sums[0].shape[1:])
                send_part(0, c, g == 2).start()

        for j in range(2):

            @pl.when(i == 3 + 6 * j)
            def _(j=j):
                small_step(j)

        return carry

    lax.fori_loop(0, chunks, produce, 0)

    def advance(k, c, odd):
        send_part(k, c, odd).wait_recv()
        bit = bits[order(k, odd)]
        mine = sums[0][c, :, :, bit] if k == 0 and not odd else sums[k][c, :, bit]
        total = mine.astype(F32) + parts[k][c].astype(F32)
        if k + 1 < stages:
            sums[k + 1][c] = total.astype(BF16).reshape(sums[k + 1].shape[1:])
            send_part(k + 1, c, odd).start()
            return
        total = total.reshape(total.shape[-2:])
        for g in (2,) if odd else (0, 1):

            @pl.when((c >= starts[g]) & (c < starts[g] + counts[g]))
            def _(g=g):
                at = pl.multiple_of((c - starts[g]) * chunk, chunk)
                out_refs[g][:, pl.ds(at, chunk)] = total

    def reduce(i, carry):
        @pl.when((lax.rem(i, 2) == 1) & (i // 2 < last))
        def _():
            advance(0, early + i // 2, True)

        for k in range(stages):
            c = i - lag * k

            @pl.when((c >= 0) & (c < early))
            def _(k=k, c=c):
                advance(k, c, False)

        for k in range(1, stages):
            c = i - 1 - lag * (k - 1)

            @pl.when((c >= early) & (c < chunks))
            def _(k=k, c=c):
                advance(k, c, True)

        for j in range(2, stages + 1):

            @pl.when(i == 3 * j - 2)
            def _(j=j):
                small_step(j)

        return carry

    lax.fori_loop(0, chunks + 1 + lag * (stages - 2), reduce, 0)

    def finish(c, carry, odd):
        for k in range(stages):
            send_part(k, c, odd).wait_send()
        return carry

    lax.fori_loop(0, early, functools.partial(finish, odd=False), 0)
    lax.fori_loop(early, chunks, functools.partial(finish, odd=True), 0)
    for j in range(stages + 1):
        send_small(j).wait_send()


def over_dp(array):
    return lax.ppermute(array, "dp", [(0, 1), (1, 0)])


def dense_gradients(lefts, lefts_peer, own, peer, small, experts):
    chunk = 512
    rows, width = lefts[0].shape
    half_rows = width // 2
    chunks = sum(y.shape[1] for y in own) // chunk
    stages = experts.bit_length() - 1
    keep = half_rows // experts
    vmem, hbm = pl.BlockSpec(memory_space=pltpu.VMEM), pl.BlockSpec(memory_space=pl.ANY)
    dma = pltpu.SemaphoreType.DMA
    sources = [*lefts, *own, *peer, lefts_peer]
    blocks = [(experts // 4, 2, 2)] + [(experts >> (k + 1), 2) for k in range(1, stages)]
    halved = [(experts // 4, 2)] + [(experts >> (k + 1),) for k in range(1, stages)]
    scratch = [pltpu.VMEM((stages + 1, *small.shape), F32)]
    scratch += [pltpu.VMEM(a.shape, BF16) for a in sources]
    scratch += [pltpu.VMEM((4, half_rows, 2 * rows), BF16)]
    scratch += [pltpu.VMEM((chunks, *b, keep, chunk), BF16) for b in blocks + halved]
    scratch += [dma((stages + 1,)), dma((stages + 1,)), dma((stages, chunks)), dma((stages, chunks))]
    scratch += [dma((len(sources),))]
    *outs, sums = pl.pallas_call(
        functools.partial(dense_kernel, stages, chunk, 2),
        in_specs=[hbm] * len(sources) + [vmem],
        out_specs=[vmem] * 4,
        out_shape=[
            *(jax.ShapeDtypeStruct((keep, y.shape[1]), F32) for y in own),
            jax.ShapeDtypeStruct((stages + 1, *small.shape), F32),
        ],
        scratch_shapes=scratch,
        compiler_params=pltpu.CompilerParams(
            collective_id=0, has_side_effects=True, vmem_limit_bytes=56 << 20
        ),
        name="dense_gradients",
    )(*sources, small)
    return outs, sums[stages]


def product_kernel(x_ref, y_ref, out_ref):
    out_ref[...] = dot(x_ref[...], y_ref[...].reshape(y_ref.shape[-2:]), TN).reshape(out_ref.shape)


def expert_gradients(rows, mixed, hidden, grads):
    total, width = rows.shape
    span = hidden.shape[1]
    tile = 256
    params = pltpu.CompilerParams(vmem_limit_bytes=40 << 20)
    din = pl.pallas_call(
        product_kernel,
        grid=(2, width // tile),
        in_specs=[
            pl.BlockSpec((total, tile), lambda g, i: (0, i)),
            pl.BlockSpec((1, total, span), lambda g, i: (g, 0, 0)),
        ],
        out_specs=pl.BlockSpec((1, tile, span), lambda g, i: (g, i, 0)),
        out_shape=jax.ShapeDtypeStruct((2, width, span), F32),
        compiler_params=params,
        name="expert_in_gradient",
    )(rows, mixed)
    ddown = pl.pallas_call(
        product_kernel,
        grid=(pl.cdiv(span, tile),),
        in_specs=[
            pl.BlockSpec((total, tile), lambda i: (0, i)),
            pl.BlockSpec((total, width), lambda i: (0, 0)),
        ],
        out_specs=pl.BlockSpec((tile, width), lambda i: (i, 0)),
        out_shape=jax.ShapeDtypeStruct((span, width), F32),
        compiler_params=params,
        name="expert_out_gradient",
    )(hidden, grads)
    return din, ddown


def body(
    tokens,
    cotangent,
    lengths,
    routes,
    self_qkv,
    self_out,
    cross_weights,
    router,
    gains,
    bias_table,
    expert_in,
    expert_out,
):
    _, seqs, length, width = tokens.shape
    heads = H
    experts = router.shape[2]
    top = routes.shape[3]
    capacity = (5 * top * length + 4 * experts - 1) // (4 * experts)
    block_rows = -(-seqs * capacity // 16) * 16
    rows = seqs * length
    slots = experts * block_rows
    half_index = lax.axis_index("half")
    decoder = half_index == 1
    wqkv, wout, wcross, wrouter, gain = (
        self_qkv[0],
        self_out[0],
        cross_weights[0],
        router[0],
        gains[0],
    )
    w_in, w_down = expert_in[0, 0], expert_out[0, 0]

    column = np.arange(2 * length)
    hot, hot_back = (
        (
            jnp.where(decoder, *reversed(diagonal_buckets(diff)))[:, None]
            == jnp.arange(BUCKETS)[None, :]
        ).astype(F32)
        for diff in (np.where(column < length, column, column - 2 * length), column - length + 1)
    )
    bias = lax.dot_general(
        bias_table[0].reshape(BUCKETS, heads),
        hot,
        (((0,), (1,)), ((), ())),
        precision=lax.Precision.HIGHEST,
        preferred_element_type=F32,
    )
    own_lengths = jnp.where(decoder, lengths[1], lengths[0])
    self_info = jnp.concatenate([own_lengths, half_index[None]]).astype(jnp.int32)
    cross_info = jnp.concatenate([lengths[0], jnp.zeros((1,), jnp.int32)]).astype(jnp.int32)

    order = jnp.transpose(routes[0], (0, 2, 1)).reshape(seqs, top * length)
    expert_ids = jnp.arange(experts, dtype=jnp.int32)
    picked = (order[:, :, None] == expert_ids).astype(BF16)
    earlier = np.tril(np.ones((top * length, top * length), np.float32), -1).astype(BF16)
    before = jnp.einsum("pq,sqe->spe", earlier, picked, preferred_element_type=F32)
    place = jnp.sum(before * picked.astype(F32), axis=2).astype(jnp.int32)
    kept = place < capacity
    base = order * block_rows + jnp.arange(seqs, dtype=jnp.int32)[:, None] * capacity
    target = jnp.where(kept, base + place, -1).reshape(seqs, top, length)
    target = jnp.transpose(target, (1, 0, 2)).reshape(top, rows)
    slot_ids = jnp.arange(slots, dtype=jnp.int32)
    spots = (target[:, :, None] == slot_ids).astype(BF16)
    both = jnp.sum(spots.astype(F32), axis=0).astype(BF16)
    stacked = spots.reshape(top * rows, slots)
    kept_hot = picked.astype(F32) * kept[:, :, None].astype(F32)
    kept_count = jnp.sum(kept_hot, axis=(0, 1))
    all_count = jnp.sum(picked.astype(F32), axis=(0, 1))
    tallies = jnp.concatenate([kept_count, all_count - kept_count])
    route_hot = (routes[0].reshape(rows, top, 1) == expert_ids).astype(F32)

    def route(values):
        normed, scale = norm_parts(values, gain[1])
        low = normed.astype(BF16)
        rest = (normed - low.astype(F32)).astype(BF16)
        logits = dot(low, wrouter) + dot(rest, wrouter)
        probs = jax.nn.softmax(logits, axis=-1)
        chosen = jnp.sum(probs[:, None, :] * route_hot, axis=-1)
        total = jnp.sum(chosen, axis=-1, keepdims=True)
        gates = chosen / total
        send = dot(both, low, TN).astype(BF16).reshape(experts, block_rows, width)
        return dict(scale=scale, low=low, probs=probs, gates=gates, total=total, send=send)

    def fetch(returned):
        flat = returned.reshape(slots, width)
        return dot(stacked, flat).reshape(top, rows, width)

    def combine(values, gates, results):
        return values + jnp.sum(jnp.transpose(gates)[:, :, None] * results, axis=0)

    values = tokens[0].reshape(rows, width).astype(F32)
    normed, scale0 = norm_parts(values, gain[0])
    low0 = normed.astype(BF16)
    qkv = dot(low0, wqkv).astype(BF16)
    mixed0, log0 = attend(self_info, bias, qkv, qkv, (0, 1, 2), length, width)
    first = values + dot(mixed0, wout)

    state = route(first)
    returned, received = moe_forward(state["send"], w_in, w_down, 0, None)
    final_enc = combine(first, state["gates"], fetch(returned))
    normed, scale_m = norm_parts(final_enc, gain[2])
    low_m = normed.astype(BF16)
    memory = dot(low_m, wcross).astype(BF16)
    names = ("half", "dp", "expert")
    forward_pairs, back_pairs = half_pairs(lax.axis_size("dp") * lax.axis_size("expert"))
    memory = lax.ppermute(memory, names, forward_pairs)

    normed, scale_c = norm_parts(first, gain[2])
    low_c = normed.astype(BF16)
    query = dot(low_c, wcross[:, :width]).astype(BF16)
    mixed_c, log_c = attend(cross_info, None, query, memory, (0, 0, 1), length, width)
    second = jnp.where(decoder, first + dot(mixed_c, wcross[:, width:]), first)

    state = route(second)
    returned, received = moe_forward(state["send"], w_in, w_down, 1, (returned, received))
    results = fetch(returned)
    final = combine(second, state["gates"], results)
    outputs = final.astype(BF16)

    def moe_gradient(grad):
        dgates = jnp.transpose(jnp.sum(grad[None] * results, axis=-1))
        spread = (jnp.transpose(state["gates"])[:, :, None] * grad[None]).astype(BF16)
        send = dot(stacked, spread.reshape(top * rows, width), TN)
        return dgates, send.astype(BF16).reshape(experts, block_rows, width)

    def moe_input_gradient(grad, dgates, back):
        gates, total, probs = state["gates"], state["total"], state["probs"]
        dchosen = (dgates - jnp.sum(dgates * gates, axis=-1, keepdims=True)) / total
        dprobs = jnp.sum(dchosen[:, :, None] * route_hot, axis=1)
        dlogits = probs * (dprobs - jnp.sum(dprobs * probs, axis=-1, keepdims=True))
        dnormed = dot(both, back.reshape(slots, width)) + lax.dot_general(
            dlogits, wrouter.astype(F32), NT, preferred_element_type=F32
        )
        dvalues, dgain = norm_back(second, state["scale"], gain[1], dnormed)
        normed = second * state["scale"] * gain[1]
        drouter = lax.dot_general(
            normed, dlogits, TN, precision=lax.Precision.HIGHEST, preferred_element_type=F32
        )
        return grad + dvalues, dgain, drouter

    grad_dec = cotangent[0].reshape(rows, width).astype(F32)
    dgates, grad_send = moe_gradient(grad_dec)
    kept_from = moe_backward(grad_send, received, w_in, w_down, 1, None, [])
    grad_second, _, _ = moe_input_gradient(grad_dec, dgates, kept_from[0])

    dbranch_c = grad_second.astype(BF16)
    dmixed_c = dot(dbranch_c, wcross[:, width:], NT).astype(BF16)
    dquery, dmemory = attend_back(
        cross_info, None, query, memory, (0, 0, 1), (mixed_c, log_c), dmixed_c, length, width
    )
    dmemory = lax.ppermute(dmemory, names, back_pairs)
    dnormed = dot(dquery, wcross[:, :width], NT)
    dvalues, dgain_c = norm_back(first, scale_c, gain[2], dnormed)
    grad_first_dec = grad_second + dvalues

    dnormed = dot(dmemory, wcross, NT)
    dvalues, dgain_m = norm_back(final_enc, scale_m, gain[2], dnormed)
    grad = jnp.where(decoder, grad_dec, grad_dec + dvalues)
    dgates, grad_send = moe_gradient(grad)
    lefts = [low0, mixed0, jnp.where(decoder, low_c, low_m), jnp.where(decoder, mixed_c, low_m)]
    back, mixed_grads, hidden, all_rows, all_grad, lefts_peer = moe_backward(
        grad_send, received, w_in, w_down, 0, kept_from, lefts
    )
    grad_second, dgain_moe, drouter = moe_input_gradient(grad, dgates, back)
    grad_first = jnp.where(decoder, grad_first_dec, grad_second)

    dbranch = grad_first.astype(BF16)
    dmixed = dot(dbranch, wout, NT).astype(BF16)
    dqkv_rows, diag = attend_back(
        self_info, bias, qkv, qkv, (0, 1, 2), (mixed0, log0), dmixed, length, width
    )
    dnormed = dot(dqkv_rows, wqkv, NT)
    dvalues, dgain_self = norm_back(values, scale0, gain[0], dnormed)
    d_tokens = (grad_first + dvalues).astype(BF16)
    dtable = lax.dot_general(
        hot_back, diag, (((0,), (1,)), ((), ())), precision=lax.Precision.HIGHEST,
        preferred_element_type=F32,
    ).reshape(-1)

    cross_grad = jnp.where(decoder, jnp.concatenate([dquery, dbranch_c], axis=1), dmemory)
    own_grads = (dqkv_rows, dbranch, cross_grad)
    peer_grads = tuple(map(over_dp, own_grads))
    places = 2 * experts
    own = width // places
    extra = jnp.concatenate([dtable.reshape(places, -1), tallies.reshape(places, 1)], axis=1)
    extra = jnp.pad(extra, ((0, 0), (0, -extra.shape[1] % own)))
    small = jnp.concatenate(
        [
            jnp.transpose(drouter),
            jnp.stack([dgain_self, dgain_moe, jnp.where(decoder, dgain_c, dgain_m)]),
            jnp.swapaxes(extra.reshape(places, -1, own), 0, 1).reshape(-1, width),
        ]
    )
    small = jnp.pad(small, ((0, -small.shape[0] % 8), (0, 0)))
    (dqkv, dout, dcross), small = dense_gradients(
        lefts, lefts_peer, own_grads, peer_grads, small, experts
    )
    place = lax.axis_index("dp") * experts + lax.axis_index("expert")
    mine = lax.dynamic_slice_in_dim(small, place * own, own, 1)
    tail = mine[experts + 3 :].reshape(-1)
    own_table = dtable.shape[0] // places
    d_table = tail[:own_table]
    counts = tail[own_table].astype(jnp.int32)

    ff_half = hidden.shape[-1]
    din, ddown = expert_gradients(
        all_rows.reshape(-1, width),
        mixed_grads.reshape(2, -1, ff_half),
        hidden.reshape(-1, ff_half),
        all_grad.reshape(-1, width),
    )
    return (
        outputs.reshape(1, seqs, length, width),
        d_tokens.reshape(1, seqs, length, width),
        dqkv[None],
        dout[None],
        dcross[None],
        jnp.transpose(mine[:experts])[None],
        mine[experts : experts + 3][None],
        d_table[None],
        din[None, None],
        ddown[None, None],
        counts.reshape(1, 1, 1),
    )


def half_pairs(count):
    return (
        [(i, count + i) for i in range(count)],
        [(count + i, i) for i in range(count)],
    )


def solution(mesh):
    placed = (
        P("half", ("dp", "expert"), None, None),
        P("half", ("dp", "expert"), None, None),
        P(None, ("dp", "expert")),
        P("half", ("dp", "expert"), None, None),
        P("half", None, None),
        P("half", None, None),
        P("half", None, None),
        P("half", None, None),
        P("half", None, None),
        P("half", None),
        P("half", "expert", None, None, None),
        P("half", "expert", None, None),
    )
    return jax.shard_map(
        body,
        mesh=mesh,
        in_specs=placed,
        out_specs=(
            P("half", ("dp", "expert"), None, None),
            P("half", ("dp", "expert"), None, None),
            P("half", ("dp", "expert"), None),
            P("half", ("dp", "expert"), None),
            P("half", ("dp", "expert"), None),
            P("half", ("dp", "expert"), None),
            P("half", None, ("dp", "expert")),
            P("half", ("dp", "expert")),
            P("half", "expert", None, None, "dp"),
            P("half", "expert", "dp", None),
            P("half", "dp", "expert"),
        ),
        check_vma=False,
    )
```

```python
import functools

import jax
import jax.numpy as jnp
import numpy as np
from jax import lax
from jax.experimental import pallas as pl
from jax.experimental.pallas import tpu as pltpu
from jax.sharding import PartitionSpec as P

H = 16
BUCKETS = 32
EPS = 1e-06
ENC_STEPS = (12, 16, 23, 32, 46, 64, 91)
DEC_STEPS = (19, 21, 24, 27, 31, 35, 40, 46, 52, 59, 67, 77, 87, 99, 113)
F32 = jnp.float32
BF16 = jnp.bfloat16
MESH = pl.DeviceIdType.MESH
NT = (((1,), (1,)), ((), ()))
TN = (((0,), (0,)), ((), ()))


def dot(a, b, dims=(((1,), (0,)), ((), ()))):
    return lax.dot_general(a, b, dims, preferred_element_type=F32)


def diagonal_buckets(diff):
    apart = np.abs(diff)
    coarse = 8 + sum((apart >= step).astype(np.int32) for step in ENC_STEPS)
    enc = np.where(apart < 8, apart, coarse) + 16 * (diff > 0)
    behind = np.maximum(-diff, 0)
    coarse = 16 + sum((behind >= step).astype(np.int32) for step in DEC_STEPS)
    dec = np.where(behind < 16, behind, coarse)
    return enc.astype(np.int32), dec.astype(np.int32)


def diagonals(bias_ref, head, length):
    row = jnp.broadcast_to(bias_ref[pl.ds(head, 1), :], (length, 2 * length))
    return pltpu.roll(row, 0, 1, stride=1, stride_axis=0)[:, :length]


def fill_masks(info, mask_ref):
    seqs, length, _ = mask_ref.shape
    row_id = lax.broadcasted_iota(jnp.int32, (length, length), 0)
    col_id = lax.broadcasted_iota(jnp.int32, (length, length), 1)
    reach = jnp.where(info[seqs] > 0, row_id, length)
    for seq in range(seqs):
        allowed = (col_id < info[seq]) & (col_id <= reach)
        mask_ref[seq] = jnp.where(allowed, 0.0, -1000000000.0)


def attend_kernel(has_bias, info, *refs):
    bias_ref, refs = (refs[0], refs[1:]) if has_bias else (None, refs)
    q_ref, k_ref, v_ref, out_ref, log_ref, mask_ref = refs
    seqs, length, _ = mask_ref.shape
    low = lax.broadcasted_iota(jnp.int32, (length, 128), 1) < 64
    fill_masks(info, mask_ref)

    @pl.loop(0, q_ref.shape[1] // 128, unroll=True)
    def _(pair):
        cols = pl.ds(pl.multiple_of(pair * 128, 128), 128)
        biases = [diagonals(bias_ref, 2 * pair + side, length) if has_bias else 0.0 for side in range(2)]
        for seq in range(seqs):
            rows = pl.ds(seq * length, length)
            q, k, v = q_ref[rows, cols] * 0.125, k_ref[rows, cols], v_ref[rows, cols]
            mixed, peaks = [], []
            for side in range(2):
                mine = low if side == 0 else jnp.logical_not(low)
                part = jnp.where(mine, q, jnp.zeros_like(q))
                scores = dot(part, k, NT) + (mask_ref[seq] + biases[side])
                peak = jnp.max(scores, axis=-1, keepdims=True)
                spread = jnp.exp(scores - peak).astype(BF16)
                mixed.append(dot(spread, jnp.where(mine, v, jnp.ones_like(v))))
                peaks.append(peak)
            total = pltpu.roll(jnp.where(low, mixed[1], mixed[0]), 64, 1)
            out_ref[rows, cols] = (jnp.where(low, mixed[0], mixed[1]) / total).astype(BF16)
            log_ref[rows, cols] = jnp.where(low, peaks[0], peaks[1]) + jnp.log(total)


def attend_back_kernel(has_bias, info, *refs):
    if has_bias:
        bias_ref, q_ref, k_ref, v_ref, a_ref, log_ref, g_ref, dq_ref, diag_ref, mask_ref = refs
        dkv_ref, shift = dq_ref, q_ref.shape[1]
    else:
        q_ref, k_ref, v_ref, a_ref, log_ref, g_ref, dq_ref, dkv_ref, mask_ref = refs
        shift = 0
    seqs, length, _ = mask_ref.shape
    width = q_ref.shape[1]
    low = lax.broadcasted_iota(jnp.int32, (length, 128), 1) < 64
    fill_masks(info, mask_ref)
    if has_bias:
        row_id = lax.broadcasted_iota(jnp.int32, (length, length), 0)
        col_id = lax.broadcasted_iota(jnp.int32, (length, length), 1)
        flip = (row_id + col_id == length - 1).astype(F32).astype(BF16)

    @pl.loop(0, width // 128, unroll=True)
    def _(pair):
        cols = pl.ds(pl.multiple_of(pair * 128, 128), 128)
        kcols = pl.ds(pl.multiple_of(shift + pair * 128, 128), 128)
        vcols = pl.ds(pl.multiple_of(shift + width + pair * 128, 128), 128)
        biases = [diagonals(bias_ref, 2 * pair + side, length) if has_bias else 0.0 for side in range(2)]
        sums = [0.0, 0.0]
        for seq in range(seqs):
            rows = pl.ds(seq * length, length)
            q, k, v, g = q_ref[rows, cols] * 0.125, k_ref[rows, cols], v_ref[rows, cols], g_ref[rows, cols]
            logs = log_ref[rows, cols]
            turned = pltpu.roll(logs, 64, 1)
            product = g.astype(F32) * a_ref[rows, cols].astype(F32)
            minus = (-pltpu.roll(product, 64, 1)).astype(BF16)
            scaled = k * 0.125
            dqs, dks, dvs = [], [], []
            for side in range(2):
                mine = low if side == 0 else jnp.logical_not(low)
                part = jnp.where(mine, q, jnp.zeros_like(q))
                scores = dot(part, k, NT) + (mask_ref[seq] + biases[side])
                probs = jnp.exp(scores - jnp.where(mine, logs, turned))
                dvs.append(dot(probs.astype(BF16), g, TN))
                centred = dot(jnp.where(mine, g, minus), jnp.where(mine, v, jnp.ones_like(v)), NT)
                dlow = (probs * centred).astype(BF16)
                dqs.append(dot(dlow, scaled))
                dks.append(dot(dlow, q, TN))
                if has_bias:
                    sums[side] = sums[side] + dlow.astype(F32)
            dq_ref[rows, cols] = jnp.where(low, dqs[0], dqs[1]).astype(BF16)
            dkv_ref[rows, kcols] = jnp.where(low, dks[0], dks[1]).astype(BF16)
            dkv_ref[rows, vcols] = jnp.where(low, dvs[0], dvs[1]).astype(BF16)
        if has_bias:
            for side in range(2):
                upside = dot(flip, sums[side].astype(BF16))
                wide = jnp.concatenate([upside, jnp.zeros((length, length), F32)], axis=1)
                turned = pltpu.roll(wide, 0, 1, stride=1, stride_axis=0)
                diag_ref[pl.ds(2 * pair + side, 1), :] = jnp.sum(turned, axis=0, keepdims=True)


def attend_call(kernel, info, bias, q, kv, blocks, more, out_shape, length, name):
    rows = q.shape[0]
    seqs = rows // length
    width = more[0].shape[1] if more else out_shape[0].shape[1]
    lead = [] if bias is None else [bias]
    whole = [pl.BlockSpec(a.shape, lambda i: (0, 0)) for a in lead]
    picked = [pl.BlockSpec((rows, width), lambda i, b=b: (0, b)) for b in blocks]
    rest = [pl.BlockSpec(a.shape, lambda i: (0, 0)) for a in more]
    return pl.pallas_call(
        functools.partial(kernel, bias is not None),
        grid=(1,),
        in_specs=[pl.BlockSpec(memory_space=pltpu.SMEM)] + whole + picked + rest,
        out_specs=[pl.BlockSpec(o.shape, lambda i: (0, 0)) for o in out_shape],
        out_shape=out_shape,
        scratch_shapes=[pltpu.VMEM((seqs, length, length), F32)],
        compiler_params=pltpu.CompilerParams(vmem_limit_bytes=40 << 20),
        name=name,
    )(info, *lead, q, kv, kv, *more)


def attend(info, bias, q, kv, blocks, length, width):
    rows = q.shape[0]
    out_shape = [
        jax.ShapeDtypeStruct((rows, width), BF16),
        jax.ShapeDtypeStruct((rows, width), F32),
    ]
    return attend_call(attend_kernel, info, bias, q, kv, blocks, [], out_shape, length, "attend")


def attend_back(info, bias, q, kv, blocks, saved, grad, length, width):
    rows = q.shape[0]
    widths = (width, 2 * width) if bias is None else (3 * width,)
    out_shape = [jax.ShapeDtypeStruct((rows, w), BF16) for w in widths]
    if bias is not None:
        out_shape.append(jax.ShapeDtypeStruct(bias.shape, F32))
    more = [*saved, grad]
    return attend_call(attend_back_kernel, info, bias, q, kv, blocks, more, out_shape, length, "attend_back")


def norm_parts(values, gain):
    scale = lax.rsqrt(jnp.mean(values * values, axis=-1, keepdims=True) + EPS)
    return values * scale * gain, scale


def norm_back(values, scale, gain, grad):
    unit = values * scale
    gain_grad = jnp.sum(grad * unit, axis=0)
    pushed = grad * gain
    back = scale * (pushed - unit * jnp.mean(pushed * unit, axis=-1, keepdims=True))
    return back, gain_grad


def gelu_parts(gate):
    c = 0.7978845608028654
    inner = c * (gate + 0.044715 * gate * gate * gate)
    t = jnp.tanh(inner)
    value = 0.5 * gate * (1.0 + t)
    slope = 0.5 * (1.0 + t) + 0.5 * gate * (1.0 - t * t) * c * (1.0 + 3.0 * 0.044715 * gate * gate)
    return value, slope


def moe_forward(send, w_in, w_down, turn, kept_from):
    experts, rows, width = send.shape
    arrived = lax.all_to_all(send, "expert", split_axis=0, concat_axis=0, tiled=True)
    flat = arrived.reshape(-1, width)
    value, _ = gelu_parts(dot(flat, w_in[0]))
    hidden = (value * dot(flat, w_in[1])).astype(BF16)
    result = dot(hidden, w_down).astype(BF16).reshape(send.shape)
    back = lax.all_to_all(result, "expert", split_axis=0, concat_axis=0, tiled=True)
    if kept_from is None:
        return back, arrived
    mine = lax.axis_index("half") == turn
    return jnp.where(mine, back, kept_from[0]), jnp.where(mine, arrived, kept_from[1])


def flipped(value, bit):
    step = 1 << bit
    return value + step * (1 - 2 * (value // step % 2))


def crossed(value, other):
    for bit in range(other.bit_length()):
        if other >> bit & 1:
            value = flipped(value, bit)
    return value


def greet(partners):
    barrier = pltpu.get_barrier_semaphore()
    for partner in partners:
        pl.semaphore_signal(barrier, inc=1, device_id=partner, device_id_type=MESH)
    pl.semaphore_wait(barrier, len(partners))


def remote(src, dst, out_sem, in_sem, device):
    return pltpu.make_async_remote_copy(
        src_ref=src,
        dst_ref=dst,
        send_sem=out_sem,
        recv_sem=in_sem,
        device_id=device,
        device_id_type=MESH,
    )


def tile_loop(count, step, body):
    @pl.loop(0, count // step)
    def _(i):
        body(pl.multiple_of(i * step, step), step)

    if count % step:
        body(count // step * step, count % step)


def groups_of(experts, block):
    size = 1
    while size * 2 * block <= 320 and size * 2 <= experts:
        size *= 2
    if experts <= 2 * size:
        half = max(size // 2, 1)
        return [(0, size), *((k, half) for k in range(size, experts, half))]
    return [(k, size) for k in range(0, experts, size)]


class Turn:
    def __init__(self, experts, block, there, home):
        self.me, self.dp = lax.axis_index("expert"), lax.axis_index("dp")
        self.experts, self.block = experts, block
        self.peer = {"dp": 1 - self.dp}
        self.groups = groups_of(experts, block)
        self.there_refs, self.home_refs = there, home

    def greet(self):
        greet([{"expert": crossed(self.me, k)} for k in range(1, self.experts)] + [self.peer])

    def there(self, k):
        src, dst, out_sems, in_sems = self.there_refs
        partner = crossed(self.me, k)
        return remote(src.at[partner], dst.at[self.me], out_sems.at[k], in_sems.at[k], {"expert": partner})

    def home(self, k):
        src, dst, out_sems, in_sems = self.home_refs
        partner = crossed(self.me, k)
        return remote(src.at[partner], dst.at[self.me], out_sems.at[k], in_sems.at[k], {"expert": partner})

    def base(self, first, size):
        return crossed(self.me // size, first // size) * size

    def spans(self, first, size):
        base = self.base(first, size)
        rows = pl.ds(pl.multiple_of(base * self.block, size * self.block), size * self.block)
        return pl.ds(base, size), rows


def transpose_kernel_part(loads, tall, wide, wsem, tsem):
    copies = [pltpu.make_async_copy(src, dst, wsem.at[i]) for i, (src, dst, _) in enumerate(loads)]
    for copy in copies:
        copy.start()
    for i, (_, held, out) in enumerate(loads):
        stage = tall if out.shape[1] == tall.shape[2] else wide
        steps = out.shape[0] // 256
        copies[i].wait()

        def put(t, slot, stage=stage, out=out):
            rows = pl.ds(pl.multiple_of(t * 256, 256), 256)
            return pltpu.make_async_copy(stage.at[slot], out.at[rows], tsem.at[slot])

        def step(t, carry, stage=stage, held=held, put=put):
            slot = lax.rem(t, 2)

            @pl.when(t >= 2)
            def _():
                put(t - 2, slot).wait()

            stage[slot] = jnp.transpose(held[:, pl.ds(pl.multiple_of(t * 256, 256), 256)])
            put(t, slot).start()
            return carry

        lax.fori_loop(0, steps, step, 0)
        for t in (steps - 2, steps - 1):
            put(t, t % 2).wait()


def expert_forward_kernel(turn, has_prev, *refs):
    send_ref, w_in, w_down = refs[:3]
    refs = refs[3 + 10 * has_prev :]
    back_out, rows_out, slope_out, value_out, hidden_out, slope_peer_out, value_peer_out = refs[:7]
    wgt_out, wut_out, wdt_out = refs[7:10]
    wg, wu, wd, rows, back, made, rows_peer, slopes, values, hidden = refs[10:20]
    slopes_peer, values_peer, tall, wide = refs[20:24]
    wsem, s1, r1, s2, r2, sx, rx, osem, tsem = refs[24:]
    experts, block, width = send_ref.shape
    ff = wd.shape[0]
    span = ff // 2

    @pl.when(lax.axis_index("half") != turn)
    def _():
        loads = ((w_in.at[0], wg, wgt_out), (w_in.at[1], wu, wut_out), (w_down, wd, wdt_out))
        transpose_kernel_part(loads, tall, wide, wsem, tsem)

    @pl.when(lax.axis_index("half") == turn)
    def _():
        t = Turn(experts, block, (send_ref, rows, s1, r1), (made, back, s2, r2))
        t.greet()

        def rows_over(part):
            blocks, _ = t.spans(*t.groups[part])
            return remote(rows.at[blocks], rows_peer.at[blocks], sx.at[part], rx.at[part], t.peer)

        for k in range(1, experts):
            t.there(k).start()
        loads = [
            pltpu.make_async_copy(src, dst, wsem.at[i])
            for i, (src, dst) in enumerate(((w_in.at[0], wg), (w_in.at[1], wu), (w_down, wd)))
        ]
        for load in loads:
            load.start()
        rows[t.me] = send_ref[t.me]
        for part, (first, size) in enumerate(t.groups):
            for k in range(max(first, 1), first + size):
                t.there(k).wait_recv()
            rows_over(part).start()
            blocks, span_rows = t.spans(first, size)
            if part == 0:
                loads[0].wait()
                loads[1].wait()

            def up_tile(start, count, blocks=blocks, span_rows=span_rows, size=size):
                x = rows[blocks].reshape(size * block, width)
                cols = pl.ds(start, count)
                value, slope = gelu_parts(dot(x, wg[:, cols]))
                up = dot(x, wu[:, cols])
                hidden[span_rows, cols] = (value * up).astype(BF16)
                values[span_rows, cols] = value.astype(BF16)
                slopes[span_rows, cols] = (up * slope).astype(BF16)

            tile_loop(ff, 512, up_tile)
            if part == 0:
                loads[2].wait()

            def down_tile(start, count, blocks=blocks, span_rows=span_rows, size=size):
                cols = pl.ds(start, count)
                y = dot(hidden[span_rows, :], wd[:, cols]).astype(BF16)
                made[blocks, :, cols] = y.reshape(size, block, count)

            tile_loop(width, 512, down_tile)
            for k in range(max(first, 1), first + size):
                t.home(k).start()
        back[t.me] = made[t.me]
        half_cols = pl.ds(pl.multiple_of(t.dp * span, 128), span)
        other_cols = pl.ds(pl.multiple_of((1 - t.dp) * span, 128), span)
        outs = [
            (slopes, slope_out),
            (values, value_out),
            (hidden.at[:, half_cols], hidden_out.at[0]),
            (rows, rows_out.at[0]),
        ]
        outs = [pltpu.make_async_copy(src, dst, osem.at[i]) for i, (src, dst) in enumerate(outs)]
        for out in outs:
            out.start()

        for part in range(len(t.groups)):
            rows_over(part).wait_recv()

        def peer_tile(start, count):
            x = rows_peer[...].reshape(experts * block, width)
            here = pl.ds(start, count)
            cols = pl.ds(pl.multiple_of(t.dp * span + start, 128), count)
            value, slope = gelu_parts(dot(x, wg[:, cols]))
            up = dot(x, wu[:, cols])
            hidden[:, pl.ds(pl.multiple_of((1 - t.dp) * span + start, 128), count)] = (value * up).astype(BF16)
            values_peer[:, here] = value.astype(BF16)
            slopes_peer[:, here] = (up * slope).astype(BF16)

        tile_loop(span, 512, peer_tile)
        more = [
            (slopes_peer, slope_peer_out),
            (values_peer, value_peer_out),
            (hidden.at[:, other_cols], hidden_out.at[1]),
            (rows_peer, rows_out.at[1]),
        ]
        more = [pltpu.make_async_copy(src, dst, osem.at[4 + i]) for i, (src, dst) in enumerate(more)]
        for out in more:
            out.start()
        for k in range(1, experts):
            t.home(k).wait_recv()
        back_copy = pltpu.make_async_copy(back, back_out, osem.at[8])
        back_copy.start()
        for k in range(1, experts):
            t.there(k).wait_send()
            t.home(k).wait_send()
        for part in range(len(t.groups)):
            rows_over(part).wait_send()
        for out in [*outs, *more, back_copy]:
            out.wait()


def expert_backward_kernel(turn, has_prev, *refs):
    send_ref = refs[0]
    sources = refs[1:8]
    lefts, refs = refs[8 + 3 * has_prev : 8 + 7 * has_prev], refs[8 + 7 * has_prev :]
    back_out, mixed_out, grad_out = refs[:3]
    lefts_out, refs = refs[3 : 3 + has_prev], refs[3 + has_prev :]
    wdt, dgate, dup, wgt, wut, dgate_peer, dup_peer = refs[:7]
    grads, back, made, grads_peer = refs[7:11]
    wsem, s1, r1, s2, r2, sx, rx, osem = refs[11:19]
    left_refs = refs[19:]
    experts, block, width = send_ref.shape
    ff = wdt.shape[1]
    span = ff // 2
    half_width = width // 2
    dp = lax.axis_index("dp")
    t = Turn(experts, block, (send_ref, grads, s1, r1), (made, back, s2, r2))

    fetch = []
    if has_prev:
        left_held, left_stage, ll, sl, rl = left_refs
        fetch = [pltpu.make_async_copy(lefts[i], left_held.at[i], ll.at[i]) for i in range(4)]

    def left_over(i):
        return remote(left_stage.at[i], lefts_out[0].at[i], sl.at[i], rl.at[i], t.peer)

    def send_lefts():
        for i in range(4):
            fetch[i].wait()
            cols = pl.ds(pl.multiple_of((1 - dp) * half_width, 128), half_width)
            left_stage[i] = left_held[i, :, cols]
            left_over(i).start()

    if has_prev:

        @pl.when(lax.axis_index("half") != turn)
        def _():
            for copy in fetch:
                copy.start()
            greet([t.peer])
            send_lefts()
            for i in range(4):
                left_over(i).wait()

    @pl.when(lax.axis_index("half") == turn)
    def _():
        t.greet()

        def grads_over(part):
            blocks, _ = t.spans(*t.groups[part])
            return remote(grads.at[blocks], grads_peer.at[blocks], sx.at[part], rx.at[part], t.peer)

        for k in range(1, experts):
            t.there(k).start()
        held = (wdt, dgate, dup, wgt, wut, dgate_peer, dup_peer)
        loads = [pltpu.make_async_copy(src, dst, wsem.at[i]) for i, (src, dst) in enumerate(zip(sources, held))]
        for copy in fetch:
            copy.start()
        for load in loads:
            load.start()
        grads[t.me] = send_ref[t.me]
        if has_prev:
            send_lefts()
        for load in loads[:3]:
            load.wait()
        for part, (first, size) in enumerate(t.groups):
            for k in range(max(first, 1), first + size):
                t.there(k).wait_recv()
            grads_over(part).start()
            blocks, span_rows = t.spans(first, size)

            def hidden_tile(start, count, blocks=blocks, span_rows=span_rows, size=size):
                dy = grads[blocks].reshape(size * block, width)
                cols = pl.ds(start, count)
                dhidden = dot(dy, wdt[:, cols])
                dgate[span_rows, cols] = (dhidden * dgate[span_rows, cols].astype(F32)).astype(BF16)
                dup[span_rows, cols] = (dhidden * dup[span_rows, cols].astype(F32)).astype(BF16)

            tile_loop(ff, 512, hidden_tile)
            if part == 0:
                loads[3].wait()
                loads[4].wait()

            def rows_tile(start, count, blocks=blocks, span_rows=span_rows, size=size):
                cols = pl.ds(start, count)
                dr = dot(dgate[span_rows, :], wgt[:, cols]) + dot(dup[span_rows, :], wut[:, cols])
                made[blocks, :, cols] = dr.astype(BF16).reshape(size, block, count)

            tile_loop(width, 512, rows_tile)
            for k in range(max(first, 1), first + size):
                t.home(k).start()
        back[t.me] = made[t.me]
        half_cols = pl.ds(pl.multiple_of(dp * span, 128), span)
        outs = [
            (dgate.at[:, half_cols], mixed_out.at[0, 0]),
            (dup.at[:, half_cols], mixed_out.at[1, 0]),
            (grads, grad_out.at[0]),
        ]
        outs = [pltpu.make_async_copy(src, dst, osem.at[i]) for i, (src, dst) in enumerate(outs)]
        for out in outs:
            out.start()

        for load in loads[5:]:
            load.wait()
        for part in range(len(t.groups)):
            grads_over(part).wait_recv()

        def peer_tile(start, count):
            dy = grads_peer[...].reshape(experts * block, width)
            here = pl.ds(start, count)
            dhidden = dot(dy, wdt[:, pl.ds(pl.multiple_of(dp * span + start, 128), count)])
            dgate_peer[:, here] = (dhidden * dgate_peer[:, here].astype(F32)).astype(BF16)
            dup_peer[:, here] = (dhidden * dup_peer[:, here].astype(F32)).astype(BF16)

        tile_loop(span, 512, peer_tile)
        more = [
            (dgate_peer, mixed_out.at[0, 1]),
            (dup_peer, mixed_out.at[1, 1]),
            (grads_peer, grad_out.at[1]),
        ]
        more = [pltpu.make_async_copy(src, dst, osem.at[3 + i]) for i, (src, dst) in enumerate(more)]
        for out in more:
            out.start()
        for k in range(1, experts):
            t.home(k).wait_recv()
        back_copy = pltpu.make_async_copy(back, back_out, osem.at[6])
        back_copy.start()
        for k in range(1, experts):
            t.there(k).wait_send()
            t.home(k).wait_send()
        for part in range(len(t.groups)):
            grads_over(part).wait_send()
        if has_prev:
            for i in range(4):
                left_over(i).wait()
        for out in [*outs, *more, back_copy]:
            out.wait()


def expert_call(kernel, number, turn, send, sources, prev, more, out_shape, scratch, name):
    vmem, hbm = pl.BlockSpec(memory_space=pltpu.VMEM), pl.BlockSpec(memory_space=pl.ANY)
    prev = list(prev or [])
    return pl.pallas_call(
        functools.partial(kernel, turn, bool(prev)),
        in_specs=[vmem] + [hbm] * (len(sources) + len(prev) + len(more)),
        out_specs=[hbm] * len(out_shape),
        out_shape=out_shape,
        input_output_aliases={1 + len(sources) + i: i for i in range(len(prev))},
        scratch_shapes=scratch,
        compiler_params=pltpu.CompilerParams(
            collective_id=number, has_side_effects=True, vmem_limit_bytes=60 << 20
        ),
        name=name,
    )(send, *sources, *prev, *more)


def moe_forward(send, w_in, w_down, turn, prev):
    experts, block, width = send.shape
    ff = w_down.shape[0]
    total = experts * block
    parts = len(groups_of(experts, block))
    dma = pltpu.SemaphoreType.DMA
    scratch = [
        pltpu.VMEM((width, ff), BF16),
        pltpu.VMEM((width, ff), BF16),
        pltpu.VMEM((ff, width), BF16),
        *[pltpu.VMEM(send.shape, BF16)] * 4,
        *[pltpu.VMEM((total, ff), BF16)] * 3,
        *[pltpu.VMEM((total, ff // 2), BF16)] * 2,
        pltpu.VMEM((2, 256, width), BF16),
        pltpu.VMEM((2, 256, ff), BF16),
        dma((3,)),
        *[dma((experts,))] * 4,
        *[dma((parts,))] * 2,
        dma((9,)),
        dma((2,)),
    ]
    shapes = [
        send.shape,
        (2, *send.shape),
        (total, ff),
        (total, ff),
        (2, total, ff // 2),
        (total, ff // 2),
        (total, ff // 2),
        (ff, width),
        (ff, width),
        (width, ff),
    ]
    out_shape = [jax.ShapeDtypeStruct(shape, BF16) for shape in shapes]
    return expert_call(
        expert_forward_kernel, 1 + turn, turn, send, [w_in, w_down], prev, [], out_shape, scratch, "moe_forward"
    )


def moe_backward(grad_send, saved, turn, prev, lefts):
    experts, block, width = grad_send.shape
    _, _, slope, value, _, slope_peer, value_peer, wgt, wut, wdt = saved
    total, ff = slope.shape
    parts = len(groups_of(experts, block))
    dma = pltpu.SemaphoreType.DMA
    scratch = [
        pltpu.VMEM((width, ff), BF16),
        *[pltpu.VMEM((total, ff), BF16)] * 2,
        *[pltpu.VMEM((ff, width), BF16)] * 2,
        *[pltpu.VMEM((total, ff // 2), BF16)] * 2,
        *[pltpu.VMEM(grad_send.shape, BF16)] * 4,
        dma((7,)),
        *[dma((experts,))] * 4,
        *[dma((parts,))] * 2,
        dma((7,)),
    ]
    out_shape = [
        jax.ShapeDtypeStruct(grad_send.shape, BF16),
        jax.ShapeDtypeStruct((2, 2, total, ff // 2), BF16),
        jax.ShapeDtypeStruct((2, *grad_send.shape), BF16),
    ]
    if lefts:
        rows = lefts[0].shape[0]
        out_shape.append(jax.ShapeDtypeStruct((4, rows, width // 2), BF16))
        scratch += [pltpu.VMEM((4, rows, width), BF16), pltpu.VMEM((4, rows, width // 2), BF16)]
        scratch += [dma((4,))] * 3
    return expert_call(
        expert_backward_kernel,
        3 + turn,
        turn,
        grad_send,
        [wdt, slope, value, wgt, wut, slope_peer, value_peer],
        prev,
        lefts,
        out_shape,
        scratch,
        "moe_backward",
    )


def dense_kernel(stages, chunk, lag, *refs):
    sources, small_ref = refs[:11], refs[11]
    out_refs, small_out, small_in = refs[12:15], refs[15], refs[16]
    held, xt_ref, refs = refs[17:28], refs[28], refs[29:]
    x_refs, own_refs, peer_refs, xp = held[:4], held[4:7], held[7:10], held[10]
    sums, parts = refs[:stages], refs[stages : 2 * stages]
    ss, rs, sk, rk, sl = refs[2 * stages :]
    counts = [ref.shape[1] // chunk for ref in own_refs]
    starts = [sum(counts[:i]) for i in range(3)]
    chunks = sum(counts)
    per_cross = counts[2] // 2
    rows, half = xp.shape[1:]
    dp, me = lax.axis_index("dp"), lax.axis_index("expert")
    peer = {"dp": 1 - dp}
    partners = [flipped(me, k) for k in range(stages)]
    bits = [me // (1 << k) % 2 for k in range(stages)]
    load = [pltpu.make_async_copy(sources[i], held[i], sl.at[i]) for i in range(11)]
    for i in (10, 2, 3, 6, 9, 0, 4, 7, 1, 5, 8):
        load[i].start()
    greet([peer] + [{"expert": p} for p in partners])

    def send_small(step):
        src = small_ref if step == 0 else small_out.at[step - 1]
        device = peer if step == 0 else {"expert": partners[stages - step]}
        return remote(src, small_in.at[step], ss.at[step], rs.at[step], device)

    def order(k, odd):
        return 1 - k if odd and k < 2 else k

    def send_part(k, c, odd):
        bit = order(k, odd)
        other = 1 - bits[bit]
        src = sums[0].at[c, :, :, other] if k == 0 and not odd else sums[k].at[c, :, other]
        return remote(src, parts[k].at[c], sk.at[k, c], rk.at[k, c], {"expert": partners[bit]})

    def turn_x(g):
        load[g].wait()
        cols = pl.ds(pl.multiple_of(dp * half, half), half)
        xt_ref[g, :, :rows] = jnp.transpose(x_refs[g][:, cols])
        xt_ref[g, :, rows:] = jnp.transpose(xp[g])

    def small_step(j):
        send_small(j).wait_recv()
        own = small_ref[...] if j == 0 else small_out[j - 1]
        small_out[j] = own + small_in[j]
        if j < stages:
            send_small(j + 1).start()

    send_small(0).start()
    load[10].wait()
    last = counts[2]
    early = chunks - last
    per = chunks // last

    def produce(i, carry):
        c = jnp.where(lax.rem(i, per) == 0, early + i // per, i - i // per - 1)
        for g in range(3):

            @pl.when(c == starts[g])
            def _(g=g):
                load[4 + g].wait()
                load[7 + g].wait()
                for x in (g,) if g < 2 else (2, 3):
                    turn_x(x)

            @pl.when((c >= starts[g]) & (c < starts[g] + counts[g]))
            def _(g=g):
                at = c - starts[g]
                cols = pl.ds(pl.multiple_of(at * chunk, chunk), chunk)
                which = g if g < 2 else 2 + at // per_cross
                total = dot(xt_ref[which, :, :rows], own_refs[g][:, cols])
                total += dot(xt_ref[which, :, rows:], peer_refs[g][:, cols])
                sums[0][c] = total.astype(BF16).reshape(sums[0].shape[1:])
                send_part(0, c, g == 2).start()

        for j in range(2):

            @pl.when(i == 3 + 6 * j)
            def _(j=j):
                small_step(j)

        return carry

    lax.fori_loop(0, chunks, produce, 0)

    def advance(k, c, odd):
        send_part(k, c, odd).wait_recv()
        bit = bits[order(k, odd)]
        mine = sums[0][c, :, :, bit] if k == 0 and not odd else sums[k][c, :, bit]
        total = mine.astype(F32) + parts[k][c].astype(F32)
        if k + 1 < stages:
            sums[k + 1][c] = total.astype(BF16).reshape(sums[k + 1].shape[1:])
            send_part(k + 1, c, odd).start()
            return
        total = total.reshape(total.shape[-2:])
        for g in (2,) if odd else (0, 1):

            @pl.when((c >= starts[g]) & (c < starts[g] + counts[g]))
            def _(g=g):
                at = pl.multiple_of((c - starts[g]) * chunk, chunk)
                out_refs[g][:, pl.ds(at, chunk)] = total

    def reduce(i, carry):
        @pl.when((lax.rem(i, 2) == 1) & (i // 2 < last))
        def _():
            advance(0, early + i // 2, True)

        for k in range(stages):
            c = i - lag * k

            @pl.when((c >= 0) & (c < early))
            def _(k=k, c=c):
                advance(k, c, False)

        for k in range(1, stages):
            c = i - 1 - lag * (k - 1)

            @pl.when((c >= early) & (c < chunks))
            def _(k=k, c=c):
                advance(k, c, True)

        for j in range(2, stages + 1):

            @pl.when(i == 3 * j - 2)
            def _(j=j):
                small_step(j)

        return carry

    lax.fori_loop(0, chunks + 1 + lag * (stages - 2), reduce, 0)

    def finish(c, carry, odd):
        for k in range(stages):
            send_part(k, c, odd).wait_send()
        return carry

    lax.fori_loop(0, early, functools.partial(finish, odd=False), 0)
    lax.fori_loop(early, chunks, functools.partial(finish, odd=True), 0)
    for j in range(stages + 1):
        send_small(j).wait_send()


def over_dp(array):
    return lax.ppermute(array, "dp", [(0, 1), (1, 0)])


def dense_gradients(lefts, lefts_peer, own, peer, small, experts):
    chunk = 512
    rows, width = lefts[0].shape
    half_rows = width // 2
    chunks = sum(y.shape[1] for y in own) // chunk
    stages = experts.bit_length() - 1
    keep = half_rows // experts
    vmem, hbm = pl.BlockSpec(memory_space=pltpu.VMEM), pl.BlockSpec(memory_space=pl.ANY)
    dma = pltpu.SemaphoreType.DMA
    sources = [*lefts, *own, *peer, lefts_peer]
    blocks = [(experts // 4, 2, 2)] + [(experts >> (k + 1), 2) for k in range(1, stages)]
    halved = [(experts // 4, 2)] + [(experts >> (k + 1),) for k in range(1, stages)]
    scratch = [pltpu.VMEM((stages + 1, *small.shape), F32)]
    scratch += [pltpu.VMEM(a.shape, BF16) for a in sources]
    scratch += [pltpu.VMEM((4, half_rows, 2 * rows), BF16)]
    scratch += [pltpu.VMEM((chunks, *b, keep, chunk), BF16) for b in blocks + halved]
    scratch += [dma((stages + 1,)), dma((stages + 1,)), dma((stages, chunks)), dma((stages, chunks))]
    scratch += [dma((len(sources),))]
    *outs, sums = pl.pallas_call(
        functools.partial(dense_kernel, stages, chunk, 2),
        in_specs=[hbm] * len(sources) + [vmem],
        out_specs=[vmem] * 4,
        out_shape=[
            *(jax.ShapeDtypeStruct((keep, y.shape[1]), F32) for y in own),
            jax.ShapeDtypeStruct((stages + 1, *small.shape), F32),
        ],
        scratch_shapes=scratch,
        compiler_params=pltpu.CompilerParams(
            collective_id=0, has_side_effects=True, vmem_limit_bytes=56 << 20
        ),
        name="dense_gradients",
    )(*sources, small)
    return outs, sums[stages]


def product_kernel(x_ref, y_ref, out_ref):
    out_ref[...] = dot(x_ref[...], y_ref[...].reshape(y_ref.shape[-2:]), TN).reshape(out_ref.shape)


def expert_gradients(rows, mixed, hidden, grads):
    total, width = rows.shape
    span = hidden.shape[1]
    tile = 256
    params = pltpu.CompilerParams(vmem_limit_bytes=40 << 20)
    din = pl.pallas_call(
        product_kernel,
        grid=(2, width // tile),
        in_specs=[
            pl.BlockSpec((total, tile), lambda g, i: (0, i)),
            pl.BlockSpec((1, total, span), lambda g, i: (g, 0, 0)),
        ],
        out_specs=pl.BlockSpec((1, tile, span), lambda g, i: (g, i, 0)),
        out_shape=jax.ShapeDtypeStruct((2, width, span), F32),
        compiler_params=params,
        name="expert_in_gradient",
    )(rows, mixed)
    ddown = pl.pallas_call(
        product_kernel,
        grid=(pl.cdiv(span, tile),),
        in_specs=[
            pl.BlockSpec((total, tile), lambda i: (0, i)),
            pl.BlockSpec((total, width), lambda i: (0, 0)),
        ],
        out_specs=pl.BlockSpec((tile, width), lambda i: (i, 0)),
        out_shape=jax.ShapeDtypeStruct((span, width), F32),
        compiler_params=params,
        name="expert_out_gradient",
    )(hidden, grads)
    return din, ddown


def body(
    tokens,
    cotangent,
    lengths,
    routes,
    self_qkv,
    self_out,
    cross_weights,
    router,
    gains,
    bias_table,
    expert_in,
    expert_out,
):
    _, seqs, length, width = tokens.shape
    heads = H
    experts = router.shape[2]
    top = routes.shape[3]
    capacity = (5 * top * length + 4 * experts - 1) // (4 * experts)
    block_rows = -(-seqs * capacity // 16) * 16
    rows = seqs * length
    slots = experts * block_rows
    half_index = lax.axis_index("half")
    decoder = half_index == 1
    wqkv, wout, wcross, wrouter, gain = (
        self_qkv[0],
        self_out[0],
        cross_weights[0],
        router[0],
        gains[0],
    )
    w_in, w_down = expert_in[0, 0], expert_out[0, 0]

    column = np.arange(2 * length)
    hot, hot_back = (
        (
            jnp.where(decoder, *reversed(diagonal_buckets(diff)))[:, None]
            == jnp.arange(BUCKETS)[None, :]
        ).astype(F32)
        for diff in (np.where(column < length, column, column - 2 * length), column - length + 1)
    )
    bias = lax.dot_general(
        bias_table[0].reshape(BUCKETS, heads),
        hot,
        (((0,), (1,)), ((), ())),
        precision=lax.Precision.HIGHEST,
        preferred_element_type=F32,
    )
    own_lengths = jnp.where(decoder, lengths[1], lengths[0])
    self_info = jnp.concatenate([own_lengths, half_index[None]]).astype(jnp.int32)
    cross_info = jnp.concatenate([lengths[0], jnp.zeros((1,), jnp.int32)]).astype(jnp.int32)

    order = jnp.transpose(routes[0], (0, 2, 1)).reshape(seqs, top * length)
    expert_ids = jnp.arange(experts, dtype=jnp.int32)
    picked = (order[:, :, None] == expert_ids).astype(BF16)
    earlier = np.tril(np.ones((top * length, top * length), np.float32), -1).astype(BF16)
    before = jnp.einsum("pq,sqe->spe", earlier, picked, preferred_element_type=F32)
    place = jnp.sum(before * picked.astype(F32), axis=2).astype(jnp.int32)
    kept = place < capacity
    base = order * block_rows + jnp.arange(seqs, dtype=jnp.int32)[:, None] * capacity
    target = jnp.where(kept, base + place, -1).reshape(seqs, top, length)
    target = jnp.transpose(target, (1, 0, 2)).reshape(top, rows)
    slot_ids = jnp.arange(slots, dtype=jnp.int32)
    spots = (target[:, :, None] == slot_ids).astype(BF16)
    both = jnp.sum(spots.astype(F32), axis=0).astype(BF16)
    stacked = spots.reshape(top * rows, slots)
    kept_hot = picked.astype(F32) * kept[:, :, None].astype(F32)
    kept_count = jnp.sum(kept_hot, axis=(0, 1))
    all_count = jnp.sum(picked.astype(F32), axis=(0, 1))
    tallies = jnp.concatenate([kept_count, all_count - kept_count])
    route_hot = (routes[0].reshape(rows, top, 1) == expert_ids).astype(F32)

    def route(values):
        normed, scale = norm_parts(values, gain[1])
        low = normed.astype(BF16)
        rest = (normed - low.astype(F32)).astype(BF16)
        logits = dot(low, wrouter) + dot(rest, wrouter)
        probs = jax.nn.softmax(logits, axis=-1)
        chosen = jnp.sum(probs[:, None, :] * route_hot, axis=-1)
        total = jnp.sum(chosen, axis=-1, keepdims=True)
        gates = chosen / total
        send = dot(both, low, TN).astype(BF16).reshape(experts, block_rows, width)
        return dict(scale=scale, low=low, probs=probs, gates=gates, total=total, send=send)

    def fetch(returned):
        flat = returned.reshape(slots, width)
        return dot(stacked, flat).reshape(top, rows, width)

    def combine(values, gates, results):
        return values + jnp.sum(jnp.transpose(gates)[:, :, None] * results, axis=0)

    values = tokens[0].reshape(rows, width).astype(F32)
    normed, scale0 = norm_parts(values, gain[0])
    low0 = normed.astype(BF16)
    qkv = dot(low0, wqkv).astype(BF16)
    mixed0, log0 = attend(self_info, bias, qkv, qkv, (0, 1, 2), length, width)
    first = values + dot(mixed0, wout)

    state = route(first)
    saved = moe_forward(state["send"], w_in, w_down, 0, None)
    final_enc = combine(first, state["gates"], fetch(saved[0]))
    normed, scale_m = norm_parts(final_enc, gain[2])
    low_m = normed.astype(BF16)
    memory = dot(low_m, wcross).astype(BF16)
    names = ("half", "dp", "expert")
    forward_pairs, back_pairs = half_pairs(lax.axis_size("dp") * lax.axis_size("expert"))
    memory = lax.ppermute(memory, names, forward_pairs)

    normed, scale_c = norm_parts(first, gain[2])
    low_c = normed.astype(BF16)
    query = dot(low_c, wcross[:, :width]).astype(BF16)
    mixed_c, log_c = attend(cross_info, None, query, memory, (0, 0, 1), length, width)
    second = jnp.where(decoder, first + dot(mixed_c, wcross[:, width:]), first)

    state = route(second)
    saved = moe_forward(state["send"], w_in, w_down, 1, saved)
    results = fetch(saved[0])
    final = combine(second, state["gates"], results)
    outputs = final.astype(BF16)

    def moe_gradient(grad):
        dgates = jnp.transpose(jnp.sum(grad[None] * results, axis=-1))
        spread = (jnp.transpose(state["gates"])[:, :, None] * grad[None]).astype(BF16)
        send = dot(stacked, spread.reshape(top * rows, width), TN)
        return dgates, send.astype(BF16).reshape(experts, block_rows, width)

    def moe_input_gradient(grad, dgates, back):
        gates, total, probs = state["gates"], state["total"], state["probs"]
        dchosen = (dgates - jnp.sum(dgates * gates, axis=-1, keepdims=True)) / total
        dprobs = jnp.sum(dchosen[:, :, None] * route_hot, axis=1)
        dlogits = probs * (dprobs - jnp.sum(dprobs * probs, axis=-1, keepdims=True))
        dnormed = dot(both, back.reshape(slots, width)) + lax.dot_general(
            dlogits, wrouter.astype(F32), NT, preferred_element_type=F32
        )
        dvalues, dgain = norm_back(second, state["scale"], gain[1], dnormed)
        normed = second * state["scale"] * gain[1]
        drouter = lax.dot_general(
            normed, dlogits, TN, precision=lax.Precision.HIGHEST, preferred_element_type=F32
        )
        return grad + dvalues, dgain, drouter

    grad_dec = cotangent[0].reshape(rows, width).astype(F32)
    dgates, grad_send = moe_gradient(grad_dec)
    kept_from = moe_backward(grad_send, saved, 1, None, [])
    grad_second, _, _ = moe_input_gradient(grad_dec, dgates, kept_from[0])

    dbranch_c = grad_second.astype(BF16)
    dmixed_c = dot(dbranch_c, wcross[:, width:], NT).astype(BF16)
    dquery, dmemory = attend_back(
        cross_info, None, query, memory, (0, 0, 1), (mixed_c, log_c), dmixed_c, length, width
    )
    dmemory = lax.ppermute(dmemory, names, back_pairs)
    dnormed = dot(dquery, wcross[:, :width], NT)
    dvalues, dgain_c = norm_back(first, scale_c, gain[2], dnormed)
    grad_first_dec = grad_second + dvalues

    dnormed = dot(dmemory, wcross, NT)
    dvalues, dgain_m = norm_back(final_enc, scale_m, gain[2], dnormed)
    grad = jnp.where(decoder, grad_dec, grad_dec + dvalues)
    dgates, grad_send = moe_gradient(grad)
    lefts = [low0, mixed0, jnp.where(decoder, low_c, low_m), jnp.where(decoder, mixed_c, low_m)]
    back, mixed_grads, all_grad, lefts_peer = moe_backward(grad_send, saved, 0, kept_from, lefts)
    all_rows, hidden = saved[1], saved[4]
    grad_second, dgain_moe, drouter = moe_input_gradient(grad, dgates, back)
    grad_first = jnp.where(decoder, grad_first_dec, grad_second)

    dbranch = grad_first.astype(BF16)
    dmixed = dot(dbranch, wout, NT).astype(BF16)
    dqkv_rows, diag = attend_back(
        self_info, bias, qkv, qkv, (0, 1, 2), (mixed0, log0), dmixed, length, width
    )
    dnormed = dot(dqkv_rows, wqkv, NT)
    dvalues, dgain_self = norm_back(values, scale0, gain[0], dnormed)
    d_tokens = (grad_first + dvalues).astype(BF16)
    dtable = lax.dot_general(
        hot_back, diag, (((0,), (1,)), ((), ())), precision=lax.Precision.HIGHEST,
        preferred_element_type=F32,
    ).reshape(-1)

    cross_grad = jnp.where(decoder, jnp.concatenate([dquery, dbranch_c], axis=1), dmemory)
    own_grads = (dqkv_rows, dbranch, cross_grad)
    peer_grads = tuple(map(over_dp, own_grads))
    places = 2 * experts
    own = width // places
    extra = jnp.concatenate([dtable.reshape(places, -1), tallies.reshape(places, 1)], axis=1)
    extra = jnp.pad(extra, ((0, 0), (0, -extra.shape[1] % own)))
    small = jnp.concatenate(
        [
            jnp.transpose(drouter),
            jnp.stack([dgain_self, dgain_moe, jnp.where(decoder, dgain_c, dgain_m)]),
            jnp.swapaxes(extra.reshape(places, -1, own), 0, 1).reshape(-1, width),
        ]
    )
    small = jnp.pad(small, ((0, -small.shape[0] % 8), (0, 0)))
    (dqkv, dout, dcross), small = dense_gradients(
        lefts, lefts_peer, own_grads, peer_grads, small, experts
    )
    place = lax.axis_index("dp") * experts + lax.axis_index("expert")
    mine = lax.dynamic_slice_in_dim(small, place * own, own, 1)
    tail = mine[experts + 3 :].reshape(-1)
    own_table = dtable.shape[0] // places
    d_table = tail[:own_table]
    counts = tail[own_table].astype(jnp.int32)

    ff_half = hidden.shape[-1]
    din, ddown = expert_gradients(
        all_rows.reshape(-1, width),
        mixed_grads.reshape(2, -1, ff_half),
        hidden.reshape(-1, ff_half),
        all_grad.reshape(-1, width),
    )
    return (
        outputs.reshape(1, seqs, length, width),
        d_tokens.reshape(1, seqs, length, width),
        dqkv[None],
        dout[None],
        dcross[None],
        jnp.transpose(mine[:experts])[None],
        mine[experts : experts + 3][None],
        d_table[None],
        din[None, None],
        ddown[None, None],
        counts.reshape(1, 1, 1),
    )


def half_pairs(count):
    return (
        [(i, count + i) for i in range(count)],
        [(count + i, i) for i in range(count)],
    )


def solution(mesh):
    placed = (
        P("half", ("dp", "expert"), None, None),
        P("half", ("dp", "expert"), None, None),
        P(None, ("dp", "expert")),
        P("half", ("dp", "expert"), None, None),
        P("half", None, None),
        P("half", None, None),
        P("half", None, None),
        P("half", None, None),
        P("half", None, None),
        P("half", None),
        P("half", "expert", None, None, None),
        P("half", "expert", None, None),
    )
    return jax.shard_map(
        body,
        mesh=mesh,
        in_specs=placed,
        out_specs=(
            P("half", ("dp", "expert"), None, None),
            P("half", ("dp", "expert"), None, None),
            P("half", ("dp", "expert"), None),
            P("half", ("dp", "expert"), None),
            P("half", ("dp", "expert"), None),
            P("half", ("dp", "expert"), None),
            P("half", None, ("dp", "expert")),
            P("half", ("dp", "expert")),
            P("half", "expert", None, None, "dp"),
            P("half", "expert", "dp", None),
            P("half", "dp", "expert"),
        ),
        check_vma=False,
    )
```

```python
import functools

import jax
import jax.numpy as jnp
import numpy as np
from jax import lax
from jax.experimental import pallas as pl
from jax.experimental.pallas import tpu as pltpu
from jax.sharding import PartitionSpec as P

H = 16
BUCKETS = 32
EPS = 1e-06
ENC_STEPS = (12, 16, 23, 32, 46, 64, 91)
DEC_STEPS = (19, 21, 24, 27, 31, 35, 40, 46, 52, 59, 67, 77, 87, 99, 113)
F32 = jnp.float32
BF16 = jnp.bfloat16
MESH = pl.DeviceIdType.MESH
NT = (((1,), (1,)), ((), ()))
TN = (((0,), (0,)), ((), ()))


def dot(a, b, dims=(((1,), (0,)), ((), ()))):
    return lax.dot_general(a, b, dims, preferred_element_type=F32)


def diagonal_buckets(diff):
    apart = np.abs(diff)
    coarse = 8 + sum((apart >= step).astype(np.int32) for step in ENC_STEPS)
    enc = np.where(apart < 8, apart, coarse) + 16 * (diff > 0)
    behind = np.maximum(-diff, 0)
    coarse = 16 + sum((behind >= step).astype(np.int32) for step in DEC_STEPS)
    dec = np.where(behind < 16, behind, coarse)
    return enc.astype(np.int32), dec.astype(np.int32)


def diagonals(bias_ref, head, length):
    row = jnp.broadcast_to(bias_ref[pl.ds(head, 1), :], (length, 2 * length))
    return pltpu.roll(row, 0, 1, stride=1, stride_axis=0)[:, :length]


def fill_masks(info, mask_ref):
    seqs, length, _ = mask_ref.shape
    row_id = lax.broadcasted_iota(jnp.int32, (length, length), 0)
    col_id = lax.broadcasted_iota(jnp.int32, (length, length), 1)
    reach = jnp.where(info[seqs] > 0, row_id, length)
    for seq in range(seqs):
        allowed = (col_id < info[seq]) & (col_id <= reach)
        mask_ref[seq] = jnp.where(allowed, 0.0, -1000000000.0)


def attend_kernel(has_bias, info, *refs):
    bias_ref, refs = (refs[0], refs[1:]) if has_bias else (None, refs)
    q_ref, k_ref, v_ref, out_ref, log_ref, mask_ref = refs
    seqs, length, _ = mask_ref.shape
    low = lax.broadcasted_iota(jnp.int32, (length, 128), 1) < 64
    fill_masks(info, mask_ref)

    @pl.loop(0, q_ref.shape[1] // 128, unroll=True)
    def _(pair):
        cols = pl.ds(pl.multiple_of(pair * 128, 128), 128)
        biases = [diagonals(bias_ref, 2 * pair + side, length) if has_bias else 0.0 for side in range(2)]
        for seq in range(seqs):
            rows = pl.ds(seq * length, length)
            q, k, v = q_ref[rows, cols] * 0.125, k_ref[rows, cols], v_ref[rows, cols]
            mixed, peaks = [], []
            for side in range(2):
                mine = low if side == 0 else jnp.logical_not(low)
                part = jnp.where(mine, q, jnp.zeros_like(q))
                scores = dot(part, k, NT) + (mask_ref[seq] + biases[side])
                peak = jnp.max(scores, axis=-1, keepdims=True)
                spread = jnp.exp(scores - peak).astype(BF16)
                mixed.append(dot(spread, jnp.where(mine, v, jnp.ones_like(v))))
                peaks.append(peak)
            total = pltpu.roll(jnp.where(low, mixed[1], mixed[0]), 64, 1)
            out_ref[rows, cols] = (jnp.where(low, mixed[0], mixed[1]) / total).astype(BF16)
            log_ref[rows, cols] = jnp.where(low, peaks[0], peaks[1]) + jnp.log(total)


def attend_back_kernel(has_bias, info, *refs):
    if has_bias:
        bias_ref, q_ref, k_ref, v_ref, a_ref, log_ref, g_ref, dq_ref, diag_ref, mask_ref = refs
        dkv_ref, shift = dq_ref, q_ref.shape[1]
    else:
        q_ref, k_ref, v_ref, a_ref, log_ref, g_ref, dq_ref, dkv_ref, mask_ref = refs
        shift = 0
    seqs, length, _ = mask_ref.shape
    width = q_ref.shape[1]
    low = lax.broadcasted_iota(jnp.int32, (length, 128), 1) < 64
    fill_masks(info, mask_ref)
    if has_bias:
        row_id = lax.broadcasted_iota(jnp.int32, (length, length), 0)
        col_id = lax.broadcasted_iota(jnp.int32, (length, length), 1)
        flip = (row_id + col_id == length - 1).astype(F32).astype(BF16)

    @pl.loop(0, width // 128, unroll=True)
    def _(pair):
        cols = pl.ds(pl.multiple_of(pair * 128, 128), 128)
        kcols = pl.ds(pl.multiple_of(shift + pair * 128, 128), 128)
        vcols = pl.ds(pl.multiple_of(shift + width + pair * 128, 128), 128)
        biases = [diagonals(bias_ref, 2 * pair + side, length) if has_bias else 0.0 for side in range(2)]
        sums = [0.0, 0.0]
        for seq in range(seqs):
            rows = pl.ds(seq * length, length)
            q, k, v, g = q_ref[rows, cols] * 0.125, k_ref[rows, cols], v_ref[rows, cols], g_ref[rows, cols]
            logs = log_ref[rows, cols]
            turned = pltpu.roll(logs, 64, 1)
            product = g.astype(F32) * a_ref[rows, cols].astype(F32)
            minus = (-pltpu.roll(product, 64, 1)).astype(BF16)
            scaled = k * 0.125
            dqs, dks, dvs = [], [], []
            for side in range(2):
                mine = low if side == 0 else jnp.logical_not(low)
                part = jnp.where(mine, q, jnp.zeros_like(q))
                scores = dot(part, k, NT) + (mask_ref[seq] + biases[side])
                probs = jnp.exp(scores - jnp.where(mine, logs, turned))
                dvs.append(dot(probs.astype(BF16), g, TN))
                centred = dot(jnp.where(mine, g, minus), jnp.where(mine, v, jnp.ones_like(v)), NT)
                dlow = (probs * centred).astype(BF16)
                dqs.append(dot(dlow, scaled))
                dks.append(dot(dlow, q, TN))
                if has_bias:
                    sums[side] = sums[side] + dlow.astype(F32)
            dq_ref[rows, cols] = jnp.where(low, dqs[0], dqs[1]).astype(BF16)
            dkv_ref[rows, kcols] = jnp.where(low, dks[0], dks[1]).astype(BF16)
            dkv_ref[rows, vcols] = jnp.where(low, dvs[0], dvs[1]).astype(BF16)
        if has_bias:
            for side in range(2):
                upside = dot(flip, sums[side].astype(BF16))
                wide = jnp.concatenate([upside, jnp.zeros((length, length), F32)], axis=1)
                turned = pltpu.roll(wide, 0, 1, stride=1, stride_axis=0)
                diag_ref[pl.ds(2 * pair + side, 1), :] = jnp.sum(turned, axis=0, keepdims=True)


def attend_call(kernel, info, bias, q, kv, blocks, more, out_shape, length, name):
    rows = q.shape[0]
    seqs = rows // length
    width = more[0].shape[1] if more else out_shape[0].shape[1]
    lead = [] if bias is None else [bias]
    whole = [pl.BlockSpec(a.shape, lambda i: (0, 0)) for a in lead]
    picked = [pl.BlockSpec((rows, width), lambda i, b=b: (0, b)) for b in blocks]
    rest = [pl.BlockSpec(a.shape, lambda i: (0, 0)) for a in more]
    return pl.pallas_call(
        functools.partial(kernel, bias is not None),
        grid=(1,),
        in_specs=[pl.BlockSpec(memory_space=pltpu.SMEM)] + whole + picked + rest,
        out_specs=[pl.BlockSpec(o.shape, lambda i: (0, 0)) for o in out_shape],
        out_shape=out_shape,
        scratch_shapes=[pltpu.VMEM((seqs, length, length), F32)],
        compiler_params=pltpu.CompilerParams(vmem_limit_bytes=40 << 20),
        name=name,
    )(info, *lead, q, kv, kv, *more)


def attend(info, bias, q, kv, blocks, length, width):
    rows = q.shape[0]
    out_shape = [
        jax.ShapeDtypeStruct((rows, width), BF16),
        jax.ShapeDtypeStruct((rows, width), F32),
    ]
    return attend_call(attend_kernel, info, bias, q, kv, blocks, [], out_shape, length, "attend")


def attend_back(info, bias, q, kv, blocks, saved, grad, length, width):
    rows = q.shape[0]
    widths = (width, 2 * width) if bias is None else (3 * width,)
    out_shape = [jax.ShapeDtypeStruct((rows, w), BF16) for w in widths]
    if bias is not None:
        out_shape.append(jax.ShapeDtypeStruct(bias.shape, F32))
    more = [*saved, grad]
    return attend_call(attend_back_kernel, info, bias, q, kv, blocks, more, out_shape, length, "attend_back")


def norm_parts(values, gain):
    scale = lax.rsqrt(jnp.mean(values * values, axis=-1, keepdims=True) + EPS)
    return values * scale * gain, scale


def norm_back(values, scale, gain, grad):
    unit = values * scale
    gain_grad = jnp.sum(grad * unit, axis=0)
    pushed = grad * gain
    back = scale * (pushed - unit * jnp.mean(pushed * unit, axis=-1, keepdims=True))
    return back, gain_grad


def gelu_parts(gate):
    c = 0.7978845608028654
    inner = c * (gate + 0.044715 * gate * gate * gate)
    t = jnp.tanh(inner)
    value = 0.5 * gate * (1.0 + t)
    slope = 0.5 * (1.0 + t) + 0.5 * gate * (1.0 - t * t) * c * (1.0 + 3.0 * 0.044715 * gate * gate)
    return value, slope


def moe_forward(send, w_in, w_down, turn, kept_from):
    experts, rows, width = send.shape
    arrived = lax.all_to_all(send, "expert", split_axis=0, concat_axis=0, tiled=True)
    flat = arrived.reshape(-1, width)
    value, _ = gelu_parts(dot(flat, w_in[0]))
    hidden = (value * dot(flat, w_in[1])).astype(BF16)
    result = dot(hidden, w_down).astype(BF16).reshape(send.shape)
    back = lax.all_to_all(result, "expert", split_axis=0, concat_axis=0, tiled=True)
    if kept_from is None:
        return back, arrived
    mine = lax.axis_index("half") == turn
    return jnp.where(mine, back, kept_from[0]), jnp.where(mine, arrived, kept_from[1])


def flipped(value, bit):
    step = 1 << bit
    return value + step * (1 - 2 * (value // step % 2))


def crossed(value, other):
    for bit in range(other.bit_length()):
        if other >> bit & 1:
            value = flipped(value, bit)
    return value


def greet(partners):
    barrier = pltpu.get_barrier_semaphore()
    for partner in partners:
        pl.semaphore_signal(barrier, inc=1, device_id=partner, device_id_type=MESH)
    pl.semaphore_wait(barrier, len(partners))


def remote(src, dst, out_sem, in_sem, device):
    return pltpu.make_async_remote_copy(
        src_ref=src,
        dst_ref=dst,
        send_sem=out_sem,
        recv_sem=in_sem,
        device_id=device,
        device_id_type=MESH,
    )


def tile_loop(count, step, body):
    @pl.loop(0, count // step)
    def _(i):
        body(pl.multiple_of(i * step, step), step)

    if count % step:
        body(count // step * step, count % step)


def groups_of(experts, block):
    size = 1
    while size * 2 * block <= 320 and size * 2 <= experts:
        size *= 2
    if experts <= 2 * size:
        half = max(size // 2, 1)
        return [(0, size), *((k, half) for k in range(size, experts, half))]
    return [(k, size) for k in range(0, experts, size)]


class Turn:
    def __init__(self, experts, block, there, home):
        self.me, self.dp = lax.axis_index("expert"), lax.axis_index("dp")
        self.experts, self.block = experts, block
        self.peer = {"dp": 1 - self.dp}
        self.groups = groups_of(experts, block)
        self.there_refs, self.home_refs = there, home

    def greet(self):
        greet([{"expert": crossed(self.me, k)} for k in range(1, self.experts)] + [self.peer])

    def there(self, k):
        src, dst, out_sems, in_sems = self.there_refs
        partner = crossed(self.me, k)
        return remote(src.at[partner], dst.at[self.me], out_sems.at[k], in_sems.at[k], {"expert": partner})

    def home(self, k):
        src, dst, out_sems, in_sems = self.home_refs
        partner = crossed(self.me, k)
        return remote(src.at[partner], dst.at[self.me], out_sems.at[k], in_sems.at[k], {"expert": partner})

    def arrive(self, first, size):
        for k in range(max(first, 1), first + size):
            self.there(k).wait_recv()

    def base(self, first, size):
        return crossed(self.me // size, first // size) * size

    def spans(self, first, size):
        base = self.base(first, size)
        rows = pl.ds(pl.multiple_of(base * self.block, size * self.block), size * self.block)
        return pl.ds(base, size), rows


class Lefts:
    def __init__(self, refs, out, scratch, width):
        self.refs, self.out = refs, out
        self.held, self.stage, self.loaded, self.sent, self.came = scratch
        self.half = width // 2
        self.dp = lax.axis_index("dp")

    def fetch(self, i):
        return pltpu.make_async_copy(self.refs[i], self.held.at[i % 2], self.loaded.at[i])

    def copy(self, i):
        return remote(self.stage.at[i], self.out.at[i], self.sent.at[i], self.came.at[i], {"dp": 1 - self.dp})

    def load(self):
        for i in range(2):
            self.fetch(i).start()

    def send(self):
        for i in range(4):
            self.fetch(i).wait()
            cols = pl.ds(pl.multiple_of((1 - self.dp) * self.half, 128), self.half)
            self.stage[i] = self.held[i % 2, :, cols]
            self.copy(i).start()
            if i + 2 < 4:
                self.fetch(i + 2).start()

    def wait(self):
        for i in range(4):
            self.copy(i).wait()


def transpose_kernel_part(loads, tall, wide, wsem, tsem):
    copies = [pltpu.make_async_copy(src, dst, wsem.at[i]) for i, (src, dst, _) in enumerate(loads)]
    for copy in copies:
        copy.start()
    for i, (_, held, out) in enumerate(loads):
        slab = tall.shape[1]
        stages = [tall.at[i] if out.shape[1] == tall.shape[2] else wide.at[pl.ds(i * slab, slab)] for i in range(2)]
        steps = out.shape[0] // slab
        copies[i].wait()

        def put(t, slot, stages=stages, out=out, slab=slab):
            rows = pl.ds(pl.multiple_of(t * slab, slab), slab)
            return pltpu.make_async_copy(stages[slot], out.at[rows], tsem.at[slot])

        def step(pair, carry, stages=stages, held=held, put=put, slab=slab, steps=steps):
            for slot in range(2):
                t = 2 * pair + slot

                @pl.when(t < steps)
                def _(t=t, slot=slot):
                    @pl.when(pair > 0)
                    def _():
                        put(t - 2, slot).wait()

                    cols = pl.ds(pl.multiple_of(t * slab, slab), slab)
                    stages[slot][...] = jnp.transpose(held[:, cols])
                    put(t, slot).start()

            return carry

        lax.fori_loop(0, pl.cdiv(steps, 2), step, 0)
        for t in (steps - 2, steps - 1):
            put(t, t % 2).wait()


def expert_forward_kernel(turn, has_prev, *refs):
    send_ref, w_in, w_down = refs[:3]
    left_refs, refs = refs[3 + 10 * has_prev : 3 + 14 * has_prev], refs[3 + 14 * has_prev :]
    back_out, rows_out, slope_out, value_out, hidden_out, slope_peer_out, value_peer_out = refs[:7]
    wgt_out, wut_out, wdt_out = refs[7:10]
    left_out, refs = refs[10 : 10 + has_prev], refs[10 + has_prev :]
    wg, wu, wd, rows, back, made, rows_peer, slopes, values, hidden = refs[:10]
    slopes_peer, values_peer, tall = refs[10:13]
    wsem, s1, r1, s2, r2, sx, rx, osem, tsem = refs[13:22]
    experts, block, width = send_ref.shape
    ff = wd.shape[0]
    span = ff // 2
    lefts = Lefts(left_refs, left_out[0], (tall, *refs[22:]), width) if has_prev else None

    @pl.when(lax.axis_index("half") != turn)
    def _():
        if lefts:
            lefts.load()
            greet([{"dp": 1 - lax.axis_index("dp")}])
            lefts.send()
        loads = ((w_in.at[0], wg, wgt_out), (w_in.at[1], wu, wut_out), (w_down, wd, wdt_out))
        transpose_kernel_part(loads, tall, slopes, wsem, tsem)
        if lefts:
            lefts.wait()

    @pl.when(lax.axis_index("half") == turn)
    def _():
        t = Turn(experts, block, (send_ref, rows, s1, r1), (made, back, s2, r2))
        t.greet()

        def rows_over(part):
            blocks, _ = t.spans(*t.groups[part])
            return remote(rows.at[blocks], rows_peer.at[blocks], sx.at[part], rx.at[part], t.peer)

        for k in range(1, experts):
            t.there(k).start()
        rows[t.me] = send_ref[t.me]
        loads = [
            pltpu.make_async_copy(src, dst, wsem.at[i])
            for i, (src, dst) in enumerate(((w_in.at[0], wg), (w_in.at[1], wu), (w_down, wd)))
        ]
        for load in loads:
            load.start()
        if lefts:
            lefts.load()
        for part, (first, size) in enumerate(t.groups):
            t.arrive(first, size)
            rows_over(part).start()
            blocks, span_rows = t.spans(first, size)
            if part == 0:
                loads[0].wait()
                loads[1].wait()

            def up_tile(start, count, blocks=blocks, span_rows=span_rows, size=size):
                x = rows[blocks].reshape(size * block, width)
                cols = pl.ds(start, count)
                value, slope = gelu_parts(dot(x, wg[:, cols]))
                up = dot(x, wu[:, cols])
                hidden[span_rows, cols] = (value * up).astype(BF16)
                values[span_rows, cols] = value.astype(BF16)
                slopes[span_rows, cols] = (up * slope).astype(BF16)

            tile_loop(ff, 512, up_tile)
            if part == 0:
                loads[2].wait()

            def down_tile(start, count, blocks=blocks, span_rows=span_rows, size=size):
                cols = pl.ds(start, count)
                y = dot(hidden[span_rows, :], wd[:, cols]).astype(BF16)
                made[blocks, :, cols] = y.reshape(size, block, count)

            tile_loop(width, 512, down_tile)
            for k in range(max(first, 1), first + size):
                t.home(k).start()
        back[t.me] = made[t.me]
        half_cols = pl.ds(pl.multiple_of(t.dp * span, 128), span)
        other_cols = pl.ds(pl.multiple_of((1 - t.dp) * span, 128), span)
        outs = [
            (slopes, slope_out),
            (values, value_out),
            (hidden.at[:, half_cols], hidden_out.at[0]),
            (rows, rows_out.at[0]),
        ]
        outs = [pltpu.make_async_copy(src, dst, osem.at[i]) for i, (src, dst) in enumerate(outs)]
        for out in outs:
            out.start()
        if lefts:
            lefts.send()

        for part in range(len(t.groups)):
            rows_over(part).wait_recv()

        def peer_tile(start, count):
            x = rows_peer[...].reshape(experts * block, width)
            here = pl.ds(start, count)
            cols = pl.ds(pl.multiple_of(t.dp * span + start, 128), count)
            value, slope = gelu_parts(dot(x, wg[:, cols]))
            up = dot(x, wu[:, cols])
            hidden[:, pl.ds(pl.multiple_of((1 - t.dp) * span + start, 128), count)] = (value * up).astype(BF16)
            values_peer[:, here] = value.astype(BF16)
            slopes_peer[:, here] = (up * slope).astype(BF16)

        tile_loop(span, 512, peer_tile)
        more = [
            (slopes_peer, slope_peer_out),
            (values_peer, value_peer_out),
            (hidden.at[:, other_cols], hidden_out.at[1]),
            (rows_peer, rows_out.at[1]),
        ]
        more = [pltpu.make_async_copy(src, dst, osem.at[4 + i]) for i, (src, dst) in enumerate(more)]
        for out in more:
            out.start()
        for k in range(1, experts):
            t.home(k).wait_recv()
        back_copy = pltpu.make_async_copy(back, back_out, osem.at[8])
        back_copy.start()
        for k in range(1, experts):
            t.there(k).wait_send()
            t.home(k).wait_send()
        for part in range(len(t.groups)):
            rows_over(part).wait_send()
        if lefts:
            lefts.wait()
        for out in [*outs, *more, back_copy]:
            out.wait()


def expert_backward_kernel(turn, has_prev, *refs):
    send_ref = refs[0]
    sources = refs[1:8]
    refs = refs[8 + 3 * has_prev :]
    back_out, mixed_out, grad_out = refs[:3]
    wdt, dgate, dup, wgt, wut, dgate_peer, dup_peer = refs[3:10]
    grads, back, made, grads_peer = refs[10:14]
    wsem, s1, r1, s2, r2, sx, rx, osem = refs[14:]
    experts, block, width = send_ref.shape
    ff = wdt.shape[1]
    span = ff // 2
    dp = lax.axis_index("dp")
    t = Turn(experts, block, (send_ref, grads, s1, r1), (made, back, s2, r2))

    @pl.when(lax.axis_index("half") == turn)
    def _():
        t.greet()

        def grads_over(part):
            blocks, _ = t.spans(*t.groups[part])
            return remote(grads.at[blocks], grads_peer.at[blocks], sx.at[part], rx.at[part], t.peer)

        for k in range(1, experts):
            t.there(k).start()
        grads[t.me] = send_ref[t.me]
        held = (wdt, dgate, dup, wgt, wut, dgate_peer, dup_peer)
        loads = [pltpu.make_async_copy(src, dst, wsem.at[i]) for i, (src, dst) in enumerate(zip(sources, held))]
        for load in loads:
            load.start()
        for load in loads[:3]:
            load.wait()
        for part, (first, size) in enumerate(t.groups):
            t.arrive(first, size)
            grads_over(part).start()
            blocks, span_rows = t.spans(first, size)

            def hidden_tile(start, count, blocks=blocks, span_rows=span_rows, size=size):
                dy = grads[blocks].reshape(size * block, width)
                cols = pl.ds(start, count)
                dhidden = dot(dy, wdt[:, cols])
                dgate[span_rows, cols] = (dhidden * dgate[span_rows, cols].astype(F32)).astype(BF16)
                dup[span_rows, cols] = (dhidden * dup[span_rows, cols].astype(F32)).astype(BF16)

            tile_loop(ff, 512, hidden_tile)
            if part == 0:
                loads[3].wait()
                loads[4].wait()

            def rows_tile(start, count, blocks=blocks, span_rows=span_rows, size=size):
                cols = pl.ds(start, count)
                dr = dot(dgate[span_rows, :], wgt[:, cols]) + dot(dup[span_rows, :], wut[:, cols])
                made[blocks, :, cols] = dr.astype(BF16).reshape(size, block, count)

            tile_loop(width, 512, rows_tile)
            for k in range(max(first, 1), first + size):
                t.home(k).start()
        back[t.me] = made[t.me]
        half_cols = pl.ds(pl.multiple_of(dp * span, 128), span)
        outs = [
            (dgate.at[:, half_cols], mixed_out.at[0, 0]),
            (dup.at[:, half_cols], mixed_out.at[1, 0]),
            (grads, grad_out.at[0]),
        ]
        outs = [pltpu.make_async_copy(src, dst, osem.at[i]) for i, (src, dst) in enumerate(outs)]
        for out in outs:
            out.start()

        for load in loads[5:]:
            load.wait()
        for part in range(len(t.groups)):
            grads_over(part).wait_recv()

        def peer_tile(start, count):
            dy = grads_peer[...].reshape(experts * block, width)
            here = pl.ds(start, count)
            dhidden = dot(dy, wdt[:, pl.ds(pl.multiple_of(dp * span + start, 128), count)])
            dgate_peer[:, here] = (dhidden * dgate_peer[:, here].astype(F32)).astype(BF16)
            dup_peer[:, here] = (dhidden * dup_peer[:, here].astype(F32)).astype(BF16)

        tile_loop(span, 512, peer_tile)
        more = [
            (dgate_peer, mixed_out.at[0, 1]),
            (dup_peer, mixed_out.at[1, 1]),
            (grads_peer, grad_out.at[1]),
        ]
        more = [pltpu.make_async_copy(src, dst, osem.at[3 + i]) for i, (src, dst) in enumerate(more)]
        for out in more:
            out.start()
        for k in range(1, experts):
            t.home(k).wait_recv()
        back_copy = pltpu.make_async_copy(back, back_out, osem.at[6])
        back_copy.start()
        for k in range(1, experts):
            t.there(k).wait_send()
            t.home(k).wait_send()
        for part in range(len(t.groups)):
            grads_over(part).wait_send()
        for out in [*outs, *more, back_copy]:
            out.wait()


def expert_call(kernel, number, turn, send, sources, prev, more, out_shape, scratch, name):
    vmem, hbm = pl.BlockSpec(memory_space=pltpu.VMEM), pl.BlockSpec(memory_space=pl.ANY)
    prev = list(prev or [])
    return pl.pallas_call(
        functools.partial(kernel, turn, bool(prev)),
        in_specs=[vmem] + [hbm] * (len(sources) + len(prev) + len(more)),
        out_specs=[hbm] * len(out_shape),
        out_shape=out_shape,
        input_output_aliases={1 + len(sources) + i: i for i in range(len(prev))},
        scratch_shapes=scratch,
        compiler_params=pltpu.CompilerParams(
            collective_id=number, has_side_effects=True, vmem_limit_bytes=60 << 20
        ),
        name=name,
    )(send, *sources, *prev, *more)


def moe_forward(send, w_in, w_down, turn, prev, lefts, slab):
    experts, block, width = send.shape
    ff = w_down.shape[0]
    total = experts * block
    parts = len(groups_of(experts, block))
    dma = pltpu.SemaphoreType.DMA
    scratch = [
        pltpu.VMEM((width, ff), BF16),
        pltpu.VMEM((width, ff), BF16),
        pltpu.VMEM((ff, width), BF16),
        *[pltpu.VMEM(send.shape, BF16)] * 4,
        *[pltpu.VMEM((total, ff), BF16)] * 3,
        *[pltpu.VMEM((total, ff // 2), BF16)] * 2,
        pltpu.VMEM((2, slab, width), BF16),
        dma((3,)),
        *[dma((experts,))] * 4,
        *[dma((parts,))] * 2,
        dma((9,)),
        dma((2,)),
    ]
    shapes = [
        send.shape,
        (2, *send.shape),
        (total, ff),
        (total, ff),
        (2, total, ff // 2),
        (total, ff // 2),
        (total, ff // 2),
        (ff, width),
        (ff, width),
        (width, ff),
    ]
    if lefts:
        rows = lefts[0].shape[0]
        shapes.append((4, rows, width // 2))
        scratch += [pltpu.VMEM((4, rows, width // 2), BF16), *[dma((4,))] * 3]
    out_shape = [jax.ShapeDtypeStruct(shape, BF16) for shape in shapes]
    return expert_call(
        expert_forward_kernel, 1 + turn, turn, send, [w_in, w_down], prev, lefts, out_shape, scratch, "moe_forward"
    )


def moe_backward(grad_send, saved, turn, prev):
    experts, block, width = grad_send.shape
    _, _, slope, value, _, slope_peer, value_peer, wgt, wut, wdt, _ = saved
    total, ff = slope.shape
    parts = len(groups_of(experts, block))
    dma = pltpu.SemaphoreType.DMA
    scratch = [
        pltpu.VMEM((width, ff), BF16),
        *[pltpu.VMEM((total, ff), BF16)] * 2,
        *[pltpu.VMEM((ff, width), BF16)] * 2,
        *[pltpu.VMEM((total, ff // 2), BF16)] * 2,
        *[pltpu.VMEM(grad_send.shape, BF16)] * 4,
        dma((7,)),
        *[dma((experts,))] * 4,
        *[dma((parts,))] * 2,
        dma((7,)),
    ]
    out_shape = [
        jax.ShapeDtypeStruct(grad_send.shape, BF16),
        jax.ShapeDtypeStruct((2, 2, total, ff // 2), BF16),
        jax.ShapeDtypeStruct((2, *grad_send.shape), BF16),
    ]
    return expert_call(
        expert_backward_kernel,
        3 + turn,
        turn,
        grad_send,
        [wdt, slope, value, wgt, wut, slope_peer, value_peer],
        prev,
        [],
        out_shape,
        scratch,
        "moe_backward",
    )


def dense_kernel(stages, chunk, lag, *refs):
    sources, small_ref = refs[:11], refs[11]
    out_refs, small_out, small_in = refs[12:15], refs[15], refs[16]
    held, xt_ref, refs = refs[17:28], refs[28], refs[29:]
    x_refs, own_refs, peer_refs, xp = held[:4], held[4:7], held[7:10], held[10]
    sums, parts = refs[:stages], refs[stages : 2 * stages]
    ss, rs, sk, rk, sl = refs[2 * stages :]
    counts = [ref.shape[1] // chunk for ref in own_refs]
    starts = [sum(counts[:i]) for i in range(3)]
    chunks = sum(counts)
    per_cross = counts[2] // 2
    rows, half = xp.shape[1:]
    dp, me = lax.axis_index("dp"), lax.axis_index("expert")
    peer = {"dp": 1 - dp}
    partners = [flipped(me, k) for k in range(stages)]
    bits = [me // (1 << k) % 2 for k in range(stages)]
    load = [pltpu.make_async_copy(sources[i], held[i], sl.at[i]) for i in range(11)]
    for i in (10, 2, 3, 6, 9, 0, 4, 7, 1, 5, 8):
        load[i].start()
    greet([peer] + [{"expert": p} for p in partners])

    def send_small(step):
        src = small_ref if step == 0 else small_out.at[step - 1]
        device = peer if step == 0 else {"expert": partners[stages - step]}
        return remote(src, small_in.at[step], ss.at[step], rs.at[step], device)

    def order(k, odd):
        return 1 - k if odd and k < 2 else k

    def send_part(k, c, odd):
        bit = order(k, odd)
        other = 1 - bits[bit]
        src = sums[0].at[c, :, :, other] if k == 0 and not odd else sums[k].at[c, :, other]
        return remote(src, parts[k].at[c], sk.at[k, c], rk.at[k, c], {"expert": partners[bit]})

    def turn_x(g):
        load[g].wait()
        cols = pl.ds(pl.multiple_of(dp * half, half), half)
        xt_ref[g, :, :rows] = jnp.transpose(x_refs[g][:, cols])
        xt_ref[g, :, rows:] = jnp.transpose(xp[g])

    def small_step(j):
        send_small(j).wait_recv()
        own = small_ref[...] if j == 0 else small_out[j - 1]
        small_out[j] = own + small_in[j]
        if j < stages:
            send_small(j + 1).start()

    send_small(0).start()
    load[10].wait()
    last = counts[2]
    early = chunks - last
    per = chunks // last

    def produce(i, carry):
        c = jnp.where(lax.rem(i, per) == 0, early + i // per, i - i // per - 1)
        for g in range(3):

            @pl.when(c == starts[g])
            def _(g=g):
                load[4 + g].wait()
                load[7 + g].wait()
                for x in (g,) if g < 2 else (2, 3):
                    turn_x(x)

            @pl.when((c >= starts[g]) & (c < starts[g] + counts[g]))
            def _(g=g):
                at = c - starts[g]
                cols = pl.ds(pl.multiple_of(at * chunk, chunk), chunk)
                which = g if g < 2 else 2 + at // per_cross
                total = dot(xt_ref[which, :, :rows], own_refs[g][:, cols])
                total += dot(xt_ref[which, :, rows:], peer_refs[g][:, cols])
                sums[0][c] = total.astype(BF16).reshape(sums[0].shape[1:])
                send_part(0, c, g == 2).start()

        for j in range(2):

            @pl.when(i == 3 + 6 * j)
            def _(j=j):
                small_step(j)

        return carry

    lax.fori_loop(0, chunks, produce, 0)

    def advance(k, c, odd):
        send_part(k, c, odd).wait_recv()
        bit = bits[order(k, odd)]
        mine = sums[0][c, :, :, bit] if k == 0 and not odd else sums[k][c, :, bit]
        total = mine.astype(F32) + parts[k][c].astype(F32)
        if k + 1 < stages:
            sums[k + 1][c] = total.astype(BF16).reshape(sums[k + 1].shape[1:])
            send_part(k + 1, c, odd).start()
            return
        total = total.reshape(total.shape[-2:])
        for g in (2,) if odd else (0, 1):

            @pl.when((c >= starts[g]) & (c < starts[g] + counts[g]))
            def _(g=g):
                at = pl.multiple_of((c - starts[g]) * chunk, chunk)
                out_refs[g][:, pl.ds(at, chunk)] = total

    def reduce(i, carry):
        @pl.when((lax.rem(i, 2) == 1) & (i // 2 < last))
        def _():
            advance(0, early + i // 2, True)

        for k in range(stages):
            c = i - lag * k

            @pl.when((c >= 0) & (c < early))
            def _(k=k, c=c):
                advance(k, c, False)

        for k in range(1, stages):
            c = i - 1 - lag * (k - 1)

            @pl.when((c >= early) & (c < chunks))
            def _(k=k, c=c):
                advance(k, c, True)

        for j in range(2, stages + 1):

            @pl.when(i == 3 * j - 2)
            def _(j=j):
                small_step(j)

        return carry

    lax.fori_loop(0, chunks + 1 + lag * (stages - 2), reduce, 0)

    def finish(c, carry, odd):
        for k in range(stages):
            send_part(k, c, odd).wait_send()
        return carry

    lax.fori_loop(0, early, functools.partial(finish, odd=False), 0)
    lax.fori_loop(early, chunks, functools.partial(finish, odd=True), 0)
    for j in range(stages + 1):
        send_small(j).wait_send()


def over_dp(array):
    return lax.ppermute(array, "dp", [(0, 1), (1, 0)])


def dense_gradients(lefts, lefts_peer, own, peer, small, experts):
    chunk = 512
    rows, width = lefts[0].shape
    half_rows = width // 2
    chunks = sum(y.shape[1] for y in own) // chunk
    stages = experts.bit_length() - 1
    keep = half_rows // experts
    vmem, hbm = pl.BlockSpec(memory_space=pltpu.VMEM), pl.BlockSpec(memory_space=pl.ANY)
    dma = pltpu.SemaphoreType.DMA
    sources = [*lefts, *own, *peer, lefts_peer]
    blocks = [(experts // 4, 2, 2)] + [(experts >> (k + 1), 2) for k in range(1, stages)]
    halved = [(experts // 4, 2)] + [(experts >> (k + 1),) for k in range(1, stages)]
    scratch = [pltpu.VMEM((stages + 1, *small.shape), F32)]
    scratch += [pltpu.VMEM(a.shape, BF16) for a in sources]
    scratch += [pltpu.VMEM((4, half_rows, 2 * rows), BF16)]
    scratch += [pltpu.VMEM((chunks, *b, keep, chunk), BF16) for b in blocks + halved]
    scratch += [dma((stages + 1,)), dma((stages + 1,)), dma((stages, chunks)), dma((stages, chunks))]
    scratch += [dma((len(sources),))]
    *outs, sums = pl.pallas_call(
        functools.partial(dense_kernel, stages, chunk, 2),
        in_specs=[hbm] * len(sources) + [vmem],
        out_specs=[vmem] * 4,
        out_shape=[
            *(jax.ShapeDtypeStruct((keep, y.shape[1]), F32) for y in own),
            jax.ShapeDtypeStruct((stages + 1, *small.shape), F32),
        ],
        scratch_shapes=scratch,
        compiler_params=pltpu.CompilerParams(
            collective_id=0, has_side_effects=True, vmem_limit_bytes=56 << 20
        ),
        name="dense_gradients",
    )(*sources, small)
    return outs, sums[stages]


def product_kernel(x_ref, y_ref, out_ref):
    out_ref[...] = dot(x_ref[...], y_ref[...].reshape(y_ref.shape[-2:]), TN).reshape(out_ref.shape)


def expert_gradients(rows, mixed, hidden, grads):
    total, width = rows.shape
    span = hidden.shape[1]
    tile = 256
    params = pltpu.CompilerParams(vmem_limit_bytes=40 << 20)
    din = pl.pallas_call(
        product_kernel,
        grid=(2, width // tile),
        in_specs=[
            pl.BlockSpec((total, tile), lambda g, i: (0, i)),
            pl.BlockSpec((1, total, span), lambda g, i: (g, 0, 0)),
        ],
        out_specs=pl.BlockSpec((1, tile, span), lambda g, i: (g, i, 0)),
        out_shape=jax.ShapeDtypeStruct((2, width, span), F32),
        compiler_params=params,
        name="expert_in_gradient",
    )(rows, mixed)
    ddown = pl.pallas_call(
        product_kernel,
        grid=(pl.cdiv(span, tile),),
        in_specs=[
            pl.BlockSpec((total, tile), lambda i: (0, i)),
            pl.BlockSpec((total, width), lambda i: (0, 0)),
        ],
        out_specs=pl.BlockSpec((tile, width), lambda i: (i, 0)),
        out_shape=jax.ShapeDtypeStruct((span, width), F32),
        compiler_params=params,
        name="expert_out_gradient",
    )(hidden, grads)
    return din, ddown


def body(
    tokens,
    cotangent,
    lengths,
    routes,
    self_qkv,
    self_out,
    cross_weights,
    router,
    gains,
    bias_table,
    expert_in,
    expert_out,
):
    _, seqs, length, width = tokens.shape
    heads = H
    experts = router.shape[2]
    top = routes.shape[3]
    capacity = (5 * top * length + 4 * experts - 1) // (4 * experts)
    block_rows = -(-seqs * capacity // 16) * 16
    rows = seqs * length
    slots = experts * block_rows
    half_index = lax.axis_index("half")
    decoder = half_index == 1
    wqkv, wout, wcross, wrouter, gain = (
        self_qkv[0],
        self_out[0],
        cross_weights[0],
        router[0],
        gains[0],
    )
    w_in, w_down = expert_in[0, 0], expert_out[0, 0]

    column = np.arange(2 * length)
    entry = np.arange(BUCKETS * heads)
    hot, hot_back = (
        jnp.where(
            decoder,
            *(
                (entry[:, None] // heads == bucket[None, :]).astype(np.float32)
                for bucket in reversed(diagonal_buckets(diff))
            ),
        )
        for diff in (np.where(column < length, column, column - 2 * length), column - length + 1)
    )
    own_head = entry[None, :] % heads == np.arange(heads)[:, None]
    bias = lax.dot_general(
        jnp.where(own_head, bias_table, 0.0),
        hot,
        (((1,), (0,)), ((), ())),
        precision=lax.Precision.HIGHEST,
        preferred_element_type=F32,
    )
    own_lengths = jnp.where(decoder, lengths[1], lengths[0])
    self_info = jnp.concatenate([own_lengths, half_index[None]]).astype(jnp.int32)
    cross_info = jnp.concatenate([lengths[0], jnp.zeros((1,), jnp.int32)]).astype(jnp.int32)

    order = jnp.transpose(routes[0], (0, 2, 1)).reshape(seqs, top * length)
    expert_ids = jnp.arange(experts, dtype=jnp.int32)
    picked = (order[:, :, None] == expert_ids).astype(BF16)
    earlier = np.tril(np.ones((top * length, top * length), np.float32), -1).astype(BF16)
    before = jnp.einsum("pq,sqe->spe", earlier, picked, preferred_element_type=F32)
    place = jnp.sum(before * picked.astype(F32), axis=2).astype(jnp.int32)
    kept = place < capacity
    base = order * block_rows + jnp.arange(seqs, dtype=jnp.int32)[:, None] * capacity
    target = jnp.where(kept, base + place, -1).reshape(seqs, top, length)
    target = jnp.transpose(target, (1, 0, 2)).reshape(top, rows)
    slot_ids = jnp.arange(slots, dtype=jnp.int32)
    spots = (target[:, :, None] == slot_ids).astype(BF16)
    both = jnp.sum(spots.astype(F32), axis=0).astype(BF16)
    stacked = spots.reshape(top * rows, slots)
    kept_hot = picked.astype(F32) * kept[:, :, None].astype(F32)
    kept_count = jnp.sum(kept_hot, axis=(0, 1))
    all_count = jnp.sum(picked.astype(F32), axis=(0, 1))
    tallies = jnp.concatenate([kept_count, all_count - kept_count])
    route_hot = (routes[0].reshape(rows, top, 1) == expert_ids).astype(F32)

    def route(values):
        normed, scale = norm_parts(values, gain[1])
        low = normed.astype(BF16)
        rest = (normed - low.astype(F32)).astype(BF16)
        logits = dot(low, wrouter) + dot(rest, wrouter)
        probs = jax.nn.softmax(logits, axis=-1)
        chosen = jnp.sum(probs[:, None, :] * route_hot, axis=-1)
        total = jnp.sum(chosen, axis=-1, keepdims=True)
        gates = chosen / total
        send = dot(both, low, TN).astype(BF16).reshape(experts, block_rows, width)
        return dict(scale=scale, low=low, probs=probs, gates=gates, total=total, send=send)

    def fetch(returned):
        flat = returned.reshape(slots, width)
        return dot(stacked, flat).reshape(top, rows, width)

    def combine(values, gates, results):
        return values + jnp.sum(jnp.transpose(gates)[:, :, None] * results, axis=0)

    values = tokens[0].reshape(rows, width).astype(F32)
    normed, scale0 = norm_parts(values, gain[0])
    low0 = normed.astype(BF16)
    qkv = dot(low0, wqkv).astype(BF16)
    mixed0, log0 = attend(self_info, bias, qkv, qkv, (0, 1, 2), length, width)
    first = values + dot(mixed0, wout)

    state = route(first)
    saved = moe_forward(state["send"], w_in, w_down, 0, None, [], rows)
    final_enc = combine(first, state["gates"], fetch(saved[0]))
    normed, scale_m = norm_parts(final_enc, gain[2])
    low_m = normed.astype(BF16)
    memory = dot(low_m, wcross).astype(BF16)
    names = ("half", "dp", "expert")
    forward_pairs, back_pairs = half_pairs(lax.axis_size("dp") * lax.axis_size("expert"))
    memory = lax.ppermute(memory, names, forward_pairs)

    normed, scale_c = norm_parts(first, gain[2])
    low_c = normed.astype(BF16)
    query = dot(low_c, wcross[:, :width]).astype(BF16)
    mixed_c, log_c = attend(cross_info, None, query, memory, (0, 0, 1), length, width)
    second = jnp.where(decoder, first + dot(mixed_c, wcross[:, width:]), first)

    state = route(second)
    lefts = [low0, mixed0, jnp.where(decoder, low_c, low_m), jnp.where(decoder, mixed_c, low_m)]
    saved = moe_forward(state["send"], w_in, w_down, 1, saved, lefts, rows)
    results = fetch(saved[0])
    final = combine(second, state["gates"], results)
    outputs = final.astype(BF16)

    def moe_gradient(grad):
        dgates = jnp.transpose(jnp.sum(grad[None] * results, axis=-1))
        spread = (jnp.transpose(state["gates"])[:, :, None] * grad[None]).astype(BF16)
        send = dot(stacked, spread.reshape(top * rows, width), TN)
        return dgates, send.astype(BF16).reshape(experts, block_rows, width)

    def moe_input_gradient(grad, dgates, back):
        gates, total, probs = state["gates"], state["total"], state["probs"]
        dchosen = (dgates - jnp.sum(dgates * gates, axis=-1, keepdims=True)) / total
        dprobs = jnp.sum(dchosen[:, :, None] * route_hot, axis=1)
        dlogits = probs * (dprobs - jnp.sum(dprobs * probs, axis=-1, keepdims=True))
        dnormed = dot(both, back.reshape(slots, width)) + lax.dot_general(
            dlogits, wrouter.astype(F32), NT, preferred_element_type=F32
        )
        dvalues, dgain = norm_back(second, state["scale"], gain[1], dnormed)
        normed = second * state["scale"] * gain[1]
        drouter = lax.dot_general(
            normed, dlogits, TN, precision=lax.Precision.HIGHEST, preferred_element_type=F32
        )
        return grad + dvalues, dgain, drouter

    grad_dec = cotangent[0].reshape(rows, width).astype(F32)
    dgates, grad_send = moe_gradient(grad_dec)
    kept_from = moe_backward(grad_send, saved, 1, None)
    grad_second, _, _ = moe_input_gradient(grad_dec, dgates, kept_from[0])

    dbranch_c = grad_second.astype(BF16)
    dmixed_c = dot(dbranch_c, wcross[:, width:], NT).astype(BF16)
    dquery, dmemory = attend_back(
        cross_info, None, query, memory, (0, 0, 1), (mixed_c, log_c), dmixed_c, length, width
    )
    dmemory = lax.ppermute(dmemory, names, back_pairs)
    dnormed = dot(dquery, wcross[:, :width], NT)
    dvalues, dgain_c = norm_back(first, scale_c, gain[2], dnormed)
    grad_first_dec = grad_second + dvalues

    dnormed = dot(dmemory, wcross, NT)
    dvalues, dgain_m = norm_back(final_enc, scale_m, gain[2], dnormed)
    grad = jnp.where(decoder, grad_dec, grad_dec + dvalues)
    dgates, grad_send = moe_gradient(grad)
    back, mixed_grads, all_grad = moe_backward(grad_send, saved, 0, kept_from)
    all_rows, hidden, lefts_peer = saved[1], saved[4], saved[10]
    grad_second, dgain_moe, drouter = moe_input_gradient(grad, dgates, back)
    grad_first = jnp.where(decoder, grad_first_dec, grad_second)

    dbranch = grad_first.astype(BF16)
    dmixed = dot(dbranch, wout, NT).astype(BF16)
    dqkv_rows, diag = attend_back(
        self_info, bias, qkv, qkv, (0, 1, 2), (mixed0, log0), dmixed, length, width
    )
    dnormed = dot(dqkv_rows, wqkv, NT)
    dvalues, dgain_self = norm_back(values, scale0, gain[0], dnormed)
    d_tokens = (grad_first + dvalues).astype(BF16)
    by_entry = lax.dot_general(
        diag, hot_back, NT, precision=lax.Precision.HIGHEST, preferred_element_type=F32
    )
    dtable = jnp.sum(jnp.where(own_head, by_entry, 0.0), axis=0)

    cross_grad = jnp.where(decoder, jnp.concatenate([dquery, dbranch_c], axis=1), dmemory)
    own_grads = (dqkv_rows, dbranch, cross_grad)
    peer_grads = tuple(map(over_dp, own_grads))
    places = 2 * experts
    own = width // places
    extra = jnp.concatenate([dtable.reshape(places, -1), tallies.reshape(places, 1)], axis=1)
    extra = jnp.pad(extra, ((0, 0), (0, -extra.shape[1] % own)))
    small = jnp.concatenate(
        [
            jnp.transpose(drouter),
            jnp.stack([dgain_self, dgain_moe, jnp.where(decoder, dgain_c, dgain_m)]),
            jnp.swapaxes(extra.reshape(places, -1, own), 0, 1).reshape(-1, width),
        ]
    )
    small = jnp.pad(small, ((0, -small.shape[0] % 8), (0, 0)))
    (dqkv, dout, dcross), small = dense_gradients(
        lefts, lefts_peer, own_grads, peer_grads, small, experts
    )
    place = lax.axis_index("dp") * experts + lax.axis_index("expert")
    mine = lax.dynamic_slice_in_dim(small, place * own, own, 1)
    tail = mine[experts + 3 :].reshape(-1)
    own_table = dtable.shape[0] // places
    d_table = tail[:own_table]
    counts = tail[own_table].astype(jnp.int32)

    ff_half = hidden.shape[-1]
    din, ddown = expert_gradients(
        all_rows.reshape(-1, width),
        mixed_grads.reshape(2, -1, ff_half),
        hidden.reshape(-1, ff_half),
        all_grad.reshape(-1, width),
    )
    return (
        outputs.reshape(1, seqs, length, width),
        d_tokens.reshape(1, seqs, length, width),
        dqkv[None],
        dout[None],
        dcross[None],
        jnp.transpose(mine[:experts])[None],
        mine[experts : experts + 3][None],
        d_table[None],
        din[None, None],
        ddown[None, None],
        counts.reshape(1, 1, 1),
    )


def half_pairs(count):
    return (
        [(i, count + i) for i in range(count)],
        [(count + i, i) for i in range(count)],
    )


def solution(mesh):
    placed = (
        P("half", ("dp", "expert"), None, None),
        P("half", ("dp", "expert"), None, None),
        P(None, ("dp", "expert")),
        P("half", ("dp", "expert"), None, None),
        P("half", None, None),
        P("half", None, None),
        P("half", None, None),
        P("half", None, None),
        P("half", None, None),
        P("half", None),
        P("half", "expert", None, None, None),
        P("half", "expert", None, None),
    )
    return jax.shard_map(
        body,
        mesh=mesh,
        in_specs=placed,
        out_specs=(
            P("half", ("dp", "expert"), None, None),
            P("half", ("dp", "expert"), None, None),
            P("half", ("dp", "expert"), None),
            P("half", ("dp", "expert"), None),
            P("half", ("dp", "expert"), None),
            P("half", ("dp", "expert"), None),
            P("half", None, ("dp", "expert")),
            P("half", ("dp", "expert")),
            P("half", "expert", None, None, "dp"),
            P("half", "expert", "dp", None),
            P("half", "dp", "expert"),
        ),
        check_vma=False,
    )
```

```python
import functools

import jax
import jax.numpy as jnp
import numpy as np
from jax import lax
from jax.experimental import pallas as pl
from jax.experimental.pallas import tpu as pltpu
from jax.sharding import PartitionSpec as P

H = 16
BUCKETS = 32
EPS = 1e-06
ENC_STEPS = (12, 16, 23, 32, 46, 64, 91)
DEC_STEPS = (19, 21, 24, 27, 31, 35, 40, 46, 52, 59, 67, 77, 87, 99, 113)
F32 = jnp.float32
BF16 = jnp.bfloat16
MESH = pl.DeviceIdType.MESH
NT = (((1,), (1,)), ((), ()))
TN = (((0,), (0,)), ((), ()))


def dot(a, b, dims=(((1,), (0,)), ((), ()))):
    return lax.dot_general(a, b, dims, preferred_element_type=F32)


def diagonal_buckets(diff):
    apart = np.abs(diff)
    coarse = 8 + sum((apart >= step).astype(np.int32) for step in ENC_STEPS)
    enc = np.where(apart < 8, apart, coarse) + 16 * (diff > 0)
    behind = np.maximum(-diff, 0)
    coarse = 16 + sum((behind >= step).astype(np.int32) for step in DEC_STEPS)
    dec = np.where(behind < 16, behind, coarse)
    return enc.astype(np.int32), dec.astype(np.int32)


def diagonals(bias_ref, head, length):
    row = jnp.broadcast_to(bias_ref[pl.ds(head, 1), :], (length, 2 * length))
    return pltpu.roll(row, 0, 1, stride=1, stride_axis=0)[:, :length]


def fill_masks(info, mask_ref):
    seqs, length, _ = mask_ref.shape
    row_id = lax.broadcasted_iota(jnp.int32, (length, length), 0)
    col_id = lax.broadcasted_iota(jnp.int32, (length, length), 1)
    reach = jnp.where(info[seqs] > 0, row_id, length)
    for seq in range(seqs):
        allowed = (col_id < info[seq]) & (col_id <= reach)
        mask_ref[seq] = jnp.where(allowed, 0.0, -1000000000.0)


def attend_kernel(has_bias, info, *refs):
    bias_ref, refs = (refs[0], refs[1:]) if has_bias else (None, refs)
    q_ref, k_ref, v_ref, out_ref, log_ref, mask_ref = refs
    seqs, length, _ = mask_ref.shape
    low = lax.broadcasted_iota(jnp.int32, (length, 128), 1) < 64
    fill_masks(info, mask_ref)

    @pl.loop(0, q_ref.shape[1] // 128, unroll=True)
    def _(pair):
        cols = pl.ds(pl.multiple_of(pair * 128, 128), 128)
        biases = [diagonals(bias_ref, 2 * pair + side, length) if has_bias else 0.0 for side in range(2)]
        for seq in range(seqs):
            rows = pl.ds(seq * length, length)
            q, k, v = q_ref[rows, cols] * 0.125, k_ref[rows, cols], v_ref[rows, cols]
            mixed, peaks = [], []
            for side in range(2):
                mine = low if side == 0 else jnp.logical_not(low)
                part = jnp.where(mine, q, jnp.zeros_like(q))
                scores = dot(part, k, NT) + (mask_ref[seq] + biases[side])
                peak = jnp.max(scores, axis=-1, keepdims=True)
                spread = jnp.exp(scores - peak).astype(BF16)
                mixed.append(dot(spread, jnp.where(mine, v, jnp.ones_like(v))))
                peaks.append(peak)
            total = pltpu.roll(jnp.where(low, mixed[1], mixed[0]), 64, 1)
            out_ref[rows, cols] = (jnp.where(low, mixed[0], mixed[1]) / total).astype(BF16)
            log_ref[rows, cols] = jnp.where(low, peaks[0], peaks[1]) + jnp.log(total)


def attend_back(info, bias_ref, q_ref, k_ref, v_ref, a_ref, log_ref, g_ref, dq_ref, dkv_ref, shift, diag_ref, mask_ref):
    has_bias = bias_ref is not None
    seqs, length, _ = mask_ref.shape
    width = q_ref.shape[1]
    low = lax.broadcasted_iota(jnp.int32, (length, 128), 1) < 64
    fill_masks(info, mask_ref)
    if has_bias:
        row_id = lax.broadcasted_iota(jnp.int32, (length, length), 0)
        col_id = lax.broadcasted_iota(jnp.int32, (length, length), 1)
        flip = (row_id + col_id == length - 1).astype(F32).astype(BF16)

    @pl.loop(0, width // 128, unroll=True)
    def _(pair):
        cols = pl.ds(pl.multiple_of(pair * 128, 128), 128)
        kcols = pl.ds(pl.multiple_of(shift + pair * 128, 128), 128)
        vcols = pl.ds(pl.multiple_of(shift + width + pair * 128, 128), 128)
        biases = [diagonals(bias_ref, 2 * pair + side, length) if has_bias else 0.0 for side in range(2)]
        sums = [0.0, 0.0]
        for seq in range(seqs):
            rows = pl.ds(seq * length, length)
            q, k, v, g = q_ref[rows, cols] * 0.125, k_ref[rows, cols], v_ref[rows, cols], g_ref[rows, cols]
            logs = log_ref[rows, cols]
            turned = pltpu.roll(logs, 64, 1)
            product = g.astype(F32) * a_ref[rows, cols].astype(F32)
            minus = (-pltpu.roll(product, 64, 1)).astype(BF16)
            scaled = k * 0.125
            dqs, dks, dvs = [], [], []
            for side in range(2):
                mine = low if side == 0 else jnp.logical_not(low)
                part = jnp.where(mine, q, jnp.zeros_like(q))
                scores = dot(part, k, NT) + (mask_ref[seq] + biases[side])
                probs = jnp.exp(scores - jnp.where(mine, logs, turned))
                dvs.append(dot(probs.astype(BF16), g, TN))
                centred = dot(jnp.where(mine, g, minus), jnp.where(mine, v, jnp.ones_like(v)), NT)
                dlow = (probs * centred).astype(BF16)
                dqs.append(dot(dlow, scaled))
                dks.append(dot(dlow, q, TN))
                if has_bias:
                    sums[side] = sums[side] + dlow.astype(F32)
            dq_ref[rows, cols] = jnp.where(low, dqs[0], dqs[1]).astype(BF16)
            dkv_ref[rows, kcols] = jnp.where(low, dks[0], dks[1]).astype(BF16)
            dkv_ref[rows, vcols] = jnp.where(low, dvs[0], dvs[1]).astype(BF16)
        if has_bias:
            for side in range(2):
                upside = dot(flip, sums[side].astype(BF16))
                wide = jnp.concatenate([upside, jnp.zeros((length, length), F32)], axis=1)
                turned = pltpu.roll(wide, 0, 1, stride=1, stride_axis=0)
                diag_ref[pl.ds(2 * pair + side, 1), :] = jnp.sum(turned, axis=0, keepdims=True)


def attend_call(kernel, info, bias, q, kv, blocks, more, out_shape, length, name):
    rows = q.shape[0]
    seqs = rows // length
    width = more[0].shape[1] if more else out_shape[0].shape[1]
    lead = [] if bias is None else [bias]
    whole = [pl.BlockSpec(a.shape, lambda i: (0, 0)) for a in lead]
    picked = [pl.BlockSpec((rows, width), lambda i, b=b: (0, b)) for b in blocks]
    rest = [pl.BlockSpec(a.shape, lambda i: (0, 0)) for a in more]
    return pl.pallas_call(
        functools.partial(kernel, bias is not None),
        grid=(1,),
        in_specs=[pl.BlockSpec(memory_space=pltpu.SMEM)] + whole + picked + rest,
        out_specs=[pl.BlockSpec(o.shape, lambda i: (0, 0)) for o in out_shape],
        out_shape=out_shape,
        scratch_shapes=[pltpu.VMEM((seqs, length, length), F32)],
        compiler_params=pltpu.CompilerParams(vmem_limit_bytes=40 << 20),
        name=name,
    )(info, *lead, q, kv, kv, *more)


def attend(info, bias, q, kv, blocks, length, width):
    rows = q.shape[0]
    out_shape = [
        jax.ShapeDtypeStruct((rows, width), BF16),
        jax.ShapeDtypeStruct((rows, width), F32),
    ]
    return attend_call(attend_kernel, info, bias, q, kv, blocks, [], out_shape, length, "attend")


def norm_parts(values, gain):
    scale = lax.rsqrt(jnp.mean(values * values, axis=-1, keepdims=True) + EPS)
    return values * scale * gain, scale


def norm_back(values, scale, gain, grad):
    unit = values * scale
    gain_grad = jnp.sum(grad * unit, axis=0)
    pushed = grad * gain
    back = scale * (pushed - unit * jnp.mean(pushed * unit, axis=-1, keepdims=True))
    return back, gain_grad


def gelu_parts(gate):
    c, a = 0.7978845608028654, 0.044715
    square = gate * gate
    u = 0.5 + 0.5 * jnp.tanh(gate * (c + c * a * square))
    slope = u * (1.0 + (gate * (2.0 * c + 6.0 * c * a * square)) * (1.0 - u))
    return gate * u, slope


def flipped(value, bit):
    step = 1 << bit
    return value + step * (1 - 2 * (value // step % 2))


def crossed(value, other):
    for bit in range(other.bit_length()):
        if other >> bit & 1:
            value = flipped(value, bit)
    return value


def greet(partners):
    barrier = pltpu.get_barrier_semaphore()
    for partner in partners:
        pl.semaphore_signal(barrier, inc=1, device_id=partner, device_id_type=MESH)
    pl.semaphore_wait(barrier, len(partners))


def remote(src, dst, out_sem, in_sem, device):
    return pltpu.make_async_remote_copy(
        src_ref=src,
        dst_ref=dst,
        send_sem=out_sem,
        recv_sem=in_sem,
        device_id=device,
        device_id_type=MESH,
    )


def tile_loop(count, step, body):
    @pl.loop(0, count // step)
    def _(i):
        body(pl.multiple_of(i * step, step), step)

    if count % step:
        body(count // step * step, count % step)


def groups_of(experts, block):
    size = 1
    while size * 2 * block <= 320 and size * 2 <= experts:
        size *= 2
    if experts <= 2 * size:
        half = max(size // 2, 1)
        return [(0, size), *((k, half) for k in range(size, experts, half))]
    return [(k, size) for k in range(0, experts, size)]


class Turn:
    def __init__(self, experts, block, there, home):
        self.me, self.dp = lax.axis_index("expert"), lax.axis_index("dp")
        self.experts, self.block = experts, block
        self.peer = {"dp": 1 - self.dp}
        self.groups = groups_of(experts, block)
        self.there_refs, self.home_refs = there, home

    def greet(self):
        greet([{"expert": crossed(self.me, k)} for k in range(1, self.experts)] + [self.peer])

    def there(self, k):
        src, dst, out_sems, in_sems = self.there_refs
        partner = crossed(self.me, k)
        return remote(src.at[partner], dst.at[self.me], out_sems.at[k], in_sems.at[k], {"expert": partner})

    def home(self, k):
        src, dst, out_sems, in_sems = self.home_refs
        partner = crossed(self.me, k)
        return remote(src.at[partner], dst.at[self.me], out_sems.at[k], in_sems.at[k], {"expert": partner})

    def arrive(self, first, size):
        for k in range(max(first, 1), first + size):
            self.there(k).wait_recv()

    def base(self, first, size):
        return crossed(self.me // size, first // size) * size

    def spans(self, first, size):
        base = self.base(first, size)
        rows = pl.ds(pl.multiple_of(base * self.block, size * self.block), size * self.block)
        return pl.ds(base, size), rows


class Lefts:
    def __init__(self, refs, out, scratch, width):
        self.refs, self.out = refs, out
        self.held, self.stage, self.loaded, self.sent, self.came = scratch
        self.half = width // 2
        self.dp = lax.axis_index("dp")

    def fetch(self, i):
        return pltpu.make_async_copy(self.refs[i], self.held.at[i % 2], self.loaded.at[i])

    def copy(self, i):
        return remote(self.stage.at[i], self.out.at[i], self.sent.at[i], self.came.at[i], {"dp": 1 - self.dp})

    def load(self):
        for i in range(2):
            self.fetch(i).start()

    def send(self):
        for i in range(4):
            self.fetch(i).wait()
            cols = pl.ds(pl.multiple_of((1 - self.dp) * self.half, 128), self.half)
            self.stage[i] = self.held[i % 2, :, cols]
            self.copy(i).start()
            if i + 2 < 4:
                self.fetch(i + 2).start()

    def wait(self):
        for i in range(4):
            self.copy(i).wait()


def transpose_kernel_part(loads, tall, wide, wsem, tsem):
    copies = [pltpu.make_async_copy(src, dst, wsem.at[i]) for i, (src, dst, _) in enumerate(loads)]
    for copy in copies:
        copy.start()
    for i, (_, held, out) in enumerate(loads):
        slab = tall.shape[1]
        stages = [tall.at[i] if out.shape[1] == tall.shape[2] else wide.at[pl.ds(i * slab, slab)] for i in range(2)]
        steps = out.shape[0] // slab
        copies[i].wait()

        def put(t, slot, stages=stages, out=out, slab=slab):
            rows = pl.ds(pl.multiple_of(t * slab, slab), slab)
            return pltpu.make_async_copy(stages[slot], out.at[rows], tsem.at[slot])

        def step(pair, carry, stages=stages, held=held, put=put, slab=slab, steps=steps):
            for slot in range(2):
                t = 2 * pair + slot

                @pl.when(t < steps)
                def _(t=t, slot=slot):
                    @pl.when(pair > 0)
                    def _():
                        put(t - 2, slot).wait()

                    cols = pl.ds(pl.multiple_of(t * slab, slab), slab)
                    stages[slot][...] = jnp.transpose(held[:, cols])
                    put(t, slot).start()

            return carry

        lax.fori_loop(0, pl.cdiv(steps, 2), step, 0)
        for t in (steps - 2, steps - 1):
            put(t, t % 2).wait()


def expert_forward_kernel(turn, has_prev, *refs):
    has_prev = has_prev > 0
    send_ref, w_in, w_down = refs[:3]
    left_refs, refs = refs[3 + 10 * has_prev : 3 + 14 * has_prev], refs[3 + 14 * has_prev :]
    back_out, rows_out, slope_out, value_out, hidden_out, slope_peer_out, value_peer_out = refs[:7]
    wgt_out, wut_out, wdt_out = refs[7:10]
    left_out, refs = refs[10 : 10 + has_prev], refs[10 + has_prev :]
    wg, wu, wd, rows, back, made, rows_peer, slopes, values, hidden = refs[:10]
    slopes_peer, values_peer, tall = refs[10:13]
    wsem, s1, r1, s2, r2, sx, rx, osem, tsem = refs[13:22]
    experts, block, width = send_ref.shape
    ff = wd.shape[0]
    span = ff // 2
    lefts = Lefts(left_refs, left_out[0], (tall, *refs[22:]), width) if has_prev else None

    @pl.when(lax.axis_index("half") != turn)
    def _():
        if lefts:
            lefts.load()
            greet([{"dp": 1 - lax.axis_index("dp")}])
            lefts.send()
        loads = ((w_in.at[0], wg, wgt_out), (w_in.at[1], wu, wut_out), (w_down, wd, wdt_out))
        transpose_kernel_part(loads, tall, slopes, wsem, tsem)
        if lefts:
            lefts.wait()

    @pl.when(lax.axis_index("half") == turn)
    def _():
        t = Turn(experts, block, (send_ref, rows, s1, r1), (made, back, s2, r2))
        t.greet()

        def rows_over(part):
            blocks, _ = t.spans(*t.groups[part])
            return remote(rows.at[blocks], rows_peer.at[blocks], sx.at[part], rx.at[part], t.peer)

        for k in range(1, experts):
            t.there(k).start()
        rows[t.me] = send_ref[t.me]
        loads = [
            pltpu.make_async_copy(src, dst, wsem.at[i])
            for i, (src, dst) in enumerate(((w_in.at[0], wg), (w_in.at[1], wu), (w_down, wd)))
        ]
        for load in loads:
            load.start()
        for part, (first, size) in enumerate(t.groups):
            t.arrive(first, size)
            rows_over(part).start()
            blocks, span_rows = t.spans(first, size)
            if part == 0:
                loads[0].wait()
                loads[1].wait()

            def up_tile(start, count, blocks=blocks, span_rows=span_rows, size=size):
                x = rows[blocks].reshape(size * block, width)
                cols = pl.ds(start, count)
                value, slope = gelu_parts(dot(x, wg[:, cols]))
                up = dot(x, wu[:, cols])
                hidden[span_rows, cols] = (value * up).astype(BF16)
                values[span_rows, cols] = value.astype(BF16)
                slopes[span_rows, cols] = (up * slope).astype(BF16)

            tile_loop(ff, 512, up_tile)
            if part == 0:
                loads[2].wait()

            def down_tile(start, count, blocks=blocks, span_rows=span_rows, size=size):
                cols = pl.ds(start, count)
                y = dot(hidden[span_rows, :], wd[:, cols]).astype(BF16)
                made[blocks, :, cols] = y.reshape(size, block, count)

            tile_loop(width, 512, down_tile)
            for k in range(max(first, 1), first + size):
                t.home(k).start()
        back[t.me] = made[t.me]
        half_cols = pl.ds(pl.multiple_of(t.dp * span, 128), span)
        other_cols = pl.ds(pl.multiple_of((1 - t.dp) * span, 128), span)
        outs = [
            (slopes, slope_out),
            (values, value_out),
            (hidden.at[:, half_cols], hidden_out.at[0]),
            (rows, rows_out.at[0]),
        ]
        outs = [pltpu.make_async_copy(src, dst, osem.at[i]) for i, (src, dst) in enumerate(outs)]
        for out in outs:
            out.start()

        for part in range(len(t.groups)):
            rows_over(part).wait_recv()

        def peer_tile(start, count):
            x = rows_peer[...].reshape(experts * block, width)
            here = pl.ds(start, count)
            cols = pl.ds(pl.multiple_of(t.dp * span + start, 128), count)
            value, slope = gelu_parts(dot(x, wg[:, cols]))
            up = dot(x, wu[:, cols])
            hidden[:, pl.ds(pl.multiple_of((1 - t.dp) * span + start, 128), count)] = (value * up).astype(BF16)
            values_peer[:, here] = value.astype(BF16)
            slopes_peer[:, here] = (up * slope).astype(BF16)

        tile_loop(span, 512, peer_tile)
        more = [
            (slopes_peer, slope_peer_out),
            (values_peer, value_peer_out),
            (hidden.at[:, other_cols], hidden_out.at[1]),
            (rows_peer, rows_out.at[1]),
        ]
        more = [pltpu.make_async_copy(src, dst, osem.at[4 + i]) for i, (src, dst) in enumerate(more)]
        for out in more:
            out.start()
        for k in range(1, experts):
            t.home(k).wait_recv()
        back_copy = pltpu.make_async_copy(back, back_out, osem.at[8])
        back_copy.start()
        for k in range(1, experts):
            t.there(k).wait_send()
            t.home(k).wait_send()
        for part in range(len(t.groups)):
            rows_over(part).wait_send()
        for out in [*outs, *more, back_copy]:
            out.wait()


def expert_backward_kernel(turn, has_prev, *refs):
    send_ref = refs[0]
    sources = refs[1:8]
    left_refs, refs = refs[8 + has_prev : 8 + has_prev + 4 * (has_prev == 1)], refs[8 + has_prev + 4 * (has_prev == 1) :]
    back_out, mixed_out, grad_out = refs[:3]
    left_out, refs = refs[3 : 3 + (has_prev == 1)], refs[3 + (has_prev == 1) :]
    wdt, dgate, dup, wgt, wut, dgate_peer, dup_peer = refs[:7]
    grads, back, made, grads_peer = refs[7:11]
    wsem, s1, r1, s2, r2, sx, rx, osem = refs[11:19]
    experts, block, width = send_ref.shape
    ff = wdt.shape[1]
    span = ff // 2
    dp = lax.axis_index("dp")
    t = Turn(experts, block, (send_ref, grads, s1, r1), (made, back, s2, r2))
    lefts = Lefts(left_refs, left_out[0], refs[19:], width) if left_refs else None

    @pl.when(lax.axis_index("half") == turn)
    def _():
        t.greet()

        def grads_over(part):
            blocks, _ = t.spans(*t.groups[part])
            return remote(grads.at[blocks], grads_peer.at[blocks], sx.at[part], rx.at[part], t.peer)

        for k in range(1, experts):
            t.there(k).start()
        grads[t.me] = send_ref[t.me]
        if lefts:
            lefts.load()
        held = (wdt, dgate, dup, wgt, wut, dgate_peer, dup_peer)
        loads = [pltpu.make_async_copy(src, dst, wsem.at[i]) for i, (src, dst) in enumerate(zip(sources, held))]
        for load in loads:
            load.start()
        if lefts:
            lefts.send()
        for load in loads[:3]:
            load.wait()
        for part, (first, size) in enumerate(t.groups):
            t.arrive(first, size)
            grads_over(part).start()
            blocks, span_rows = t.spans(first, size)

            def hidden_tile(start, count, blocks=blocks, span_rows=span_rows, size=size):
                dy = grads[blocks].reshape(size * block, width)
                cols = pl.ds(start, count)
                dhidden = dot(dy, wdt[:, cols])
                dgate[span_rows, cols] = (dhidden * dgate[span_rows, cols].astype(F32)).astype(BF16)
                dup[span_rows, cols] = (dhidden * dup[span_rows, cols].astype(F32)).astype(BF16)

            tile_loop(ff, 512, hidden_tile)
            if part == 0:
                loads[3].wait()
                loads[4].wait()

            def rows_tile(start, count, blocks=blocks, span_rows=span_rows, size=size):
                cols = pl.ds(start, count)
                dr = dot(dgate[span_rows, :], wgt[:, cols]) + dot(dup[span_rows, :], wut[:, cols])
                made[blocks, :, cols] = dr.astype(BF16).reshape(size, block, count)

            tile_loop(width, 512, rows_tile)
            for k in range(max(first, 1), first + size):
                t.home(k).start()
        back[t.me] = made[t.me]
        half_cols = pl.ds(pl.multiple_of(dp * span, 128), span)
        outs = [
            (dgate.at[:, half_cols], mixed_out.at[0, 0]),
            (dup.at[:, half_cols], mixed_out.at[1, 0]),
            (grads, grad_out.at[0]),
        ]
        outs = [pltpu.make_async_copy(src, dst, osem.at[i]) for i, (src, dst) in enumerate(outs)]
        for out in outs:
            out.start()

        for load in loads[5:]:
            load.wait()
        for part in range(len(t.groups)):
            grads_over(part).wait_recv()

        def peer_tile(start, count):
            dy = grads_peer[...].reshape(experts * block, width)
            here = pl.ds(start, count)
            dhidden = dot(dy, wdt[:, pl.ds(pl.multiple_of(dp * span + start, 128), count)])
            dgate_peer[:, here] = (dhidden * dgate_peer[:, here].astype(F32)).astype(BF16)
            dup_peer[:, here] = (dhidden * dup_peer[:, here].astype(F32)).astype(BF16)

        tile_loop(span, 512, peer_tile)
        more = [
            (dgate_peer, mixed_out.at[0, 1]),
            (dup_peer, mixed_out.at[1, 1]),
            (grads_peer, grad_out.at[1]),
        ]
        more = [pltpu.make_async_copy(src, dst, osem.at[3 + i]) for i, (src, dst) in enumerate(more)]
        for out in more:
            out.start()
        for k in range(1, experts):
            t.home(k).wait_recv()
        back_copy = pltpu.make_async_copy(back, back_out, osem.at[6])
        back_copy.start()
        for k in range(1, experts):
            t.there(k).wait_send()
            t.home(k).wait_send()
        for part in range(len(t.groups)):
            grads_over(part).wait_send()
        if lefts:
            lefts.wait()
        for out in [*outs, *more, back_copy]:
            out.wait()


def expert_call(kernel, number, turn, send, sources, prev, more, out_shape, scratch, name, shift=0):
    vmem, hbm = pl.BlockSpec(memory_space=pltpu.VMEM), pl.BlockSpec(memory_space=pl.ANY)
    prev = list(prev or [])
    return pl.pallas_call(
        functools.partial(kernel, turn, len(prev)),
        in_specs=[vmem] + [hbm] * (len(sources) + len(prev) + len(more)),
        out_specs=[hbm] * len(out_shape),
        out_shape=out_shape,
        input_output_aliases={1 + len(sources) + i: i + shift for i in range(len(prev))},
        scratch_shapes=scratch,
        compiler_params=pltpu.CompilerParams(
            collective_id=number, has_side_effects=True, vmem_limit_bytes=60 << 20
        ),
        name=name,
    )(send, *sources, *prev, *more)


def moe_forward(send, w_in, w_down, turn, prev, lefts, slab):
    experts, block, width = send.shape
    ff = w_down.shape[0]
    total = experts * block
    parts = len(groups_of(experts, block))
    dma = pltpu.SemaphoreType.DMA
    scratch = [
        pltpu.VMEM((width, ff), BF16),
        pltpu.VMEM((width, ff), BF16),
        pltpu.VMEM((ff, width), BF16),
        *[pltpu.VMEM(send.shape, BF16)] * 4,
        *[pltpu.VMEM((total, ff), BF16)] * 3,
        *[pltpu.VMEM((total, ff // 2), BF16)] * 2,
        pltpu.VMEM((2, slab, width), BF16),
        dma((3,)),
        *[dma((experts,))] * 4,
        *[dma((parts,))] * 2,
        dma((9,)),
        dma((2,)),
    ]
    shapes = [
        send.shape,
        (2, *send.shape),
        (total, ff),
        (total, ff),
        (2, total, ff // 2),
        (total, ff // 2),
        (total, ff // 2),
        (ff, width),
        (ff, width),
        (width, ff),
    ]
    if lefts:
        rows = lefts[0].shape[0]
        shapes.append((4, rows, width // 2))
        scratch += [pltpu.VMEM((4, rows, width // 2), BF16), *[dma((4,))] * 3]
    out_shape = [jax.ShapeDtypeStruct(shape, BF16) for shape in shapes]
    return expert_call(
        expert_forward_kernel, 1 + turn, turn, send, [w_in, w_down], prev, lefts, out_shape, scratch, "moe_forward"
    )


def moe_backward(grad_send, saved, turn, prev, lefts):
    experts, block, width = grad_send.shape
    _, _, slope, value, _, slope_peer, value_peer, wgt, wut, wdt, lefts_peer = saved
    total, ff = slope.shape
    parts = len(groups_of(experts, block))
    dma = pltpu.SemaphoreType.DMA
    scratch = [
        pltpu.VMEM((width, ff), BF16),
        *[pltpu.VMEM((total, ff), BF16)] * 2,
        *[pltpu.VMEM((ff, width), BF16)] * 2,
        *[pltpu.VMEM((total, ff // 2), BF16)] * 2,
        *[pltpu.VMEM(grad_send.shape, BF16)] * 4,
        dma((7,)),
        *[dma((experts,))] * 4,
        *[dma((parts,))] * 2,
        dma((7,)),
    ]
    out_shape = [
        jax.ShapeDtypeStruct(grad_send.shape, BF16),
        jax.ShapeDtypeStruct((2, 2, total, ff // 2), BF16),
        jax.ShapeDtypeStruct((2, *grad_send.shape), BF16),
    ]
    if lefts:
        prev = [lefts_peer]
        out_shape.append(jax.ShapeDtypeStruct(lefts_peer.shape, BF16))
        rows = lefts[0].shape[0]
        scratch += [pltpu.VMEM((2, rows, width), BF16), pltpu.VMEM(lefts_peer.shape, BF16), *[dma((4,))] * 3]
    return expert_call(
        expert_backward_kernel,
        3 + turn,
        turn,
        grad_send,
        [wdt, slope, value, wgt, wut, slope_peer, value_peer],
        prev,
        lefts,
        out_shape,
        scratch,
        "moe_backward",
        3 if lefts else 0,
    )


GATE, TOTAL, SCALE, ROUTE, SCALE_M, FIRST = 0, 2, 3, 4, 6, 8


class Loads:
    def __init__(self, pairs, sems):
        self.copies = [pltpu.make_async_copy(src, dst, sems.at[i]) for i, (src, dst) in enumerate(pairs)]

    def start(self):
        for copy in self.copies:
            copy.start()

    def wait(self, *which):
        for i in which:
            self.copies[i].wait()


def norm_back_rows(values, scale, gain, grad):
    unit = values * scale
    pushed = grad * gain
    back = scale * (pushed - unit * jnp.mean(pushed * unit, axis=-1, keepdims=True))
    return back, jnp.sum(grad * unit, axis=0, keepdims=True)


def leave_kernel(cross, experts, count, info, stats_ref, gain_ref, router_ref, *refs):
    bias_ref, refs = (None, refs) if cross else (refs[0], refs[1:])
    sources, refs = refs[:count], refs[count:]
    grad_out, branch_out, dgain_out, dlog_out, dq_out, last_out = refs[:6]
    held, (dmixed, mask_ref, sems) = refs[6 : 6 + count], refs[6 + count :]
    back, both, grad, results, x, w_out, a, log = held[:8]
    seqs, length, _ = mask_ref.shape
    width = x.shape[1]
    loads = Loads(zip(sources, held), sems)
    if cross:
        q_ref, kv = held[8:]
        k_ref, v_ref = kv.at[:, pl.ds(0, width)], kv.at[:, pl.ds(width, width)]
        dkv_out, shift, diag_out = last_out, 0, None
    else:
        qkv, ready = held[8:]
        q_ref, k_ref, v_ref = (qkv.at[:, pl.ds(i * width, width)] for i in range(3))
        dkv_out, shift, diag_out = dq_out, width, last_out

    def leave():
        loads.wait(0, 1, 2, 3, 4)
        dgain = jnp.zeros((1, width), F32)
        lane = lax.broadcasted_iota(jnp.int32, (length, 128), 1)
        for seq in range(seqs):
            rows = pl.ds(seq * length, length)
            stats = stats_ref[rows, :]
            gates = [stats[:, GATE + k : GATE + k + 1] for k in range(2)]
            hots = [
                (lane == stats[:, ROUTE + k : ROUTE + k + 1].astype(jnp.int32) + FIRST).astype(F32)
                for k in range(2)
            ]
            probs = jnp.where((lane >= FIRST) & (lane < FIRST + experts), stats, 0.0)
            g = grad[rows, :]
            dgates = [
                jnp.sum(g * results[k, rows, :].astype(F32), axis=-1, keepdims=True) for k in range(2)
            ]
            shared = dgates[0] * gates[0] + dgates[1] * gates[1]
            dprobs = sum((dgates[k] - shared) / stats[:, TOTAL : TOTAL + 1] * hots[k] for k in range(2))
            dlog = probs * (dprobs - jnp.sum(dprobs * probs, axis=-1, keepdims=True))
            dlog_out[rows, :] = dlog
            dnormed = dot(both[rows, :], back[...]) + dot(dlog.astype(BF16), router_ref[...], NT)
            dx, part = norm_back_rows(x[rows, :], stats[:, SCALE : SCALE + 1], gain_ref[...], dnormed)
            dgain = dgain + part
            grad_out[rows, :] = g + dx
        dgain_out[...] = jnp.broadcast_to(dgain, dgain_out.shape)

    def attention():
        loads.wait(5)
        branch_out[...] = grad_out[...].astype(BF16)
        step = min(512, width)
        for start in range(0, width, step):
            cols = pl.ds(start, step)
            dmixed[:, cols] = dot(branch_out[...], w_out[cols, :], NT).astype(BF16)
        loads.wait(*((6, 7, 8, 9) if cross else (6, 7, 8)))
        attend_back(
            info, bias_ref, q_ref, k_ref, v_ref, a, log, dmixed, dq_out, dkv_out, shift, diag_out, mask_ref
        )

    decoder = lax.axis_index("half") == 1
    if cross:

        @pl.when(decoder)
        def _():
            loads.start()
            leave()
            attention()

    else:
        loads.start()

        @pl.when(jnp.logical_not(decoder))
        def _():
            leave()
            loads.wait(9)

        @pl.when(decoder)
        def _():
            loads.wait(0, 1, 2, 3, 4, 9)
            grad_out[...] = ready[...]

        attention()


def leave(info, stats, gain, router, bias, sources, experts, length):
    cross = bias is None
    rows, width = sources[4].shape
    seqs = rows // length
    vmem, hbm = pl.BlockSpec(memory_space=pltpu.VMEM), pl.BlockSpec(memory_space=pl.ANY)
    lead = [] if cross else [bias]
    out_shape = [
        jax.ShapeDtypeStruct((rows, width), F32),
        jax.ShapeDtypeStruct((rows, width), BF16),
        jax.ShapeDtypeStruct((8, width), F32),
        jax.ShapeDtypeStruct((rows, 128), F32),
        jax.ShapeDtypeStruct((rows, width if cross else 3 * width), BF16),
        jax.ShapeDtypeStruct((rows, 2 * width), BF16) if cross else jax.ShapeDtypeStruct(bias.shape, F32),
    ]
    return pl.pallas_call(
        functools.partial(leave_kernel, cross, experts, len(sources)),
        in_specs=[pl.BlockSpec(memory_space=pltpu.SMEM)] + [vmem] * (3 + len(lead)) + [hbm] * len(sources),
        out_specs=[vmem] * 6,
        out_shape=out_shape,
        scratch_shapes=[
            *(pltpu.VMEM(a.shape, a.dtype) for a in sources),
            pltpu.VMEM((rows, width), BF16),
            pltpu.VMEM((seqs, length, length), F32),
            pltpu.SemaphoreType.DMA((len(sources),)),
        ],
        compiler_params=pltpu.CompilerParams(vmem_limit_bytes=56 << 20),
        name="leave_cross" if cross else "leave_self",
    )(info, stats, gain, router, *lead, *sources)


def memory_kernel(stats_ref, gain_ref, *refs):
    sources, refs = refs[:5], refs[5:]
    grad_out, send_out, dgain_out = refs[:3]
    held, (dnormed, spread, sems) = refs[3:8], refs[8:]
    dmemory, w, x, cotangent, spots = held
    rows, width = x.shape

    @pl.when(lax.axis_index("half") == 0)
    def _():
        loads = Loads(zip(sources, held), sems)
        loads.start()
        loads.wait(0, 1)
        step = min(512, width)
        for start in range(0, width, step):
            cols = pl.ds(start, step)
            dnormed[:, cols] = dot(dmemory[...], w[cols, :], NT)
        loads.wait(2, 3)
        dx, dgain = norm_back_rows(
            x[...], stats_ref[:, SCALE_M : SCALE_M + 1], gain_ref[...], dnormed[...]
        )
        dgain_out[...] = jnp.broadcast_to(dgain, dgain_out.shape)
        grad = cotangent[...].astype(F32) + dx
        grad_out[...] = grad
        for k in range(2):
            gate = stats_ref[:, GATE + k : GATE + k + 1]
            spread[pl.ds(k * rows, rows), :] = (gate * grad).astype(BF16)
        loads.wait(4)
        for start in range(0, width, step):
            cols = pl.ds(start, step)
            send_out[:, cols] = dot(spots[...], spread[:, cols]).astype(BF16)


def memory_gradient(stats, gain, sources):
    rows, width = sources[2].shape
    vmem, hbm = pl.BlockSpec(memory_space=pltpu.VMEM), pl.BlockSpec(memory_space=pl.ANY)
    return pl.pallas_call(
        memory_kernel,
        in_specs=[vmem] * 2 + [hbm] * len(sources),
        out_specs=[vmem] * 3,
        out_shape=[
            jax.ShapeDtypeStruct((rows, width), F32),
            jax.ShapeDtypeStruct((sources[4].shape[0], width), BF16),
            jax.ShapeDtypeStruct((8, width), F32),
        ],
        scratch_shapes=[
            *(pltpu.VMEM(a.shape, a.dtype) for a in sources),
            pltpu.VMEM((rows, width), F32),
            pltpu.VMEM((2 * rows, width), BF16),
            pltpu.SemaphoreType.DMA((len(sources),)),
        ],
        compiler_params=pltpu.CompilerParams(vmem_limit_bytes=48 << 20),
        name="memory_gradient",
    )(stats, gain, *sources)


def dense_kernel(stages, chunk, lag, *refs):
    sources, small_ref = refs[:11], refs[11]
    out_refs, small_out, small_in = refs[12:15], refs[15], refs[16]
    held, xt_ref, refs = refs[17:28], refs[28], refs[29:]
    x_refs, own_refs, peer_refs, xp = held[:4], held[4:7], held[7:10], held[10]
    sums, parts = refs[:stages], refs[stages : 2 * stages]
    ss, rs, sk, rk, sl = refs[2 * stages :]
    counts = [ref.shape[1] // chunk for ref in own_refs]
    starts = [sum(counts[:i]) for i in range(3)]
    chunks = sum(counts)
    per_cross = counts[2] // 2
    rows, half = xp.shape[1:]
    dp, me = lax.axis_index("dp"), lax.axis_index("expert")
    peer = {"dp": 1 - dp}
    partners = [flipped(me, k) for k in range(stages)]
    bits = [me // (1 << k) % 2 for k in range(stages)]
    load = [pltpu.make_async_copy(sources[i], held[i], sl.at[i]) for i in range(11)]
    for i in (10, 2, 3, 6, 9, 0, 4, 7, 1, 5, 8):
        load[i].start()
    greet([peer] + [{"expert": p} for p in partners])

    def send_small(step):
        src = small_ref if step == 0 else small_out.at[step - 1]
        device = peer if step == 0 else {"expert": partners[stages - step]}
        return remote(src, small_in.at[step], ss.at[step], rs.at[step], device)

    def order(k, odd):
        return 1 - k if odd and k < 2 else k

    def send_part(k, c, odd):
        bit = order(k, odd)
        other = 1 - bits[bit]
        src = sums[0].at[c, :, :, other] if k == 0 and not odd else sums[k].at[c, :, other]
        return remote(src, parts[k].at[c], sk.at[k, c], rk.at[k, c], {"expert": partners[bit]})

    def turn_x(g):
        load[g].wait()
        cols = pl.ds(pl.multiple_of(dp * half, half), half)
        xt_ref[g, :, :rows] = jnp.transpose(x_refs[g][:, cols])
        xt_ref[g, :, rows:] = jnp.transpose(xp[g])

    def small_step(j):
        send_small(j).wait_recv()
        own = small_ref[...] if j == 0 else small_out[j - 1]
        small_out[j] = own + small_in[j]
        if j < stages:
            send_small(j + 1).start()

    send_small(0).start()
    load[10].wait()
    last = counts[2]
    early = chunks - last
    per = chunks // last

    def produce(i, carry):
        c = jnp.where(lax.rem(i, per) == 0, early + i // per, i - i // per - 1)
        for g in range(3):

            @pl.when(c == starts[g])
            def _(g=g):
                load[4 + g].wait()
                load[7 + g].wait()
                for x in (g,) if g < 2 else (2, 3):
                    turn_x(x)

            @pl.when((c >= starts[g]) & (c < starts[g] + counts[g]))
            def _(g=g):
                at = c - starts[g]
                cols = pl.ds(pl.multiple_of(at * chunk, chunk), chunk)
                which = g if g < 2 else 2 + at // per_cross
                total = dot(xt_ref[which, :, :rows], own_refs[g][:, cols])
                total += dot(xt_ref[which, :, rows:], peer_refs[g][:, cols])
                sums[0][c] = total.astype(BF16).reshape(sums[0].shape[1:])
                send_part(0, c, g == 2).start()

        for j in range(2):

            @pl.when(i == 3 + 6 * j)
            def _(j=j):
                small_step(j)

        return carry

    lax.fori_loop(0, chunks, produce, 0)

    def advance(k, c, odd):
        send_part(k, c, odd).wait_recv()
        bit = bits[order(k, odd)]
        mine = sums[0][c, :, :, bit] if k == 0 and not odd else sums[k][c, :, bit]
        total = mine.astype(F32) + parts[k][c].astype(F32)
        if k + 1 < stages:
            sums[k + 1][c] = total.astype(BF16).reshape(sums[k + 1].shape[1:])
            send_part(k + 1, c, odd).start()
            return
        total = total.reshape(total.shape[-2:])
        for g in (2,) if odd else (0, 1):

            @pl.when((c >= starts[g]) & (c < starts[g] + counts[g]))
            def _(g=g):
                at = pl.multiple_of((c - starts[g]) * chunk, chunk)
                out_refs[g][:, pl.ds(at, chunk)] = total

    def reduce(i, carry):
        @pl.when((lax.rem(i, 2) == 1) & (i // 2 < last))
        def _():
            advance(0, early + i // 2, True)

        for k in range(stages):
            c = i - lag * k

            @pl.when((c >= 0) & (c < early))
            def _(k=k, c=c):
                advance(k, c, False)

        for k in range(1, stages):
            c = i - 1 - lag * (k - 1)

            @pl.when((c >= early) & (c < chunks))
            def _(k=k, c=c):
                advance(k, c, True)

        for j in range(2, stages + 1):

            @pl.when(i == 3 * j - 2)
            def _(j=j):
                small_step(j)

        return carry

    lax.fori_loop(0, chunks + 1 + lag * (stages - 2), reduce, 0)

    def finish(c, carry, odd):
        for k in range(stages):
            send_part(k, c, odd).wait_send()
        return carry

    lax.fori_loop(0, early, functools.partial(finish, odd=False), 0)
    lax.fori_loop(early, chunks, functools.partial(finish, odd=True), 0)
    for j in range(stages + 1):
        send_small(j).wait_send()


def over_dp(array):
    return lax.ppermute(array, "dp", [(0, 1), (1, 0)])


def dense_gradients(lefts, lefts_peer, own, peer, small, experts):
    chunk = 512
    rows, width = lefts[0].shape
    half_rows = width // 2
    chunks = sum(y.shape[1] for y in own) // chunk
    stages = experts.bit_length() - 1
    keep = half_rows // experts
    vmem, hbm = pl.BlockSpec(memory_space=pltpu.VMEM), pl.BlockSpec(memory_space=pl.ANY)
    dma = pltpu.SemaphoreType.DMA
    sources = [*lefts, *own, *peer, lefts_peer]
    blocks = [(experts // 4, 2, 2)] + [(experts >> (k + 1), 2) for k in range(1, stages)]
    halved = [(experts // 4, 2)] + [(experts >> (k + 1),) for k in range(1, stages)]
    scratch = [pltpu.VMEM((stages + 1, *small.shape), F32)]
    scratch += [pltpu.VMEM(a.shape, BF16) for a in sources]
    scratch += [pltpu.VMEM((4, half_rows, 2 * rows), BF16)]
    scratch += [pltpu.VMEM((chunks, *b, keep, chunk), BF16) for b in blocks + halved]
    scratch += [dma((stages + 1,)), dma((stages + 1,)), dma((stages, chunks)), dma((stages, chunks))]
    scratch += [dma((len(sources),))]
    *outs, sums = pl.pallas_call(
        functools.partial(dense_kernel, stages, chunk, 2),
        in_specs=[hbm] * len(sources) + [vmem],
        out_specs=[vmem] * 4,
        out_shape=[
            *(jax.ShapeDtypeStruct((keep, y.shape[1]), F32) for y in own),
            jax.ShapeDtypeStruct((stages + 1, *small.shape), F32),
        ],
        scratch_shapes=scratch,
        compiler_params=pltpu.CompilerParams(
            collective_id=0, has_side_effects=True, vmem_limit_bytes=56 << 20
        ),
        name="dense_gradients",
    )(*sources, small)
    return outs, sums[stages]


def product_kernel(x_ref, y_ref, out_ref):
    out_ref[...] = dot(x_ref[...], y_ref[...].reshape(y_ref.shape[-2:]), TN).reshape(out_ref.shape)


def expert_gradients(rows, mixed, hidden, grads):
    total, width = rows.shape
    span = hidden.shape[1]
    tile = 256
    params = pltpu.CompilerParams(vmem_limit_bytes=40 << 20)
    din = pl.pallas_call(
        product_kernel,
        grid=(2, width // tile),
        in_specs=[
            pl.BlockSpec((total, tile), lambda g, i: (0, i)),
            pl.BlockSpec((1, total, span), lambda g, i: (g, 0, 0)),
        ],
        out_specs=pl.BlockSpec((1, tile, span), lambda g, i: (g, i, 0)),
        out_shape=jax.ShapeDtypeStruct((2, width, span), F32),
        compiler_params=params,
        name="expert_in_gradient",
    )(rows, mixed)
    ddown = pl.pallas_call(
        product_kernel,
        grid=(pl.cdiv(span, tile),),
        in_specs=[
            pl.BlockSpec((total, tile), lambda i: (0, i)),
            pl.BlockSpec((total, width), lambda i: (0, 0)),
        ],
        out_specs=pl.BlockSpec((tile, width), lambda i: (i, 0)),
        out_shape=jax.ShapeDtypeStruct((span, width), F32),
        compiler_params=params,
        name="expert_out_gradient",
    )(hidden, grads)
    return din, ddown


def body(
    tokens,
    cotangent,
    lengths,
    routes,
    self_qkv,
    self_out,
    cross_weights,
    router,
    gains,
    bias_table,
    expert_in,
    expert_out,
):
    _, seqs, length, width = tokens.shape
    heads = H
    experts = router.shape[2]
    top = routes.shape[3]
    capacity = (5 * top * length + 4 * experts - 1) // (4 * experts)
    block_rows = -(-seqs * capacity // 16) * 16
    rows = seqs * length
    slots = experts * block_rows
    half_index = lax.axis_index("half")
    decoder = half_index == 1
    wqkv, wout, wcross, wrouter, gain = (
        self_qkv[0],
        self_out[0],
        cross_weights[0],
        router[0],
        gains[0],
    )
    w_in, w_down = expert_in[0, 0], expert_out[0, 0]

    column = np.arange(2 * length)
    entry = np.arange(BUCKETS * heads)
    hot, hot_back = (
        jnp.where(
            decoder,
            *(
                (entry[:, None] // heads == bucket[None, :]).astype(np.float32)
                for bucket in reversed(diagonal_buckets(diff))
            ),
        )
        for diff in (np.where(column < length, column, column - 2 * length), column - length + 1)
    )
    own_head = entry[None, :] % heads == np.arange(heads)[:, None]
    bias = lax.dot_general(
        jnp.where(own_head, bias_table, 0.0),
        hot,
        (((1,), (0,)), ((), ())),
        precision=lax.Precision.HIGHEST,
        preferred_element_type=F32,
    )
    own_lengths = jnp.where(decoder, lengths[1], lengths[0])
    self_info = jnp.concatenate([own_lengths, half_index[None]]).astype(jnp.int32)
    cross_info = jnp.concatenate([lengths[0], jnp.zeros((1,), jnp.int32)]).astype(jnp.int32)

    order = jnp.transpose(routes[0], (0, 2, 1)).reshape(seqs, top * length)
    expert_ids = jnp.arange(experts, dtype=jnp.int32)
    picked = (order[:, :, None] == expert_ids).astype(BF16)
    earlier = np.tril(np.ones((top * length, top * length), np.float32), -1).astype(BF16)
    before = jnp.einsum("pq,sqe->spe", earlier, picked, preferred_element_type=F32)
    place = jnp.sum(before * picked.astype(F32), axis=2).astype(jnp.int32)
    kept = place < capacity
    base = order * block_rows + jnp.arange(seqs, dtype=jnp.int32)[:, None] * capacity
    target = jnp.where(kept, base + place, -1).reshape(seqs, top, length)
    target = jnp.transpose(target, (1, 0, 2)).reshape(top, rows)
    slot_ids = jnp.arange(slots, dtype=jnp.int32)
    spots = (target[:, :, None] == slot_ids).astype(BF16)
    both = jnp.sum(spots.astype(F32), axis=0).astype(BF16)
    stacked = spots.reshape(top * rows, slots)
    spots_turned = (slot_ids[:, None] == target.reshape(1, top * rows)).astype(BF16)
    kept_hot = picked.astype(F32) * kept[:, :, None].astype(F32)
    kept_count = jnp.sum(kept_hot, axis=(0, 1))
    all_count = jnp.sum(picked.astype(F32), axis=(0, 1))
    tallies = jnp.concatenate([kept_count, all_count - kept_count])
    route_hot = (routes[0].reshape(rows, top, 1) == expert_ids).astype(F32)

    def route(values):
        normed, scale = norm_parts(values, gain[1])
        low = normed.astype(BF16)
        rest = (normed - low.astype(F32)).astype(BF16)
        logits = dot(low, wrouter) + dot(rest, wrouter)
        probs = jax.nn.softmax(logits, axis=-1)
        chosen = jnp.sum(probs[:, None, :] * route_hot, axis=-1)
        total = jnp.sum(chosen, axis=-1, keepdims=True)
        gates = chosen / total
        send = dot(both, low, TN).astype(BF16).reshape(experts, block_rows, width)
        return dict(scale=scale, low=low, probs=probs, gates=gates, total=total, send=send)

    def fetch(returned):
        flat = returned.reshape(slots, width)
        return dot(stacked, flat).astype(BF16).reshape(top, rows, width)

    def combine(values, gates, results):
        return values + jnp.sum(jnp.transpose(gates)[:, :, None] * results, axis=0)

    values = tokens[0].reshape(rows, width).astype(F32)
    normed, scale0 = norm_parts(values, gain[0])
    low0 = normed.astype(BF16)
    qkv = dot(low0, wqkv).astype(BF16)
    mixed0, log0 = attend(self_info, bias, qkv, qkv, (0, 1, 2), length, width)
    first = values + dot(mixed0, wout)

    state = route(first)
    saved = moe_forward(state["send"], w_in, w_down, 0, None, [], rows)
    final_enc = combine(first, state["gates"], fetch(saved[0]))
    normed, scale_m = norm_parts(final_enc, gain[2])
    low_m = normed.astype(BF16)
    memory = dot(low_m, wcross).astype(BF16)
    names = ("half", "dp", "expert")
    forward_pairs, back_pairs = half_pairs(lax.axis_size("dp") * lax.axis_size("expert"))
    memory = lax.ppermute(memory, names, forward_pairs)

    normed, scale_c = norm_parts(first, gain[2])
    low_c = normed.astype(BF16)
    query = dot(low_c, wcross[:, :width]).astype(BF16)
    mixed_c, log_c = attend(cross_info, None, query, memory, (0, 0, 1), length, width)
    second = jnp.where(decoder, first + dot(mixed_c, wcross[:, width:]), first)

    state = route(second)
    lefts = [low0, mixed0, jnp.where(decoder, low_c, low_m), jnp.where(decoder, mixed_c, low_m)]
    saved = moe_forward(state["send"], w_in, w_down, 1, saved, lefts, rows)
    results = fetch(saved[0])
    final = combine(second, state["gates"], results)
    outputs = final.astype(BF16)

    stats = jnp.concatenate(
        [
            state["gates"],
            state["total"],
            state["scale"],
            routes[0].reshape(rows, top).astype(F32),
            scale_m,
            jnp.zeros((rows, 1), F32),
            state["probs"],
            jnp.zeros((rows, 128 - FIRST - experts), F32),
        ],
        axis=1,
    )
    router_wide = jnp.pad(wrouter, ((0, 0), (FIRST, 128 - FIRST - experts)))
    grad_dec = cotangent[0].reshape(rows, width)
    spread = (jnp.transpose(state["gates"])[:, :, None] * grad_dec.astype(F32)[None]).astype(BF16)
    grad_send = dot(spots_turned, spread.reshape(top * rows, width)).astype(BF16)
    *kept_from, lefts_peer = moe_backward(
        grad_send.reshape(experts, block_rows, width), saved, 1, None, lefts
    )

    grad_second, dbranch_c, dgain_moe_dec, dlog_dec, dquery, dmemory = leave(
        cross_info,
        stats,
        gain[1:2],
        router_wide,
        None,
        [
            kept_from[0].reshape(slots, width),
            both,
            grad_dec.astype(F32),
            results,
            second,
            wcross[:, width:],
            mixed_c,
            log_c,
            query,
            memory,
        ],
        experts,
        length,
    )
    dmemory = lax.ppermute(dmemory, names, back_pairs)
    dnormed = dot(dquery, wcross[:, :width], NT)
    dvalues, dgain_c = norm_back(first, scale_c, gain[2], dnormed)
    grad_first_dec = grad_second + dvalues

    grad, grad_send, dgain_m = memory_gradient(
        stats, gain[2:3], [dmemory, wcross, final_enc, grad_dec, spots_turned]
    )
    back, mixed_grads, all_grad = moe_backward(
        grad_send.reshape(experts, block_rows, width), saved, 0, kept_from, []
    )
    all_rows, hidden = saved[1], saved[4]
    grad_first, dbranch, dgain_moe, dlog, dqkv_rows, diag = leave(
        self_info,
        stats,
        gain[1:2],
        router_wide,
        bias,
        [
            back.reshape(slots, width),
            both,
            grad,
            results,
            second,
            wout,
            mixed0,
            log0,
            qkv,
            grad_first_dec,
        ],
        experts,
        length,
    )
    dlog = jnp.where(decoder, dlog_dec, dlog)[:, FIRST : FIRST + experts]
    dgain_moe = jnp.where(decoder, dgain_moe_dec[0], dgain_moe[0])
    drouter = lax.dot_general(
        second * state["scale"] * gain[1],
        dlog,
        TN,
        precision=lax.Precision.HIGHEST,
        preferred_element_type=F32,
    )
    dnormed = dot(dqkv_rows, wqkv, NT)
    dvalues, dgain_self = norm_back(values, scale0, gain[0], dnormed)
    d_tokens = (grad_first + dvalues).astype(BF16)
    by_entry = lax.dot_general(
        diag, hot_back, NT, precision=lax.Precision.HIGHEST, preferred_element_type=F32
    )
    dtable = jnp.sum(jnp.where(own_head, by_entry, 0.0), axis=0)

    cross_grad = jnp.where(decoder, jnp.concatenate([dquery, dbranch_c], axis=1), dmemory)
    own_grads = (dqkv_rows, dbranch, cross_grad)
    peer_grads = tuple(map(over_dp, own_grads))
    places = 2 * experts
    own = width // places
    extra = jnp.concatenate([dtable.reshape(places, -1), tallies.reshape(places, 1)], axis=1)
    extra = jnp.pad(extra, ((0, 0), (0, -extra.shape[1] % own)))
    small = jnp.concatenate(
        [
            jnp.transpose(drouter),
            jnp.stack([dgain_self, dgain_moe, jnp.where(decoder, dgain_c, dgain_m[0])]),
            jnp.swapaxes(extra.reshape(places, -1, own), 0, 1).reshape(-1, width),
        ]
    )
    small = jnp.pad(small, ((0, -small.shape[0] % 8), (0, 0)))
    (dqkv, dout, dcross), small = dense_gradients(
        lefts, lefts_peer, own_grads, peer_grads, small, experts
    )
    place = lax.axis_index("dp") * experts + lax.axis_index("expert")
    mine = lax.dynamic_slice_in_dim(small, place * own, own, 1)
    tail = mine[experts + 3 :].reshape(-1)
    own_table = dtable.shape[0] // places
    d_table = tail[:own_table]
    counts = tail[own_table].astype(jnp.int32)

    ff_half = hidden.shape[-1]
    din, ddown = expert_gradients(
        all_rows.reshape(-1, width),
        mixed_grads.reshape(2, -1, ff_half),
        hidden.reshape(-1, ff_half),
        all_grad.reshape(-1, width),
    )
    return (
        outputs.reshape(1, seqs, length, width),
        d_tokens.reshape(1, seqs, length, width),
        dqkv[None],
        dout[None],
        dcross[None],
        jnp.transpose(mine[:experts])[None],
        mine[experts : experts + 3][None],
        d_table[None],
        din[None, None],
        ddown[None, None],
        counts.reshape(1, 1, 1),
    )


def half_pairs(count):
    return (
        [(i, count + i) for i in range(count)],
        [(count + i, i) for i in range(count)],
    )


def solution(mesh):
    placed = (
        P("half", ("dp", "expert"), None, None),
        P("half", ("dp", "expert"), None, None),
        P(None, ("dp", "expert")),
        P("half", ("dp", "expert"), None, None),
        P("half", None, None),
        P("half", None, None),
        P("half", None, None),
        P("half", None, None),
        P("half", None, None),
        P("half", None),
        P("half", "expert", None, None, None),
        P("half", "expert", None, None),
    )
    return jax.shard_map(
        body,
        mesh=mesh,
        in_specs=placed,
        out_specs=(
            P("half", ("dp", "expert"), None, None),
            P("half", ("dp", "expert"), None, None),
            P("half", ("dp", "expert"), None),
            P("half", ("dp", "expert"), None),
            P("half", ("dp", "expert"), None),
            P("half", ("dp", "expert"), None),
            P("half", None, ("dp", "expert")),
            P("half", ("dp", "expert")),
            P("half", "expert", None, None, "dp"),
            P("half", "expert", "dp", None),
            P("half", "dp", "expert"),
        ),
        check_vma=False,
    )
```

```python
import functools

import jax
import jax.numpy as jnp
import numpy as np
from jax import lax
from jax.experimental import pallas as pl
from jax.experimental.pallas import tpu as pltpu
from jax.sharding import PartitionSpec as P

H = 16
BUCKETS = 32
EPS = 1e-06
ENC_STEPS = (12, 16, 23, 32, 46, 64, 91)
DEC_STEPS = (19, 21, 24, 27, 31, 35, 40, 46, 52, 59, 67, 77, 87, 99, 113)
F32 = jnp.float32
BF16 = jnp.bfloat16
MESH = pl.DeviceIdType.MESH
NT = (((1,), (1,)), ((), ()))
TN = (((0,), (0,)), ((), ()))


def dot(a, b, dims=(((1,), (0,)), ((), ()))):
    return lax.dot_general(a, b, dims, preferred_element_type=F32)


def diagonal_buckets(diff):
    apart = np.abs(diff)
    coarse = 8 + sum((apart >= step).astype(np.int32) for step in ENC_STEPS)
    enc = np.where(apart < 8, apart, coarse) + 16 * (diff > 0)
    behind = np.maximum(-diff, 0)
    coarse = 16 + sum((behind >= step).astype(np.int32) for step in DEC_STEPS)
    dec = np.where(behind < 16, behind, coarse)
    return enc.astype(np.int32), dec.astype(np.int32)


def diagonals(bias_ref, head, length):
    row = jnp.broadcast_to(bias_ref[pl.ds(head, 1), :], (length, 2 * length))
    return pltpu.roll(row, 0, 1, stride=1, stride_axis=0)[:, :length]


def fill_masks(info, mask_ref):
    seqs, length, _ = mask_ref.shape
    row_id = lax.broadcasted_iota(jnp.int32, (length, length), 0)
    col_id = lax.broadcasted_iota(jnp.int32, (length, length), 1)
    reach = jnp.where(info[seqs] > 0, row_id, length)
    for seq in range(seqs):
        allowed = (col_id < info[seq]) & (col_id <= reach)
        mask_ref[seq] = jnp.where(allowed, 0.0, -1000000000.0)


def attend_kernel(has_bias, info, *refs):
    bias_ref, refs = (refs[0], refs[1:]) if has_bias else (None, refs)
    q_ref, k_ref, v_ref, out_ref, log_ref, mask_ref = refs
    seqs, length, _ = mask_ref.shape
    low = lax.broadcasted_iota(jnp.int32, (length, 128), 1) < 64
    fill_masks(info, mask_ref)

    @pl.loop(0, q_ref.shape[1] // 128, unroll=True)
    def _(pair):
        cols = pl.ds(pl.multiple_of(pair * 128, 128), 128)
        biases = [diagonals(bias_ref, 2 * pair + side, length) if has_bias else 0.0 for side in range(2)]
        for seq in range(seqs):
            rows = pl.ds(seq * length, length)
            q, k, v = q_ref[rows, cols] * 0.125, k_ref[rows, cols], v_ref[rows, cols]
            mixed, peaks = [], []
            for side in range(2):
                mine = low if side == 0 else jnp.logical_not(low)
                part = jnp.where(mine, q, jnp.zeros_like(q))
                scores = dot(part, k, NT) + (mask_ref[seq] + biases[side])
                peak = jnp.max(scores, axis=-1, keepdims=True)
                spread = jnp.exp(scores - peak).astype(BF16)
                mixed.append(dot(spread, jnp.where(mine, v, jnp.ones_like(v))))
                peaks.append(peak)
            total = pltpu.roll(jnp.where(low, mixed[1], mixed[0]), 64, 1)
            out_ref[rows, cols] = (jnp.where(low, mixed[0], mixed[1]) / total).astype(BF16)
            log_ref[rows, cols] = jnp.where(low, peaks[0], peaks[1]) + jnp.log(total)


def attend_back(info, bias_ref, q_ref, k_ref, v_ref, a_ref, log_ref, g_ref, dq_ref, dkv_ref, shift, diag_ref, mask_ref):
    has_bias = bias_ref is not None
    seqs, length, _ = mask_ref.shape
    width = q_ref.shape[1]
    low = lax.broadcasted_iota(jnp.int32, (length, 128), 1) < 64
    fill_masks(info, mask_ref)
    if has_bias:
        row_id = lax.broadcasted_iota(jnp.int32, (length, length), 0)
        col_id = lax.broadcasted_iota(jnp.int32, (length, length), 1)
        flip = (row_id + col_id == length - 1).astype(F32).astype(BF16)

    @pl.loop(0, width // 128, unroll=True)
    def _(pair):
        cols = pl.ds(pl.multiple_of(pair * 128, 128), 128)
        kcols = pl.ds(pl.multiple_of(shift + pair * 128, 128), 128)
        vcols = pl.ds(pl.multiple_of(shift + width + pair * 128, 128), 128)
        biases = [diagonals(bias_ref, 2 * pair + side, length) if has_bias else 0.0 for side in range(2)]
        sums = [0.0, 0.0]
        for seq in range(seqs):
            rows = pl.ds(seq * length, length)
            q, k, v, g = q_ref[rows, cols] * 0.125, k_ref[rows, cols], v_ref[rows, cols], g_ref[rows, cols]
            logs = log_ref[rows, cols]
            turned = pltpu.roll(logs, 64, 1)
            product = g.astype(F32) * a_ref[rows, cols].astype(F32)
            minus = (-pltpu.roll(product, 64, 1)).astype(BF16)
            scaled = k * 0.125
            dqs, dks, dvs = [], [], []
            for side in range(2):
                mine = low if side == 0 else jnp.logical_not(low)
                part = jnp.where(mine, q, jnp.zeros_like(q))
                scores = dot(part, k, NT) + (mask_ref[seq] + biases[side])
                probs = jnp.exp(scores - jnp.where(mine, logs, turned))
                dvs.append(dot(probs.astype(BF16), g, TN))
                centred = dot(jnp.where(mine, g, minus), jnp.where(mine, v, jnp.ones_like(v)), NT)
                dlow = (probs * centred).astype(BF16)
                dqs.append(dot(dlow, scaled))
                dks.append(dot(dlow, q, TN))
                if has_bias:
                    sums[side] = sums[side] + dlow.astype(F32)
            dq_ref[rows, cols] = jnp.where(low, dqs[0], dqs[1]).astype(BF16)
            dkv_ref[rows, kcols] = jnp.where(low, dks[0], dks[1]).astype(BF16)
            dkv_ref[rows, vcols] = jnp.where(low, dvs[0], dvs[1]).astype(BF16)
        if has_bias:
            for side in range(2):
                upside = dot(flip, sums[side].astype(BF16))
                wide = jnp.concatenate([upside, jnp.zeros((length, length), F32)], axis=1)
                turned = pltpu.roll(wide, 0, 1, stride=1, stride_axis=0)
                diag_ref[pl.ds(2 * pair + side, 1), :] = jnp.sum(turned, axis=0, keepdims=True)


def attend_call(kernel, info, bias, q, kv, blocks, more, out_shape, length, name):
    rows = q.shape[0]
    seqs = rows // length
    width = more[0].shape[1] if more else out_shape[0].shape[1]
    lead = [] if bias is None else [bias]
    whole = [pl.BlockSpec(a.shape, lambda i: (0, 0)) for a in lead]
    picked = [pl.BlockSpec((rows, width), lambda i, b=b: (0, b)) for b in blocks]
    rest = [pl.BlockSpec(a.shape, lambda i: (0, 0)) for a in more]
    return pl.pallas_call(
        functools.partial(kernel, bias is not None),
        grid=(1,),
        in_specs=[pl.BlockSpec(memory_space=pltpu.SMEM)] + whole + picked + rest,
        out_specs=[pl.BlockSpec(o.shape, lambda i: (0, 0)) for o in out_shape],
        out_shape=out_shape,
        scratch_shapes=[pltpu.VMEM((seqs, length, length), F32)],
        compiler_params=pltpu.CompilerParams(vmem_limit_bytes=40 << 20),
        name=name,
    )(info, *lead, q, kv, kv, *more)


def attend(info, bias, q, kv, blocks, length, width):
    rows = q.shape[0]
    out_shape = [
        jax.ShapeDtypeStruct((rows, width), BF16),
        jax.ShapeDtypeStruct((rows, width), F32),
    ]
    return attend_call(attend_kernel, info, bias, q, kv, blocks, [], out_shape, length, "attend")


def norm_parts(values, gain):
    scale = lax.rsqrt(jnp.mean(values * values, axis=-1, keepdims=True) + EPS)
    return values * scale * gain, scale


def norm_back(values, scale, gain, grad):
    unit = values * scale
    gain_grad = jnp.sum(grad * unit, axis=0)
    pushed = grad * gain
    back = scale * (pushed - unit * jnp.mean(pushed * unit, axis=-1, keepdims=True))
    return back, gain_grad


def gelu_parts(gate):
    c, a = 0.7978845608028654, 0.044715
    square = gate * gate
    u = 0.5 + 0.5 * jnp.tanh(gate * (c + c * a * square))
    slope = u * (1.0 + (gate * (2.0 * c + 6.0 * c * a * square)) * (1.0 - u))
    return gate * u, slope


def flipped(value, bit):
    step = 1 << bit
    return value + step * (1 - 2 * (value // step % 2))


def crossed(value, other):
    for bit in range(other.bit_length()):
        if other >> bit & 1:
            value = flipped(value, bit)
    return value


def greet(partners):
    barrier = pltpu.get_barrier_semaphore()
    for partner in partners:
        pl.semaphore_signal(barrier, inc=1, device_id=partner, device_id_type=MESH)
    pl.semaphore_wait(barrier, len(partners))


def remote(src, dst, out_sem, in_sem, device):
    return pltpu.make_async_remote_copy(
        src_ref=src,
        dst_ref=dst,
        send_sem=out_sem,
        recv_sem=in_sem,
        device_id=device,
        device_id_type=MESH,
    )


def tile_loop(count, step, body):
    @pl.loop(0, count // step)
    def _(i):
        body(pl.multiple_of(i * step, step), step)

    if count % step:
        body(count // step * step, count % step)


def groups_of(experts, block):
    size = 1
    while size * 2 * block <= 320 and size * 2 <= experts:
        size *= 2
    if experts <= 2 * size:
        half = max(size // 2, 1)
        return [(0, size), *((k, half) for k in range(size, experts, half))]
    return [(k, size) for k in range(0, experts, size)]


class Turn:
    def __init__(self, experts, block, there, home):
        self.me, self.dp = lax.axis_index("expert"), lax.axis_index("dp")
        self.experts, self.block = experts, block
        self.peer = {"dp": 1 - self.dp}
        self.groups = groups_of(experts, block)
        self.there_refs, self.home_refs = there, home

    def greet(self):
        greet([{"expert": crossed(self.me, k)} for k in range(1, self.experts)] + [self.peer])

    def there(self, k):
        src, dst, out_sems, in_sems = self.there_refs
        partner = crossed(self.me, k)
        return remote(src.at[partner], dst.at[self.me], out_sems.at[k], in_sems.at[k], {"expert": partner})

    def home(self, k):
        src, dst, out_sems, in_sems = self.home_refs
        partner = crossed(self.me, k)
        return remote(src.at[partner], dst.at[self.me], out_sems.at[k], in_sems.at[k], {"expert": partner})

    def arrive(self, first, size):
        for k in range(max(first, 1), first + size):
            self.there(k).wait_recv()

    def base(self, first, size):
        return crossed(self.me // size, first // size) * size

    def spans(self, first, size):
        base = self.base(first, size)
        rows = pl.ds(pl.multiple_of(base * self.block, size * self.block), size * self.block)
        return pl.ds(base, size), rows


class Lefts:
    def __init__(self, refs, out, scratch, width):
        self.refs, self.out = refs, out
        self.held, self.stage, self.loaded, self.sent, self.came = scratch
        self.half, self.slots = width // 2, self.held.shape[0]
        self.dp = lax.axis_index("dp")

    def fetch(self, i):
        return pltpu.make_async_copy(self.refs[i], self.held.at[i % self.slots], self.loaded.at[i])

    def copy(self, i):
        return remote(self.stage.at[i], self.out.at[i], self.sent.at[i], self.came.at[i], {"dp": 1 - self.dp})

    def load(self):
        for i in range(self.slots):
            self.fetch(i).start()

    def send(self):
        for i in range(4):
            self.fetch(i).wait()
            cols = pl.ds(pl.multiple_of((1 - self.dp) * self.half, 128), self.half)
            self.stage[i] = self.held[i % self.slots, :, cols]
            self.copy(i).start()
            if i + self.slots < 4:
                self.fetch(i + self.slots).start()

    def wait(self):
        for i in range(4):
            self.copy(i).wait()


def transpose_kernel_part(loads, tall, wide, wsem, tsem):
    copies = [pltpu.make_async_copy(src, dst, wsem.at[i]) for i, (src, dst, _) in enumerate(loads)]
    for copy in copies:
        copy.start()
    for i, (_, held, out) in enumerate(loads):
        slab = tall.shape[1]
        stages = [tall.at[i] if out.shape[1] == tall.shape[2] else wide.at[pl.ds(i * slab, slab)] for i in range(2)]
        steps = out.shape[0] // slab
        copies[i].wait()

        def put(t, slot, stages=stages, out=out, slab=slab):
            rows = pl.ds(pl.multiple_of(t * slab, slab), slab)
            return pltpu.make_async_copy(stages[slot], out.at[rows], tsem.at[slot])

        def step(pair, carry, stages=stages, held=held, put=put, slab=slab, steps=steps):
            for slot in range(2):
                t = 2 * pair + slot

                @pl.when(t < steps)
                def _(t=t, slot=slot):
                    @pl.when(pair > 0)
                    def _():
                        put(t - 2, slot).wait()

                    cols = pl.ds(pl.multiple_of(t * slab, slab), slab)
                    stages[slot][...] = jnp.transpose(held[:, cols])
                    put(t, slot).start()

            return carry

        lax.fori_loop(0, pl.cdiv(steps, 2), step, 0)
        for t in (steps - 2, steps - 1):
            put(t, t % 2).wait()


def expert_forward_kernel(turn, has_prev, *refs):
    has_prev = has_prev > 0
    send_ref, w_in, w_down = refs[:3]
    left_refs, refs = refs[3 + 10 * has_prev : 3 + 14 * has_prev], refs[3 + 14 * has_prev :]
    back_out, rows_out, slope_out, value_out, hidden_out, slope_peer_out, value_peer_out = refs[:7]
    wgt_out, wut_out, wdt_out = refs[7:10]
    left_out, refs = refs[10 : 10 + has_prev], refs[10 + has_prev :]
    wg, wu, wd, rows, back, made, rows_peer, slopes, values, hidden = refs[:10]
    slopes_peer, values_peer, tall = refs[10:13]
    wsem, s1, r1, s2, r2, sx, rx, osem, tsem = refs[13:22]
    experts, block, width = send_ref.shape
    ff = wd.shape[0]
    span = ff // 2
    lefts = Lefts(left_refs, left_out[0], (tall, *refs[22:]), width) if has_prev else None

    @pl.when(lax.axis_index("half") != turn)
    def _():
        if lefts:
            greet([{"dp": 1 - lax.axis_index("dp")}])
        loads = ((w_in.at[0], wg, wgt_out), (w_in.at[1], wu, wut_out), (w_down, wd, wdt_out))
        transpose_kernel_part(loads, tall, slopes, wsem, tsem)
        if lefts:
            lefts.load()
            lefts.send()
            lefts.wait()

    @pl.when(lax.axis_index("half") == turn)
    def _():
        t = Turn(experts, block, (send_ref, rows, s1, r1), (made, back, s2, r2))
        t.greet()

        def rows_over(part):
            blocks, _ = t.spans(*t.groups[part])
            return remote(rows.at[blocks], rows_peer.at[blocks], sx.at[part], rx.at[part], t.peer)

        for k in range(1, experts):
            t.there(k).start()
        rows[t.me] = send_ref[t.me]
        loads = [
            pltpu.make_async_copy(src, dst, wsem.at[i])
            for i, (src, dst) in enumerate(((w_in.at[0], wg), (w_in.at[1], wu), (w_down, wd)))
        ]
        for load in loads:
            load.start()
        for part, (first, size) in enumerate(t.groups):
            t.arrive(first, size)
            rows_over(part).start()
            blocks, span_rows = t.spans(first, size)
            if part == 0:
                loads[0].wait()
                loads[1].wait()

            def up_tile(start, count, blocks=blocks, span_rows=span_rows, size=size):
                x = rows[blocks].reshape(size * block, width)
                cols = pl.ds(start, count)
                value, slope = gelu_parts(dot(x, wg[:, cols]))
                up = dot(x, wu[:, cols])
                hidden[span_rows, cols] = (value * up).astype(BF16)
                values[span_rows, cols] = value.astype(BF16)
                slopes[span_rows, cols] = (up * slope).astype(BF16)

            tile_loop(ff, 512, up_tile)
            if part == 0:
                loads[2].wait()

            def down_tile(start, count, blocks=blocks, span_rows=span_rows, size=size):
                cols = pl.ds(start, count)
                y = dot(hidden[span_rows, :], wd[:, cols]).astype(BF16)
                made[blocks, :, cols] = y.reshape(size, block, count)

            tile_loop(width, 512, down_tile)
            for k in range(max(first, 1), first + size):
                t.home(k).start()
        back[t.me] = made[t.me]
        half_cols = pl.ds(pl.multiple_of(t.dp * span, 128), span)
        other_cols = pl.ds(pl.multiple_of((1 - t.dp) * span, 128), span)
        outs = [
            (slopes, slope_out),
            (values, value_out),
            (hidden.at[:, half_cols], hidden_out.at[0]),
            (rows, rows_out.at[0]),
        ]
        outs = [pltpu.make_async_copy(src, dst, osem.at[i]) for i, (src, dst) in enumerate(outs)]
        for out in outs:
            out.start()

        for part in range(len(t.groups)):
            rows_over(part).wait_recv()

        def peer_tile(start, count):
            x = rows_peer[...].reshape(experts * block, width)
            here = pl.ds(start, count)
            cols = pl.ds(pl.multiple_of(t.dp * span + start, 128), count)
            value, slope = gelu_parts(dot(x, wg[:, cols]))
            up = dot(x, wu[:, cols])
            hidden[:, pl.ds(pl.multiple_of((1 - t.dp) * span + start, 128), count)] = (value * up).astype(BF16)
            values_peer[:, here] = value.astype(BF16)
            slopes_peer[:, here] = (up * slope).astype(BF16)

        tile_loop(span, 512, peer_tile)
        more = [
            (slopes_peer, slope_peer_out),
            (values_peer, value_peer_out),
            (hidden.at[:, other_cols], hidden_out.at[1]),
            (rows_peer, rows_out.at[1]),
        ]
        more = [pltpu.make_async_copy(src, dst, osem.at[4 + i]) for i, (src, dst) in enumerate(more)]
        for out in more:
            out.start()
        for k in range(1, experts):
            t.home(k).wait_recv()
        back_copy = pltpu.make_async_copy(back, back_out, osem.at[8])
        back_copy.start()
        for k in range(1, experts):
            t.there(k).wait_send()
            t.home(k).wait_send()
        for part in range(len(t.groups)):
            rows_over(part).wait_send()
        for out in [*outs, *more, back_copy]:
            out.wait()


def expert_backward_kernel(turn, has_prev, *refs):
    send_ref = refs[0]
    sources = refs[1:8]
    left_refs, refs = refs[8 + has_prev : 8 + has_prev + 4 * (has_prev == 1)], refs[8 + has_prev + 4 * (has_prev == 1) :]
    back_out, mixed_out, grad_out = refs[:3]
    left_out, refs = refs[3 : 3 + (has_prev == 1)], refs[3 + (has_prev == 1) :]
    wdt, dgate, dup, wgt, wut, dgate_peer, dup_peer = refs[:7]
    grads, back, made, grads_peer = refs[7:11]
    wsem, s1, r1, s2, r2, sx, rx, osem = refs[11:19]
    experts, block, width = send_ref.shape
    ff = wdt.shape[1]
    span = ff // 2
    dp = lax.axis_index("dp")
    t = Turn(experts, block, (send_ref, grads, s1, r1), (made, back, s2, r2))
    lefts = Lefts(left_refs, left_out[0], refs[19:], width) if left_refs else None

    @pl.when(lax.axis_index("half") == turn)
    def _():
        t.greet()

        def grads_over(part):
            blocks, _ = t.spans(*t.groups[part])
            return remote(grads.at[blocks], grads_peer.at[blocks], sx.at[part], rx.at[part], t.peer)

        for k in range(1, experts):
            t.there(k).start()
        grads[t.me] = send_ref[t.me]
        if lefts:
            lefts.load()
        held = (wdt, dgate, dup, wgt, wut, dgate_peer, dup_peer)
        loads = [pltpu.make_async_copy(src, dst, wsem.at[i]) for i, (src, dst) in enumerate(zip(sources, held))]
        for load in loads:
            load.start()
        if lefts:
            lefts.send()
        for load in loads[:3]:
            load.wait()
        for part, (first, size) in enumerate(t.groups):
            t.arrive(first, size)
            grads_over(part).start()
            blocks, span_rows = t.spans(first, size)

            def hidden_tile(start, count, blocks=blocks, span_rows=span_rows, size=size):
                dy = grads[blocks].reshape(size * block, width)
                cols = pl.ds(start, count)
                dhidden = dot(dy, wdt[:, cols])
                dgate[span_rows, cols] = (dhidden * dgate[span_rows, cols].astype(F32)).astype(BF16)
                dup[span_rows, cols] = (dhidden * dup[span_rows, cols].astype(F32)).astype(BF16)

            tile_loop(ff, 512, hidden_tile)
            if part == 0:
                loads[3].wait()
                loads[4].wait()

            def rows_tile(start, count, blocks=blocks, span_rows=span_rows, size=size):
                cols = pl.ds(start, count)
                dr = dot(dgate[span_rows, :], wgt[:, cols]) + dot(dup[span_rows, :], wut[:, cols])
                made[blocks, :, cols] = dr.astype(BF16).reshape(size, block, count)

            tile_loop(width, 512, rows_tile)
            for k in range(max(first, 1), first + size):
                t.home(k).start()
        back[t.me] = made[t.me]
        half_cols = pl.ds(pl.multiple_of(dp * span, 128), span)
        outs = [
            (dgate.at[:, half_cols], mixed_out.at[0, 0]),
            (dup.at[:, half_cols], mixed_out.at[1, 0]),
            (grads, grad_out.at[0]),
        ]
        outs = [pltpu.make_async_copy(src, dst, osem.at[i]) for i, (src, dst) in enumerate(outs)]
        for out in outs:
            out.start()

        for load in loads[5:]:
            load.wait()
        for part in range(len(t.groups)):
            grads_over(part).wait_recv()

        def peer_tile(start, count):
            dy = grads_peer[...].reshape(experts * block, width)
            here = pl.ds(start, count)
            dhidden = dot(dy, wdt[:, pl.ds(pl.multiple_of(dp * span + start, 128), count)])
            dgate_peer[:, here] = (dhidden * dgate_peer[:, here].astype(F32)).astype(BF16)
            dup_peer[:, here] = (dhidden * dup_peer[:, here].astype(F32)).astype(BF16)

        tile_loop(span, 512, peer_tile)
        more = [
            (dgate_peer, mixed_out.at[0, 1]),
            (dup_peer, mixed_out.at[1, 1]),
            (grads_peer, grad_out.at[1]),
        ]
        more = [pltpu.make_async_copy(src, dst, osem.at[3 + i]) for i, (src, dst) in enumerate(more)]
        for out in more:
            out.start()
        for k in range(1, experts):
            t.home(k).wait_recv()
        back_copy = pltpu.make_async_copy(back, back_out, osem.at[6])
        back_copy.start()
        for k in range(1, experts):
            t.there(k).wait_send()
            t.home(k).wait_send()
        for part in range(len(t.groups)):
            grads_over(part).wait_send()
        if lefts:
            lefts.wait()
        for out in [*outs, *more, back_copy]:
            out.wait()


def expert_call(kernel, number, turn, send, sources, prev, more, out_shape, scratch, name, shift=0):
    vmem, hbm = pl.BlockSpec(memory_space=pltpu.VMEM), pl.BlockSpec(memory_space=pl.ANY)
    prev = list(prev or [])
    return pl.pallas_call(
        functools.partial(kernel, turn, len(prev)),
        in_specs=[vmem] + [hbm] * (len(sources) + len(prev) + len(more)),
        out_specs=[hbm] * len(out_shape),
        out_shape=out_shape,
        input_output_aliases={1 + len(sources) + i: i + shift for i in range(len(prev))},
        scratch_shapes=scratch,
        compiler_params=pltpu.CompilerParams(
            collective_id=number, has_side_effects=True, vmem_limit_bytes=60 << 20
        ),
        name=name,
    )(send, *sources, *prev, *more)


def moe_forward(send, w_in, w_down, turn, prev, lefts, slab):
    experts, block, width = send.shape
    ff = w_down.shape[0]
    total = experts * block
    parts = len(groups_of(experts, block))
    dma = pltpu.SemaphoreType.DMA
    scratch = [
        pltpu.VMEM((width, ff), BF16),
        pltpu.VMEM((width, ff), BF16),
        pltpu.VMEM((ff, width), BF16),
        *[pltpu.VMEM(send.shape, BF16)] * 4,
        *[pltpu.VMEM((total, ff), BF16)] * 3,
        *[pltpu.VMEM((total, ff // 2), BF16)] * 2,
        pltpu.VMEM((2, slab, width), BF16),
        dma((3,)),
        *[dma((experts,))] * 4,
        *[dma((parts,))] * 2,
        dma((9,)),
        dma((2,)),
    ]
    shapes = [
        send.shape,
        (2, *send.shape),
        (total, ff),
        (total, ff),
        (2, total, ff // 2),
        (total, ff // 2),
        (total, ff // 2),
        (ff, width),
        (ff, width),
        (width, ff),
    ]
    if lefts:
        rows = lefts[0].shape[0]
        shapes.append((4, rows, width // 2))
        scratch += [pltpu.VMEM((4, rows, width // 2), BF16), *[dma((4,))] * 3]
    out_shape = [jax.ShapeDtypeStruct(shape, BF16) for shape in shapes]
    return expert_call(
        expert_forward_kernel, 1 + turn, turn, send, [w_in, w_down], prev, lefts, out_shape, scratch, "moe_forward"
    )


def moe_backward(grad_send, saved, turn, prev, lefts):
    experts, block, width = grad_send.shape
    _, _, slope, value, _, slope_peer, value_peer, wgt, wut, wdt, lefts_peer = saved
    total, ff = slope.shape
    parts = len(groups_of(experts, block))
    dma = pltpu.SemaphoreType.DMA
    scratch = [
        pltpu.VMEM((width, ff), BF16),
        *[pltpu.VMEM((total, ff), BF16)] * 2,
        *[pltpu.VMEM((ff, width), BF16)] * 2,
        *[pltpu.VMEM((total, ff // 2), BF16)] * 2,
        *[pltpu.VMEM(grad_send.shape, BF16)] * 4,
        dma((7,)),
        *[dma((experts,))] * 4,
        *[dma((parts,))] * 2,
        dma((7,)),
    ]
    out_shape = [
        jax.ShapeDtypeStruct(grad_send.shape, BF16),
        jax.ShapeDtypeStruct((2, 2, total, ff // 2), BF16),
        jax.ShapeDtypeStruct((2, *grad_send.shape), BF16),
    ]
    if lefts:
        prev = [lefts_peer]
        out_shape.append(jax.ShapeDtypeStruct(lefts_peer.shape, BF16))
        rows = lefts[0].shape[0]
        scratch += [pltpu.VMEM((4, rows, width), BF16), pltpu.VMEM(lefts_peer.shape, BF16), *[dma((4,))] * 3]
    return expert_call(
        expert_backward_kernel,
        3 + turn,
        turn,
        grad_send,
        [wdt, slope, value, wgt, wut, slope_peer, value_peer],
        prev,
        lefts,
        out_shape,
        scratch,
        "moe_backward",
        3 if lefts else 0,
    )


GATE, TOTAL, SCALE, ROUTE, FIRST = 0, 2, 3, 4, 8


class Loads:
    def __init__(self, pairs, sems):
        self.copies = [pltpu.make_async_copy(src, dst, sems.at[i]) for i, (src, dst) in enumerate(pairs)]

    def start(self):
        for copy in self.copies:
            copy.start()

    def wait(self, *which):
        for i in which:
            self.copies[i].wait()


def slots_kernel(experts, capacity, block, order_ref, spots_out, both_out, turned_out, both_turned_out, tally_out, route_out, route_rows):
    seqs, pairs = order_ref.shape
    top = spots_out.shape[1] // both_out.shape[1]
    length = pairs // top
    rows = seqs * length
    slots = spots_out.shape[0]
    expert_id = lax.broadcasted_iota(jnp.int32, (experts, pairs), 0)
    slot_id = lax.broadcasted_iota(jnp.int32, (slots, length), 0)
    row_id = lax.broadcasted_iota(jnp.int32, (pairs, pairs), 0)
    col_id = lax.broadcasted_iota(jnp.int32, (pairs, pairs), 1)
    earlier = (row_id < col_id).astype(F32).astype(BF16)
    route_rows[...] = jnp.zeros_like(route_rows)
    tally = jnp.zeros((experts, 128), F32)
    lane = lax.broadcasted_iota(jnp.int32, (experts, 128), 1)
    for seq in range(seqs):
        order = order_ref[seq : seq + 1, :]
        picked = (expert_id == order).astype(F32)
        place = jnp.sum(dot(picked.astype(BF16), earlier) * picked, axis=0, keepdims=True)
        kept = place < capacity
        target = jnp.where(kept, order * block + seq * capacity + place.astype(jnp.int32), -1)
        taken = jnp.sum(picked * kept.astype(F32), axis=1, keepdims=True)
        whole = jnp.sum(picked, axis=1, keepdims=True)
        tally = tally + jnp.where(lane == 0, taken, jnp.where(lane == 1, whole, 0.0))
        total = jnp.zeros((slots, length), F32)
        for k in range(top):
            part = pl.ds(k * length, length)
            hot = (slot_id == target[:, k * length : (k + 1) * length]).astype(F32)
            spots_out[:, pl.ds(k * rows + seq * length, length)] = hot.astype(BF16)
            total = total + hot
            route_rows[pl.ds(ROUTE + k, 1), pl.ds(seq * length, length)] = order_ref[
                pl.ds(seq, 1), part
            ].astype(F32)
        both_out[:, pl.ds(seq * length, length)] = total.astype(BF16)
    tally_out[...] = tally
    turned_out[...] = jnp.transpose(spots_out[...])
    both_turned_out[...] = jnp.transpose(both_out[...])
    route_out[...] = jnp.transpose(route_rows[...])


def find_slots(order, experts, capacity, block, top):
    seqs, pairs = order.shape
    rows = seqs * pairs // top
    slots = experts * block
    vmem = pl.BlockSpec(memory_space=pltpu.VMEM)
    return pl.pallas_call(
        functools.partial(slots_kernel, experts, capacity, block),
        in_specs=[vmem],
        out_specs=[vmem] * 6,
        out_shape=[
            jax.ShapeDtypeStruct((slots, top * rows), BF16),
            jax.ShapeDtypeStruct((slots, rows), BF16),
            jax.ShapeDtypeStruct((top * rows, slots), BF16),
            jax.ShapeDtypeStruct((rows, slots), BF16),
            jax.ShapeDtypeStruct((experts, 128), F32),
            jax.ShapeDtypeStruct((rows, 128), F32),
        ],
        scratch_shapes=[pltpu.VMEM((128, rows), F32)],
        compiler_params=pltpu.CompilerParams(vmem_limit_bytes=32 << 20),
        name="find_slots",
    )(order)


def route_kernel(cross, experts, gain_ref, router_ref, lanes_ref, *refs):
    prev_ref, refs = (refs[0], refs[1:]) if cross else (None, refs)
    sources, refs = refs[:4], refs[4:]
    result_out, stats_out, send_out = refs[:3]
    held, (low_ref, sems) = refs[3:7], refs[7:]
    mixed, w_out, x, spots = held
    rows, width = x.shape
    step = min(512, width)
    loads = Loads(zip(sources, held), sems)
    loads.start()

    def work():
        loads.wait(0, 1, 2)
        for start in range(0, width, step):
            cols = pl.ds(start, step)
            result_out[:, cols] = x[:, cols] + dot(mixed[...], w_out[:, cols])
        values = result_out[...]
        scale = lax.rsqrt(jnp.mean(values * values, axis=-1, keepdims=True) + EPS)
        normed = values * scale * gain_ref[...]
        low = normed.astype(BF16)
        low_ref[...] = low
        logits = dot(low, router_ref[...]) + dot((normed - low.astype(F32)).astype(BF16), router_ref[...])
        lane = lax.broadcasted_iota(jnp.int32, (rows, 128), 1)
        valid = (lane >= FIRST) & (lane < FIRST + experts)
        logits = jnp.where(valid, logits, -1e30)
        spread = jnp.where(valid, jnp.exp(logits - jnp.max(logits, axis=-1, keepdims=True)), 0.0)
        probs = spread / jnp.sum(spread, axis=-1, keepdims=True)
        routes = lanes_ref[...]
        chosen = [
            jnp.sum(
                jnp.where(lane == routes[:, ROUTE + k : ROUTE + k + 1].astype(jnp.int32) + FIRST, probs, 0.0),
                axis=-1,
                keepdims=True,
            )
            for k in range(2)
        ]
        total = chosen[0] + chosen[1]
        stats = probs + routes
        for at, column in ((GATE, chosen[0] / total), (GATE + 1, chosen[1] / total), (TOTAL, total), (SCALE, scale)):
            stats = jnp.where(lane == at, column, stats)
        stats_out[...] = stats
        loads.wait(3)
        for start in range(0, width, step):
            cols = pl.ds(start, step)
            send_out[:, cols] = dot(spots[...], low_ref[:, cols]).astype(BF16)

    if not cross:
        work()
        return
    decoder = lax.axis_index("half") == 1
    pl.when(decoder)(work)

    @pl.when(jnp.logical_not(decoder))
    def _():
        loads.wait(0, 1, 2, 3)
        result_out[...] = x[...]
        stats_out[...] = prev_ref[...]


def route(gain, router, lanes, prev, sources, experts):
    rows, width = sources[2].shape
    vmem, hbm = pl.BlockSpec(memory_space=pltpu.VMEM), pl.BlockSpec(memory_space=pl.ANY)
    lead = [] if prev is None else [prev]
    return pl.pallas_call(
        functools.partial(route_kernel, prev is not None, experts),
        in_specs=[vmem] * (3 + len(lead)) + [hbm] * 4,
        out_specs=[vmem] * 3,
        out_shape=[
            jax.ShapeDtypeStruct((rows, width), F32),
            jax.ShapeDtypeStruct((rows, 128), F32),
            jax.ShapeDtypeStruct((sources[3].shape[0], width), BF16),
        ],
        scratch_shapes=[
            *(pltpu.VMEM(a.shape, a.dtype) for a in sources),
            pltpu.VMEM((rows, width), BF16),
            pltpu.SemaphoreType.DMA((4,)),
        ],
        compiler_params=pltpu.CompilerParams(vmem_limit_bytes=48 << 20),
        name="route",
    )(gain, router, lanes, *lead, *sources)


def norm_back_rows(values, scale, gain, grad):
    unit = values * scale
    pushed = grad * gain
    back = scale * (pushed - unit * jnp.mean(pushed * unit, axis=-1, keepdims=True))
    return back, jnp.sum(grad * unit, axis=0, keepdims=True)


def leave_kernel(cross, experts, count, info, stats_ref, gain_ref, router_ref, *refs):
    bias_ref, refs = (None, refs) if cross else (refs[0], refs[1:])
    sources, refs = refs[:count], refs[count:]
    grad_out, branch_out, dgain_out, dlog_out, dq_out, last_out = refs[:6]
    held, (dmixed, mask_ref, sems) = refs[6 : 6 + count], refs[6 + count :]
    back, both, grad, results, x, w_out, a, log = held[:8]
    seqs, length, _ = mask_ref.shape
    width = x.shape[1]
    loads = Loads(zip(sources, held), sems)
    if cross:
        q_ref, kv = held[8:]
        k_ref, v_ref = kv.at[:, pl.ds(0, width)], kv.at[:, pl.ds(width, width)]
        dkv_out, shift, diag_out = last_out, 0, None
    else:
        qkv, ready = held[8:]
        q_ref, k_ref, v_ref = (qkv.at[:, pl.ds(i * width, width)] for i in range(3))
        dkv_out, shift, diag_out = dq_out, width, last_out

    def leave():
        loads.wait(0, 1, 2, 3, 4)
        dgain = jnp.zeros((1, width), F32)
        lane = lax.broadcasted_iota(jnp.int32, (length, 128), 1)
        for seq in range(seqs):
            rows = pl.ds(seq * length, length)
            stats = stats_ref[rows, :]
            gates = [stats[:, GATE + k : GATE + k + 1] for k in range(2)]
            hots = [
                (lane == stats[:, ROUTE + k : ROUTE + k + 1].astype(jnp.int32) + FIRST).astype(F32)
                for k in range(2)
            ]
            probs = jnp.where((lane >= FIRST) & (lane < FIRST + experts), stats, 0.0)
            g = grad[rows, :]
            dgates = [
                jnp.sum(g * results[k, rows, :].astype(F32), axis=-1, keepdims=True) for k in range(2)
            ]
            shared = dgates[0] * gates[0] + dgates[1] * gates[1]
            dprobs = sum((dgates[k] - shared) / stats[:, TOTAL : TOTAL + 1] * hots[k] for k in range(2))
            dlog = probs * (dprobs - jnp.sum(dprobs * probs, axis=-1, keepdims=True))
            dlog_out[rows, :] = dlog
            dnormed = dot(both[rows, :], back[...]) + dot(dlog.astype(BF16), router_ref[...], NT)
            dx, part = norm_back_rows(x[rows, :], stats[:, SCALE : SCALE + 1], gain_ref[...], dnormed)
            dgain = dgain + part
            grad_out[rows, :] = g + dx
        dgain_out[...] = jnp.broadcast_to(dgain, dgain_out.shape)

    def attention():
        loads.wait(5)
        branch_out[...] = grad_out[...].astype(BF16)
        step = min(512, width)
        for start in range(0, width, step):
            cols = pl.ds(start, step)
            dmixed[:, cols] = dot(branch_out[...], w_out[cols, :], NT).astype(BF16)
        loads.wait(*((6, 7, 8, 9) if cross else (6, 7, 8)))
        attend_back(
            info, bias_ref, q_ref, k_ref, v_ref, a, log, dmixed, dq_out, dkv_out, shift, diag_out, mask_ref
        )

    decoder = lax.axis_index("half") == 1
    if cross:

        @pl.when(decoder)
        def _():
            loads.start()
            leave()
            attention()

    else:
        loads.start()

        @pl.when(jnp.logical_not(decoder))
        def _():
            leave()
            loads.wait(9)

        @pl.when(decoder)
        def _():
            loads.wait(0, 1, 2, 3, 4, 9)
            grad_out[...] = ready[...]

        attention()


def leave(info, stats, gain, router, bias, sources, experts, length):
    cross = bias is None
    rows, width = sources[4].shape
    seqs = rows // length
    vmem, hbm = pl.BlockSpec(memory_space=pltpu.VMEM), pl.BlockSpec(memory_space=pl.ANY)
    lead = [] if cross else [bias]
    out_shape = [
        jax.ShapeDtypeStruct((rows, width), F32),
        jax.ShapeDtypeStruct((rows, width), BF16),
        jax.ShapeDtypeStruct((8, width), F32),
        jax.ShapeDtypeStruct((rows, 128), F32),
        jax.ShapeDtypeStruct((rows, width if cross else 3 * width), BF16),
        jax.ShapeDtypeStruct((rows, 2 * width), BF16) if cross else jax.ShapeDtypeStruct(bias.shape, F32),
    ]
    return pl.pallas_call(
        functools.partial(leave_kernel, cross, experts, len(sources)),
        in_specs=[pl.BlockSpec(memory_space=pltpu.SMEM)] + [vmem] * (3 + len(lead)) + [hbm] * len(sources),
        out_specs=[vmem] * 6,
        out_shape=out_shape,
        scratch_shapes=[
            *(pltpu.VMEM(a.shape, a.dtype) for a in sources),
            pltpu.VMEM((rows, width), BF16),
            pltpu.VMEM((seqs, length, length), F32),
            pltpu.SemaphoreType.DMA((len(sources),)),
        ],
        compiler_params=pltpu.CompilerParams(vmem_limit_bytes=56 << 20),
        name="leave_cross" if cross else "leave_self",
    )(info, stats, gain, router, *lead, *sources)


def memory_kernel(stats_ref, gain_ref, *refs):
    sources, refs = refs[:5], refs[5:]
    grad_out, send_out, dgain_out = refs[:3]
    held, (dnormed, spread, sems) = refs[3:8], refs[8:]
    dmemory, w, x, cotangent, spots = held
    rows, width = x.shape

    @pl.when(lax.axis_index("half") == 0)
    def _():
        loads = Loads(zip(sources, held), sems)
        loads.start()
        loads.wait(0, 1)
        step = min(512, width)
        for start in range(0, width, step):
            cols = pl.ds(start, step)
            dnormed[:, cols] = dot(dmemory[...], w[cols, :], NT)
        loads.wait(2, 3)
        scale = lax.rsqrt(jnp.mean(x[...] * x[...], axis=-1, keepdims=True) + EPS)
        dx, dgain = norm_back_rows(x[...], scale, gain_ref[...], dnormed[...])
        dgain_out[...] = jnp.broadcast_to(dgain, dgain_out.shape)
        grad = cotangent[...].astype(F32) + dx
        grad_out[...] = grad
        for k in range(2):
            gate = stats_ref[:, GATE + k : GATE + k + 1]
            spread[pl.ds(k * rows, rows), :] = (gate * grad).astype(BF16)
        loads.wait(4)
        for start in range(0, width, step):
            cols = pl.ds(start, step)
            send_out[:, cols] = dot(spots[...], spread[:, cols]).astype(BF16)


def memory_gradient(stats, gain, sources):
    rows, width = sources[2].shape
    vmem, hbm = pl.BlockSpec(memory_space=pltpu.VMEM), pl.BlockSpec(memory_space=pl.ANY)
    return pl.pallas_call(
        memory_kernel,
        in_specs=[vmem] * 2 + [hbm] * len(sources),
        out_specs=[vmem] * 3,
        out_shape=[
            jax.ShapeDtypeStruct((rows, width), F32),
            jax.ShapeDtypeStruct((sources[4].shape[0], width), BF16),
            jax.ShapeDtypeStruct((8, width), F32),
        ],
        scratch_shapes=[
            *(pltpu.VMEM(a.shape, a.dtype) for a in sources),
            pltpu.VMEM((rows, width), F32),
            pltpu.VMEM((2 * rows, width), BF16),
            pltpu.SemaphoreType.DMA((len(sources),)),
        ],
        compiler_params=pltpu.CompilerParams(vmem_limit_bytes=48 << 20),
        name="memory_gradient",
    )(stats, gain, *sources)


def dense_kernel(stages, chunk, lag, *refs):
    sources, small_ref = refs[:11], refs[11]
    out_refs, small_out, small_in = refs[12:15], refs[15], refs[16]
    held, xt_ref, refs = refs[17:28], refs[28], refs[29:]
    x_refs, own_refs, peer_refs, xp = held[:4], held[4:7], held[7:10], held[10]
    sums, parts = refs[:stages], refs[stages : 2 * stages]
    ss, rs, sk, rk, sl = refs[2 * stages :]
    counts = [ref.shape[1] // chunk for ref in own_refs]
    starts = [sum(counts[:i]) for i in range(3)]
    chunks = sum(counts)
    per_cross = counts[2] // 2
    rows, half = xp.shape[1:]
    dp, me = lax.axis_index("dp"), lax.axis_index("expert")
    peer = {"dp": 1 - dp}
    partners = [flipped(me, k) for k in range(stages)]
    bits = [me // (1 << k) % 2 for k in range(stages)]
    load = [pltpu.make_async_copy(sources[i], held[i], sl.at[i]) for i in range(11)]
    for i in (10, 2, 3, 6, 9, 0, 4, 7, 1, 5, 8):
        load[i].start()
    greet([peer] + [{"expert": p} for p in partners])

    def send_small(step):
        src = small_ref if step == 0 else small_out.at[step - 1]
        device = peer if step == 0 else {"expert": partners[stages - step]}
        return remote(src, small_in.at[step], ss.at[step], rs.at[step], device)

    def order(k, odd):
        return 1 - k if odd and k < 2 else k

    def send_part(k, c, odd):
        bit = order(k, odd)
        other = 1 - bits[bit]
        src = sums[0].at[c, :, :, other] if k == 0 and not odd else sums[k].at[c, :, other]
        return remote(src, parts[k].at[c], sk.at[k, c], rk.at[k, c], {"expert": partners[bit]})

    def turn_x(g):
        load[g].wait()
        cols = pl.ds(pl.multiple_of(dp * half, half), half)
        xt_ref[g, :, :rows] = jnp.transpose(x_refs[g][:, cols])
        xt_ref[g, :, rows:] = jnp.transpose(xp[g])

    def small_step(j):
        send_small(j).wait_recv()
        own = small_ref[...] if j == 0 else small_out[j - 1]
        small_out[j] = own + small_in[j]
        if j < stages:
            send_small(j + 1).start()

    send_small(0).start()
    load[10].wait()
    last = counts[2]
    early = chunks - last
    per = chunks // last

    def produce(i, carry):
        c = jnp.where(lax.rem(i, per) == 0, early + i // per, i - i // per - 1)
        for g in range(3):

            @pl.when(c == starts[g])
            def _(g=g):
                load[4 + g].wait()
                load[7 + g].wait()
                for x in (g,) if g < 2 else (2, 3):
                    turn_x(x)

            @pl.when((c >= starts[g]) & (c < starts[g] + counts[g]))
            def _(g=g):
                at = c - starts[g]
                cols = pl.ds(pl.multiple_of(at * chunk, chunk), chunk)
                which = g if g < 2 else 2 + at // per_cross
                total = dot(xt_ref[which, :, :rows], own_refs[g][:, cols])
                total += dot(xt_ref[which, :, rows:], peer_refs[g][:, cols])
                sums[0][c] = total.astype(BF16).reshape(sums[0].shape[1:])
                send_part(0, c, g == 2).start()

        for j in range(2):

            @pl.when(i == 3 + 6 * j)
            def _(j=j):
                small_step(j)

        return carry

    lax.fori_loop(0, chunks, produce, 0)

    def advance(k, c, odd):
        send_part(k, c, odd).wait_recv()
        bit = bits[order(k, odd)]
        mine = sums[0][c, :, :, bit] if k == 0 and not odd else sums[k][c, :, bit]
        total = mine.astype(F32) + parts[k][c].astype(F32)
        if k + 1 < stages:
            sums[k + 1][c] = total.astype(BF16).reshape(sums[k + 1].shape[1:])
            send_part(k + 1, c, odd).start()
            return
        total = total.reshape(total.shape[-2:])
        for g in (2,) if odd else (0, 1):

            @pl.when((c >= starts[g]) & (c < starts[g] + counts[g]))
            def _(g=g):
                at = pl.multiple_of((c - starts[g]) * chunk, chunk)
                out_refs[g][:, pl.ds(at, chunk)] = total

    def reduce(i, carry):
        @pl.when((lax.rem(i, 2) == 1) & (i // 2 < last))
        def _():
            advance(0, early + i // 2, True)

        for k in range(stages):
            c = i - lag * k

            @pl.when((c >= 0) & (c < early))
            def _(k=k, c=c):
                advance(k, c, False)

        for k in range(1, stages):
            c = i - 1 - lag * (k - 1)

            @pl.when((c >= early) & (c < chunks))
            def _(k=k, c=c):
                advance(k, c, True)

        for j in range(2, stages + 1):

            @pl.when(i == 3 * j - 2)
            def _(j=j):
                small_step(j)

        return carry

    lax.fori_loop(0, chunks + 1 + lag * (stages - 2), reduce, 0)

    def finish(c, carry, odd):
        for k in range(stages):
            send_part(k, c, odd).wait_send()
        return carry

    lax.fori_loop(0, early, functools.partial(finish, odd=False), 0)
    lax.fori_loop(early, chunks, functools.partial(finish, odd=True), 0)
    for j in range(stages + 1):
        send_small(j).wait_send()


def over_dp(array):
    return lax.ppermute(array, "dp", [(0, 1), (1, 0)])


def dense_gradients(lefts, lefts_peer, own, peer, small, experts):
    chunk = 512
    rows, width = lefts[0].shape
    half_rows = width // 2
    chunks = sum(y.shape[1] for y in own) // chunk
    stages = experts.bit_length() - 1
    keep = half_rows // experts
    vmem, hbm = pl.BlockSpec(memory_space=pltpu.VMEM), pl.BlockSpec(memory_space=pl.ANY)
    dma = pltpu.SemaphoreType.DMA
    sources = [*lefts, *own, *peer, lefts_peer]
    blocks = [(experts // 4, 2, 2)] + [(experts >> (k + 1), 2) for k in range(1, stages)]
    halved = [(experts // 4, 2)] + [(experts >> (k + 1),) for k in range(1, stages)]
    scratch = [pltpu.VMEM((stages + 1, *small.shape), F32)]
    scratch += [pltpu.VMEM(a.shape, BF16) for a in sources]
    scratch += [pltpu.VMEM((4, half_rows, 2 * rows), BF16)]
    scratch += [pltpu.VMEM((chunks, *b, keep, chunk), BF16) for b in blocks + halved]
    scratch += [dma((stages + 1,)), dma((stages + 1,)), dma((stages, chunks)), dma((stages, chunks))]
    scratch += [dma((len(sources),))]
    *outs, sums = pl.pallas_call(
        functools.partial(dense_kernel, stages, chunk, 2),
        in_specs=[hbm] * len(sources) + [vmem],
        out_specs=[vmem] * 4,
        out_shape=[
            *(jax.ShapeDtypeStruct((keep, y.shape[1]), F32) for y in own),
            jax.ShapeDtypeStruct((stages + 1, *small.shape), F32),
        ],
        scratch_shapes=scratch,
        compiler_params=pltpu.CompilerParams(
            collective_id=0, has_side_effects=True, vmem_limit_bytes=56 << 20
        ),
        name="dense_gradients",
    )(*sources, small)
    return outs, sums[stages]


def product_kernel(x_ref, y_ref, out_ref):
    out_ref[...] = dot(x_ref[...], y_ref[...].reshape(y_ref.shape[-2:]), TN).reshape(out_ref.shape)


def expert_gradients(rows, mixed, hidden, grads):
    total, width = rows.shape
    span = hidden.shape[1]
    tile = 256
    params = pltpu.CompilerParams(vmem_limit_bytes=40 << 20)
    din = pl.pallas_call(
        product_kernel,
        grid=(2, width // tile),
        in_specs=[
            pl.BlockSpec((total, tile), lambda g, i: (0, i)),
            pl.BlockSpec((1, total, span), lambda g, i: (g, 0, 0)),
        ],
        out_specs=pl.BlockSpec((1, tile, span), lambda g, i: (g, i, 0)),
        out_shape=jax.ShapeDtypeStruct((2, width, span), F32),
        compiler_params=params,
        name="expert_in_gradient",
    )(rows, mixed)
    ddown = pl.pallas_call(
        product_kernel,
        grid=(pl.cdiv(span, tile),),
        in_specs=[
            pl.BlockSpec((total, tile), lambda i: (0, i)),
            pl.BlockSpec((total, width), lambda i: (0, 0)),
        ],
        out_specs=pl.BlockSpec((tile, width), lambda i: (i, 0)),
        out_shape=jax.ShapeDtypeStruct((span, width), F32),
        compiler_params=params,
        name="expert_out_gradient",
    )(hidden, grads)
    return din, ddown


def body(
    tokens,
    cotangent,
    lengths,
    routes,
    self_qkv,
    self_out,
    cross_weights,
    router,
    gains,
    bias_table,
    expert_in,
    expert_out,
):
    _, seqs, length, width = tokens.shape
    heads = H
    experts = router.shape[2]
    top = routes.shape[3]
    capacity = (5 * top * length + 4 * experts - 1) // (4 * experts)
    block_rows = -(-seqs * capacity // 16) * 16
    rows = seqs * length
    slots = experts * block_rows
    half_index = lax.axis_index("half")
    decoder = half_index == 1
    wqkv, wout, wcross, wrouter, gain = (
        self_qkv[0],
        self_out[0],
        cross_weights[0],
        router[0],
        gains[0],
    )
    w_in, w_down = expert_in[0, 0], expert_out[0, 0]

    column = np.arange(2 * length)
    entry = np.arange(BUCKETS * heads)
    hot, hot_back = (
        jnp.where(
            decoder,
            *(
                (entry[:, None] // heads == bucket[None, :]).astype(np.float32)
                for bucket in reversed(diagonal_buckets(diff))
            ),
        )
        for diff in (np.where(column < length, column, column - 2 * length), column - length + 1)
    )
    own_head = entry[None, :] % heads == np.arange(heads)[:, None]
    bias = lax.dot_general(
        jnp.where(own_head, bias_table, 0.0),
        hot,
        (((1,), (0,)), ((), ())),
        precision=lax.Precision.HIGHEST,
        preferred_element_type=F32,
    )
    own_lengths = jnp.where(decoder, lengths[1], lengths[0])
    self_info = jnp.concatenate([own_lengths, half_index[None]]).astype(jnp.int32)
    cross_info = jnp.concatenate([lengths[0], jnp.zeros((1,), jnp.int32)]).astype(jnp.int32)

    order = jnp.transpose(routes[0], (0, 2, 1)).reshape(seqs, top * length)
    spots, both_spots, stacked, both, tally, route_lanes = find_slots(order, experts, capacity, block_rows, top)
    tallies = jnp.concatenate([tally[:, 0], tally[:, 1] - tally[:, 0]])
    router_wide = jnp.pad(wrouter, ((0, 0), (FIRST, 128 - FIRST - experts)))

    def fetch(returned):
        flat = returned.reshape(slots, width)
        return dot(stacked, flat).astype(BF16).reshape(top, rows, width)

    def combine(values, stats, results):
        return values + sum(stats[:, GATE + k : GATE + k + 1] * results[k] for k in range(top))

    values = tokens[0].reshape(rows, width).astype(F32)
    normed, scale0 = norm_parts(values, gain[0])
    low0 = normed.astype(BF16)
    qkv = dot(low0, wqkv).astype(BF16)
    mixed0, log0 = attend(self_info, bias, qkv, qkv, (0, 1, 2), length, width)
    first, stats, send = route(gain[1:2], router_wide, route_lanes, None, [mixed0, wout, values, both_spots], experts)

    send_shape = (experts, block_rows, width)
    saved = moe_forward(send.reshape(send_shape), w_in, w_down, 0, None, [], rows)
    final_enc = combine(first, stats, fetch(saved[0]))
    normed, scale_m = norm_parts(final_enc, gain[2])
    low_m = normed.astype(BF16)
    memory = dot(low_m, wcross).astype(BF16)
    names = ("half", "dp", "expert")
    forward_pairs, back_pairs = half_pairs(lax.axis_size("dp") * lax.axis_size("expert"))
    memory = lax.ppermute(memory, names, forward_pairs)

    normed, scale_c = norm_parts(first, gain[2])
    low_c = normed.astype(BF16)
    query = dot(low_c, wcross[:, :width]).astype(BF16)
    mixed_c, log_c = attend(cross_info, None, query, memory, (0, 0, 1), length, width)
    second, stats, send = route(
        gain[1:2], router_wide, route_lanes, stats, [mixed_c, wcross[:, width:], first, both_spots], experts
    )

    lefts = [low0, mixed0, jnp.where(decoder, low_c, low_m), jnp.where(decoder, mixed_c, low_m)]
    saved = moe_forward(send.reshape(send_shape), w_in, w_down, 1, saved, lefts, rows)
    results = fetch(saved[0])
    final = combine(second, stats, results)
    outputs = final.astype(BF16)

    grad_dec = cotangent[0].reshape(rows, width)
    spread = [(stats[:, GATE + k : GATE + k + 1] * grad_dec.astype(F32)).astype(BF16) for k in range(top)]
    grad_send = dot(spots, jnp.concatenate(spread)).astype(BF16)
    *kept_from, lefts_peer = moe_backward(
        grad_send.reshape(experts, block_rows, width), saved, 1, None, lefts
    )

    grad_second, dbranch_c, dgain_moe_dec, dlog_dec, dquery, dmemory = leave(
        cross_info,
        stats,
        gain[1:2],
        router_wide,
        None,
        [
            kept_from[0].reshape(slots, width),
            both,
            grad_dec.astype(F32),
            results,
            second,
            wcross[:, width:],
            mixed_c,
            log_c,
            query,
            memory,
        ],
        experts,
        length,
    )
    dmemory = lax.ppermute(dmemory, names, back_pairs)
    dnormed = dot(dquery, wcross[:, :width], NT)
    dvalues, dgain_c = norm_back(first, scale_c, gain[2], dnormed)
    grad_first_dec = grad_second + dvalues

    grad, grad_send, dgain_m = memory_gradient(
        stats, gain[2:3], [dmemory, wcross, final_enc, grad_dec, spots]
    )
    back, mixed_grads, all_grad = moe_backward(
        grad_send.reshape(experts, block_rows, width), saved, 0, kept_from, []
    )
    all_rows, hidden = saved[1], saved[4]
    grad_first, dbranch, dgain_moe, dlog, dqkv_rows, diag = leave(
        self_info,
        stats,
        gain[1:2],
        router_wide,
        bias,
        [
            back.reshape(slots, width),
            both,
            grad,
            results,
            second,
            wout,
            mixed0,
            log0,
            qkv,
            grad_first_dec,
        ],
        experts,
        length,
    )
    dlog = jnp.where(decoder, dlog_dec, dlog)[:, FIRST : FIRST + experts]
    dgain_moe = jnp.where(decoder, dgain_moe_dec[0], dgain_moe[0])
    drouter = lax.dot_general(
        second * stats[:, SCALE : SCALE + 1] * gain[1],
        dlog,
        TN,
        precision=lax.Precision.HIGHEST,
        preferred_element_type=F32,
    )
    dnormed = dot(dqkv_rows, wqkv, NT)
    dvalues, dgain_self = norm_back(values, scale0, gain[0], dnormed)
    d_tokens = (grad_first + dvalues).astype(BF16)
    by_entry = lax.dot_general(
        diag, hot_back, NT, precision=lax.Precision.HIGHEST, preferred_element_type=F32
    )
    dtable = jnp.sum(jnp.where(own_head, by_entry, 0.0), axis=0)

    cross_grad = jnp.where(decoder, jnp.concatenate([dquery, dbranch_c], axis=1), dmemory)
    own_grads = (dqkv_rows, dbranch, cross_grad)
    peer_grads = tuple(map(over_dp, own_grads))
    places = 2 * experts
    own = width // places
    extra = jnp.concatenate([dtable.reshape(places, -1), tallies.reshape(places, 1)], axis=1)
    extra = jnp.pad(extra, ((0, 0), (0, -extra.shape[1] % own)))
    small = jnp.concatenate(
        [
            jnp.transpose(drouter),
            jnp.stack([dgain_self, dgain_moe, jnp.where(decoder, dgain_c, dgain_m[0])]),
            jnp.swapaxes(extra.reshape(places, -1, own), 0, 1).reshape(-1, width),
        ]
    )
    small = jnp.pad(small, ((0, -small.shape[0] % 8), (0, 0)))
    (dqkv, dout, dcross), small = dense_gradients(
        lefts, lefts_peer, own_grads, peer_grads, small, experts
    )
    place = lax.axis_index("dp") * experts + lax.axis_index("expert")
    mine = lax.dynamic_slice_in_dim(small, place * own, own, 1)
    tail = mine[experts + 3 :].reshape(-1)
    own_table = dtable.shape[0] // places
    d_table = tail[:own_table]
    counts = tail[own_table].astype(jnp.int32)

    ff_half = hidden.shape[-1]
    din, ddown = expert_gradients(
        all_rows.reshape(-1, width),
        mixed_grads.reshape(2, -1, ff_half),
        hidden.reshape(-1, ff_half),
        all_grad.reshape(-1, width),
    )
    return (
        outputs.reshape(1, seqs, length, width),
        d_tokens.reshape(1, seqs, length, width),
        dqkv[None],
        dout[None],
        dcross[None],
        jnp.transpose(mine[:experts])[None],
        mine[experts : experts + 3][None],
        d_table[None],
        din[None, None],
        ddown[None, None],
        counts.reshape(1, 1, 1),
    )


def half_pairs(count):
    return (
        [(i, count + i) for i in range(count)],
        [(count + i, i) for i in range(count)],
    )


def solution(mesh):
    placed = (
        P("half", ("dp", "expert"), None, None),
        P("half", ("dp", "expert"), None, None),
        P(None, ("dp", "expert")),
        P("half", ("dp", "expert"), None, None),
        P("half", None, None),
        P("half", None, None),
        P("half", None, None),
        P("half", None, None),
        P("half", None, None),
        P("half", None),
        P("half", "expert", None, None, None),
        P("half", "expert", None, None),
    )
    return jax.shard_map(
        body,
        mesh=mesh,
        in_specs=placed,
        out_specs=(
            P("half", ("dp", "expert"), None, None),
            P("half", ("dp", "expert"), None, None),
            P("half", ("dp", "expert"), None),
            P("half", ("dp", "expert"), None),
            P("half", ("dp", "expert"), None),
            P("half", ("dp", "expert"), None),
            P("half", None, ("dp", "expert")),
            P("half", ("dp", "expert")),
            P("half", "expert", None, None, "dp"),
            P("half", "expert", "dp", None),
            P("half", "dp", "expert"),
        ),
        check_vma=False,
    )
```

```python
import functools

import jax
import jax.numpy as jnp
import numpy as np
from jax import lax
from jax.experimental import pallas as pl
from jax.experimental.pallas import tpu as pltpu
from jax.sharding import PartitionSpec as P

H = 16
BUCKETS = 32
EPS = 1e-06
ENC_STEPS = (12, 16, 23, 32, 46, 64, 91)
DEC_STEPS = (19, 21, 24, 27, 31, 35, 40, 46, 52, 59, 67, 77, 87, 99, 113)
F32 = jnp.float32
BF16 = jnp.bfloat16
MESH = pl.DeviceIdType.MESH
NT = (((1,), (1,)), ((), ()))
TN = (((0,), (0,)), ((), ()))


def dot(a, b, dims=(((1,), (0,)), ((), ()))):
    return lax.dot_general(a, b, dims, preferred_element_type=F32)


def diagonal_buckets(diff):
    apart = np.abs(diff)
    coarse = 8 + sum((apart >= step).astype(np.int32) for step in ENC_STEPS)
    enc = np.where(apart < 8, apart, coarse) + 16 * (diff > 0)
    behind = np.maximum(-diff, 0)
    coarse = 16 + sum((behind >= step).astype(np.int32) for step in DEC_STEPS)
    dec = np.where(behind < 16, behind, coarse)
    return enc.astype(np.int32), dec.astype(np.int32)


def diagonals(bias_ref, head, length):
    row = jnp.broadcast_to(bias_ref[pl.ds(head, 1), :], (length, 2 * length))
    return pltpu.roll(row, 0, 1, stride=1, stride_axis=0)[:, :length]


def fill_masks(info, mask_ref):
    seqs, length, _ = mask_ref.shape
    row_id = lax.broadcasted_iota(jnp.int32, (length, length), 0)
    col_id = lax.broadcasted_iota(jnp.int32, (length, length), 1)
    reach = jnp.where(info[seqs] > 0, row_id, length)
    for seq in range(seqs):
        allowed = (col_id < info[seq]) & (col_id <= reach)
        mask_ref[seq] = jnp.where(allowed, 0.0, -1000000000.0)


def attend(info, bias_ref, q_ref, k_ref, v_ref, out_ref, log_ref, mask_ref):
    has_bias = bias_ref is not None
    seqs, length, _ = mask_ref.shape
    low = lax.broadcasted_iota(jnp.int32, (length, 128), 1) < 64
    fill_masks(info, mask_ref)

    @pl.loop(0, q_ref.shape[1] // 128, unroll=True)
    def _(pair):
        cols = pl.ds(pl.multiple_of(pair * 128, 128), 128)
        biases = [diagonals(bias_ref, 2 * pair + side, length) if has_bias else 0.0 for side in range(2)]
        for seq in range(seqs):
            rows = pl.ds(seq * length, length)
            q, k, v = q_ref[rows, cols] * 0.125, k_ref[rows, cols], v_ref[rows, cols]
            mixed, peaks = [], []
            for side in range(2):
                mine = low if side == 0 else jnp.logical_not(low)
                part = jnp.where(mine, q, jnp.zeros_like(q))
                scores = dot(part, k, NT) + (mask_ref[seq] + biases[side])
                peak = jnp.max(scores, axis=-1, keepdims=True)
                spread = jnp.exp(scores - peak).astype(BF16)
                mixed.append(dot(spread, jnp.where(mine, v, jnp.ones_like(v))))
                peaks.append(peak)
            total = pltpu.roll(jnp.where(low, mixed[1], mixed[0]), 64, 1)
            out_ref[rows, cols] = (jnp.where(low, mixed[0], mixed[1]) / total).astype(BF16)
            log_ref[rows, cols] = jnp.where(low, peaks[0], peaks[1]) + jnp.log(total)


def attend_back(info, bias_ref, q_ref, k_ref, v_ref, a_ref, log_ref, g_ref, dq_ref, dkv_ref, shift, diag_ref, mask_ref):
    has_bias = bias_ref is not None
    seqs, length, _ = mask_ref.shape
    width = q_ref.shape[1]
    low = lax.broadcasted_iota(jnp.int32, (length, 128), 1) < 64
    fill_masks(info, mask_ref)
    if has_bias:
        row_id = lax.broadcasted_iota(jnp.int32, (length, length), 0)
        col_id = lax.broadcasted_iota(jnp.int32, (length, length), 1)
        flip = (row_id + col_id == length - 1).astype(F32).astype(BF16)

    @pl.loop(0, width // 128, unroll=True)
    def _(pair):
        cols = pl.ds(pl.multiple_of(pair * 128, 128), 128)
        kcols = pl.ds(pl.multiple_of(shift + pair * 128, 128), 128)
        vcols = pl.ds(pl.multiple_of(shift + width + pair * 128, 128), 128)
        biases = [diagonals(bias_ref, 2 * pair + side, length) if has_bias else 0.0 for side in range(2)]
        sums = [0.0, 0.0]
        for seq in range(seqs):
            rows = pl.ds(seq * length, length)
            q, k, v, g = q_ref[rows, cols] * 0.125, k_ref[rows, cols], v_ref[rows, cols], g_ref[rows, cols]
            logs = log_ref[rows, cols]
            turned = pltpu.roll(logs, 64, 1)
            product = g.astype(F32) * a_ref[rows, cols].astype(F32)
            minus = (-pltpu.roll(product, 64, 1)).astype(BF16)
            scaled = k * 0.125
            dqs, dks, dvs = [], [], []
            for side in range(2):
                mine = low if side == 0 else jnp.logical_not(low)
                part = jnp.where(mine, q, jnp.zeros_like(q))
                scores = dot(part, k, NT) + (mask_ref[seq] + biases[side])
                probs = jnp.exp(scores - jnp.where(mine, logs, turned))
                dvs.append(dot(probs.astype(BF16), g, TN))
                centred = dot(jnp.where(mine, g, minus), jnp.where(mine, v, jnp.ones_like(v)), NT)
                dlow = (probs * centred).astype(BF16)
                dqs.append(dot(dlow, scaled))
                dks.append(dot(dlow, q, TN))
                if has_bias:
                    sums[side] = sums[side] + dlow.astype(F32)
            dq_ref[rows, cols] = jnp.where(low, dqs[0], dqs[1]).astype(BF16)
            dkv_ref[rows, kcols] = jnp.where(low, dks[0], dks[1]).astype(BF16)
            dkv_ref[rows, vcols] = jnp.where(low, dvs[0], dvs[1]).astype(BF16)
        if has_bias:
            for side in range(2):
                upside = dot(flip, sums[side].astype(BF16))
                wide = jnp.concatenate([upside, jnp.zeros((length, length), F32)], axis=1)
                turned = pltpu.roll(wide, 0, 1, stride=1, stride_axis=0)
                diag_ref[pl.ds(2 * pair + side, 1), :] = jnp.sum(turned, axis=0, keepdims=True)


def norm_parts(values, gain):
    scale = lax.rsqrt(jnp.mean(values * values, axis=-1, keepdims=True) + EPS)
    return values * scale * gain, scale


def norm_back(values, scale, gain, grad):
    unit = values * scale
    gain_grad = jnp.sum(grad * unit, axis=0)
    pushed = grad * gain
    back = scale * (pushed - unit * jnp.mean(pushed * unit, axis=-1, keepdims=True))
    return back, gain_grad


def gelu_parts(gate):
    c, a = 0.7978845608028654, 0.044715
    square = gate * gate
    u = 0.5 + 0.5 * jnp.tanh(gate * (c + c * a * square))
    slope = u * (1.0 + (gate * (2.0 * c + 6.0 * c * a * square)) * (1.0 - u))
    return gate * u, slope


def flipped(value, bit):
    step = 1 << bit
    return value + step * (1 - 2 * (value // step % 2))


def crossed(value, other):
    for bit in range(other.bit_length()):
        if other >> bit & 1:
            value = flipped(value, bit)
    return value


def greet(partners):
    barrier = pltpu.get_barrier_semaphore()
    for partner in partners:
        pl.semaphore_signal(barrier, inc=1, device_id=partner, device_id_type=MESH)
    pl.semaphore_wait(barrier, len(partners))


def remote(src, dst, out_sem, in_sem, device):
    return pltpu.make_async_remote_copy(
        src_ref=src,
        dst_ref=dst,
        send_sem=out_sem,
        recv_sem=in_sem,
        device_id=device,
        device_id_type=MESH,
    )


def tile_loop(count, step, body):
    @pl.loop(0, count // step)
    def _(i):
        body(pl.multiple_of(i * step, step), step)

    if count % step:
        body(count // step * step, count % step)


def groups_of(experts, block):
    size = 1
    while size * 2 * block <= 320 and size * 2 <= experts:
        size *= 2
    if experts <= 2 * size:
        half = max(size // 2, 1)
        return [(0, size), *((k, half) for k in range(size, experts, half))]
    return [(k, size) for k in range(0, experts, size)]


class Turn:
    def __init__(self, experts, block, there, home):
        self.me, self.dp = lax.axis_index("expert"), lax.axis_index("dp")
        self.experts, self.block = experts, block
        self.peer = {"dp": 1 - self.dp}
        self.groups = groups_of(experts, block)
        self.there_refs, self.home_refs = there, home

    def greet(self):
        greet([{"expert": crossed(self.me, k)} for k in range(1, self.experts)] + [self.peer])

    def there(self, k):
        src, dst, out_sems, in_sems = self.there_refs
        partner = crossed(self.me, k)
        return remote(src.at[partner], dst.at[self.me], out_sems.at[k], in_sems.at[k], {"expert": partner})

    def home(self, k):
        src, dst, out_sems, in_sems = self.home_refs
        partner = crossed(self.me, k)
        return remote(src.at[partner], dst.at[self.me], out_sems.at[k], in_sems.at[k], {"expert": partner})

    def arrive(self, first, size):
        for k in range(max(first, 1), first + size):
            self.there(k).wait_recv()

    def base(self, first, size):
        return crossed(self.me // size, first // size) * size

    def spans(self, first, size):
        base = self.base(first, size)
        rows = pl.ds(pl.multiple_of(base * self.block, size * self.block), size * self.block)
        return pl.ds(base, size), rows


class Lefts:
    def __init__(self, refs, out, scratch, width):
        self.refs, self.out = refs, out
        self.held, self.stage, self.loaded, self.sent, self.came = scratch
        self.half, self.slots = width // 2, self.held.shape[0]
        self.dp = lax.axis_index("dp")

    def fetch(self, i):
        return pltpu.make_async_copy(self.refs[i], self.held.at[i % self.slots], self.loaded.at[i])

    def copy(self, i):
        return remote(self.stage.at[i], self.out.at[i], self.sent.at[i], self.came.at[i], {"dp": 1 - self.dp})

    def load(self):
        for i in range(self.slots):
            self.fetch(i).start()

    def send(self):
        for i in range(len(self.refs)):
            self.fetch(i).wait()
            cols = pl.ds(pl.multiple_of((1 - self.dp) * self.half, 128), self.half)
            self.stage[i] = self.held[i % self.slots, :, cols]
            self.copy(i).start()
            if i + self.slots < len(self.refs):
                self.fetch(i + self.slots).start()

    def wait(self):
        for i in range(len(self.refs)):
            self.copy(i).wait()


def transpose_kernel_part(loads, tall, wide, wsem, tsem):
    copies = [pltpu.make_async_copy(src, dst, wsem.at[i]) for i, (src, dst, _) in enumerate(loads)]
    for copy in copies:
        copy.start()
    for i, (_, held, out) in enumerate(loads):
        slab = tall.shape[1]
        stages = [tall.at[i] if out.shape[1] == tall.shape[2] else wide.at[pl.ds(i * slab, slab)] for i in range(2)]
        steps = out.shape[0] // slab
        copies[i].wait()

        def put(t, slot, stages=stages, out=out, slab=slab):
            rows = pl.ds(pl.multiple_of(t * slab, slab), slab)
            return pltpu.make_async_copy(stages[slot], out.at[rows], tsem.at[slot])

        def step(pair, carry, stages=stages, held=held, put=put, slab=slab, steps=steps):
            for slot in range(2):
                t = 2 * pair + slot

                @pl.when(t < steps)
                def _(t=t, slot=slot):
                    @pl.when(pair > 0)
                    def _():
                        put(t - 2, slot).wait()

                    cols = pl.ds(pl.multiple_of(t * slab, slab), slab)
                    stages[slot][...] = jnp.transpose(held[:, cols])
                    put(t, slot).start()

            return carry

        lax.fori_loop(0, pl.cdiv(steps, 2), step, 0)
        for t in (steps - 2, steps - 1):
            put(t, t % 2).wait()


def expert_forward_kernel(turn, has_prev, *refs):
    has_prev = has_prev > 0
    send_ref, w_in, w_down = refs[:3]
    left_refs, refs = refs[3 + 10 * has_prev : 5 + 10 * has_prev], refs[5 + 10 * has_prev :]
    back_out, rows_out, slope_out, value_out, hidden_out, slope_peer_out, value_peer_out = refs[:7]
    wgt_out, wut_out, wdt_out = refs[7:10]
    left_out, refs = refs[10], refs[11:]
    wg, wu, wd, rows, back, made, rows_peer, slopes, values, hidden = refs[:10]
    slopes_peer, values_peer, tall = refs[10:13]
    wsem, s1, r1, s2, r2, sx, rx, osem, tsem = refs[13:22]
    experts, block, width = send_ref.shape
    ff = wd.shape[0]
    span = ff // 2
    lefts = Lefts(left_refs, left_out, (tall, *refs[22:]), width)

    @pl.when(lax.axis_index("half") != turn)
    def _():
        greet([{"dp": 1 - lax.axis_index("dp")}])
        loads = ((w_in.at[0], wg, wgt_out), (w_in.at[1], wu, wut_out), (w_down, wd, wdt_out))
        transpose_kernel_part(loads, tall, slopes, wsem, tsem)
        lefts.load()
        lefts.send()
        lefts.wait()

    @pl.when(lax.axis_index("half") == turn)
    def _():
        t = Turn(experts, block, (send_ref, rows, s1, r1), (made, back, s2, r2))
        t.greet()

        def rows_over(part):
            blocks, _ = t.spans(*t.groups[part])
            return remote(rows.at[blocks], rows_peer.at[blocks], sx.at[part], rx.at[part], t.peer)

        if not has_prev:
            lefts.load()
        for k in range(1, experts):
            t.there(k).start()
        rows[t.me] = send_ref[t.me]
        loads = [
            pltpu.make_async_copy(src, dst, wsem.at[i])
            for i, (src, dst) in enumerate(((w_in.at[0], wg), (w_in.at[1], wu), (w_down, wd)))
        ]
        for load in loads:
            load.start()
        if not has_prev:
            lefts.send()
        for part, (first, size) in enumerate(t.groups):
            t.arrive(first, size)
            rows_over(part).start()
            blocks, span_rows = t.spans(first, size)
            if part == 0:
                loads[0].wait()
                loads[1].wait()

            def up_tile(start, count, blocks=blocks, span_rows=span_rows, size=size):
                x = rows[blocks].reshape(size * block, width)
                cols = pl.ds(start, count)
                value, slope = gelu_parts(dot(x, wg[:, cols]))
                up = dot(x, wu[:, cols])
                hidden[span_rows, cols] = (value * up).astype(BF16)
                values[span_rows, cols] = value.astype(BF16)
                slopes[span_rows, cols] = (up * slope).astype(BF16)

            tile_loop(ff, 512, up_tile)
            if part == 0:
                loads[2].wait()

            def down_tile(start, count, blocks=blocks, span_rows=span_rows, size=size):
                cols = pl.ds(start, count)
                y = dot(hidden[span_rows, :], wd[:, cols]).astype(BF16)
                made[blocks, :, cols] = y.reshape(size, block, count)

            tile_loop(width, 512, down_tile)
            for k in range(max(first, 1), first + size):
                t.home(k).start()
        back[t.me] = made[t.me]
        half_cols = pl.ds(pl.multiple_of(t.dp * span, 128), span)
        other_cols = pl.ds(pl.multiple_of((1 - t.dp) * span, 128), span)
        outs = [
            (slopes, slope_out),
            (values, value_out),
            (hidden.at[:, half_cols], hidden_out.at[0]),
            (rows, rows_out.at[0]),
        ]
        outs = [pltpu.make_async_copy(src, dst, osem.at[i]) for i, (src, dst) in enumerate(outs)]
        for out in outs:
            out.start()

        for part in range(len(t.groups)):
            rows_over(part).wait_recv()

        def peer_tile(start, count):
            x = rows_peer[...].reshape(experts * block, width)
            here = pl.ds(start, count)
            cols = pl.ds(pl.multiple_of(t.dp * span + start, 128), count)
            value, slope = gelu_parts(dot(x, wg[:, cols]))
            up = dot(x, wu[:, cols])
            hidden[:, pl.ds(pl.multiple_of((1 - t.dp) * span + start, 128), count)] = (value * up).astype(BF16)
            values_peer[:, here] = value.astype(BF16)
            slopes_peer[:, here] = (up * slope).astype(BF16)

        tile_loop(span, 512, peer_tile)
        more = [
            (slopes_peer, slope_peer_out),
            (values_peer, value_peer_out),
            (hidden.at[:, other_cols], hidden_out.at[1]),
            (rows_peer, rows_out.at[1]),
        ]
        more = [pltpu.make_async_copy(src, dst, osem.at[4 + i]) for i, (src, dst) in enumerate(more)]
        for out in more:
            out.start()
        for k in range(1, experts):
            t.home(k).wait_recv()
        back_copy = pltpu.make_async_copy(back, back_out, osem.at[8])
        back_copy.start()
        for k in range(1, experts):
            t.there(k).wait_send()
            t.home(k).wait_send()
        for part in range(len(t.groups)):
            rows_over(part).wait_send()
        if not has_prev:
            lefts.wait()
        for out in [*outs, *more, back_copy]:
            out.wait()


def expert_backward_kernel(turn, has_prev, *refs):
    send_ref = refs[0]
    sources = refs[1:8]
    left_refs, refs = refs[8 + has_prev : 8 + has_prev + 2 * (has_prev == 1)], refs[8 + has_prev + 2 * (has_prev == 1) :]
    back_out, mixed_out, grad_out = refs[:3]
    left_out, refs = refs[3 : 3 + (has_prev == 1)], refs[3 + (has_prev == 1) :]
    wdt, dgate, dup, wgt, wut, dgate_peer, dup_peer = refs[:7]
    grads, back, made, grads_peer = refs[7:11]
    wsem, s1, r1, s2, r2, sx, rx, osem = refs[11:19]
    experts, block, width = send_ref.shape
    ff = wdt.shape[1]
    span = ff // 2
    dp = lax.axis_index("dp")
    t = Turn(experts, block, (send_ref, grads, s1, r1), (made, back, s2, r2))
    lefts = Lefts(left_refs, left_out[0], refs[19:], width) if left_refs else None

    @pl.when(lax.axis_index("half") == turn)
    def _():
        t.greet()

        def grads_over(part):
            blocks, _ = t.spans(*t.groups[part])
            return remote(grads.at[blocks], grads_peer.at[blocks], sx.at[part], rx.at[part], t.peer)

        for k in range(1, experts):
            t.there(k).start()
        grads[t.me] = send_ref[t.me]
        if lefts:
            lefts.load()
        held = (wdt, dgate, dup, wgt, wut, dgate_peer, dup_peer)
        loads = [pltpu.make_async_copy(src, dst, wsem.at[i]) for i, (src, dst) in enumerate(zip(sources, held))]
        for load in loads:
            load.start()
        if lefts:
            lefts.send()
        for load in loads[:3]:
            load.wait()
        for part, (first, size) in enumerate(t.groups):
            t.arrive(first, size)
            grads_over(part).start()
            blocks, span_rows = t.spans(first, size)

            def hidden_tile(start, count, blocks=blocks, span_rows=span_rows, size=size):
                dy = grads[blocks].reshape(size * block, width)
                cols = pl.ds(start, count)
                dhidden = dot(dy, wdt[:, cols])
                dgate[span_rows, cols] = (dhidden * dgate[span_rows, cols].astype(F32)).astype(BF16)
                dup[span_rows, cols] = (dhidden * dup[span_rows, cols].astype(F32)).astype(BF16)

            tile_loop(ff, 512, hidden_tile)
            if part == 0:
                loads[3].wait()
                loads[4].wait()

            def rows_tile(start, count, blocks=blocks, span_rows=span_rows, size=size):
                cols = pl.ds(start, count)
                dr = dot(dgate[span_rows, :], wgt[:, cols]) + dot(dup[span_rows, :], wut[:, cols])
                made[blocks, :, cols] = dr.astype(BF16).reshape(size, block, count)

            tile_loop(width, 512, rows_tile)
            for k in range(max(first, 1), first + size):
                t.home(k).start()
        back[t.me] = made[t.me]
        half_cols = pl.ds(pl.multiple_of(dp * span, 128), span)
        outs = [
            (dgate.at[:, half_cols], mixed_out.at[0, 0]),
            (dup.at[:, half_cols], mixed_out.at[1, 0]),
            (grads, grad_out.at[0]),
        ]
        outs = [pltpu.make_async_copy(src, dst, osem.at[i]) for i, (src, dst) in enumerate(outs)]
        for out in outs:
            out.start()

        for load in loads[5:]:
            load.wait()
        for part in range(len(t.groups)):
            grads_over(part).wait_recv()

        def peer_tile(start, count):
            dy = grads_peer[...].reshape(experts * block, width)
            here = pl.ds(start, count)
            dhidden = dot(dy, wdt[:, pl.ds(pl.multiple_of(dp * span + start, 128), count)])
            dgate_peer[:, here] = (dhidden * dgate_peer[:, here].astype(F32)).astype(BF16)
            dup_peer[:, here] = (dhidden * dup_peer[:, here].astype(F32)).astype(BF16)

        tile_loop(span, 512, peer_tile)
        more = [
            (dgate_peer, mixed_out.at[0, 1]),
            (dup_peer, mixed_out.at[1, 1]),
            (grads_peer, grad_out.at[1]),
        ]
        more = [pltpu.make_async_copy(src, dst, osem.at[3 + i]) for i, (src, dst) in enumerate(more)]
        for out in more:
            out.start()
        for k in range(1, experts):
            t.home(k).wait_recv()
        back_copy = pltpu.make_async_copy(back, back_out, osem.at[6])
        back_copy.start()
        for k in range(1, experts):
            t.there(k).wait_send()
            t.home(k).wait_send()
        for part in range(len(t.groups)):
            grads_over(part).wait_send()
        if lefts:
            lefts.wait()
        for out in [*outs, *more, back_copy]:
            out.wait()


def expert_call(kernel, number, turn, send, sources, prev, more, out_shape, scratch, name, shift=0):
    vmem, hbm = pl.BlockSpec(memory_space=pltpu.VMEM), pl.BlockSpec(memory_space=pl.ANY)
    prev = list(prev or [])
    return pl.pallas_call(
        functools.partial(kernel, turn, len(prev)),
        in_specs=[vmem] + [hbm] * (len(sources) + len(prev) + len(more)),
        out_specs=[hbm] * len(out_shape),
        out_shape=out_shape,
        input_output_aliases={1 + len(sources) + i: i + shift for i in range(len(prev))},
        scratch_shapes=scratch,
        compiler_params=pltpu.CompilerParams(
            collective_id=number, has_side_effects=True, vmem_limit_bytes=60 << 20
        ),
        name=name,
    )(send, *sources, *prev, *more)


def moe_forward(send, w_in, w_down, turn, prev, lefts, slab):
    experts, block, width = send.shape
    ff = w_down.shape[0]
    total = experts * block
    parts = len(groups_of(experts, block))
    dma = pltpu.SemaphoreType.DMA
    scratch = [
        pltpu.VMEM((width, ff), BF16),
        pltpu.VMEM((width, ff), BF16),
        pltpu.VMEM((ff, width), BF16),
        *[pltpu.VMEM(send.shape, BF16)] * 4,
        *[pltpu.VMEM((total, ff), BF16)] * 3,
        *[pltpu.VMEM((total, ff // 2), BF16)] * 2,
        pltpu.VMEM((2, slab, width), BF16),
        dma((3,)),
        *[dma((experts,))] * 4,
        *[dma((parts,))] * 2,
        dma((9,)),
        dma((2,)),
    ]
    shapes = [
        send.shape,
        (2, *send.shape),
        (total, ff),
        (total, ff),
        (2, total, ff // 2),
        (total, ff // 2),
        (total, ff // 2),
        (ff, width),
        (ff, width),
        (width, ff),
    ]
    left_shape = (2, lefts[0].shape[0], width // 2)
    shapes.append(left_shape)
    scratch += [pltpu.VMEM(left_shape, BF16), *[dma((2,))] * 3]
    out_shape = [jax.ShapeDtypeStruct(shape, BF16) for shape in shapes]
    return expert_call(
        expert_forward_kernel, 1 + turn, turn, send, [w_in, w_down], prev, lefts, out_shape, scratch, "moe_forward"
    )


def moe_backward(grad_send, saved, turn, prev, lefts):
    experts, block, width = grad_send.shape
    _, _, slope, value, _, slope_peer, value_peer, wgt, wut, wdt, lefts_peer = saved
    total, ff = slope.shape
    parts = len(groups_of(experts, block))
    dma = pltpu.SemaphoreType.DMA
    scratch = [
        pltpu.VMEM((width, ff), BF16),
        *[pltpu.VMEM((total, ff), BF16)] * 2,
        *[pltpu.VMEM((ff, width), BF16)] * 2,
        *[pltpu.VMEM((total, ff // 2), BF16)] * 2,
        *[pltpu.VMEM(grad_send.shape, BF16)] * 4,
        dma((7,)),
        *[dma((experts,))] * 4,
        *[dma((parts,))] * 2,
        dma((7,)),
    ]
    out_shape = [
        jax.ShapeDtypeStruct(grad_send.shape, BF16),
        jax.ShapeDtypeStruct((2, 2, total, ff // 2), BF16),
        jax.ShapeDtypeStruct((2, *grad_send.shape), BF16),
    ]
    if lefts:
        prev = [lefts_peer]
        out_shape.append(jax.ShapeDtypeStruct(lefts_peer.shape, BF16))
        rows = lefts[0].shape[0]
        scratch += [pltpu.VMEM((2, rows, width), BF16), pltpu.VMEM(lefts_peer.shape, BF16), *[dma((2,))] * 3]
    return expert_call(
        expert_backward_kernel,
        3 + turn,
        turn,
        grad_send,
        [wdt, slope, value, wgt, wut, slope_peer, value_peer],
        prev,
        lefts,
        out_shape,
        scratch,
        "moe_backward",
        3 if lefts else 0,
    )


GATE, TOTAL, SCALE, ROUTE, FIRST = 0, 2, 3, 4, 8


class Loads:
    def __init__(self, pairs, sems):
        self.copies = [pltpu.make_async_copy(src, dst, sems.at[i]) for i, (src, dst) in enumerate(pairs)]

    def start(self):
        for copy in self.copies:
            copy.start()

    def wait(self, *which):
        for i in which:
            self.copies[i].wait()


def slots_kernel(experts, capacity, block, order_ref, spots_out, both_out, turned_out, both_turned_out, tally_out, route_out, route_rows):
    seqs, pairs = order_ref.shape
    top = spots_out.shape[1] // both_out.shape[1]
    length = pairs // top
    rows = seqs * length
    slots = spots_out.shape[0]
    expert_id = lax.broadcasted_iota(jnp.int32, (experts, pairs), 0)
    slot_id = lax.broadcasted_iota(jnp.int32, (slots, length), 0)
    row_id = lax.broadcasted_iota(jnp.int32, (pairs, pairs), 0)
    col_id = lax.broadcasted_iota(jnp.int32, (pairs, pairs), 1)
    earlier = (row_id < col_id).astype(F32).astype(BF16)
    route_rows[...] = jnp.zeros_like(route_rows)
    tally = jnp.zeros((experts, 128), F32)
    lane = lax.broadcasted_iota(jnp.int32, (experts, 128), 1)
    for seq in range(seqs):
        order = order_ref[seq : seq + 1, :]
        picked = (expert_id == order).astype(F32)
        place = jnp.sum(dot(picked.astype(BF16), earlier) * picked, axis=0, keepdims=True)
        kept = place < capacity
        target = jnp.where(kept, order * block + seq * capacity + place.astype(jnp.int32), -1)
        taken = jnp.sum(picked * kept.astype(F32), axis=1, keepdims=True)
        whole = jnp.sum(picked, axis=1, keepdims=True)
        tally = tally + jnp.where(lane == 0, taken, jnp.where(lane == 1, whole, 0.0))
        total = jnp.zeros((slots, length), F32)
        for k in range(top):
            part = pl.ds(k * length, length)
            hot = (slot_id == target[:, k * length : (k + 1) * length]).astype(F32)
            spots_out[:, pl.ds(k * rows + seq * length, length)] = hot.astype(BF16)
            total = total + hot
            route_rows[pl.ds(ROUTE + k, 1), pl.ds(seq * length, length)] = order_ref[
                pl.ds(seq, 1), part
            ].astype(F32)
        both_out[:, pl.ds(seq * length, length)] = total.astype(BF16)
    tally_out[...] = tally
    turned_out[...] = jnp.transpose(spots_out[...])
    both_turned_out[...] = jnp.transpose(both_out[...])
    route_out[...] = jnp.transpose(route_rows[...])


def find_slots(order, experts, capacity, block, top):
    seqs, pairs = order.shape
    rows = seqs * pairs // top
    slots = experts * block
    vmem = pl.BlockSpec(memory_space=pltpu.VMEM)
    return pl.pallas_call(
        functools.partial(slots_kernel, experts, capacity, block),
        in_specs=[vmem],
        out_specs=[vmem] * 6,
        out_shape=[
            jax.ShapeDtypeStruct((slots, top * rows), BF16),
            jax.ShapeDtypeStruct((slots, rows), BF16),
            jax.ShapeDtypeStruct((top * rows, slots), BF16),
            jax.ShapeDtypeStruct((rows, slots), BF16),
            jax.ShapeDtypeStruct((experts, 128), F32),
            jax.ShapeDtypeStruct((rows, 128), F32),
        ],
        scratch_shapes=[pltpu.VMEM((128, rows), F32)],
        compiler_params=pltpu.CompilerParams(vmem_limit_bytes=32 << 20),
        name="find_slots",
    )(order)


def enter_kernel(cross, experts, count, info, gain_ref, router_ref, lanes_ref, lead_ref, *refs):
    sources, refs = refs[:count], refs[count:]
    mixed_out, log_out, result_out, stats_out, send_out = refs[:5]
    held, (low_ref, mask_ref, sems) = refs[5 : 5 + count], refs[5 + count :]
    w_out, x, spots = held[count - 3 :]
    rows, width = x.shape
    step = min(512, width)
    loads = Loads(zip(sources, held), sems)
    loads.start()
    if cross:
        q_ref, kv = held[:2]
        k_ref, v_ref = kv.at[:, pl.ds(0, width)], kv.at[:, pl.ds(width, width)]
    else:
        q_ref, k_ref, v_ref = (held[0].at[:, pl.ds(i * width, width)] for i in range(3))

    def work():
        loads.wait(*range(count - 3))
        attend(info, None if cross else lead_ref, q_ref, k_ref, v_ref, mixed_out, log_out, mask_ref)
        loads.wait(count - 3, count - 2)
        for start in range(0, width, step):
            cols = pl.ds(start, step)
            result_out[:, cols] = x[:, cols].astype(F32) + dot(mixed_out[...], w_out[:, cols])
        values = result_out[...]
        scale = lax.rsqrt(jnp.mean(values * values, axis=-1, keepdims=True) + EPS)
        normed = values * scale * gain_ref[...]
        low = normed.astype(BF16)
        low_ref[...] = low
        logits = dot(low, router_ref[...]) + dot((normed - low.astype(F32)).astype(BF16), router_ref[...])
        lane = lax.broadcasted_iota(jnp.int32, (rows, 128), 1)
        valid = (lane >= FIRST) & (lane < FIRST + experts)
        logits = jnp.where(valid, logits, -1e30)
        spread = jnp.where(valid, jnp.exp(logits - jnp.max(logits, axis=-1, keepdims=True)), 0.0)
        probs = spread / jnp.sum(spread, axis=-1, keepdims=True)
        routes = lanes_ref[...]
        chosen = [
            jnp.sum(
                jnp.where(lane == routes[:, ROUTE + k : ROUTE + k + 1].astype(jnp.int32) + FIRST, probs, 0.0),
                axis=-1,
                keepdims=True,
            )
            for k in range(2)
        ]
        total = chosen[0] + chosen[1]
        stats = probs + routes
        for at, column in ((GATE, chosen[0] / total), (GATE + 1, chosen[1] / total), (TOTAL, total), (SCALE, scale)):
            stats = jnp.where(lane == at, column, stats)
        stats_out[...] = stats
        loads.wait(count - 1)
        for start in range(0, width, step):
            cols = pl.ds(start, step)
            send_out[:, cols] = dot(spots[...], low_ref[:, cols]).astype(BF16)

    if not cross:
        work()
        return
    decoder = lax.axis_index("half") == 1
    pl.when(decoder)(work)

    @pl.when(jnp.logical_not(decoder))
    def _():
        loads.wait(*range(count))
        result_out[...] = x[...].astype(F32)
        stats_out[...] = lead_ref[...]


def enter(info, gain, router, lanes, lead, cross, sources, experts, length):
    rows, width = sources[-2].shape
    vmem, hbm = pl.BlockSpec(memory_space=pltpu.VMEM), pl.BlockSpec(memory_space=pl.ANY)
    count = len(sources)
    return pl.pallas_call(
        functools.partial(enter_kernel, cross, experts, count),
        in_specs=[pl.BlockSpec(memory_space=pltpu.SMEM)] + [vmem] * 4 + [hbm] * count,
        out_specs=[vmem] * 5,
        out_shape=[
            jax.ShapeDtypeStruct((rows, width), BF16),
            jax.ShapeDtypeStruct((rows, width), F32),
            jax.ShapeDtypeStruct((rows, width), F32),
            jax.ShapeDtypeStruct((rows, 128), F32),
            jax.ShapeDtypeStruct((sources[-1].shape[0], width), BF16),
        ],
        scratch_shapes=[
            *(pltpu.VMEM(a.shape, a.dtype) for a in sources),
            pltpu.VMEM((rows, width), BF16),
            pltpu.VMEM((rows // length, length, length), F32),
            pltpu.SemaphoreType.DMA((count,)),
        ],
        compiler_params=pltpu.CompilerParams(vmem_limit_bytes=56 << 20),
        name="enter_cross" if cross else "enter_self",
    )(info, gain, router, lanes, lead, *sources)


def norm_back_rows(values, scale, gain, grad):
    unit = values * scale
    pushed = grad * gain
    back = scale * (pushed - unit * jnp.mean(pushed * unit, axis=-1, keepdims=True))
    return back, jnp.sum(grad * unit, axis=0, keepdims=True)


def leave_kernel(cross, experts, count, info, stats_ref, gain_ref, router_ref, *refs):
    bias_ref, refs = (None, refs) if cross else (refs[0], refs[1:])
    sources, refs = refs[:count], refs[count:]
    grad_out, branch_out, dgain_out, dlog_out, dq_out, last_out = refs[:6]
    held, (dmixed, mask_ref, sems) = refs[6 : 6 + count], refs[6 + count :]
    back, both, grad, results, x, w_out, a, log = held[:8]
    seqs, length, _ = mask_ref.shape
    width = x.shape[1]
    loads = Loads(zip(sources, held), sems)
    if cross:
        q_ref, kv = held[8:]
        k_ref, v_ref = kv.at[:, pl.ds(0, width)], kv.at[:, pl.ds(width, width)]
        dkv_out, shift, diag_out = last_out, 0, None
    else:
        qkv, ready = held[8:]
        q_ref, k_ref, v_ref = (qkv.at[:, pl.ds(i * width, width)] for i in range(3))
        dkv_out, shift, diag_out = dq_out, width, last_out

    def leave():
        loads.wait(0, 1, 2, 3, 4)
        dgain = jnp.zeros((1, width), F32)
        lane = lax.broadcasted_iota(jnp.int32, (length, 128), 1)
        for seq in range(seqs):
            rows = pl.ds(seq * length, length)
            stats = stats_ref[rows, :]
            gates = [stats[:, GATE + k : GATE + k + 1] for k in range(2)]
            hots = [
                (lane == stats[:, ROUTE + k : ROUTE + k + 1].astype(jnp.int32) + FIRST).astype(F32)
                for k in range(2)
            ]
            probs = jnp.where((lane >= FIRST) & (lane < FIRST + experts), stats, 0.0)
            g = grad[rows, :].astype(F32)
            dgates = [
                jnp.sum(g * results[k, rows, :].astype(F32), axis=-1, keepdims=True) for k in range(2)
            ]
            shared = dgates[0] * gates[0] + dgates[1] * gates[1]
            dprobs = sum((dgates[k] - shared) / stats[:, TOTAL : TOTAL + 1] * hots[k] for k in range(2))
            dlog = probs * (dprobs - jnp.sum(dprobs * probs, axis=-1, keepdims=True))
            dlog_out[rows, :] = dlog
            dnormed = dot(both[rows, :], back[...]) + dot(dlog.astype(BF16), router_ref[...], NT)
            dx, part = norm_back_rows(x[rows, :], stats[:, SCALE : SCALE + 1], gain_ref[...], dnormed)
            dgain = dgain + part
            grad_out[rows, :] = g + dx
        dgain_out[...] = jnp.broadcast_to(dgain, dgain_out.shape)

    def attention():
        loads.wait(5)
        branch_out[...] = grad_out[...].astype(BF16)
        step = min(512, width)
        for start in range(0, width, step):
            cols = pl.ds(start, step)
            dmixed[:, cols] = dot(branch_out[...], w_out[cols, :], NT).astype(BF16)
        loads.wait(*((6, 7, 8, 9) if cross else (6, 7, 8)))
        attend_back(
            info, bias_ref, q_ref, k_ref, v_ref, a, log, dmixed, dq_out, dkv_out, shift, diag_out, mask_ref
        )

    decoder = lax.axis_index("half") == 1
    if cross:

        @pl.when(decoder)
        def _():
            loads.start()
            leave()
            attention()

    else:
        loads.start()

        @pl.when(jnp.logical_not(decoder))
        def _():
            leave()
            loads.wait(9)

        @pl.when(decoder)
        def _():
            loads.wait(0, 1, 2, 3, 4, 9)
            grad_out[...] = ready[...]

        attention()


def leave(info, stats, gain, router, bias, sources, experts, length):
    cross = bias is None
    rows, width = sources[4].shape
    seqs = rows // length
    vmem, hbm = pl.BlockSpec(memory_space=pltpu.VMEM), pl.BlockSpec(memory_space=pl.ANY)
    lead = [] if cross else [bias]
    out_shape = [
        jax.ShapeDtypeStruct((rows, width), F32),
        jax.ShapeDtypeStruct((rows, width), BF16),
        jax.ShapeDtypeStruct((8, width), F32),
        jax.ShapeDtypeStruct((rows, 128), F32),
        jax.ShapeDtypeStruct((rows, width if cross else 3 * width), BF16),
        jax.ShapeDtypeStruct((rows, 2 * width), BF16) if cross else jax.ShapeDtypeStruct(bias.shape, F32),
    ]
    return pl.pallas_call(
        functools.partial(leave_kernel, cross, experts, len(sources)),
        in_specs=[pl.BlockSpec(memory_space=pltpu.SMEM)] + [vmem] * (3 + len(lead)) + [hbm] * len(sources),
        out_specs=[vmem] * 6,
        out_shape=out_shape,
        scratch_shapes=[
            *(pltpu.VMEM(a.shape, a.dtype) for a in sources),
            pltpu.VMEM((rows, width), BF16),
            pltpu.VMEM((seqs, length, length), F32),
            pltpu.SemaphoreType.DMA((len(sources),)),
        ],
        compiler_params=pltpu.CompilerParams(vmem_limit_bytes=56 << 20),
        name="leave_cross" if cross else "leave_self",
    )(info, stats, gain, router, *lead, *sources)


def memory_kernel(stats_ref, gain_ref, *refs):
    sources, parts, refs = refs[:5], refs[5:7], refs[7:]
    grad_out, send_out, dgain_out, cross_out = refs[:4]
    held, (dnormed, spread, sems) = refs[4:9], refs[9:]
    dmemory, w, x, cotangent, spots = held
    rows, width = x.shape

    @pl.when(lax.axis_index("half") == 1)
    def _():
        loads = Loads(((part, cross_out.at[:, pl.ds(i * width, width)]) for i, part in enumerate(parts)), sems)
        loads.start()
        loads.wait(0, 1)

    @pl.when(lax.axis_index("half") == 0)
    def _():
        loads = Loads(zip(sources, held), sems)
        loads.start()
        loads.wait(0, 1)
        cross_out[...] = dmemory[...]
        step = min(512, width)
        for start in range(0, width, step):
            cols = pl.ds(start, step)
            dnormed[:, cols] = dot(dmemory[...], w[cols, :], NT)
        loads.wait(2, 3)
        scale = lax.rsqrt(jnp.mean(x[...] * x[...], axis=-1, keepdims=True) + EPS)
        dx, dgain = norm_back_rows(x[...], scale, gain_ref[...], dnormed[...])
        dgain_out[...] = jnp.broadcast_to(dgain, dgain_out.shape)
        grad = cotangent[...].astype(F32) + dx
        grad_out[...] = grad
        for k in range(2):
            gate = stats_ref[:, GATE + k : GATE + k + 1]
            spread[pl.ds(k * rows, rows), :] = (gate * grad).astype(BF16)
        loads.wait(4)
        for start in range(0, width, step):
            cols = pl.ds(start, step)
            send_out[:, cols] = dot(spots[...], spread[:, cols]).astype(BF16)


def memory_gradient(stats, gain, sources, parts):
    rows, width = sources[2].shape
    vmem, hbm = pl.BlockSpec(memory_space=pltpu.VMEM), pl.BlockSpec(memory_space=pl.ANY)
    return pl.pallas_call(
        memory_kernel,
        in_specs=[vmem] * 2 + [hbm] * (len(sources) + len(parts)),
        out_specs=[vmem] * 4,
        out_shape=[
            jax.ShapeDtypeStruct((rows, width), F32),
            jax.ShapeDtypeStruct((sources[4].shape[0], width), BF16),
            jax.ShapeDtypeStruct((8, width), F32),
            jax.ShapeDtypeStruct((rows, 2 * width), BF16),
        ],
        scratch_shapes=[
            *(pltpu.VMEM(a.shape, a.dtype) for a in sources),
            pltpu.VMEM((rows, width), F32),
            pltpu.VMEM((2 * rows, width), BF16),
            pltpu.SemaphoreType.DMA((len(sources),)),
        ],
        compiler_params=pltpu.CompilerParams(vmem_limit_bytes=48 << 20),
        name="memory_gradient",
    )(stats, gain, *sources, *parts)


def dense_kernel(stages, chunk, lag, *refs):
    sources, small_ref = refs[:12], refs[12]
    out_refs, small_out, small_in = refs[13:16], refs[16], refs[17]
    held, xt_ref, refs = refs[18:30], refs[30], refs[31:]
    x_refs, own_refs, peer_refs, xps = held[:4], held[4:7], held[7:10], held[10:12]
    sums, parts = refs[:stages], refs[stages : 2 * stages]
    ss, rs, sk, rk, sl = refs[2 * stages :]
    counts = [ref.shape[1] // chunk for ref in own_refs]
    starts = [sum(counts[:i]) for i in range(3)]
    chunks = sum(counts)
    per_cross = counts[2] // 2
    rows, half = xps[0].shape[1:]
    dp, me = lax.axis_index("dp"), lax.axis_index("expert")
    peer = {"dp": 1 - dp}
    partners = [flipped(me, k) for k in range(stages)]
    bits = [me // (1 << k) % 2 for k in range(stages)]
    load = [pltpu.make_async_copy(sources[i], held[i], sl.at[i]) for i in range(12)]
    for i in (11, 2, 3, 6, 9, 10, 0, 4, 7, 1, 5, 8):
        load[i].start()
    greet([peer] + [{"expert": p} for p in partners])

    def send_small(step):
        src = small_ref if step == 0 else small_out.at[step - 1]
        device = peer if step == 0 else {"expert": partners[stages - step]}
        return remote(src, small_in.at[step], ss.at[step], rs.at[step], device)

    def order(k, odd):
        return 1 - k if odd and k < 2 else k

    def send_part(k, c, odd):
        bit = order(k, odd)
        other = 1 - bits[bit]
        src = sums[0].at[c, :, :, other] if k == 0 and not odd else sums[k].at[c, :, other]
        return remote(src, parts[k].at[c], sk.at[k, c], rk.at[k, c], {"expert": partners[bit]})

    def turn_x(g):
        load[g].wait()
        cols = pl.ds(pl.multiple_of(dp * half, half), half)
        xt_ref[g, :, :rows] = jnp.transpose(x_refs[g][:, cols])
        xt_ref[g, :, rows:] = jnp.transpose(xps[g // 2][g % 2])

    def small_step(j):
        send_small(j).wait_recv()
        own = small_ref[...] if j == 0 else small_out[j - 1]
        small_out[j] = own + small_in[j]
        if j < stages:
            send_small(j + 1).start()

    send_small(0).start()
    load[11].wait()
    load[10].wait()
    last = counts[2]
    early = chunks - last
    per = chunks // last

    def produce(i, carry):
        c = jnp.where(lax.rem(i, per) == 0, early + i // per, i - i // per - 1)
        for g in range(3):

            @pl.when(c == starts[g])
            def _(g=g):
                load[4 + g].wait()
                load[7 + g].wait()
                for x in (g,) if g < 2 else (2, 3):
                    turn_x(x)

            @pl.when((c >= starts[g]) & (c < starts[g] + counts[g]))
            def _(g=g):
                at = c - starts[g]
                cols = pl.ds(pl.multiple_of(at * chunk, chunk), chunk)
                which = g if g < 2 else 2 + at // per_cross
                total = dot(xt_ref[which, :, :rows], own_refs[g][:, cols])
                total += dot(xt_ref[which, :, rows:], peer_refs[g][:, cols])
                sums[0][c] = total.astype(BF16).reshape(sums[0].shape[1:])
                send_part(0, c, g == 2).start()

        for j in range(2):

            @pl.when(i == 3 + 6 * j)
            def _(j=j):
                small_step(j)

        return carry

    lax.fori_loop(0, chunks, produce, 0)

    def advance(k, c, odd):
        send_part(k, c, odd).wait_recv()
        bit = bits[order(k, odd)]
        mine = sums[0][c, :, :, bit] if k == 0 and not odd else sums[k][c, :, bit]
        total = mine.astype(F32) + parts[k][c].astype(F32)
        if k + 1 < stages:
            sums[k + 1][c] = total.astype(BF16).reshape(sums[k + 1].shape[1:])
            send_part(k + 1, c, odd).start()
            return
        total = total.reshape(total.shape[-2:])
        for g in (2,) if odd else (0, 1):

            @pl.when((c >= starts[g]) & (c < starts[g] + counts[g]))
            def _(g=g):
                at = pl.multiple_of((c - starts[g]) * chunk, chunk)
                out_refs[g][:, pl.ds(at, chunk)] = total

    def reduce(i, carry):
        @pl.when((lax.rem(i, 2) == 1) & (i // 2 < last))
        def _():
            advance(0, early + i // 2, True)

        for k in range(stages):
            c = i - lag * k

            @pl.when((c >= 0) & (c < early))
            def _(k=k, c=c):
                advance(k, c, False)

        for k in range(1, stages):
            c = i - 1 - lag * (k - 1)

            @pl.when((c >= early) & (c < chunks))
            def _(k=k, c=c):
                advance(k, c, True)

        for j in range(2, stages + 1):

            @pl.when(i == 3 * j - 2)
            def _(j=j):
                small_step(j)

        return carry

    lax.fori_loop(0, chunks + 1 + lag * (stages - 2), reduce, 0)

    def finish(c, carry, odd):
        for k in range(stages):
            send_part(k, c, odd).wait_send()
        return carry

    lax.fori_loop(0, early, functools.partial(finish, odd=False), 0)
    lax.fori_loop(early, chunks, functools.partial(finish, odd=True), 0)
    for j in range(stages + 1):
        send_small(j).wait_send()


def over_dp(array):
    return lax.ppermute(array, "dp", [(0, 1), (1, 0)])


def dense_gradients(lefts, lefts_peers, own, peer, small, experts):
    chunk = 512
    rows, width = lefts[0].shape
    half_rows = width // 2
    chunks = sum(y.shape[1] for y in own) // chunk
    stages = experts.bit_length() - 1
    keep = half_rows // experts
    vmem, hbm = pl.BlockSpec(memory_space=pltpu.VMEM), pl.BlockSpec(memory_space=pl.ANY)
    dma = pltpu.SemaphoreType.DMA
    sources = [*lefts, *own, *peer, *lefts_peers]
    blocks = [(experts // 4, 2, 2)] + [(experts >> (k + 1), 2) for k in range(1, stages)]
    halved = [(experts // 4, 2)] + [(experts >> (k + 1),) for k in range(1, stages)]
    scratch = [pltpu.VMEM((stages + 1, *small.shape), F32)]
    scratch += [pltpu.VMEM(a.shape, BF16) for a in sources]
    scratch += [pltpu.VMEM((4, half_rows, 2 * rows), BF16)]
    scratch += [pltpu.VMEM((chunks, *b, keep, chunk), BF16) for b in blocks + halved]
    scratch += [dma((stages + 1,)), dma((stages + 1,)), dma((stages, chunks)), dma((stages, chunks))]
    scratch += [dma((len(sources),))]
    *outs, sums = pl.pallas_call(
        functools.partial(dense_kernel, stages, chunk, 2),
        in_specs=[hbm] * len(sources) + [vmem],
        out_specs=[vmem] * 4,
        out_shape=[
            *(jax.ShapeDtypeStruct((keep, y.shape[1]), F32) for y in own),
            jax.ShapeDtypeStruct((stages + 1, *small.shape), F32),
        ],
        scratch_shapes=scratch,
        compiler_params=pltpu.CompilerParams(
            collective_id=0, has_side_effects=True, vmem_limit_bytes=56 << 20
        ),
        name="dense_gradients",
    )(*sources, small)
    return outs, sums[stages]


def product_kernel(x_ref, y_ref, out_ref):
    out_ref[...] = dot(x_ref[...], y_ref[...].reshape(y_ref.shape[-2:]), TN).reshape(out_ref.shape)


def expert_gradients(rows, mixed, hidden, grads):
    total, width = rows.shape
    span = hidden.shape[1]
    tile = 256
    params = pltpu.CompilerParams(vmem_limit_bytes=40 << 20)
    din = pl.pallas_call(
        product_kernel,
        grid=(2, width // tile),
        in_specs=[
            pl.BlockSpec((total, tile), lambda g, i: (0, i)),
            pl.BlockSpec((1, total, span), lambda g, i: (g, 0, 0)),
        ],
        out_specs=pl.BlockSpec((1, tile, span), lambda g, i: (g, i, 0)),
        out_shape=jax.ShapeDtypeStruct((2, width, span), F32),
        compiler_params=params,
        name="expert_in_gradient",
    )(rows, mixed)
    ddown = pl.pallas_call(
        product_kernel,
        grid=(pl.cdiv(span, tile),),
        in_specs=[
            pl.BlockSpec((total, tile), lambda i: (0, i)),
            pl.BlockSpec((total, width), lambda i: (0, 0)),
        ],
        out_specs=pl.BlockSpec((tile, width), lambda i: (i, 0)),
        out_shape=jax.ShapeDtypeStruct((span, width), F32),
        compiler_params=params,
        name="expert_out_gradient",
    )(hidden, grads)
    return din, ddown


def body(
    tokens,
    cotangent,
    lengths,
    routes,
    self_qkv,
    self_out,
    cross_weights,
    router,
    gains,
    bias_table,
    expert_in,
    expert_out,
):
    _, seqs, length, width = tokens.shape
    heads = H
    experts = router.shape[2]
    top = routes.shape[3]
    capacity = (5 * top * length + 4 * experts - 1) // (4 * experts)
    block_rows = -(-seqs * capacity // 16) * 16
    rows = seqs * length
    slots = experts * block_rows
    half_index = lax.axis_index("half")
    decoder = half_index == 1
    wqkv, wout, wcross, wrouter, gain = (
        self_qkv[0],
        self_out[0],
        cross_weights[0],
        router[0],
        gains[0],
    )
    w_in, w_down = expert_in[0, 0], expert_out[0, 0]

    column = np.arange(2 * length)
    entry = np.arange(BUCKETS * heads)
    hot, hot_back = (
        jnp.where(
            decoder,
            *(
                (entry[:, None] // heads == bucket[None, :]).astype(np.float32)
                for bucket in reversed(diagonal_buckets(diff))
            ),
        )
        for diff in (np.where(column < length, column, column - 2 * length), column - length + 1)
    )
    own_head = entry[None, :] % heads == np.arange(heads)[:, None]
    bias = lax.dot_general(
        jnp.where(own_head, bias_table, 0.0),
        hot,
        (((1,), (0,)), ((), ())),
        precision=lax.Precision.HIGHEST,
        preferred_element_type=F32,
    )
    own_lengths = jnp.where(decoder, lengths[1], lengths[0])
    self_info = jnp.concatenate([own_lengths, half_index[None]]).astype(jnp.int32)
    cross_info = jnp.concatenate([lengths[0], jnp.zeros((1,), jnp.int32)]).astype(jnp.int32)

    order = jnp.transpose(routes[0], (0, 2, 1)).reshape(seqs, top * length)
    spots, both_spots, stacked, both, tally, route_lanes = find_slots(order, experts, capacity, block_rows, top)
    tallies = jnp.concatenate([tally[:, 0], tally[:, 1] - tally[:, 0]])
    router_wide = jnp.pad(wrouter, ((0, 0), (FIRST, 128 - FIRST - experts)))

    def fetch(returned):
        flat = returned.reshape(slots, width)
        return dot(stacked, flat).astype(BF16).reshape(top, rows, width)

    def combine(values, stats, results):
        return values + sum(stats[:, GATE + k : GATE + k + 1] * results[k] for k in range(top))

    values = tokens[0].reshape(rows, width).astype(F32)
    normed, scale0 = norm_parts(values, gain[0])
    low0 = normed.astype(BF16)
    qkv = dot(low0, wqkv).astype(BF16)
    mixed0, log0, first, stats, send = enter(
        self_info,
        gain[1:2],
        router_wide,
        route_lanes,
        bias,
        False,
        [qkv, wout, tokens[0].reshape(rows, width), both_spots],
        experts,
        length,
    )

    send_shape = (experts, block_rows, width)
    *saved, lefts_self = moe_forward(send.reshape(send_shape), w_in, w_down, 0, None, [low0, mixed0], rows)
    final_enc = combine(first, stats, fetch(saved[0]))
    normed, scale_m = norm_parts(final_enc, gain[2])
    low_m = normed.astype(BF16)
    memory = dot(low_m, wcross).astype(BF16)
    names = ("half", "dp", "expert")
    forward_pairs, back_pairs = half_pairs(lax.axis_size("dp") * lax.axis_size("expert"))
    memory = lax.ppermute(memory, names, forward_pairs)

    normed, scale_c = norm_parts(first, gain[2])
    low_c = normed.astype(BF16)
    query = dot(low_c, wcross[:, :width]).astype(BF16)
    mixed_c, log_c, second, stats, send = enter(
        cross_info,
        gain[1:2],
        router_wide,
        route_lanes,
        stats,
        True,
        [query, memory, wcross[:, width:], first, both_spots],
        experts,
        length,
    )

    lefts = [jnp.where(decoder, low_c, low_m), jnp.where(decoder, mixed_c, low_m)]
    saved = moe_forward(send.reshape(send_shape), w_in, w_down, 1, saved, lefts, rows)
    results = fetch(saved[0])
    final = combine(second, stats, results)
    outputs = final.astype(BF16)

    grad_dec = cotangent[0].reshape(rows, width)
    spread = [(stats[:, GATE + k : GATE + k + 1] * grad_dec.astype(F32)).astype(BF16) for k in range(top)]
    grad_send = dot(spots, jnp.concatenate(spread)).astype(BF16)
    *kept_from, lefts_cross = moe_backward(
        grad_send.reshape(experts, block_rows, width), saved, 1, None, lefts
    )

    grad_second, dbranch_c, dgain_moe_dec, dlog_dec, dquery, dmemory = leave(
        cross_info,
        stats,
        gain[1:2],
        router_wide,
        None,
        [
            kept_from[0].reshape(slots, width),
            both,
            grad_dec,
            results,
            second,
            wcross[:, width:],
            mixed_c,
            log_c,
            query,
            memory,
        ],
        experts,
        length,
    )
    dmemory = lax.ppermute(dmemory, names, back_pairs)
    dnormed = dot(dquery, wcross[:, :width], NT)
    dvalues, dgain_c = norm_back(first, scale_c, gain[2], dnormed)
    grad_first_dec = grad_second + dvalues

    grad, grad_send, dgain_m, cross_grad = memory_gradient(
        stats, gain[2:3], [dmemory, wcross, final_enc, grad_dec, spots], [dquery, dbranch_c]
    )
    cross_peer = over_dp(cross_grad)
    back, mixed_grads, all_grad = moe_backward(
        grad_send.reshape(experts, block_rows, width), saved, 0, kept_from, []
    )
    all_rows, hidden = saved[1], saved[4]
    grad_first, dbranch, dgain_moe, dlog, dqkv_rows, diag = leave(
        self_info,
        stats,
        gain[1:2],
        router_wide,
        bias,
        [
            back.reshape(slots, width),
            both,
            grad,
            results,
            second,
            wout,
            mixed0,
            log0,
            qkv,
            grad_first_dec,
        ],
        experts,
        length,
    )
    dlog = jnp.where(decoder, dlog_dec, dlog)[:, FIRST : FIRST + experts]
    dgain_moe = jnp.where(decoder, dgain_moe_dec[0], dgain_moe[0])
    drouter = lax.dot_general(
        second * stats[:, SCALE : SCALE + 1] * gain[1],
        dlog,
        TN,
        precision=lax.Precision.HIGHEST,
        preferred_element_type=F32,
    )
    dnormed = dot(dqkv_rows, wqkv, NT)
    dvalues, dgain_self = norm_back(values, scale0, gain[0], dnormed)
    d_tokens = (grad_first + dvalues).astype(BF16)
    by_entry = lax.dot_general(
        diag, hot_back, NT, precision=lax.Precision.HIGHEST, preferred_element_type=F32
    )
    dtable = jnp.sum(jnp.where(own_head, by_entry, 0.0), axis=0)

    own_grads = (dqkv_rows, dbranch, cross_grad)
    peer_grads = (over_dp(dqkv_rows), over_dp(dbranch), cross_peer)
    places = 2 * experts
    own = width // places
    extra = jnp.concatenate([dtable.reshape(places, -1), tallies.reshape(places, 1)], axis=1)
    extra = jnp.pad(extra, ((0, 0), (0, -extra.shape[1] % own)))
    small = jnp.concatenate(
        [
            jnp.transpose(drouter),
            jnp.stack([dgain_self, dgain_moe, jnp.where(decoder, dgain_c, dgain_m[0])]),
            jnp.swapaxes(extra.reshape(places, -1, own), 0, 1).reshape(-1, width),
        ]
    )
    small = jnp.pad(small, ((0, -small.shape[0] % 8), (0, 0)))
    (dqkv, dout, dcross), small = dense_gradients(
        [low0, mixed0, *lefts], [lefts_self, lefts_cross], own_grads, peer_grads, small, experts
    )
    place = lax.axis_index("dp") * experts + lax.axis_index("expert")
    mine = lax.dynamic_slice_in_dim(small, place * own, own, 1)
    tail = mine[experts + 3 :].reshape(-1)
    own_table = dtable.shape[0] // places
    d_table = tail[:own_table]
    counts = tail[own_table].astype(jnp.int32)

    ff_half = hidden.shape[-1]
    din, ddown = expert_gradients(
        all_rows.reshape(-1, width),
        mixed_grads.reshape(2, -1, ff_half),
        hidden.reshape(-1, ff_half),
        all_grad.reshape(-1, width),
    )
    return (
        outputs.reshape(1, seqs, length, width),
        d_tokens.reshape(1, seqs, length, width),
        dqkv[None],
        dout[None],
        dcross[None],
        jnp.transpose(mine[:experts])[None],
        mine[experts : experts + 3][None],
        d_table[None],
        din[None, None],
        ddown[None, None],
        counts.reshape(1, 1, 1),
    )


def half_pairs(count):
    return (
        [(i, count + i) for i in range(count)],
        [(count + i, i) for i in range(count)],
    )


def solution(mesh):
    placed = (
        P("half", ("dp", "expert"), None, None),
        P("half", ("dp", "expert"), None, None),
        P(None, ("dp", "expert")),
        P("half", ("dp", "expert"), None, None),
        P("half", None, None),
        P("half", None, None),
        P("half", None, None),
        P("half", None, None),
        P("half", None, None),
        P("half", None),
        P("half", "expert", None, None, None),
        P("half", "expert", None, None),
    )
    return jax.shard_map(
        body,
        mesh=mesh,
        in_specs=placed,
        out_specs=(
            P("half", ("dp", "expert"), None, None),
            P("half", ("dp", "expert"), None, None),
            P("half", ("dp", "expert"), None),
            P("half", ("dp", "expert"), None),
            P("half", ("dp", "expert"), None),
            P("half", ("dp", "expert"), None),
            P("half", None, ("dp", "expert")),
            P("half", ("dp", "expert")),
            P("half", "expert", None, None, "dp"),
            P("half", "expert", "dp", None),
            P("half", "dp", "expert"),
        ),
        check_vma=False,
    )
```

```python
import functools

import jax
import jax.numpy as jnp
import numpy as np
from jax import lax
from jax.experimental import pallas as pl
from jax.experimental.pallas import tpu as pltpu
from jax.sharding import PartitionSpec as P

H = 16
BUCKETS = 32
EPS = 1e-06
ENC_STEPS = (12, 16, 23, 32, 46, 64, 91)
DEC_STEPS = (19, 21, 24, 27, 31, 35, 40, 46, 52, 59, 67, 77, 87, 99, 113)
F32 = jnp.float32
BF16 = jnp.bfloat16
MESH = pl.DeviceIdType.MESH
LOCAL_VMEM = 32 << 20


def cost(gigaflops):
    return pl.CostEstimate(flops=int(gigaflops * 1e9), bytes_accessed=1 << 20, transcendentals=0)
NT = (((1,), (1,)), ((), ()))
TN = (((0,), (0,)), ((), ()))


def dot(a, b, dims=(((1,), (0,)), ((), ()))):
    return lax.dot_general(a, b, dims, preferred_element_type=F32)


def diagonal_buckets(diff):
    apart = np.abs(diff)
    coarse = 8 + sum((apart >= step).astype(np.int32) for step in ENC_STEPS)
    enc = np.where(apart < 8, apart, coarse) + 16 * (diff > 0)
    behind = np.maximum(-diff, 0)
    coarse = 16 + sum((behind >= step).astype(np.int32) for step in DEC_STEPS)
    dec = np.where(behind < 16, behind, coarse)
    return enc.astype(np.int32), dec.astype(np.int32)


def diagonals(bias_ref, head, length):
    row = jnp.broadcast_to(bias_ref[pl.ds(head, 1), :], (length, 2 * length))
    return pltpu.roll(row, 0, 1, stride=1, stride_axis=0)[:, :length]


def fill_masks(info, mask_ref):
    seqs, length, _ = mask_ref.shape
    row_id = lax.broadcasted_iota(jnp.int32, (length, length), 0)
    col_id = lax.broadcasted_iota(jnp.int32, (length, length), 1)
    reach = jnp.where(info[seqs] > 0, row_id, length)
    for seq in range(seqs):
        allowed = (col_id < info[seq]) & (col_id <= reach)
        mask_ref[seq] = jnp.where(allowed, 0.0, -1000000000.0)


def attend(info, bias_ref, q_ref, k_ref, v_ref, out_ref, log_ref, mask_ref):
    has_bias = bias_ref is not None
    seqs, length, _ = mask_ref.shape
    low = lax.broadcasted_iota(jnp.int32, (length, 128), 1) < 64
    fill_masks(info, mask_ref)

    @pl.loop(0, q_ref.shape[1] // 128, unroll=True)
    def _(pair):
        cols = pl.ds(pl.multiple_of(pair * 128, 128), 128)
        biases = [diagonals(bias_ref, 2 * pair + side, length) if has_bias else 0.0 for side in range(2)]
        for seq in range(seqs):
            rows = pl.ds(seq * length, length)
            q, k, v = q_ref[rows, cols] * 0.125, k_ref[rows, cols], v_ref[rows, cols]
            mixed, peaks = [], []
            for side in range(2):
                mine = low if side == 0 else jnp.logical_not(low)
                part = jnp.where(mine, q, jnp.zeros_like(q))
                scores = dot(part, k, NT) + (mask_ref[seq] + biases[side])
                peak = jnp.max(scores, axis=-1, keepdims=True)
                spread = jnp.exp(scores - peak).astype(BF16)
                mixed.append(dot(spread, jnp.where(mine, v, jnp.ones_like(v))))
                peaks.append(peak)
            total = pltpu.roll(jnp.where(low, mixed[1], mixed[0]), 64, 1)
            out_ref[rows, cols] = (jnp.where(low, mixed[0], mixed[1]) / total).astype(BF16)
            log_ref[rows, cols] = jnp.where(low, peaks[0], peaks[1]) + jnp.log(total)


def attend_back(info, bias_ref, q_ref, k_ref, v_ref, a_ref, log_ref, g_ref, dq_ref, dkv_ref, shift, diag_ref, mask_ref):
    has_bias = bias_ref is not None
    seqs, length, _ = mask_ref.shape
    width = q_ref.shape[1]
    low = lax.broadcasted_iota(jnp.int32, (length, 128), 1) < 64
    fill_masks(info, mask_ref)
    if has_bias:
        row_id = lax.broadcasted_iota(jnp.int32, (length, length), 0)
        col_id = lax.broadcasted_iota(jnp.int32, (length, length), 1)
        flip = (row_id + col_id == length - 1).astype(F32).astype(BF16)

    @pl.loop(0, width // 128, unroll=True)
    def _(pair):
        cols = pl.ds(pl.multiple_of(pair * 128, 128), 128)
        kcols = pl.ds(pl.multiple_of(shift + pair * 128, 128), 128)
        vcols = pl.ds(pl.multiple_of(shift + width + pair * 128, 128), 128)
        biases = [diagonals(bias_ref, 2 * pair + side, length) if has_bias else 0.0 for side in range(2)]
        sums = [0.0, 0.0]
        for seq in range(seqs):
            rows = pl.ds(seq * length, length)
            q, k, v, g = q_ref[rows, cols] * 0.125, k_ref[rows, cols], v_ref[rows, cols], g_ref[rows, cols]
            logs = log_ref[rows, cols]
            turned = pltpu.roll(logs, 64, 1)
            product = g.astype(F32) * a_ref[rows, cols].astype(F32)
            minus = (-pltpu.roll(product, 64, 1)).astype(BF16)
            scaled = k * 0.125
            dqs, dks, dvs = [], [], []
            for side in range(2):
                mine = low if side == 0 else jnp.logical_not(low)
                part = jnp.where(mine, q, jnp.zeros_like(q))
                scores = dot(part, k, NT) + (mask_ref[seq] + biases[side])
                probs = jnp.exp(scores - jnp.where(mine, logs, turned))
                dvs.append(dot(probs.astype(BF16), g, TN))
                centred = dot(jnp.where(mine, g, minus), jnp.where(mine, v, jnp.ones_like(v)), NT)
                dlow = (probs * centred).astype(BF16)
                dqs.append(dot(dlow, scaled))
                dks.append(dot(dlow, q, TN))
                if has_bias:
                    sums[side] = sums[side] + dlow.astype(F32)
            dq_ref[rows, cols] = jnp.where(low, dqs[0], dqs[1]).astype(BF16)
            dkv_ref[rows, kcols] = jnp.where(low, dks[0], dks[1]).astype(BF16)
            dkv_ref[rows, vcols] = jnp.where(low, dvs[0], dvs[1]).astype(BF16)
        if has_bias:
            for side in range(2):
                upside = dot(flip, sums[side].astype(BF16))
                wide = jnp.concatenate([upside, jnp.zeros((length, length), F32)], axis=1)
                turned = pltpu.roll(wide, 0, 1, stride=1, stride_axis=0)
                diag_ref[pl.ds(2 * pair + side, 1), :] = jnp.sum(turned, axis=0, keepdims=True)


def norm_parts(values, gain):
    scale = lax.rsqrt(jnp.mean(values * values, axis=-1, keepdims=True) + EPS)
    return values * scale * gain, scale


def norm_back(values, scale, gain, grad):
    unit = values * scale
    gain_grad = jnp.sum(grad * unit, axis=0)
    pushed = grad * gain
    back = scale * (pushed - unit * jnp.mean(pushed * unit, axis=-1, keepdims=True))
    return back, gain_grad


def gelu_parts(gate):
    c, a = 0.7978845608028654, 0.044715
    square = gate * gate
    u = 0.5 + 0.5 * jnp.tanh(gate * (c + c * a * square))
    slope = u * (1.0 + (gate * (2.0 * c + 6.0 * c * a * square)) * (1.0 - u))
    return gate * u, slope


def flipped(value, bit):
    step = 1 << bit
    return value + step * (1 - 2 * (value // step % 2))


def crossed(value, other):
    for bit in range(other.bit_length()):
        if other >> bit & 1:
            value = flipped(value, bit)
    return value


def greet(partners):
    barrier = pltpu.get_barrier_semaphore()
    for partner in partners:
        pl.semaphore_signal(barrier, inc=1, device_id=partner, device_id_type=MESH)
    pl.semaphore_wait(barrier, len(partners))


def remote(src, dst, out_sem, in_sem, device):
    return pltpu.make_async_remote_copy(
        src_ref=src,
        dst_ref=dst,
        send_sem=out_sem,
        recv_sem=in_sem,
        device_id=device,
        device_id_type=MESH,
    )


def tile_loop(count, step, body):
    @pl.loop(0, count // step)
    def _(i):
        body(pl.multiple_of(i * step, step), step)

    if count % step:
        body(count // step * step, count % step)


def groups_of(experts, block):
    size = 1
    while size * 2 * block <= 320 and size * 2 <= experts:
        size *= 2
    if experts <= 2 * size:
        half = max(size // 2, 1)
        return [(0, size), *((k, half) for k in range(size, experts, half))]
    return [(k, size) for k in range(0, experts, size)]


class Turn:
    def __init__(self, experts, block, there, home):
        self.me, self.dp = lax.axis_index("expert"), lax.axis_index("dp")
        self.experts, self.block = experts, block
        self.peer = {"dp": 1 - self.dp}
        self.groups = groups_of(experts, block)
        self.there_refs, self.home_refs = there, home

    def greet(self):
        greet([{"expert": crossed(self.me, k)} for k in range(1, self.experts)] + [self.peer])

    def there(self, k):
        src, dst, out_sems, in_sems = self.there_refs
        partner = crossed(self.me, k)
        return remote(src.at[partner], dst.at[self.me], out_sems.at[k], in_sems.at[k], {"expert": partner})

    def home(self, k):
        src, dst, out_sems, in_sems = self.home_refs
        partner = crossed(self.me, k)
        return remote(src.at[partner], dst.at[self.me], out_sems.at[k], in_sems.at[k], {"expert": partner})

    def arrive(self, first, size):
        for k in range(max(first, 1), first + size):
            self.there(k).wait_recv()

    def base(self, first, size):
        return crossed(self.me // size, first // size) * size

    def spans(self, first, size):
        base = self.base(first, size)
        rows = pl.ds(pl.multiple_of(base * self.block, size * self.block), size * self.block)
        return pl.ds(base, size), rows


class Lefts:
    def __init__(self, refs, out, scratch, width):
        self.refs, self.out = refs, out
        self.held, self.stage, self.loaded, self.sent, self.came = scratch
        self.half = width // 2
        self.dp = lax.axis_index("dp")

    def fetch(self, i):
        return pltpu.make_async_copy(self.refs[i], self.held.at[i % 2], self.loaded.at[i])

    def copy(self, i):
        return remote(self.stage.at[i], self.out.at[i], self.sent.at[i], self.came.at[i], {"dp": 1 - self.dp})

    def load(self):
        for i in range(2):
            self.fetch(i).start()

    def send(self):
        for i in range(4):
            self.fetch(i).wait()
            cols = pl.ds(pl.multiple_of((1 - self.dp) * self.half, 128), self.half)
            self.stage[i] = self.held[i % 2, :, cols]
            self.copy(i).start()
            if i + 2 < 4:
                self.fetch(i + 2).start()

    def wait(self):
        for i in range(4):
            self.copy(i).wait()


def transpose_kernel_part(loads, tall, wide, wsem, tsem):
    copies = [pltpu.make_async_copy(src, dst, wsem.at[i]) for i, (src, dst, _) in enumerate(loads)]
    for copy in copies:
        copy.start()
    for i, (_, held, out) in enumerate(loads):
        slab = tall.shape[1]
        stages = [tall.at[i] if out.shape[1] == tall.shape[2] else wide.at[pl.ds(i * slab, slab)] for i in range(2)]
        steps = out.shape[0] // slab
        copies[i].wait()

        def put(t, slot, stages=stages, out=out, slab=slab):
            rows = pl.ds(pl.multiple_of(t * slab, slab), slab)
            return pltpu.make_async_copy(stages[slot], out.at[rows], tsem.at[slot])

        def step(pair, carry, stages=stages, held=held, put=put, slab=slab, steps=steps):
            for slot in range(2):
                t = 2 * pair + slot

                @pl.when(t < steps)
                def _(t=t, slot=slot):
                    @pl.when(pair > 0)
                    def _():
                        put(t - 2, slot).wait()

                    cols = pl.ds(pl.multiple_of(t * slab, slab), slab)
                    stages[slot][...] = jnp.transpose(held[:, cols])
                    put(t, slot).start()

            return carry

        lax.fori_loop(0, pl.cdiv(steps, 2), step, 0)
        for t in (steps - 2, steps - 1):
            put(t, t % 2).wait()


def expert_forward_kernel(turn, has_prev, *refs):
    send_ref, w_in, w_down = refs[:3]
    left_refs, refs = refs[3 + 10 * has_prev : 3 + 14 * has_prev], refs[3 + 14 * has_prev :]
    back_out, rows_out, slope_out, value_out, hidden_out, slope_peer_out, value_peer_out = refs[:7]
    wgt_out, wut_out, wdt_out = refs[7:10]
    left_out, refs = refs[10 : 10 + has_prev], refs[10 + has_prev :]
    wg, wu, wd, rows, back, made, rows_peer, slopes, values, hidden = refs[:10]
    slopes_peer, values_peer, tall = refs[10:13]
    wsem, s1, r1, s2, r2, sx, rx, osem, tsem = refs[13:22]
    experts, block, width = send_ref.shape
    ff = wd.shape[0]
    span = ff // 2
    lefts = Lefts(left_refs, left_out[0], (tall, *refs[22:]), width) if has_prev else None

    @pl.when(lax.axis_index("half") != turn)
    def _():
        if lefts:
            lefts.load()
            greet([{"dp": 1 - lax.axis_index("dp")}])
            lefts.send()
        loads = ((w_in.at[0], wg, wgt_out), (w_in.at[1], wu, wut_out), (w_down, wd, wdt_out))
        transpose_kernel_part(loads, tall, slopes, wsem, tsem)
        if lefts:
            lefts.wait()

    @pl.when(lax.axis_index("half") == turn)
    def _():
        t = Turn(experts, block, (send_ref, rows, s1, r1), (made, back, s2, r2))
        t.greet()

        def rows_over(part):
            blocks, _ = t.spans(*t.groups[part])
            return remote(rows.at[blocks], rows_peer.at[blocks], sx.at[part], rx.at[part], t.peer)

        for k in range(1, experts):
            t.there(k).start()
        rows[t.me] = send_ref[t.me]
        loads = [
            pltpu.make_async_copy(src, dst, wsem.at[i])
            for i, (src, dst) in enumerate(((w_in.at[0], wg), (w_in.at[1], wu), (w_down, wd)))
        ]
        for load in loads:
            load.start()
        if lefts:
            lefts.load()
        for part, (first, size) in enumerate(t.groups):
            t.arrive(first, size)
            rows_over(part).start()
            blocks, span_rows = t.spans(first, size)
            if part == 0:
                loads[0].wait()
                loads[1].wait()

            def up_tile(start, count, blocks=blocks, span_rows=span_rows, size=size):
                x = rows[blocks].reshape(size * block, width)
                cols = pl.ds(start, count)
                value, slope = gelu_parts(dot(x, wg[:, cols]))
                up = dot(x, wu[:, cols])
                hidden[span_rows, cols] = (value * up).astype(BF16)
                values[span_rows, cols] = value.astype(BF16)
                slopes[span_rows, cols] = (up * slope).astype(BF16)

            tile_loop(ff, 512, up_tile)
            if part == 0:
                loads[2].wait()

            def down_tile(start, count, blocks=blocks, span_rows=span_rows, size=size):
                cols = pl.ds(start, count)
                y = dot(hidden[span_rows, :], wd[:, cols]).astype(BF16)
                made[blocks, :, cols] = y.reshape(size, block, count)

            tile_loop(width, 512, down_tile)
            for k in range(max(first, 1), first + size):
                t.home(k).start()
        back[t.me] = made[t.me]
        half_cols = pl.ds(pl.multiple_of(t.dp * span, 128), span)
        other_cols = pl.ds(pl.multiple_of((1 - t.dp) * span, 128), span)
        outs = [
            (slopes, slope_out),
            (values, value_out),
            (hidden.at[:, half_cols], hidden_out.at[0]),
            (rows, rows_out.at[0]),
        ]
        outs = [pltpu.make_async_copy(src, dst, osem.at[i]) for i, (src, dst) in enumerate(outs)]
        for out in outs:
            out.start()
        if lefts:
            lefts.send()

        for part in range(len(t.groups)):
            rows_over(part).wait_recv()

        def peer_tile(start, count):
            x = rows_peer[...].reshape(experts * block, width)
            here = pl.ds(start, count)
            cols = pl.ds(pl.multiple_of(t.dp * span + start, 128), count)
            value, slope = gelu_parts(dot(x, wg[:, cols]))
            up = dot(x, wu[:, cols])
            hidden[:, pl.ds(pl.multiple_of((1 - t.dp) * span + start, 128), count)] = (value * up).astype(BF16)
            values_peer[:, here] = value.astype(BF16)
            slopes_peer[:, here] = (up * slope).astype(BF16)

        tile_loop(span, 512, peer_tile)
        more = [
            (slopes_peer, slope_peer_out),
            (values_peer, value_peer_out),
            (hidden.at[:, other_cols], hidden_out.at[1]),
            (rows_peer, rows_out.at[1]),
        ]
        more = [pltpu.make_async_copy(src, dst, osem.at[4 + i]) for i, (src, dst) in enumerate(more)]
        for out in more:
            out.start()
        for k in range(1, experts):
            t.home(k).wait_recv()
        back_copy = pltpu.make_async_copy(back, back_out, osem.at[8])
        back_copy.start()
        for k in range(1, experts):
            t.there(k).wait_send()
            t.home(k).wait_send()
        for part in range(len(t.groups)):
            rows_over(part).wait_send()
        if lefts:
            lefts.wait()
        for out in [*outs, *more, back_copy]:
            out.wait()


def expert_backward_kernel(turn, has_prev, *refs):
    send_ref = refs[0]
    sources = refs[1:8]
    refs = refs[8 + 3 * has_prev :]
    back_out, mixed_out, grad_out = refs[:3]
    wdt, dgate, dup, wgt, wut, dgate_peer, dup_peer = refs[3:10]
    grads, back, made, grads_peer = refs[10:14]
    wsem, s1, r1, s2, r2, sx, rx, osem = refs[14:]
    experts, block, width = send_ref.shape
    ff = wdt.shape[1]
    span = ff // 2
    dp = lax.axis_index("dp")
    t = Turn(experts, block, (send_ref, grads, s1, r1), (made, back, s2, r2))

    @pl.when(lax.axis_index("half") == turn)
    def _():
        t.greet()

        def grads_over(part):
            blocks, _ = t.spans(*t.groups[part])
            return remote(grads.at[blocks], grads_peer.at[blocks], sx.at[part], rx.at[part], t.peer)

        for k in range(1, experts):
            t.there(k).start()
        grads[t.me] = send_ref[t.me]
        held = (wdt, dgate, dup, wgt, wut, dgate_peer, dup_peer)
        loads = [pltpu.make_async_copy(src, dst, wsem.at[i]) for i, (src, dst) in enumerate(zip(sources, held))]
        for load in loads:
            load.start()
        for load in loads[:3]:
            load.wait()
        for part, (first, size) in enumerate(t.groups):
            t.arrive(first, size)
            grads_over(part).start()
            blocks, span_rows = t.spans(first, size)

            def hidden_tile(start, count, blocks=blocks, span_rows=span_rows, size=size):
                dy = grads[blocks].reshape(size * block, width)
                cols = pl.ds(start, count)
                dhidden = dot(dy, wdt[:, cols])
                dgate[span_rows, cols] = (dhidden * dgate[span_rows, cols].astype(F32)).astype(BF16)
                dup[span_rows, cols] = (dhidden * dup[span_rows, cols].astype(F32)).astype(BF16)

            tile_loop(ff, 512, hidden_tile)
            if part == 0:
                loads[3].wait()
                loads[4].wait()

            def rows_tile(start, count, blocks=blocks, span_rows=span_rows, size=size):
                cols = pl.ds(start, count)
                dr = dot(dgate[span_rows, :], wgt[:, cols]) + dot(dup[span_rows, :], wut[:, cols])
                made[blocks, :, cols] = dr.astype(BF16).reshape(size, block, count)

            tile_loop(width, 512, rows_tile)
            for k in range(max(first, 1), first + size):
                t.home(k).start()
        back[t.me] = made[t.me]
        half_cols = pl.ds(pl.multiple_of(dp * span, 128), span)
        outs = [
            (dgate.at[:, half_cols], mixed_out.at[0, 0]),
            (dup.at[:, half_cols], mixed_out.at[1, 0]),
            (grads, grad_out.at[0]),
        ]
        outs = [pltpu.make_async_copy(src, dst, osem.at[i]) for i, (src, dst) in enumerate(outs)]
        for out in outs:
            out.start()

        for load in loads[5:]:
            load.wait()
        for part in range(len(t.groups)):
            grads_over(part).wait_recv()

        def peer_tile(start, count):
            dy = grads_peer[...].reshape(experts * block, width)
            here = pl.ds(start, count)
            dhidden = dot(dy, wdt[:, pl.ds(pl.multiple_of(dp * span + start, 128), count)])
            dgate_peer[:, here] = (dhidden * dgate_peer[:, here].astype(F32)).astype(BF16)
            dup_peer[:, here] = (dhidden * dup_peer[:, here].astype(F32)).astype(BF16)

        tile_loop(span, 512, peer_tile)
        more = [
            (dgate_peer, mixed_out.at[0, 1]),
            (dup_peer, mixed_out.at[1, 1]),
            (grads_peer, grad_out.at[1]),
        ]
        more = [pltpu.make_async_copy(src, dst, osem.at[3 + i]) for i, (src, dst) in enumerate(more)]
        for out in more:
            out.start()
        for k in range(1, experts):
            t.home(k).wait_recv()
        back_copy = pltpu.make_async_copy(back, back_out, osem.at[6])
        back_copy.start()
        for k in range(1, experts):
            t.there(k).wait_send()
            t.home(k).wait_send()
        for part in range(len(t.groups)):
            grads_over(part).wait_send()
        for out in [*outs, *more, back_copy]:
            out.wait()


def expert_call(kernel, number, turn, send, sources, prev, more, out_shape, scratch, name):
    vmem, hbm = pl.BlockSpec(memory_space=pltpu.VMEM), pl.BlockSpec(memory_space=pl.ANY)
    prev = list(prev or [])
    return pl.pallas_call(
        functools.partial(kernel, turn, bool(prev)),
        in_specs=[vmem] + [hbm] * (len(sources) + len(prev) + len(more)),
        out_specs=[hbm] * len(out_shape),
        out_shape=out_shape,
        input_output_aliases={1 + len(sources) + i: i for i in range(len(prev))},
        scratch_shapes=scratch,
        compiler_params=pltpu.CompilerParams(
            collective_id=number, has_side_effects=True, vmem_limit_bytes=60 << 20
        ),
        cost_estimate=cost(40),
        name=name,
    )(send, *sources, *prev, *more)


def moe_forward(send, w_in, w_down, turn, prev, lefts, slab):
    experts, block, width = send.shape
    ff = w_down.shape[0]
    total = experts * block
    parts = len(groups_of(experts, block))
    dma = pltpu.SemaphoreType.DMA
    scratch = [
        pltpu.VMEM((width, ff), BF16),
        pltpu.VMEM((width, ff), BF16),
        pltpu.VMEM((ff, width), BF16),
        *[pltpu.VMEM(send.shape, BF16)] * 4,
        *[pltpu.VMEM((total, ff), BF16)] * 3,
        *[pltpu.VMEM((total, ff // 2), BF16)] * 2,
        pltpu.VMEM((2, slab, width), BF16),
        dma((3,)),
        *[dma((experts,))] * 4,
        *[dma((parts,))] * 2,
        dma((9,)),
        dma((2,)),
    ]
    shapes = [
        send.shape,
        (2, *send.shape),
        (total, ff),
        (total, ff),
        (2, total, ff // 2),
        (total, ff // 2),
        (total, ff // 2),
        (ff, width),
        (ff, width),
        (width, ff),
    ]
    if lefts:
        rows = lefts[0].shape[0]
        shapes.append((4, rows, width // 2))
        scratch += [pltpu.VMEM((4, rows, width // 2), BF16), *[dma((4,))] * 3]
    out_shape = [jax.ShapeDtypeStruct(shape, BF16) for shape in shapes]
    return expert_call(
        expert_forward_kernel, 1 + turn, turn, send, [w_in, w_down], prev, lefts, out_shape, scratch, "moe_forward"
    )


def moe_backward(grad_send, saved, turn, prev):
    experts, block, width = grad_send.shape
    _, _, slope, value, _, slope_peer, value_peer, wgt, wut, wdt, _ = saved
    total, ff = slope.shape
    parts = len(groups_of(experts, block))
    dma = pltpu.SemaphoreType.DMA
    scratch = [
        pltpu.VMEM((width, ff), BF16),
        *[pltpu.VMEM((total, ff), BF16)] * 2,
        *[pltpu.VMEM((ff, width), BF16)] * 2,
        *[pltpu.VMEM((total, ff // 2), BF16)] * 2,
        *[pltpu.VMEM(grad_send.shape, BF16)] * 4,
        dma((7,)),
        *[dma((experts,))] * 4,
        *[dma((parts,))] * 2,
        dma((7,)),
    ]
    out_shape = [
        jax.ShapeDtypeStruct(grad_send.shape, BF16),
        jax.ShapeDtypeStruct((2, 2, total, ff // 2), BF16),
        jax.ShapeDtypeStruct((2, *grad_send.shape), BF16),
    ]
    return expert_call(
        expert_backward_kernel,
        3 + turn,
        turn,
        grad_send,
        [wdt, slope, value, wgt, wut, slope_peer, value_peer],
        prev,
        [],
        out_shape,
        scratch,
        "moe_backward",
    )


GATE, TOTAL, SCALE, ROUTE, FIRST = 0, 2, 3, 4, 8


class Loads:
    def __init__(self, pairs, sems):
        self.copies = [pltpu.make_async_copy(src, dst, sems.at[i]) for i, (src, dst) in enumerate(pairs)]

    def start(self):
        for copy in self.copies:
            copy.start()

    def wait(self, *which):
        for i in which:
            self.copies[i].wait()


def slots_kernel(experts, capacity, block, order_ref, spots_out, both_out, turned_out, both_turned_out, tally_out, route_out, route_rows):
    seqs, pairs = order_ref.shape
    top = spots_out.shape[1] // both_out.shape[1]
    length = pairs // top
    rows = seqs * length
    slots = spots_out.shape[0]
    expert_id = lax.broadcasted_iota(jnp.int32, (experts, pairs), 0)
    slot_id = lax.broadcasted_iota(jnp.int32, (slots, length), 0)
    row_id = lax.broadcasted_iota(jnp.int32, (pairs, pairs), 0)
    col_id = lax.broadcasted_iota(jnp.int32, (pairs, pairs), 1)
    earlier = (row_id < col_id).astype(F32).astype(BF16)
    route_rows[...] = jnp.zeros_like(route_rows)
    tally = jnp.zeros((experts, 128), F32)
    lane = lax.broadcasted_iota(jnp.int32, (experts, 128), 1)
    for seq in range(seqs):
        order = order_ref[seq : seq + 1, :]
        picked = (expert_id == order).astype(F32)
        place = jnp.sum(dot(picked.astype(BF16), earlier) * picked, axis=0, keepdims=True)
        kept = place < capacity
        target = jnp.where(kept, order * block + seq * capacity + place.astype(jnp.int32), -1)
        taken = jnp.sum(picked * kept.astype(F32), axis=1, keepdims=True)
        whole = jnp.sum(picked, axis=1, keepdims=True)
        tally = tally + jnp.where(lane == 0, taken, jnp.where(lane == 1, whole, 0.0))
        total = jnp.zeros((slots, length), F32)
        for k in range(top):
            part = pl.ds(k * length, length)
            hot = (slot_id == target[:, k * length : (k + 1) * length]).astype(F32)
            spots_out[:, pl.ds(k * rows + seq * length, length)] = hot.astype(BF16)
            total = total + hot
            route_rows[pl.ds(ROUTE + k, 1), pl.ds(seq * length, length)] = order_ref[
                pl.ds(seq, 1), part
            ].astype(F32)
        both_out[:, pl.ds(seq * length, length)] = total.astype(BF16)
    tally_out[...] = tally
    turned_out[...] = jnp.transpose(spots_out[...])
    both_turned_out[...] = jnp.transpose(both_out[...])
    route_out[...] = jnp.transpose(route_rows[...])


def find_slots(order, experts, capacity, block, top):
    seqs, pairs = order.shape
    rows = seqs * pairs // top
    slots = experts * block
    vmem = pl.BlockSpec(memory_space=pltpu.VMEM)
    return pl.pallas_call(
        functools.partial(slots_kernel, experts, capacity, block),
        in_specs=[vmem],
        out_specs=[vmem] * 6,
        out_shape=[
            jax.ShapeDtypeStruct((slots, top * rows), BF16),
            jax.ShapeDtypeStruct((slots, rows), BF16),
            jax.ShapeDtypeStruct((top * rows, slots), BF16),
            jax.ShapeDtypeStruct((rows, slots), BF16),
            jax.ShapeDtypeStruct((experts, 128), F32),
            jax.ShapeDtypeStruct((rows, 128), F32),
        ],
        scratch_shapes=[pltpu.VMEM((128, rows), F32)],
        compiler_params=pltpu.CompilerParams(vmem_limit_bytes=LOCAL_VMEM),
        cost_estimate=cost(1),
        name="find_slots",
    )(order)


def enter_kernel(cross, experts, count, info, gain_ref, router_ref, lanes_ref, lead_ref, *refs):
    held, refs = refs[:count], refs[count:]
    mixed_out, log_out, result_out, stats_out, send_out, low_ref, mask_ref = refs
    w_out, x, spots = held[count - 3 :]
    rows, width = x.shape
    step = min(512, width)
    if cross:
        q_ref, kv = held[:2]
        k_ref, v_ref = kv.at[:, pl.ds(0, width)], kv.at[:, pl.ds(width, width)]
    else:
        q_ref, k_ref, v_ref = (held[0].at[:, pl.ds(i * width, width)] for i in range(3))

    def work():
        attend(info, None if cross else lead_ref, q_ref, k_ref, v_ref, mixed_out, log_out, mask_ref)
        for start in range(0, width, step):
            cols = pl.ds(start, step)
            result_out[:, cols] = x[:, cols].astype(F32) + dot(mixed_out[...], w_out[:, cols])
        values = result_out[...]
        scale = lax.rsqrt(jnp.mean(values * values, axis=-1, keepdims=True) + EPS)
        normed = values * scale * gain_ref[...]
        low = normed.astype(BF16)
        low_ref[...] = low
        logits = dot(low, router_ref[...]) + dot((normed - low.astype(F32)).astype(BF16), router_ref[...])
        lane = lax.broadcasted_iota(jnp.int32, (rows, 128), 1)
        valid = (lane >= FIRST) & (lane < FIRST + experts)
        logits = jnp.where(valid, logits, -1e30)
        spread = jnp.where(valid, jnp.exp(logits - jnp.max(logits, axis=-1, keepdims=True)), 0.0)
        probs = spread / jnp.sum(spread, axis=-1, keepdims=True)
        routes = lanes_ref[...]
        chosen = [
            jnp.sum(
                jnp.where(lane == routes[:, ROUTE + k : ROUTE + k + 1].astype(jnp.int32) + FIRST, probs, 0.0),
                axis=-1,
                keepdims=True,
            )
            for k in range(2)
        ]
        total = chosen[0] + chosen[1]
        stats = probs + routes
        for at, column in ((GATE, chosen[0] / total), (GATE + 1, chosen[1] / total), (TOTAL, total), (SCALE, scale)):
            stats = jnp.where(lane == at, column, stats)
        stats_out[...] = stats
        for start in range(0, width, step):
            cols = pl.ds(start, step)
            send_out[:, cols] = dot(spots[...], low_ref[:, cols]).astype(BF16)

    if not cross:
        work()
        return
    decoder = lax.axis_index("half") == 1
    pl.when(decoder)(work)

    @pl.when(jnp.logical_not(decoder))
    def _():
        result_out[...] = x[...].astype(F32)
        stats_out[...] = lead_ref[...]


def enter(info, gain, router, lanes, lead, cross, sources, experts, length):
    rows, width = sources[-2].shape
    vmem = pl.BlockSpec(memory_space=pltpu.VMEM)
    count = len(sources)
    return pl.pallas_call(
        functools.partial(enter_kernel, cross, experts, count),
        in_specs=[pl.BlockSpec(memory_space=pltpu.SMEM)] + [vmem] * (4 + count),
        out_specs=[vmem] * 5,
        out_shape=[
            jax.ShapeDtypeStruct((rows, width), BF16),
            jax.ShapeDtypeStruct((rows, width), F32),
            jax.ShapeDtypeStruct((rows, width), F32),
            jax.ShapeDtypeStruct((rows, 128), F32),
            jax.ShapeDtypeStruct((sources[-1].shape[0], width), BF16),
        ],
        scratch_shapes=[
            pltpu.VMEM((rows, width), BF16),
            pltpu.VMEM((rows // length, length, length), F32),
        ],
        compiler_params=pltpu.CompilerParams(vmem_limit_bytes=LOCAL_VMEM),
        cost_estimate=cost(10),
        name="enter_cross" if cross else "enter_self",
    )(info, gain, router, lanes, lead, *sources)


def norm_back_rows(values, scale, gain, grad):
    unit = values * scale
    pushed = grad * gain
    back = scale * (pushed - unit * jnp.mean(pushed * unit, axis=-1, keepdims=True))
    return back, jnp.sum(grad * unit, axis=0, keepdims=True)


def leave_kernel(cross, experts, count, info, stats_ref, gain_ref, router_ref, *refs):
    bias_ref, refs = (None, refs) if cross else (refs[0], refs[1:])
    sources, refs = refs[:count], refs[count:]
    grad_out, branch_out, dgain_out, dlog_out, dq_out, last_out = refs[:6]
    held, (dmixed, mask_ref, sems) = refs[6 : 6 + count], refs[6 + count :]
    back, both, grad, results, x, w_out, a, log = held[:8]
    seqs, length, _ = mask_ref.shape
    width = x.shape[1]
    loads = Loads(zip(sources, held), sems)
    if cross:
        q_ref, kv = held[8:]
        k_ref, v_ref = kv.at[:, pl.ds(0, width)], kv.at[:, pl.ds(width, width)]
        dkv_out, shift, diag_out = last_out, 0, None
    else:
        qkv, ready = held[8:]
        q_ref, k_ref, v_ref = (qkv.at[:, pl.ds(i * width, width)] for i in range(3))
        dkv_out, shift, diag_out = dq_out, width, last_out

    def leave():
        loads.wait(0, 1, 2, 3, 4)
        dgain = jnp.zeros((1, width), F32)
        lane = lax.broadcasted_iota(jnp.int32, (length, 128), 1)
        for seq in range(seqs):
            rows = pl.ds(seq * length, length)
            stats = stats_ref[rows, :]
            gates = [stats[:, GATE + k : GATE + k + 1] for k in range(2)]
            hots = [
                (lane == stats[:, ROUTE + k : ROUTE + k + 1].astype(jnp.int32) + FIRST).astype(F32)
                for k in range(2)
            ]
            probs = jnp.where((lane >= FIRST) & (lane < FIRST + experts), stats, 0.0)
            g = grad[rows, :].astype(F32)
            dgates = [
                jnp.sum(g * results[k, rows, :].astype(F32), axis=-1, keepdims=True) for k in range(2)
            ]
            shared = dgates[0] * gates[0] + dgates[1] * gates[1]
            dprobs = sum((dgates[k] - shared) / stats[:, TOTAL : TOTAL + 1] * hots[k] for k in range(2))
            dlog = probs * (dprobs - jnp.sum(dprobs * probs, axis=-1, keepdims=True))
            dlog_out[rows, :] = dlog
            dnormed = dot(both[rows, :], back[...]) + dot(dlog.astype(BF16), router_ref[...], NT)
            dx, part = norm_back_rows(x[rows, :], stats[:, SCALE : SCALE + 1], gain_ref[...], dnormed)
            dgain = dgain + part
            grad_out[rows, :] = g + dx
        dgain_out[...] = jnp.broadcast_to(dgain, dgain_out.shape)

    def attention():
        loads.wait(5)
        branch_out[...] = grad_out[...].astype(BF16)
        step = min(512, width)
        for start in range(0, width, step):
            cols = pl.ds(start, step)
            dmixed[:, cols] = dot(branch_out[...], w_out[cols, :], NT).astype(BF16)
        loads.wait(*((6, 7, 8, 9) if cross else (6, 7, 8)))
        attend_back(
            info, bias_ref, q_ref, k_ref, v_ref, a, log, dmixed, dq_out, dkv_out, shift, diag_out, mask_ref
        )

    decoder = lax.axis_index("half") == 1
    if cross:

        @pl.when(decoder)
        def _():
            loads.start()
            leave()
            attention()

    else:
        loads.start()

        @pl.when(jnp.logical_not(decoder))
        def _():
            leave()
            loads.wait(9)

        @pl.when(decoder)
        def _():
            loads.wait(0, 1, 2, 3, 4, 9)
            grad_out[...] = ready[...]

        attention()


def leave(info, stats, gain, router, bias, sources, experts, length):
    cross = bias is None
    rows, width = sources[4].shape
    seqs = rows // length
    vmem, hbm = pl.BlockSpec(memory_space=pltpu.VMEM), pl.BlockSpec(memory_space=pl.ANY)
    lead = [] if cross else [bias]
    out_shape = [
        jax.ShapeDtypeStruct((rows, width), F32),
        jax.ShapeDtypeStruct((rows, width), BF16),
        jax.ShapeDtypeStruct((8, width), F32),
        jax.ShapeDtypeStruct((rows, 128), F32),
        jax.ShapeDtypeStruct((rows, width if cross else 3 * width), BF16),
        jax.ShapeDtypeStruct((rows, 2 * width), BF16) if cross else jax.ShapeDtypeStruct(bias.shape, F32),
    ]
    return pl.pallas_call(
        functools.partial(leave_kernel, cross, experts, len(sources)),
        in_specs=[pl.BlockSpec(memory_space=pltpu.SMEM)] + [vmem] * (3 + len(lead)) + [hbm] * len(sources),
        out_specs=[vmem] * 6,
        out_shape=out_shape,
        scratch_shapes=[
            *(pltpu.VMEM(a.shape, a.dtype) for a in sources),
            pltpu.VMEM((rows, width), BF16),
            pltpu.VMEM((seqs, length, length), F32),
            pltpu.SemaphoreType.DMA((len(sources),)),
        ],
        compiler_params=pltpu.CompilerParams(vmem_limit_bytes=56 << 20),
        cost_estimate=cost(16),
        name="leave_cross" if cross else "leave_self",
    )(info, stats, gain, router, *lead, *sources)


def memory_kernel(stats_ref, gain_ref, *refs):
    (dmemory, w, x, cotangent, spots), parts, refs = refs[:5], refs[5:7], refs[7:]
    grad_out, send_out, dgain_out, cross_out, dnormed, spread = refs
    rows, width = x.shape

    @pl.when(lax.axis_index("half") == 1)
    def _():
        for i, part in enumerate(parts):
            cross_out[:, pl.ds(i * width, width)] = part[...]

    @pl.when(lax.axis_index("half") == 0)
    def _():
        cross_out[...] = dmemory[...]
        step = min(512, width)
        for start in range(0, width, step):
            cols = pl.ds(start, step)
            dnormed[:, cols] = dot(dmemory[...], w[cols, :], NT)
        scale = lax.rsqrt(jnp.mean(x[...] * x[...], axis=-1, keepdims=True) + EPS)
        dx, dgain = norm_back_rows(x[...], scale, gain_ref[...], dnormed[...])
        dgain_out[...] = jnp.broadcast_to(dgain, dgain_out.shape)
        grad = cotangent[...].astype(F32) + dx
        grad_out[...] = grad
        for k in range(2):
            gate = stats_ref[:, GATE + k : GATE + k + 1]
            spread[pl.ds(k * rows, rows), :] = (gate * grad).astype(BF16)
        for start in range(0, width, step):
            cols = pl.ds(start, step)
            send_out[:, cols] = dot(spots[...], spread[:, cols]).astype(BF16)


def memory_gradient(stats, gain, sources, parts):
    rows, width = sources[2].shape
    vmem = pl.BlockSpec(memory_space=pltpu.VMEM)
    return pl.pallas_call(
        memory_kernel,
        in_specs=[vmem] * (2 + len(sources) + len(parts)),
        out_specs=[vmem] * 4,
        out_shape=[
            jax.ShapeDtypeStruct((rows, width), F32),
            jax.ShapeDtypeStruct((sources[4].shape[0], width), BF16),
            jax.ShapeDtypeStruct((8, width), F32),
            jax.ShapeDtypeStruct((rows, 2 * width), BF16),
        ],
        scratch_shapes=[
            pltpu.VMEM((rows, width), F32),
            pltpu.VMEM((2 * rows, width), BF16),
        ],
        compiler_params=pltpu.CompilerParams(vmem_limit_bytes=LOCAL_VMEM),
        cost_estimate=cost(4),
        name="memory_gradient",
    )(stats, gain, *sources, *parts)


def dense_kernel(stages, chunk, lag, *refs):
    sources, small_ref = refs[:11], refs[11]
    out_refs, small_out, small_in = refs[12:15], refs[15], refs[16]
    held, xt_ref, refs = refs[17:28], refs[28], refs[29:]
    x_refs, own_refs, peer_refs, xp = held[:4], held[4:7], held[7:10], held[10]
    sums, parts = refs[:stages], refs[stages : 2 * stages]
    ss, rs, sk, rk, sl = refs[2 * stages :]
    counts = [ref.shape[1] // chunk for ref in own_refs]
    starts = [sum(counts[:i]) for i in range(3)]
    chunks = sum(counts)
    per_cross = counts[2] // 2
    rows, half = xp.shape[1:]
    dp, me = lax.axis_index("dp"), lax.axis_index("expert")
    peer = {"dp": 1 - dp}
    partners = [flipped(me, k) for k in range(stages)]
    bits = [me // (1 << k) % 2 for k in range(stages)]
    load = [pltpu.make_async_copy(sources[i], held[i], sl.at[i]) for i in range(11)]
    for i in (10, 2, 3, 6, 9, 0, 4, 7, 1, 5, 8):
        load[i].start()
    greet([peer] + [{"expert": p} for p in partners])

    def send_small(step):
        src = small_ref if step == 0 else small_out.at[step - 1]
        device = peer if step == 0 else {"expert": partners[stages - step]}
        return remote(src, small_in.at[step], ss.at[step], rs.at[step], device)

    def order(k, odd):
        return 1 - k if odd and k < 2 else k

    def send_part(k, c, odd):
        bit = order(k, odd)
        other = 1 - bits[bit]
        src = sums[0].at[c, :, :, other] if k == 0 and not odd else sums[k].at[c, :, other]
        return remote(src, parts[k].at[c], sk.at[k, c], rk.at[k, c], {"expert": partners[bit]})

    def turn_x(g):
        load[g].wait()
        cols = pl.ds(pl.multiple_of(dp * half, half), half)
        xt_ref[g, :, :rows] = jnp.transpose(x_refs[g][:, cols])
        xt_ref[g, :, rows:] = jnp.transpose(xp[g])

    def small_step(j):
        send_small(j).wait_recv()
        own = small_ref[...] if j == 0 else small_out[j - 1]
        small_out[j] = own + small_in[j]
        if j < stages:
            send_small(j + 1).start()

    send_small(0).start()
    load[10].wait()
    last = counts[2]
    early = chunks - last
    per = chunks // last

    def produce(i, carry):
        c = jnp.where(lax.rem(i, per) == 0, early + i // per, i - i // per - 1)
        for g in range(3):

            @pl.when(c == starts[g])
            def _(g=g):
                load[4 + g].wait()
                load[7 + g].wait()
                for x in (g,) if g < 2 else (2, 3):
                    turn_x(x)

            @pl.when((c >= starts[g]) & (c < starts[g] + counts[g]))
            def _(g=g):
                at = c - starts[g]
                cols = pl.ds(pl.multiple_of(at * chunk, chunk), chunk)
                which = g if g < 2 else 2 + at // per_cross
                total = dot(xt_ref[which, :, :rows], own_refs[g][:, cols])
                total += dot(xt_ref[which, :, rows:], peer_refs[g][:, cols])
                sums[0][c] = total.astype(BF16).reshape(sums[0].shape[1:])
                send_part(0, c, g == 2).start()

        for j in range(2):

            @pl.when(i == 3 + 6 * j)
            def _(j=j):
                small_step(j)

        return carry

    lax.fori_loop(0, chunks, produce, 0)

    def advance(k, c, odd):
        send_part(k, c, odd).wait_recv()
        bit = bits[order(k, odd)]
        mine = sums[0][c, :, :, bit] if k == 0 and not odd else sums[k][c, :, bit]
        total = mine.astype(F32) + parts[k][c].astype(F32)
        if k + 1 < stages:
            sums[k + 1][c] = total.astype(BF16).reshape(sums[k + 1].shape[1:])
            send_part(k + 1, c, odd).start()
            return
        total = total.reshape(total.shape[-2:])
        for g in (2,) if odd else (0, 1):

            @pl.when((c >= starts[g]) & (c < starts[g] + counts[g]))
            def _(g=g):
                at = pl.multiple_of((c - starts[g]) * chunk, chunk)
                out_refs[g][:, pl.ds(at, chunk)] = total

    def reduce(i, carry):
        @pl.when((lax.rem(i, 2) == 1) & (i // 2 < last))
        def _():
            advance(0, early + i // 2, True)

        for k in range(stages):
            c = i - lag * k

            @pl.when((c >= 0) & (c < early))
            def _(k=k, c=c):
                advance(k, c, False)

        for k in range(1, stages):
            c = i - 1 - lag * (k - 1)

            @pl.when((c >= early) & (c < chunks))
            def _(k=k, c=c):
                advance(k, c, True)

        for j in range(2, stages + 1):

            @pl.when(i == 3 * j - 2)
            def _(j=j):
                small_step(j)

        return carry

    lax.fori_loop(0, chunks + 1 + lag * (stages - 2), reduce, 0)

    def finish(c, carry, odd):
        for k in range(stages):
            send_part(k, c, odd).wait_send()
        return carry

    lax.fori_loop(0, early, functools.partial(finish, odd=False), 0)
    lax.fori_loop(early, chunks, functools.partial(finish, odd=True), 0)
    for j in range(stages + 1):
        send_small(j).wait_send()


def over_dp(array):
    return lax.ppermute(array, "dp", [(0, 1), (1, 0)])


def dense_gradients(lefts, lefts_peer, own, peer, small, experts):
    chunk = 512
    rows, width = lefts[0].shape
    half_rows = width // 2
    chunks = sum(y.shape[1] for y in own) // chunk
    stages = experts.bit_length() - 1
    keep = half_rows // experts
    vmem, hbm = pl.BlockSpec(memory_space=pltpu.VMEM), pl.BlockSpec(memory_space=pl.ANY)
    dma = pltpu.SemaphoreType.DMA
    sources = [*lefts, *own, *peer, lefts_peer]
    blocks = [(experts // 4, 2, 2)] + [(experts >> (k + 1), 2) for k in range(1, stages)]
    halved = [(experts // 4, 2)] + [(experts >> (k + 1),) for k in range(1, stages)]
    scratch = [pltpu.VMEM((stages + 1, *small.shape), F32)]
    scratch += [pltpu.VMEM(a.shape, BF16) for a in sources]
    scratch += [pltpu.VMEM((4, half_rows, 2 * rows), BF16)]
    scratch += [pltpu.VMEM((chunks, *b, keep, chunk), BF16) for b in blocks + halved]
    scratch += [dma((stages + 1,)), dma((stages + 1,)), dma((stages, chunks)), dma((stages, chunks))]
    scratch += [dma((len(sources),))]
    *outs, sums = pl.pallas_call(
        functools.partial(dense_kernel, stages, chunk, 2),
        in_specs=[hbm] * len(sources) + [vmem],
        out_specs=[vmem] * 4,
        out_shape=[
            *(jax.ShapeDtypeStruct((keep, y.shape[1]), F32) for y in own),
            jax.ShapeDtypeStruct((stages + 1, *small.shape), F32),
        ],
        scratch_shapes=scratch,
        compiler_params=pltpu.CompilerParams(
            collective_id=0, has_side_effects=True, vmem_limit_bytes=56 << 20
        ),
        cost_estimate=cost(45),
        name="dense_gradients",
    )(*sources, small)
    return outs, sums[stages]


def product_kernel(x_ref, y_ref, out_ref):
    out_ref[...] = dot(x_ref[...], y_ref[...].reshape(y_ref.shape[-2:]), TN).reshape(out_ref.shape)


def expert_gradients(rows, mixed, hidden, grads):
    total, width = rows.shape
    span = hidden.shape[1]
    tile = 256
    params = pltpu.CompilerParams(vmem_limit_bytes=40 << 20)
    din = pl.pallas_call(
        product_kernel,
        grid=(2, width // tile),
        in_specs=[
            pl.BlockSpec((total, tile), lambda g, i: (0, i)),
            pl.BlockSpec((1, total, span), lambda g, i: (g, 0, 0)),
        ],
        out_specs=pl.BlockSpec((1, tile, span), lambda g, i: (g, i, 0)),
        out_shape=jax.ShapeDtypeStruct((2, width, span), F32),
        compiler_params=params,
        cost_estimate=cost(12),
        name="expert_in_gradient",
    )(rows, mixed)
    ddown = pl.pallas_call(
        product_kernel,
        grid=(pl.cdiv(span, tile),),
        in_specs=[
            pl.BlockSpec((total, tile), lambda i: (0, i)),
            pl.BlockSpec((total, width), lambda i: (0, 0)),
        ],
        out_specs=pl.BlockSpec((tile, width), lambda i: (i, 0)),
        out_shape=jax.ShapeDtypeStruct((span, width), F32),
        compiler_params=params,
        cost_estimate=cost(7),
        name="expert_out_gradient",
    )(hidden, grads)
    return din, ddown


def body(
    tokens,
    cotangent,
    lengths,
    routes,
    self_qkv,
    self_out,
    cross_weights,
    router,
    gains,
    bias_table,
    expert_in,
    expert_out,
):
    _, seqs, length, width = tokens.shape
    heads = H
    experts = router.shape[2]
    top = routes.shape[3]
    capacity = (5 * top * length + 4 * experts - 1) // (4 * experts)
    block_rows = -(-seqs * capacity // 16) * 16
    rows = seqs * length
    slots = experts * block_rows
    half_index = lax.axis_index("half")
    decoder = half_index == 1
    wqkv, wout, wcross, wrouter, gain = (
        self_qkv[0],
        self_out[0],
        cross_weights[0],
        router[0],
        gains[0],
    )
    w_in, w_down = expert_in[0, 0], expert_out[0, 0]

    column = np.arange(2 * length)
    entry = np.arange(BUCKETS * heads)
    hot, hot_back = (
        jnp.where(
            decoder,
            *(
                (entry[:, None] // heads == bucket[None, :]).astype(np.float32)
                for bucket in reversed(diagonal_buckets(diff))
            ),
        )
        for diff in (np.where(column < length, column, column - 2 * length), column - length + 1)
    )
    own_head = entry[None, :] % heads == np.arange(heads)[:, None]
    bias = lax.dot_general(
        jnp.where(own_head, bias_table, 0.0),
        hot,
        (((1,), (0,)), ((), ())),
        precision=lax.Precision.HIGHEST,
        preferred_element_type=F32,
    )
    own_lengths = jnp.where(decoder, lengths[1], lengths[0])
    self_info = jnp.concatenate([own_lengths, half_index[None]]).astype(jnp.int32)
    cross_info = jnp.concatenate([lengths[0], jnp.zeros((1,), jnp.int32)]).astype(jnp.int32)

    order = jnp.transpose(routes[0], (0, 2, 1)).reshape(seqs, top * length)
    spots, both_spots, stacked, both, tally, route_lanes = find_slots(order, experts, capacity, block_rows, top)
    tallies = jnp.concatenate([tally[:, 0], tally[:, 1] - tally[:, 0]])
    router_wide = jnp.pad(wrouter, ((0, 0), (FIRST, 128 - FIRST - experts)))

    def fetch(returned):
        flat = returned.reshape(slots, width)
        return dot(stacked, flat).astype(BF16).reshape(top, rows, width)

    def combine(values, stats, results):
        return values + sum(stats[:, GATE + k : GATE + k + 1] * results[k] for k in range(top))

    values = tokens[0].reshape(rows, width).astype(F32)
    normed, scale0 = norm_parts(values, gain[0])
    low0 = normed.astype(BF16)
    qkv = dot(low0, wqkv).astype(BF16)
    mixed0, log0, first, stats, send = enter(
        self_info,
        gain[1:2],
        router_wide,
        route_lanes,
        bias,
        False,
        [qkv, wout, tokens[0].reshape(rows, width), both_spots],
        experts,
        length,
    )

    send_shape = (experts, block_rows, width)
    saved = moe_forward(send.reshape(send_shape), w_in, w_down, 0, None, [], rows)
    final_enc = combine(first, stats, fetch(saved[0]))
    normed, scale_m = norm_parts(final_enc, gain[2])
    low_m = normed.astype(BF16)
    memory = dot(low_m, wcross).astype(BF16)
    names = ("half", "dp", "expert")
    forward_pairs, back_pairs = half_pairs(lax.axis_size("dp") * lax.axis_size("expert"))
    memory = lax.ppermute(memory, names, forward_pairs)

    normed, scale_c = norm_parts(first, gain[2])
    low_c = normed.astype(BF16)
    query = dot(low_c, wcross[:, :width]).astype(BF16)
    mixed_c, log_c, second, stats, send = enter(
        cross_info,
        gain[1:2],
        router_wide,
        route_lanes,
        stats,
        True,
        [query, memory, wcross[:, width:], first, both_spots],
        experts,
        length,
    )

    lefts = [low0, mixed0, jnp.where(decoder, low_c, low_m), jnp.where(decoder, mixed_c, low_m)]
    saved = moe_forward(send.reshape(send_shape), w_in, w_down, 1, saved, lefts, rows)
    results = fetch(saved[0])
    final = combine(second, stats, results)
    outputs = final.astype(BF16)

    grad_dec = cotangent[0].reshape(rows, width)
    spread = [(stats[:, GATE + k : GATE + k + 1] * grad_dec.astype(F32)).astype(BF16) for k in range(top)]
    grad_send = dot(spots, jnp.concatenate(spread)).astype(BF16)
    kept_from = moe_backward(grad_send.reshape(experts, block_rows, width), saved, 1, None)

    grad_second, dbranch_c, dgain_moe_dec, dlog_dec, dquery, dmemory = leave(
        cross_info,
        stats,
        gain[1:2],
        router_wide,
        None,
        [
            kept_from[0].reshape(slots, width),
            both,
            grad_dec,
            results,
            second,
            wcross[:, width:],
            mixed_c,
            log_c,
            query,
            memory,
        ],
        experts,
        length,
    )
    dmemory = lax.ppermute(dmemory, names, back_pairs)
    dnormed = dot(dquery, wcross[:, :width], NT)
    dvalues, dgain_c = norm_back(first, scale_c, gain[2], dnormed)
    grad_first_dec = grad_second + dvalues

    grad, grad_send, dgain_m, cross_grad = memory_gradient(
        stats, gain[2:3], [dmemory, wcross, final_enc, grad_dec, spots], [dquery, dbranch_c]
    )
    back, mixed_grads, all_grad = moe_backward(
        grad_send.reshape(experts, block_rows, width), saved, 0, kept_from
    )
    all_rows, hidden, lefts_peer = saved[1], saved[4], saved[10]
    grad_first, dbranch, dgain_moe, dlog, dqkv_rows, diag = leave(
        self_info,
        stats,
        gain[1:2],
        router_wide,
        bias,
        [
            back.reshape(slots, width),
            both,
            grad,
            results,
            second,
            wout,
            mixed0,
            log0,
            qkv,
            grad_first_dec,
        ],
        experts,
        length,
    )
    ff_half = hidden.shape[-1]
    din, ddown = expert_gradients(
        all_rows.reshape(-1, width),
        mixed_grads.reshape(2, -1, ff_half),
        hidden.reshape(-1, ff_half),
        all_grad.reshape(-1, width),
    )
    dlog = jnp.where(decoder, dlog_dec, dlog)[:, FIRST : FIRST + experts]
    dgain_moe = jnp.where(decoder, dgain_moe_dec[0], dgain_moe[0])
    drouter = lax.dot_general(
        second * stats[:, SCALE : SCALE + 1] * gain[1],
        dlog,
        TN,
        precision=lax.Precision.HIGHEST,
        preferred_element_type=F32,
    )
    dnormed = dot(dqkv_rows, wqkv, NT)
    dvalues, dgain_self = norm_back(values, scale0, gain[0], dnormed)
    d_tokens = (grad_first + dvalues).astype(BF16)
    by_entry = lax.dot_general(
        diag, hot_back, NT, precision=lax.Precision.HIGHEST, preferred_element_type=F32
    )
    dtable = jnp.sum(jnp.where(own_head, by_entry, 0.0), axis=0)

    own_grads = (dqkv_rows, dbranch, cross_grad)
    peer_grads = tuple(map(over_dp, own_grads))
    places = 2 * experts
    own = width // places
    extra = jnp.concatenate([dtable.reshape(places, -1), tallies.reshape(places, 1)], axis=1)
    extra = jnp.pad(extra, ((0, 0), (0, -extra.shape[1] % own)))
    small = jnp.concatenate(
        [
            jnp.transpose(drouter),
            jnp.stack([dgain_self, dgain_moe, jnp.where(decoder, dgain_c, dgain_m[0])]),
            jnp.swapaxes(extra.reshape(places, -1, own), 0, 1).reshape(-1, width),
        ]
    )
    small = jnp.pad(small, ((0, -small.shape[0] % 8), (0, 0)))
    (dqkv, dout, dcross), small = dense_gradients(
        lefts, lefts_peer, own_grads, peer_grads, small, experts
    )
    place = lax.axis_index("dp") * experts + lax.axis_index("expert")
    mine = lax.dynamic_slice_in_dim(small, place * own, own, 1)
    tail = mine[experts + 3 :].reshape(-1)
    own_table = dtable.shape[0] // places
    d_table = tail[:own_table]
    counts = tail[own_table].astype(jnp.int32)

    return (
        outputs.reshape(1, seqs, length, width),
        d_tokens.reshape(1, seqs, length, width),
        dqkv[None],
        dout[None],
        dcross[None],
        jnp.transpose(mine[:experts])[None],
        mine[experts : experts + 3][None],
        d_table[None],
        din[None, None],
        ddown[None, None],
        counts.reshape(1, 1, 1),
    )


def half_pairs(count):
    return (
        [(i, count + i) for i in range(count)],
        [(count + i, i) for i in range(count)],
    )


def solution(mesh):
    placed = (
        P("half", ("dp", "expert"), None, None),
        P("half", ("dp", "expert"), None, None),
        P(None, ("dp", "expert")),
        P("half", ("dp", "expert"), None, None),
        P("half", None, None),
        P("half", None, None),
        P("half", None, None),
        P("half", None, None),
        P("half", None, None),
        P("half", None),
        P("half", "expert", None, None, None),
        P("half", "expert", None, None),
    )
    return jax.shard_map(
        body,
        mesh=mesh,
        in_specs=placed,
        out_specs=(
            P("half", ("dp", "expert"), None, None),
            P("half", ("dp", "expert"), None, None),
            P("half", ("dp", "expert"), None),
            P("half", ("dp", "expert"), None),
            P("half", ("dp", "expert"), None),
            P("half", ("dp", "expert"), None),
            P("half", None, ("dp", "expert")),
            P("half", ("dp", "expert")),
            P("half", "expert", None, None, "dp"),
            P("half", "expert", "dp", None),
            P("half", "dp", "expert"),
        ),
        check_vma=False,
    )
```

```python
import functools

import jax
import jax.numpy as jnp
import numpy as np
from jax import lax
from jax.experimental import pallas as pl
from jax.experimental.pallas import tpu as pltpu
from jax.sharding import PartitionSpec as P

H = 16
BUCKETS = 32
EPS = 1e-06
ENC_STEPS = (12, 16, 23, 32, 46, 64, 91)
DEC_STEPS = (19, 21, 24, 27, 31, 35, 40, 46, 52, 59, 67, 77, 87, 99, 113)
F32 = jnp.float32
BF16 = jnp.bfloat16
MESH = pl.DeviceIdType.MESH
LOCAL_VMEM = 32 << 20


def cost(gigaflops):
    return pl.CostEstimate(flops=int(gigaflops * 1e9), bytes_accessed=1 << 20, transcendentals=0)
NT = (((1,), (1,)), ((), ()))
TN = (((0,), (0,)), ((), ()))


def dot(a, b, dims=(((1,), (0,)), ((), ()))):
    return lax.dot_general(a, b, dims, preferred_element_type=F32)


def diagonal_buckets(diff):
    apart = np.abs(diff)
    coarse = 8 + sum((apart >= step).astype(np.int32) for step in ENC_STEPS)
    enc = np.where(apart < 8, apart, coarse) + 16 * (diff > 0)
    behind = np.maximum(-diff, 0)
    coarse = 16 + sum((behind >= step).astype(np.int32) for step in DEC_STEPS)
    dec = np.where(behind < 16, behind, coarse)
    return enc.astype(np.int32), dec.astype(np.int32)


def diagonals(bias_ref, head, length):
    row = jnp.broadcast_to(bias_ref[pl.ds(head, 1), :], (length, 2 * length))
    return pltpu.roll(row, 0, 1, stride=1, stride_axis=0)[:, :length]


def fill_masks(info, mask_ref):
    seqs, length, _ = mask_ref.shape
    row_id = lax.broadcasted_iota(jnp.int32, (length, length), 0)
    col_id = lax.broadcasted_iota(jnp.int32, (length, length), 1)
    reach = jnp.where(info[seqs] > 0, row_id, length)
    for seq in range(seqs):
        allowed = (col_id < info[seq]) & (col_id <= reach)
        mask_ref[seq] = jnp.where(allowed, 0.0, -1000000000.0)


def attend(info, bias_ref, q_ref, k_ref, v_ref, out_ref, log_ref, mask_ref):
    has_bias = bias_ref is not None
    seqs, length, _ = mask_ref.shape
    low = lax.broadcasted_iota(jnp.int32, (length, 128), 1) < 64
    fill_masks(info, mask_ref)

    @pl.loop(0, q_ref.shape[1] // 128, unroll=4)
    def _(pair):
        cols = pl.ds(pl.multiple_of(pair * 128, 128), 128)
        biases = [diagonals(bias_ref, 2 * pair + side, length) if has_bias else 0.0 for side in range(2)]
        for seq in range(seqs):
            rows = pl.ds(seq * length, length)
            q, k, v = q_ref[rows, cols] * 0.125, k_ref[rows, cols], v_ref[rows, cols]
            mixed, peaks = [], []
            for side in range(2):
                mine = low if side == 0 else jnp.logical_not(low)
                part = jnp.where(mine, q, jnp.zeros_like(q))
                scores = dot(part, k, NT) + (mask_ref[seq] + biases[side])
                peak = jnp.max(scores, axis=-1, keepdims=True)
                spread = jnp.exp(scores - peak).astype(BF16)
                mixed.append(dot(spread, jnp.where(mine, v, jnp.ones_like(v))))
                peaks.append(peak)
            total = pltpu.roll(jnp.where(low, mixed[1], mixed[0]), 64, 1)
            out_ref[rows, cols] = (jnp.where(low, mixed[0], mixed[1]) / total).astype(BF16)
            log_ref[rows, cols] = jnp.where(low, peaks[0], peaks[1]) + jnp.log(total)


def attend_back(info, bias_ref, q_ref, k_ref, v_ref, a_ref, log_ref, g_ref, dq_ref, dkv_ref, shift, diag_ref, mask_ref):
    has_bias = bias_ref is not None
    seqs, length, _ = mask_ref.shape
    width = q_ref.shape[1]
    low = lax.broadcasted_iota(jnp.int32, (length, 128), 1) < 64
    fill_masks(info, mask_ref)
    if has_bias:
        row_id = lax.broadcasted_iota(jnp.int32, (length, length), 0)
        col_id = lax.broadcasted_iota(jnp.int32, (length, length), 1)
        flip = (row_id + col_id == length - 1).astype(F32).astype(BF16)

    @pl.loop(0, width // 128, unroll=4)
    def _(pair):
        cols = pl.ds(pl.multiple_of(pair * 128, 128), 128)
        kcols = pl.ds(pl.multiple_of(shift + pair * 128, 128), 128)
        vcols = pl.ds(pl.multiple_of(shift + width + pair * 128, 128), 128)
        biases = [diagonals(bias_ref, 2 * pair + side, length) if has_bias else 0.0 for side in range(2)]
        sums = [0.0, 0.0]
        for seq in range(seqs):
            rows = pl.ds(seq * length, length)
            q, k, v, g = q_ref[rows, cols] * 0.125, k_ref[rows, cols], v_ref[rows, cols], g_ref[rows, cols]
            logs = log_ref[rows, cols]
            turned = pltpu.roll(logs, 64, 1)
            product = g.astype(F32) * a_ref[rows, cols].astype(F32)
            minus = (-pltpu.roll(product, 64, 1)).astype(BF16)
            scaled = k * 0.125
            dqs, dks, dvs = [], [], []
            for side in range(2):
                mine = low if side == 0 else jnp.logical_not(low)
                part = jnp.where(mine, q, jnp.zeros_like(q))
                scores = dot(part, k, NT) + (mask_ref[seq] + biases[side])
                probs = jnp.exp(scores - jnp.where(mine, logs, turned))
                dvs.append(dot(probs.astype(BF16), g, TN))
                centred = dot(jnp.where(mine, g, minus), jnp.where(mine, v, jnp.ones_like(v)), NT)
                dlow = (probs * centred).astype(BF16)
                dqs.append(dot(dlow, scaled))
                dks.append(dot(dlow, q, TN))
                if has_bias:
                    sums[side] = sums[side] + dlow.astype(F32)
            dq_ref[rows, cols] = jnp.where(low, dqs[0], dqs[1]).astype(BF16)
            dkv_ref[rows, kcols] = jnp.where(low, dks[0], dks[1]).astype(BF16)
            dkv_ref[rows, vcols] = jnp.where(low, dvs[0], dvs[1]).astype(BF16)
        if has_bias:
            for side in range(2):
                upside = dot(flip, sums[side].astype(BF16))
                wide = jnp.concatenate([upside, jnp.zeros((length, length), F32)], axis=1)
                turned = pltpu.roll(wide, 0, 1, stride=1, stride_axis=0)
                diag_ref[pl.ds(2 * pair + side, 1), :] = jnp.sum(turned, axis=0, keepdims=True)


def norm_parts(values, gain):
    scale = lax.rsqrt(jnp.mean(values * values, axis=-1, keepdims=True) + EPS)
    return values * scale * gain, scale


def norm_back(values, scale, gain, grad):
    unit = values * scale
    gain_grad = jnp.sum(grad * unit, axis=0)
    pushed = grad * gain
    back = scale * (pushed - unit * jnp.mean(pushed * unit, axis=-1, keepdims=True))
    return back, gain_grad


def gelu_parts(gate):
    c, a = 0.7978845608028654, 0.044715
    square = gate * gate
    u = 0.5 + 0.5 * jnp.tanh(gate * (c + c * a * square))
    slope = u * (1.0 + (gate * (2.0 * c + 6.0 * c * a * square)) * (1.0 - u))
    return gate * u, slope


def flipped(value, bit):
    step = 1 << bit
    return value + step * (1 - 2 * (value // step % 2))


def crossed(value, other):
    for bit in range(other.bit_length()):
        if other >> bit & 1:
            value = flipped(value, bit)
    return value


def greet(partners):
    barrier = pltpu.get_barrier_semaphore()
    for partner in partners:
        pl.semaphore_signal(barrier, inc=1, device_id=partner, device_id_type=MESH)
    pl.semaphore_wait(barrier, len(partners))


def remote(src, dst, out_sem, in_sem, device):
    return pltpu.make_async_remote_copy(
        src_ref=src,
        dst_ref=dst,
        send_sem=out_sem,
        recv_sem=in_sem,
        device_id=device,
        device_id_type=MESH,
    )


def tile_loop(count, step, body):
    @pl.loop(0, count // step)
    def _(i):
        body(pl.multiple_of(i * step, step), step)

    if count % step:
        body(count // step * step, count % step)


def groups_of(experts, block):
    size = 1
    while size * 2 * block <= 320 and size * 2 <= experts:
        size *= 2
    if experts <= 2 * size:
        half = max(size // 2, 1)
        return [(0, size), *((k, half) for k in range(size, experts, half))]
    return [(k, size) for k in range(0, experts, size)]


class Turn:
    def __init__(self, experts, block, there, home):
        self.me, self.dp = lax.axis_index("expert"), lax.axis_index("dp")
        self.experts, self.block = experts, block
        self.peer = {"dp": 1 - self.dp}
        self.groups = groups_of(experts, block)
        self.there_refs, self.home_refs = there, home

    def greet(self):
        greet([{"expert": crossed(self.me, k)} for k in range(1, self.experts)] + [self.peer])

    def there(self, k):
        src, dst, out_sems, in_sems = self.there_refs
        partner = crossed(self.me, k)
        return remote(src.at[partner], dst.at[self.me], out_sems.at[k], in_sems.at[k], {"expert": partner})

    def home(self, k):
        src, dst, out_sems, in_sems = self.home_refs
        partner = crossed(self.me, k)
        return remote(src.at[partner], dst.at[self.me], out_sems.at[k], in_sems.at[k], {"expert": partner})

    def arrive(self, first, size):
        for k in range(max(first, 1), first + size):
            self.there(k).wait_recv()

    def base(self, first, size):
        return crossed(self.me // size, first // size) * size

    def spans(self, first, size):
        base = self.base(first, size)
        rows = pl.ds(pl.multiple_of(base * self.block, size * self.block), size * self.block)
        return pl.ds(base, size), rows


def every_other(width, own, parity):
    row = lax.broadcasted_iota(jnp.int32, (width, width // 2), 0)
    col = lax.broadcasted_iota(jnp.int32, (width, width // 2), 1)
    return (row == (2 * (col // own) + parity) * own + col % own).astype(F32).astype(BF16)


class Lefts:
    def __init__(self, refs, out, scratch, width, experts):
        self.me, self.own, self.width = lax.axis_index("expert"), width // (2 * experts), width
        self.refs, self.out = refs, out
        self.held, self.stage, self.loaded, self.sent, self.came = scratch
        self.half = width // 2
        self.dp = lax.axis_index("dp")

    def fetch(self, i):
        return pltpu.make_async_copy(self.refs[i], self.held.at[i % 2], self.loaded.at[i])

    def copy(self, i):
        device = {"dp": 1 - self.dp} if i < 2 else {"expert": flipped(self.me, 0)}
        return remote(self.stage.at[i], self.out.at[i], self.sent.at[i], self.came.at[i], device)

    def load(self):
        for i in range(2):
            self.fetch(i).start()

    def send(self):
        for i in range(4):
            self.fetch(i).wait()
            slot = i % self.held.shape[0]
            if i < 2:
                cols = pl.ds(pl.multiple_of((1 - self.dp) * self.half, 128), self.half)
                self.stage[i] = self.held[slot, :, cols]
            else:
                picked = every_other(self.width, self.own, 1 - self.me % 2)
                self.stage[i] = dot(self.held[slot], picked).astype(BF16)
            self.copy(i).start()
            if i + 2 < 4:
                self.fetch(i + 2).start()

    def wait(self):
        for i in range(4):
            self.copy(i).wait()


def transpose_kernel_part(loads, tall, wide, wsem, tsem):
    copies = [pltpu.make_async_copy(src, dst, wsem.at[i]) for i, (src, dst, _) in enumerate(loads)]
    for copy in copies:
        copy.start()
    for i, (_, held, out) in enumerate(loads):
        slab = tall.shape[1]
        stages = [tall.at[i] if out.shape[1] == tall.shape[2] else wide.at[pl.ds(i * slab, slab)] for i in range(2)]
        steps = out.shape[0] // slab
        copies[i].wait()

        def put(t, slot, stages=stages, out=out, slab=slab):
            rows = pl.ds(pl.multiple_of(t * slab, slab), slab)
            return pltpu.make_async_copy(stages[slot], out.at[rows], tsem.at[slot])

        def step(pair, carry, stages=stages, held=held, put=put, slab=slab, steps=steps):
            for slot in range(2):
                t = 2 * pair + slot

                @pl.when(t < steps)
                def _(t=t, slot=slot):
                    @pl.when(pair > 0)
                    def _():
                        put(t - 2, slot).wait()

                    cols = pl.ds(pl.multiple_of(t * slab, slab), slab)
                    stages[slot][...] = jnp.transpose(held[:, cols])
                    put(t, slot).start()

            return carry

        lax.fori_loop(0, pl.cdiv(steps, 2), step, 0)
        for t in (steps - 2, steps - 1):
            put(t, t % 2).wait()


def expert_forward_kernel(turn, has_prev, *refs):
    send_ref, w_in, w_down = refs[:3]
    left_refs, refs = refs[3 + 10 * has_prev : 3 + 14 * has_prev], refs[3 + 14 * has_prev :]
    back_out, rows_out, slope_out, value_out, hidden_out, slope_peer_out, value_peer_out = refs[:7]
    wgt_out, wut_out, wdt_out = refs[7:10]
    left_out, refs = refs[10 : 10 + has_prev], refs[10 + has_prev :]
    wg, wu, wd, rows, back, made, rows_peer, slopes, values, hidden = refs[:10]
    slopes_peer, values_peer, tall = refs[10:13]
    wsem, s1, r1, s2, r2, sx, rx, osem, tsem = refs[13:22]
    experts, block, width = send_ref.shape
    ff = wd.shape[0]
    span = ff // 2
    lefts = Lefts(left_refs, left_out[0], (tall, *refs[22:]), width, experts) if has_prev else None

    @pl.when(lax.axis_index("half") != turn)
    def _():
        if lefts:
            lefts.load()
            greet([{"dp": 1 - lax.axis_index("dp")}, {"expert": flipped(lax.axis_index("expert"), 0)}])
            lefts.send()
        loads = ((w_in.at[0], wg, wgt_out), (w_in.at[1], wu, wut_out), (w_down, wd, wdt_out))
        transpose_kernel_part(loads, tall, slopes, wsem, tsem)
        if lefts:
            lefts.wait()

    @pl.when(lax.axis_index("half") == turn)
    def _():
        t = Turn(experts, block, (send_ref, rows, s1, r1), (made, back, s2, r2))
        t.greet()

        def rows_over(part):
            blocks, _ = t.spans(*t.groups[part])
            return remote(rows.at[blocks], rows_peer.at[blocks], sx.at[part], rx.at[part], t.peer)

        for k in range(1, experts):
            t.there(k).start()
        rows[t.me] = send_ref[t.me]
        loads = [
            pltpu.make_async_copy(src, dst, wsem.at[i])
            for i, (src, dst) in enumerate(((w_in.at[0], wg), (w_in.at[1], wu), (w_down, wd)))
        ]
        for load in loads:
            load.start()
        if lefts:
            lefts.load()
        for part, (first, size) in enumerate(t.groups):
            t.arrive(first, size)
            rows_over(part).start()
            blocks, span_rows = t.spans(first, size)
            if part == 0:
                loads[0].wait()
                loads[1].wait()

            def up_tile(start, count, blocks=blocks, span_rows=span_rows, size=size):
                x = rows[blocks].reshape(size * block, width)
                cols = pl.ds(start, count)
                value, slope = gelu_parts(dot(x, wg[:, cols]))
                up = dot(x, wu[:, cols])
                hidden[span_rows, cols] = (value * up).astype(BF16)
                values[span_rows, cols] = value.astype(BF16)
                slopes[span_rows, cols] = (up * slope).astype(BF16)

            tile_loop(ff, 512, up_tile)
            if part == 0:
                loads[2].wait()

            def down_tile(start, count, blocks=blocks, span_rows=span_rows, size=size):
                cols = pl.ds(start, count)
                y = dot(hidden[span_rows, :], wd[:, cols]).astype(BF16)
                made[blocks, :, cols] = y.reshape(size, block, count)

            tile_loop(width, 512, down_tile)
            for k in range(max(first, 1), first + size):
                t.home(k).start()
        back[t.me] = made[t.me]
        half_cols = pl.ds(pl.multiple_of(t.dp * span, 128), span)
        other_cols = pl.ds(pl.multiple_of((1 - t.dp) * span, 128), span)
        outs = [
            (slopes, slope_out),
            (values, value_out),
            (hidden.at[:, half_cols], hidden_out.at[0]),
            (rows, rows_out.at[0]),
        ]
        outs = [pltpu.make_async_copy(src, dst, osem.at[i]) for i, (src, dst) in enumerate(outs)]
        for out in outs:
            out.start()
        if lefts:
            lefts.send()

        for part in range(len(t.groups)):
            rows_over(part).wait_recv()

        def peer_tile(start, count):
            x = rows_peer[...].reshape(experts * block, width)
            here = pl.ds(start, count)
            cols = pl.ds(pl.multiple_of(t.dp * span + start, 128), count)
            value, slope = gelu_parts(dot(x, wg[:, cols]))
            up = dot(x, wu[:, cols])
            hidden[:, pl.ds(pl.multiple_of((1 - t.dp) * span + start, 128), count)] = (value * up).astype(BF16)
            values_peer[:, here] = value.astype(BF16)
            slopes_peer[:, here] = (up * slope).astype(BF16)

        tile_loop(span, 512, peer_tile)
        more = [
            (slopes_peer, slope_peer_out),
            (values_peer, value_peer_out),
            (hidden.at[:, other_cols], hidden_out.at[1]),
            (rows_peer, rows_out.at[1]),
        ]
        more = [pltpu.make_async_copy(src, dst, osem.at[4 + i]) for i, (src, dst) in enumerate(more)]
        for out in more:
            out.start()
        for k in range(1, experts):
            t.home(k).wait_recv()
        back_copy = pltpu.make_async_copy(back, back_out, osem.at[8])
        back_copy.start()
        for k in range(1, experts):
            t.there(k).wait_send()
            t.home(k).wait_send()
        for part in range(len(t.groups)):
            rows_over(part).wait_send()
        if lefts:
            lefts.wait()
        for out in [*outs, *more, back_copy]:
            out.wait()


def expert_backward_kernel(turn, has_prev, *refs):
    send_ref = refs[0]
    sources = refs[1:8]
    refs = refs[8 + 3 * has_prev :]
    back_out, mixed_out, grad_out = refs[:3]
    wdt, dgate, dup, wgt, wut, dgate_peer, dup_peer = refs[3:10]
    grads, back, made, grads_peer = refs[10:14]
    wsem, s1, r1, s2, r2, sx, rx, osem = refs[14:]
    experts, block, width = send_ref.shape
    ff = wdt.shape[1]
    span = ff // 2
    dp = lax.axis_index("dp")
    t = Turn(experts, block, (send_ref, grads, s1, r1), (made, back, s2, r2))

    @pl.when(lax.axis_index("half") == turn)
    def _():
        t.greet()

        def grads_over(part):
            blocks, _ = t.spans(*t.groups[part])
            return remote(grads.at[blocks], grads_peer.at[blocks], sx.at[part], rx.at[part], t.peer)

        for k in range(1, experts):
            t.there(k).start()
        grads[t.me] = send_ref[t.me]
        held = (wdt, dgate, dup, wgt, wut, dgate_peer, dup_peer)
        loads = [pltpu.make_async_copy(src, dst, wsem.at[i]) for i, (src, dst) in enumerate(zip(sources, held))]
        for load in loads:
            load.start()
        for load in loads[:3]:
            load.wait()
        for part, (first, size) in enumerate(t.groups):
            t.arrive(first, size)
            grads_over(part).start()
            blocks, span_rows = t.spans(first, size)

            def hidden_tile(start, count, blocks=blocks, span_rows=span_rows, size=size):
                dy = grads[blocks].reshape(size * block, width)
                cols = pl.ds(start, count)
                dhidden = dot(dy, wdt[:, cols])
                dgate[span_rows, cols] = (dhidden * dgate[span_rows, cols].astype(F32)).astype(BF16)
                dup[span_rows, cols] = (dhidden * dup[span_rows, cols].astype(F32)).astype(BF16)

            tile_loop(ff, 512, hidden_tile)
            if part == 0:
                loads[3].wait()
                loads[4].wait()

            def rows_tile(start, count, blocks=blocks, span_rows=span_rows, size=size):
                cols = pl.ds(start, count)
                dr = dot(dgate[span_rows, :], wgt[:, cols]) + dot(dup[span_rows, :], wut[:, cols])
                made[blocks, :, cols] = dr.astype(BF16).reshape(size, block, count)

            tile_loop(width, 512, rows_tile)
            for k in range(max(first, 1), first + size):
                t.home(k).start()
        back[t.me] = made[t.me]
        half_cols = pl.ds(pl.multiple_of(dp * span, 128), span)
        outs = [
            (dgate.at[:, half_cols], mixed_out.at[0, 0]),
            (dup.at[:, half_cols], mixed_out.at[1, 0]),
            (grads, grad_out.at[0]),
        ]
        outs = [pltpu.make_async_copy(src, dst, osem.at[i]) for i, (src, dst) in enumerate(outs)]
        for out in outs:
            out.start()

        for load in loads[5:]:
            load.wait()
        for part in range(len(t.groups)):
            grads_over(part).wait_recv()

        def peer_tile(start, count):
            dy = grads_peer[...].reshape(experts * block, width)
            here = pl.ds(start, count)
            dhidden = dot(dy, wdt[:, pl.ds(pl.multiple_of(dp * span + start, 128), count)])
            dgate_peer[:, here] = (dhidden * dgate_peer[:, here].astype(F32)).astype(BF16)
            dup_peer[:, here] = (dhidden * dup_peer[:, here].astype(F32)).astype(BF16)

        tile_loop(span, 512, peer_tile)
        more = [
            (dgate_peer, mixed_out.at[0, 1]),
            (dup_peer, mixed_out.at[1, 1]),
            (grads_peer, grad_out.at[1]),
        ]
        more = [pltpu.make_async_copy(src, dst, osem.at[3 + i]) for i, (src, dst) in enumerate(more)]
        for out in more:
            out.start()
        for k in range(1, experts):
            t.home(k).wait_recv()
        back_copy = pltpu.make_async_copy(back, back_out, osem.at[6])
        back_copy.start()
        for k in range(1, experts):
            t.there(k).wait_send()
            t.home(k).wait_send()
        for part in range(len(t.groups)):
            grads_over(part).wait_send()
        for out in [*outs, *more, back_copy]:
            out.wait()


def expert_call(kernel, number, turn, send, sources, prev, more, out_shape, scratch, name):
    vmem, hbm = pl.BlockSpec(memory_space=pltpu.VMEM), pl.BlockSpec(memory_space=pl.ANY)
    prev = list(prev or [])
    return pl.pallas_call(
        functools.partial(kernel, turn, bool(prev)),
        in_specs=[vmem] + [hbm] * (len(sources) + len(prev) + len(more)),
        out_specs=[hbm] * len(out_shape),
        out_shape=out_shape,
        input_output_aliases={1 + len(sources) + i: i for i in range(len(prev))},
        scratch_shapes=scratch,
        compiler_params=pltpu.CompilerParams(
            collective_id=number, has_side_effects=True, vmem_limit_bytes=60 << 20
        ),
        cost_estimate=cost(40),
        name=name,
    )(send, *sources, *prev, *more)


def moe_forward(send, w_in, w_down, turn, prev, lefts, slab):
    experts, block, width = send.shape
    ff = w_down.shape[0]
    total = experts * block
    parts = len(groups_of(experts, block))
    dma = pltpu.SemaphoreType.DMA
    scratch = [
        pltpu.VMEM((width, ff), BF16),
        pltpu.VMEM((width, ff), BF16),
        pltpu.VMEM((ff, width), BF16),
        *[pltpu.VMEM(send.shape, BF16)] * 4,
        *[pltpu.VMEM((total, ff), BF16)] * 3,
        *[pltpu.VMEM((total, ff // 2), BF16)] * 2,
        pltpu.VMEM((2, slab, width), BF16),
        dma((3,)),
        *[dma((experts,))] * 4,
        *[dma((parts,))] * 2,
        dma((9,)),
        dma((2,)),
    ]
    shapes = [
        send.shape,
        (2, *send.shape),
        (total, ff),
        (total, ff),
        (2, total, ff // 2),
        (total, ff // 2),
        (total, ff // 2),
        (ff, width),
        (ff, width),
        (width, ff),
    ]
    if lefts:
        rows = lefts[0].shape[0]
        shapes.append((4, rows, width // 2))
        scratch += [pltpu.VMEM((4, rows, width // 2), BF16), *[dma((4,))] * 3]
    out_shape = [jax.ShapeDtypeStruct(shape, BF16) for shape in shapes]
    return expert_call(
        expert_forward_kernel, 1 + turn, turn, send, [w_in, w_down], prev, lefts, out_shape, scratch, "moe_forward"
    )


def moe_backward(grad_send, saved, turn, prev):
    experts, block, width = grad_send.shape
    _, _, slope, value, _, slope_peer, value_peer, wgt, wut, wdt, _ = saved
    total, ff = slope.shape
    parts = len(groups_of(experts, block))
    dma = pltpu.SemaphoreType.DMA
    scratch = [
        pltpu.VMEM((width, ff), BF16),
        *[pltpu.VMEM((total, ff), BF16)] * 2,
        *[pltpu.VMEM((ff, width), BF16)] * 2,
        *[pltpu.VMEM((total, ff // 2), BF16)] * 2,
        *[pltpu.VMEM(grad_send.shape, BF16)] * 4,
        dma((7,)),
        *[dma((experts,))] * 4,
        *[dma((parts,))] * 2,
        dma((7,)),
    ]
    out_shape = [
        jax.ShapeDtypeStruct(grad_send.shape, BF16),
        jax.ShapeDtypeStruct((2, 2, total, ff // 2), BF16),
        jax.ShapeDtypeStruct((2, *grad_send.shape), BF16),
    ]
    return expert_call(
        expert_backward_kernel,
        3 + turn,
        turn,
        grad_send,
        [wdt, slope, value, wgt, wut, slope_peer, value_peer],
        prev,
        [],
        out_shape,
        scratch,
        "moe_backward",
    )


GATE, TOTAL, SCALE, ROUTE, FIRST = 0, 2, 3, 4, 8


class Loads:
    def __init__(self, pairs, sems):
        self.copies = [pltpu.make_async_copy(src, dst, sems.at[i]) for i, (src, dst) in enumerate(pairs)]

    def start(self):
        for copy in self.copies:
            copy.start()

    def wait(self, *which):
        for i in which:
            self.copies[i].wait()


def slots_kernel(experts, capacity, block, order_ref, spots_out, both_out, turned_out, both_turned_out, tally_out, route_out, route_rows):
    seqs, pairs = order_ref.shape
    top = spots_out.shape[1] // both_out.shape[1]
    length = pairs // top
    rows = seqs * length
    slots = spots_out.shape[0]
    expert_id = lax.broadcasted_iota(jnp.int32, (experts, pairs), 0)
    slot_id = lax.broadcasted_iota(jnp.int32, (slots, length), 0)
    row_id = lax.broadcasted_iota(jnp.int32, (pairs, pairs), 0)
    col_id = lax.broadcasted_iota(jnp.int32, (pairs, pairs), 1)
    earlier = (row_id < col_id).astype(F32).astype(BF16)
    route_rows[...] = jnp.zeros_like(route_rows)
    tally = jnp.zeros((experts, 128), F32)
    lane = lax.broadcasted_iota(jnp.int32, (experts, 128), 1)
    for seq in range(seqs):
        order = order_ref[seq : seq + 1, :]
        picked = (expert_id == order).astype(F32)
        place = jnp.sum(dot(picked.astype(BF16), earlier) * picked, axis=0, keepdims=True)
        kept = place < capacity
        target = jnp.where(kept, order * block + seq * capacity + place.astype(jnp.int32), -1)
        taken = jnp.sum(picked * kept.astype(F32), axis=1, keepdims=True)
        whole = jnp.sum(picked, axis=1, keepdims=True)
        tally = tally + jnp.where(lane == 0, taken, jnp.where(lane == 1, whole, 0.0))
        total = jnp.zeros((slots, length), F32)
        for k in range(top):
            part = pl.ds(k * length, length)
            hot = (slot_id == target[:, k * length : (k + 1) * length]).astype(F32)
            spots_out[:, pl.ds(k * rows + seq * length, length)] = hot.astype(BF16)
            total = total + hot
            route_rows[pl.ds(ROUTE + k, 1), pl.ds(seq * length, length)] = order_ref[
                pl.ds(seq, 1), part
            ].astype(F32)
        both_out[:, pl.ds(seq * length, length)] = total.astype(BF16)
    tally_out[...] = tally
    turned_out[...] = jnp.transpose(spots_out[...])
    both_turned_out[...] = jnp.transpose(both_out[...])
    route_out[...] = jnp.transpose(route_rows[...])


def find_slots(order, experts, capacity, block, top):
    seqs, pairs = order.shape
    rows = seqs * pairs // top
    slots = experts * block
    vmem = pl.BlockSpec(memory_space=pltpu.VMEM)
    return pl.pallas_call(
        functools.partial(slots_kernel, experts, capacity, block),
        in_specs=[vmem],
        out_specs=[vmem] * 6,
        out_shape=[
            jax.ShapeDtypeStruct((slots, top * rows), BF16),
            jax.ShapeDtypeStruct((slots, rows), BF16),
            jax.ShapeDtypeStruct((top * rows, slots), BF16),
            jax.ShapeDtypeStruct((rows, slots), BF16),
            jax.ShapeDtypeStruct((experts, 128), F32),
            jax.ShapeDtypeStruct((rows, 128), F32),
        ],
        scratch_shapes=[pltpu.VMEM((128, rows), F32)],
        compiler_params=pltpu.CompilerParams(vmem_limit_bytes=LOCAL_VMEM),
        cost_estimate=cost(1),
        name="find_slots",
    )(order)


def enter_kernel(cross, experts, count, info, gain_ref, router_ref, lanes_ref, lead_ref, *refs):
    held, refs = refs[:count], refs[count:]
    mixed_out, log_out, result_out, stats_out, send_out, low_ref, mask_ref = refs
    w_out, x, spots = held[count - 3 :]
    rows, width = x.shape
    step = min(512, width)
    if cross:
        q_ref, kv = held[:2]
        k_ref, v_ref = kv.at[:, pl.ds(0, width)], kv.at[:, pl.ds(width, width)]
    else:
        q_ref, k_ref, v_ref = (held[0].at[:, pl.ds(i * width, width)] for i in range(3))

    def work():
        attend(info, None if cross else lead_ref, q_ref, k_ref, v_ref, mixed_out, log_out, mask_ref)
        for start in range(0, width, step):
            cols = pl.ds(start, step)
            result_out[:, cols] = x[:, cols].astype(F32) + dot(mixed_out[...], w_out[:, cols])
        values = result_out[...]
        scale = lax.rsqrt(jnp.mean(values * values, axis=-1, keepdims=True) + EPS)
        normed = values * scale * gain_ref[...]
        low = normed.astype(BF16)
        low_ref[...] = low
        logits = dot(low, router_ref[...]) + dot((normed - low.astype(F32)).astype(BF16), router_ref[...])
        lane = lax.broadcasted_iota(jnp.int32, (rows, 128), 1)
        valid = (lane >= FIRST) & (lane < FIRST + experts)
        logits = jnp.where(valid, logits, -1e30)
        spread = jnp.where(valid, jnp.exp(logits - jnp.max(logits, axis=-1, keepdims=True)), 0.0)
        probs = spread / jnp.sum(spread, axis=-1, keepdims=True)
        routes = lanes_ref[...]
        chosen = [
            jnp.sum(
                jnp.where(lane == routes[:, ROUTE + k : ROUTE + k + 1].astype(jnp.int32) + FIRST, probs, 0.0),
                axis=-1,
                keepdims=True,
            )
            for k in range(2)
        ]
        total = chosen[0] + chosen[1]
        stats = probs + routes
        for at, column in ((GATE, chosen[0] / total), (GATE + 1, chosen[1] / total), (TOTAL, total), (SCALE, scale)):
            stats = jnp.where(lane == at, column, stats)
        stats_out[...] = stats
        for start in range(0, width, step):
            cols = pl.ds(start, step)
            send_out[:, cols] = dot(spots[...], low_ref[:, cols]).astype(BF16)

    if not cross:
        work()
        return
    decoder = lax.axis_index("half") == 1
    pl.when(decoder)(work)

    @pl.when(jnp.logical_not(decoder))
    def _():
        result_out[...] = x[...].astype(F32)
        stats_out[...] = lead_ref[...]


def enter(info, gain, router, lanes, lead, cross, sources, experts, length):
    rows, width = sources[-2].shape
    vmem = pl.BlockSpec(memory_space=pltpu.VMEM)
    count = len(sources)
    return pl.pallas_call(
        functools.partial(enter_kernel, cross, experts, count),
        in_specs=[pl.BlockSpec(memory_space=pltpu.SMEM)] + [vmem] * (4 + count),
        out_specs=[vmem] * 5,
        out_shape=[
            jax.ShapeDtypeStruct((rows, width), BF16),
            jax.ShapeDtypeStruct((rows, width), F32),
            jax.ShapeDtypeStruct((rows, width), F32),
            jax.ShapeDtypeStruct((rows, 128), F32),
            jax.ShapeDtypeStruct((sources[-1].shape[0], width), BF16),
        ],
        scratch_shapes=[
            pltpu.VMEM((rows, width), BF16),
            pltpu.VMEM((rows // length, length, length), F32),
        ],
        compiler_params=pltpu.CompilerParams(vmem_limit_bytes=LOCAL_VMEM),
        cost_estimate=cost(10),
        name="enter_cross" if cross else "enter_self",
    )(info, gain, router, lanes, lead, *sources)


def norm_back_rows(values, scale, gain, grad):
    unit = values * scale
    pushed = grad * gain
    back = scale * (pushed - unit * jnp.mean(pushed * unit, axis=-1, keepdims=True))
    return back, jnp.sum(grad * unit, axis=0, keepdims=True)


def leave_kernel(cross, experts, count, info, stats_ref, gain_ref, router_ref, *refs):
    bias_ref, refs = (None, refs) if cross else (refs[0], refs[1:])
    sources, refs = refs[:count], refs[count:]
    grad_out, branch_out, dgain_out, dlog_out, dq_out, last_out = refs[:6]
    held, (dmixed, mask_ref, sems) = refs[6 : 6 + count], refs[6 + count :]
    back, both, grad, results, x, w_out, a, log = held[:8]
    seqs, length, _ = mask_ref.shape
    width = x.shape[1]
    loads = Loads(zip(sources, held), sems)
    if cross:
        q_ref, kv = held[8:]
        k_ref, v_ref = kv.at[:, pl.ds(0, width)], kv.at[:, pl.ds(width, width)]
        dkv_out, shift, diag_out = last_out, 0, None
    else:
        qkv, ready = held[8:]
        q_ref, k_ref, v_ref = (qkv.at[:, pl.ds(i * width, width)] for i in range(3))
        dkv_out, shift, diag_out = dq_out, width, last_out

    def leave():
        loads.wait(0, 1, 2, 3, 4)
        dgain = jnp.zeros((1, width), F32)
        lane = lax.broadcasted_iota(jnp.int32, (length, 128), 1)
        for seq in range(seqs):
            rows = pl.ds(seq * length, length)
            stats = stats_ref[rows, :]
            gates = [stats[:, GATE + k : GATE + k + 1] for k in range(2)]
            hots = [
                (lane == stats[:, ROUTE + k : ROUTE + k + 1].astype(jnp.int32) + FIRST).astype(F32)
                for k in range(2)
            ]
            probs = jnp.where((lane >= FIRST) & (lane < FIRST + experts), stats, 0.0)
            g = grad[rows, :].astype(F32)
            dgates = [
                jnp.sum(g * results[k, rows, :].astype(F32), axis=-1, keepdims=True) for k in range(2)
            ]
            shared = dgates[0] * gates[0] + dgates[1] * gates[1]
            dprobs = sum((dgates[k] - shared) / stats[:, TOTAL : TOTAL + 1] * hots[k] for k in range(2))
            dlog = probs * (dprobs - jnp.sum(dprobs * probs, axis=-1, keepdims=True))
            dlog_out[rows, :] = dlog
            dnormed = dot(both[rows, :], back[...]) + dot(dlog.astype(BF16), router_ref[...], NT)
            dx, part = norm_back_rows(x[rows, :], stats[:, SCALE : SCALE + 1], gain_ref[...], dnormed)
            dgain = dgain + part
            grad_out[rows, :] = g + dx
        dgain_out[...] = jnp.broadcast_to(dgain, dgain_out.shape)

    def attention():
        loads.wait(5)
        branch_out[...] = grad_out[...].astype(BF16)
        step = min(512, width)
        for start in range(0, width, step):
            cols = pl.ds(start, step)
            dmixed[:, cols] = dot(branch_out[...], w_out[cols, :], NT).astype(BF16)
        loads.wait(*((6, 7, 8, 9) if cross else (6, 7, 8)))
        attend_back(
            info, bias_ref, q_ref, k_ref, v_ref, a, log, dmixed, dq_out, dkv_out, shift, diag_out, mask_ref
        )

    decoder = lax.axis_index("half") == 1
    if cross:

        @pl.when(decoder)
        def _():
            loads.start()
            leave()
            attention()

    else:
        loads.start()

        @pl.when(jnp.logical_not(decoder))
        def _():
            leave()
            loads.wait(9)

        @pl.when(decoder)
        def _():
            loads.wait(0, 1, 2, 3, 4, 9)
            grad_out[...] = ready[...]

        attention()


def leave(info, stats, gain, router, bias, sources, experts, length):
    cross = bias is None
    rows, width = sources[4].shape
    seqs = rows // length
    vmem, hbm = pl.BlockSpec(memory_space=pltpu.VMEM), pl.BlockSpec(memory_space=pl.ANY)
    lead = [] if cross else [bias]
    out_shape = [
        jax.ShapeDtypeStruct((rows, width), F32),
        jax.ShapeDtypeStruct((rows, width), BF16),
        jax.ShapeDtypeStruct((8, width), F32),
        jax.ShapeDtypeStruct((rows, 128), F32),
        jax.ShapeDtypeStruct((rows, width if cross else 3 * width), BF16),
        jax.ShapeDtypeStruct((rows, 2 * width), BF16) if cross else jax.ShapeDtypeStruct(bias.shape, F32),
    ]
    return pl.pallas_call(
        functools.partial(leave_kernel, cross, experts, len(sources)),
        in_specs=[pl.BlockSpec(memory_space=pltpu.SMEM)] + [vmem] * (3 + len(lead)) + [hbm] * len(sources),
        out_specs=[vmem] * 6,
        out_shape=out_shape,
        scratch_shapes=[
            *(pltpu.VMEM(a.shape, a.dtype) for a in sources),
            pltpu.VMEM((rows, width), BF16),
            pltpu.VMEM((seqs, length, length), F32),
            pltpu.SemaphoreType.DMA((len(sources),)),
        ],
        compiler_params=pltpu.CompilerParams(vmem_limit_bytes=56 << 20),
        cost_estimate=cost(16),
        name="leave_cross" if cross else "leave_self",
    )(info, stats, gain, router, *lead, *sources)


def memory_kernel(stats_ref, gain_ref, *refs):
    (dmemory, w, x, cotangent, spots), parts, refs = refs[:5], refs[5:7], refs[7:]
    grad_out, send_out, dgain_out, cross_out, dnormed, spread = refs
    rows, width = x.shape

    @pl.when(lax.axis_index("half") == 1)
    def _():
        for i, part in enumerate(parts):
            cross_out[:, pl.ds(i * width, width)] = part[...]

    @pl.when(lax.axis_index("half") == 0)
    def _():
        cross_out[...] = dmemory[...]
        step = min(512, width)
        for start in range(0, width, step):
            cols = pl.ds(start, step)
            dnormed[:, cols] = dot(dmemory[...], w[cols, :], NT)
        scale = lax.rsqrt(jnp.mean(x[...] * x[...], axis=-1, keepdims=True) + EPS)
        dx, dgain = norm_back_rows(x[...], scale, gain_ref[...], dnormed[...])
        dgain_out[...] = jnp.broadcast_to(dgain, dgain_out.shape)
        grad = cotangent[...].astype(F32) + dx
        grad_out[...] = grad
        for k in range(2):
            gate = stats_ref[:, GATE + k : GATE + k + 1]
            spread[pl.ds(k * rows, rows), :] = (gate * grad).astype(BF16)
        for start in range(0, width, step):
            cols = pl.ds(start, step)
            send_out[:, cols] = dot(spots[...], spread[:, cols]).astype(BF16)


def memory_gradient(stats, gain, sources, parts):
    rows, width = sources[2].shape
    vmem = pl.BlockSpec(memory_space=pltpu.VMEM)
    return pl.pallas_call(
        memory_kernel,
        in_specs=[vmem] * (2 + len(sources) + len(parts)),
        out_specs=[vmem] * 4,
        out_shape=[
            jax.ShapeDtypeStruct((rows, width), F32),
            jax.ShapeDtypeStruct((sources[4].shape[0], width), BF16),
            jax.ShapeDtypeStruct((8, width), F32),
            jax.ShapeDtypeStruct((rows, 2 * width), BF16),
        ],
        scratch_shapes=[
            pltpu.VMEM((rows, width), F32),
            pltpu.VMEM((2 * rows, width), BF16),
        ],
        compiler_params=pltpu.CompilerParams(vmem_limit_bytes=LOCAL_VMEM),
        cost_estimate=cost(4),
        name="memory_gradient",
    )(stats, gain, *sources, *parts)


def dense_kernel(stages, chunk, lag, *refs):
    sources, small_ref = refs[:11], refs[11]
    out_refs, small_out, small_in = refs[12:15], refs[15], refs[16]
    held, xt_ref, refs = refs[17:28], refs[28], refs[29:]
    x_refs, own_refs, peer_refs, xp = held[:4], held[4:7], held[7:10], held[10]
    sums, parts = refs[:stages], refs[stages : 2 * stages]
    odd_parts, ss, rs, sk, rk, sl = refs[2 * stages :]
    counts = [ref.shape[1] // chunk for ref in own_refs]
    starts = [sum(counts[:i]) for i in range(3)]
    chunks = sum(counts)
    per_cross = counts[2] // 2
    rows, half = xp.shape[1:]
    dp, me = lax.axis_index("dp"), lax.axis_index("expert")
    peer = {"dp": 1 - dp}
    partners = [flipped(me, k) for k in range(stages)]
    bits = [me // (1 << k) % 2 for k in range(stages)]
    load = [pltpu.make_async_copy(sources[i], held[i], sl.at[i]) for i in range(11)]
    for i in (10, 2, 3, 6, 9, 0, 4, 7, 1, 5, 8):
        load[i].start()
    greet([peer] + [{"expert": p} for p in partners])

    def send_small(step):
        src = small_ref if step == 0 else small_out.at[step - 1]
        device = peer if step == 0 else {"expert": partners[stages - step]}
        return remote(src, small_in.at[step], ss.at[step], rs.at[step], device)

    eighth = odd_parts.shape[1]

    def send_part(k, c, odd):
        if k == 0 and odd:
            src = sums[0].at[c, pl.ds((1 - dp) * eighth, eighth)]
            return remote(src, odd_parts.at[c - early], sk.at[0, c], rk.at[0, c], peer)
        other = 1 - bits[k]
        src = sums[0].at[c, :, :, other] if k == 0 else sums[k].at[c, :, other]
        return remote(src, parts[k].at[c], sk.at[k, c], rk.at[k, c], {"expert": partners[k]})

    def turn_x(g):
        load[g].wait()
        if g < 2:
            cols = pl.ds(pl.multiple_of(dp * half, half), half)
            own = x_refs[g][:, cols]
        else:
            own = dot(x_refs[g][...], every_other(2 * half, out_refs[0].shape[0], bits[0])).astype(BF16)
        xt_ref[g, :, :rows] = jnp.transpose(own)
        xt_ref[g, :, rows:] = jnp.transpose(xp[g])

    def small_step(j):
        send_small(j).wait_recv()
        own = small_ref[...] if j == 0 else small_out[j - 1]
        small_out[j] = own + small_in[j]
        if j < stages:
            send_small(j + 1).start()

    send_small(0).start()
    load[10].wait()
    last = counts[2]
    early = chunks - last
    per = chunks // last

    def produce(i, carry):
        c = jnp.where(lax.rem(i, per) == 0, early + i // per, i - i // per - 1)
        for g in range(3):

            @pl.when(c == starts[g])
            def _(g=g):
                load[4 + g].wait()
                load[7 + g].wait()
                for x in (g,) if g < 2 else (2, 3):
                    turn_x(x)

            @pl.when((c >= starts[g]) & (c < starts[g] + counts[g]))
            def _(g=g):
                at = c - starts[g]
                cols = pl.ds(pl.multiple_of(at * chunk, chunk), chunk)
                which = g if g < 2 else 2 + at // per_cross
                total = dot(xt_ref[which, :, :rows], own_refs[g][:, cols])
                total += dot(xt_ref[which, :, rows:], peer_refs[g][:, cols])
                sums[0][c] = total.astype(BF16).reshape(sums[0].shape[1:])
                send_part(0, c, g == 2).start()

        for j in range(2):

            @pl.when(i == 3 + 6 * j)
            def _(j=j):
                small_step(j)

        return carry

    lax.fori_loop(0, chunks, produce, 0)

    def advance(k, c, odd):
        send_part(k, c, odd).wait_recv()
        if k == 0 and odd:
            mine, other = sums[0][c, pl.ds(dp * eighth, eighth)], odd_parts[c - early]
        else:
            mine = sums[0][c, :, :, bits[0]] if k == 0 else sums[k][c, :, bits[k]]
            other = parts[k][c]
        total = mine.astype(F32) + other.astype(F32)
        if k + 1 < stages:
            sums[k + 1][c] = total.astype(BF16).reshape(sums[k + 1].shape[1:])
            send_part(k + 1, c, odd).start()
            return
        total = total.reshape(total.shape[-2:])
        for g in (2,) if odd else (0, 1):

            @pl.when((c >= starts[g]) & (c < starts[g] + counts[g]))
            def _(g=g):
                at = pl.multiple_of((c - starts[g]) * chunk, chunk)
                out_refs[g][:, pl.ds(at, chunk)] = total

    def reduce(i, carry):
        for k in range(stages):
            c = i - lag * k

            @pl.when((c >= 0) & (c < early))
            def _(k=k, c=c):
                advance(k, c, False)

        for k in range(stages):
            twice = i - 1 - 3 * k

            @pl.when((twice >= 0) & (lax.rem(twice, 2) == 0) & (twice < 2 * last))
            def _(k=k, twice=twice):
                advance(k, early + twice // 2, True)

        for j in range(2, stages + 1):

            @pl.when(i == 3 * j - 2)
            def _(j=j):
                small_step(j)

        return carry

    steps = max(early + lag * (stages - 1), 2 * last + 3 * (stages - 1), 3 * stages - 1)
    lax.fori_loop(0, steps, reduce, 0)

    def finish(c, carry, odd):
        for k in range(stages):
            send_part(k, c, odd).wait_send()
        return carry

    lax.fori_loop(0, early, functools.partial(finish, odd=False), 0)
    lax.fori_loop(early, chunks, functools.partial(finish, odd=True), 0)
    for j in range(stages + 1):
        send_small(j).wait_send()


def to_neighbour(array):
    count = lax.axis_size("expert")
    return lax.ppermute(array, "expert", [(i, i ^ 1) for i in range(count)])


def over_dp(array):
    return lax.ppermute(array, "dp", [(0, 1), (1, 0)])


def dense_gradients(lefts, lefts_peer, own, peer, small, experts):
    chunk = 512
    rows, width = lefts[0].shape
    half_rows = width // 2
    chunks = sum(y.shape[1] for y in own) // chunk
    stages = experts.bit_length() - 1
    keep = half_rows // experts
    vmem, hbm = pl.BlockSpec(memory_space=pltpu.VMEM), pl.BlockSpec(memory_space=pl.ANY)
    dma = pltpu.SemaphoreType.DMA
    sources = [*lefts, *own, *peer, lefts_peer]
    blocks = [(experts // 4, 2, 2)] + [(experts >> (k + 1), 2) for k in range(1, stages)]
    halved = [(experts // 4, 2)] + [(experts >> (k + 1),) for k in range(1, stages)]
    scratch = [pltpu.VMEM((stages + 1, *small.shape), F32)]
    scratch += [pltpu.VMEM(a.shape, BF16) for a in sources]
    scratch += [pltpu.VMEM((4, half_rows, 2 * rows), BF16)]
    scratch += [pltpu.VMEM((chunks, *b, keep, chunk), BF16) for b in blocks + halved]
    scratch += [pltpu.VMEM((own[2].shape[1] // chunk, experts // 8, 2, 2, keep, chunk), BF16)]
    scratch += [dma((stages + 1,)), dma((stages + 1,)), dma((stages, chunks)), dma((stages, chunks))]
    scratch += [dma((len(sources),))]
    *outs, sums = pl.pallas_call(
        functools.partial(dense_kernel, stages, chunk, 2),
        in_specs=[hbm] * len(sources) + [vmem],
        out_specs=[vmem] * 4,
        out_shape=[
            *(jax.ShapeDtypeStruct((keep, y.shape[1]), F32) for y in own),
            jax.ShapeDtypeStruct((stages + 1, *small.shape), F32),
        ],
        scratch_shapes=scratch,
        compiler_params=pltpu.CompilerParams(
            collective_id=0, has_side_effects=True, vmem_limit_bytes=56 << 20
        ),
        cost_estimate=cost(45),
        name="dense_gradients",
    )(*sources, small)
    return outs, sums[stages]


def product_kernel(x_ref, y_ref, out_ref):
    out_ref[...] = dot(x_ref[...], y_ref[...].reshape(y_ref.shape[-2:]), TN).reshape(out_ref.shape)


def expert_gradients(rows, mixed, hidden, grads):
    total, width = rows.shape
    span = hidden.shape[1]
    tile = 256
    params = pltpu.CompilerParams(vmem_limit_bytes=40 << 20)
    din = pl.pallas_call(
        product_kernel,
        grid=(2, width // tile),
        in_specs=[
            pl.BlockSpec((total, tile), lambda g, i: (0, i)),
            pl.BlockSpec((1, total, span), lambda g, i: (g, 0, 0)),
        ],
        out_specs=pl.BlockSpec((1, tile, span), lambda g, i: (g, i, 0)),
        out_shape=jax.ShapeDtypeStruct((2, width, span), F32),
        compiler_params=params,
        cost_estimate=cost(12),
        name="expert_in_gradient",
    )(rows, mixed)
    ddown = pl.pallas_call(
        product_kernel,
        grid=(pl.cdiv(span, tile),),
        in_specs=[
            pl.BlockSpec((total, tile), lambda i: (0, i)),
            pl.BlockSpec((total, width), lambda i: (0, 0)),
        ],
        out_specs=pl.BlockSpec((tile, width), lambda i: (i, 0)),
        out_shape=jax.ShapeDtypeStruct((span, width), F32),
        compiler_params=params,
        cost_estimate=cost(7),
        name="expert_out_gradient",
    )(hidden, grads)
    return din, ddown


def body(
    tokens,
    cotangent,
    lengths,
    routes,
    self_qkv,
    self_out,
    cross_weights,
    router,
    gains,
    bias_table,
    expert_in,
    expert_out,
):
    _, seqs, length, width = tokens.shape
    heads = H
    experts = router.shape[2]
    top = routes.shape[3]
    capacity = (5 * top * length + 4 * experts - 1) // (4 * experts)
    block_rows = -(-seqs * capacity // 16) * 16
    rows = seqs * length
    slots = experts * block_rows
    half_index = lax.axis_index("half")
    decoder = half_index == 1
    wqkv, wout, wcross, wrouter, gain = (
        self_qkv[0],
        self_out[0],
        cross_weights[0],
        router[0],
        gains[0],
    )
    w_in, w_down = expert_in[0, 0], expert_out[0, 0]

    column = np.arange(2 * length)
    entry = np.arange(BUCKETS * heads)
    hot, hot_back = (
        jnp.where(
            decoder,
            *(
                (entry[:, None] // heads == bucket[None, :]).astype(np.float32)
                for bucket in reversed(diagonal_buckets(diff))
            ),
        )
        for diff in (np.where(column < length, column, column - 2 * length), column - length + 1)
    )
    own_head = entry[None, :] % heads == np.arange(heads)[:, None]
    bias = lax.dot_general(
        jnp.where(own_head, bias_table, 0.0),
        hot,
        (((1,), (0,)), ((), ())),
        precision=lax.Precision.HIGHEST,
        preferred_element_type=F32,
    )
    own_lengths = jnp.where(decoder, lengths[1], lengths[0])
    self_info = jnp.concatenate([own_lengths, half_index[None]]).astype(jnp.int32)
    cross_info = jnp.concatenate([lengths[0], jnp.zeros((1,), jnp.int32)]).astype(jnp.int32)

    order = jnp.transpose(routes[0], (0, 2, 1)).reshape(seqs, top * length)
    spots, both_spots, stacked, both, tally, route_lanes = find_slots(order, experts, capacity, block_rows, top)
    tallies = jnp.concatenate([tally[:, 0], tally[:, 1] - tally[:, 0]])
    router_wide = jnp.pad(wrouter, ((0, 0), (FIRST, 128 - FIRST - experts)))

    def fetch(returned):
        flat = returned.reshape(slots, width)
        return dot(stacked, flat).astype(BF16).reshape(top, rows, width)

    def combine(values, stats, results):
        return values + sum(stats[:, GATE + k : GATE + k + 1] * results[k] for k in range(top))

    values = tokens[0].reshape(rows, width).astype(F32)
    normed, scale0 = norm_parts(values, gain[0])
    low0 = normed.astype(BF16)
    qkv = dot(low0, wqkv).astype(BF16)
    mixed0, log0, first, stats, send = enter(
        self_info,
        gain[1:2],
        router_wide,
        route_lanes,
        bias,
        False,
        [qkv, wout, tokens[0].reshape(rows, width), both_spots],
        experts,
        length,
    )

    send_shape = (experts, block_rows, width)
    saved = moe_forward(send.reshape(send_shape), w_in, w_down, 0, None, [], rows)
    final_enc = combine(first, stats, fetch(saved[0]))
    normed, scale_m = norm_parts(final_enc, gain[2])
    low_m = normed.astype(BF16)
    memory = dot(low_m, wcross).astype(BF16)
    names = ("half", "dp", "expert")
    forward_pairs, back_pairs = half_pairs(lax.axis_size("dp") * lax.axis_size("expert"))
    memory = lax.ppermute(memory, names, forward_pairs)

    normed, scale_c = norm_parts(first, gain[2])
    low_c = normed.astype(BF16)
    query = dot(low_c, wcross[:, :width]).astype(BF16)
    mixed_c, log_c, second, stats, send = enter(
        cross_info,
        gain[1:2],
        router_wide,
        route_lanes,
        stats,
        True,
        [query, memory, wcross[:, width:], first, both_spots],
        experts,
        length,
    )

    lefts = [low0, mixed0, jnp.where(decoder, low_c, low_m), jnp.where(decoder, mixed_c, low_m)]
    saved = moe_forward(send.reshape(send_shape), w_in, w_down, 1, saved, lefts, rows)
    results = fetch(saved[0])
    final = combine(second, stats, results)
    outputs = final.astype(BF16)

    grad_dec = cotangent[0].reshape(rows, width)
    spread = [(stats[:, GATE + k : GATE + k + 1] * grad_dec.astype(F32)).astype(BF16) for k in range(top)]
    grad_send = dot(spots, jnp.concatenate(spread)).astype(BF16)
    kept_from = moe_backward(grad_send.reshape(experts, block_rows, width), saved, 1, None)

    grad_second, dbranch_c, dgain_moe_dec, dlog_dec, dquery, dmemory = leave(
        cross_info,
        stats,
        gain[1:2],
        router_wide,
        None,
        [
            kept_from[0].reshape(slots, width),
            both,
            grad_dec,
            results,
            second,
            wcross[:, width:],
            mixed_c,
            log_c,
            query,
            memory,
        ],
        experts,
        length,
    )
    dmemory = lax.ppermute(dmemory, names, back_pairs)
    dnormed = dot(dquery, wcross[:, :width], NT)
    dvalues, dgain_c = norm_back(first, scale_c, gain[2], dnormed)
    grad_first_dec = grad_second + dvalues

    grad, grad_send, dgain_m, cross_grad = memory_gradient(
        stats, gain[2:3], [dmemory, wcross, final_enc, grad_dec, spots], [dquery, dbranch_c]
    )
    back, mixed_grads, all_grad = moe_backward(
        grad_send.reshape(experts, block_rows, width), saved, 0, kept_from
    )
    all_rows, hidden, lefts_peer = saved[1], saved[4], saved[10]
    grad_first, dbranch, dgain_moe, dlog, dqkv_rows, diag = leave(
        self_info,
        stats,
        gain[1:2],
        router_wide,
        bias,
        [
            back.reshape(slots, width),
            both,
            grad,
            results,
            second,
            wout,
            mixed0,
            log0,
            qkv,
            grad_first_dec,
        ],
        experts,
        length,
    )
    ff_half = hidden.shape[-1]
    din, ddown = expert_gradients(
        all_rows.reshape(-1, width),
        mixed_grads.reshape(2, -1, ff_half),
        hidden.reshape(-1, ff_half),
        all_grad.reshape(-1, width),
    )
    dlog = jnp.where(decoder, dlog_dec, dlog)[:, FIRST : FIRST + experts]
    dgain_moe = jnp.where(decoder, dgain_moe_dec[0], dgain_moe[0])
    drouter = lax.dot_general(
        second * stats[:, SCALE : SCALE + 1] * gain[1],
        dlog,
        TN,
        precision=lax.Precision.HIGHEST,
        preferred_element_type=F32,
    )
    dnormed = dot(dqkv_rows, wqkv, NT)
    dvalues, dgain_self = norm_back(values, scale0, gain[0], dnormed)
    d_tokens = (grad_first + dvalues).astype(BF16)
    by_entry = lax.dot_general(
        diag, hot_back, NT, precision=lax.Precision.HIGHEST, preferred_element_type=F32
    )
    dtable = jnp.sum(jnp.where(own_head, by_entry, 0.0), axis=0)

    own_grads = (dqkv_rows, dbranch, cross_grad)
    peer_grads = (over_dp(dqkv_rows), over_dp(dbranch), to_neighbour(cross_grad))
    places = 2 * experts
    own = width // places
    extra = jnp.concatenate([dtable.reshape(places, -1), tallies.reshape(places, 1)], axis=1)
    extra = jnp.pad(extra, ((0, 0), (0, -extra.shape[1] % own)))
    small = jnp.concatenate(
        [
            jnp.transpose(drouter),
            jnp.stack([dgain_self, dgain_moe, jnp.where(decoder, dgain_c, dgain_m[0])]),
            jnp.swapaxes(extra.reshape(places, -1, own), 0, 1).reshape(-1, width),
        ]
    )
    small = jnp.pad(small, ((0, -small.shape[0] % 8), (0, 0)))
    (dqkv, dout, dcross), small = dense_gradients(
        lefts, lefts_peer, own_grads, peer_grads, small, experts
    )
    place = lax.axis_index("dp") * experts + lax.axis_index("expert")
    mine = lax.dynamic_slice_in_dim(small, place * own, own, 1)
    tail = mine[experts + 3 :].reshape(-1)
    own_table = dtable.shape[0] // places
    d_table = tail[:own_table]
    counts = tail[own_table].astype(jnp.int32)

    return (
        outputs.reshape(1, seqs, length, width),
        d_tokens.reshape(1, seqs, length, width),
        dqkv[None],
        dout[None],
        dcross[None],
        jnp.transpose(mine[:experts])[None],
        mine[experts : experts + 3][None],
        d_table[None],
        din[None, None],
        ddown[None, None],
        counts.reshape(1, 1, 1),
    )


def half_pairs(count):
    return (
        [(i, count + i) for i in range(count)],
        [(count + i, i) for i in range(count)],
    )


def solution(mesh):
    placed = (
        P("half", ("dp", "expert"), None, None),
        P("half", ("dp", "expert"), None, None),
        P(None, ("dp", "expert")),
        P("half", ("dp", "expert"), None, None),
        P("half", None, None),
        P("half", None, None),
        P("half", None, None),
        P("half", None, None),
        P("half", None, None),
        P("half", None),
        P("half", "expert", None, None, None),
        P("half", "expert", None, None),
    )
    return jax.shard_map(
        body,
        mesh=mesh,
        in_specs=placed,
        out_specs=(
            P("half", ("dp", "expert"), None, None),
            P("half", ("dp", "expert"), None, None),
            P("half", ("dp", "expert"), None),
            P("half", ("dp", "expert"), None),
            P("half", ("dp", "expert"), None),
            P("half", ("dp", "expert"), None),
            P("half", None, ("dp", "expert")),
            P("half", ("dp", "expert")),
            P("half", "expert", None, None, "dp"),
            P("half", "expert", "dp", None),
            P("half", "dp", "expert"),
        ),
        check_vma=False,
    )
```

```python
import functools

import jax
import jax.numpy as jnp
import numpy as np
from jax import lax
from jax.experimental import pallas as pl
from jax.experimental.pallas import tpu as pltpu
from jax.sharding import PartitionSpec as P

H = 16
BUCKETS = 32
EPS = 1e-06
ENC_STEPS = (12, 16, 23, 32, 46, 64, 91)
DEC_STEPS = (19, 21, 24, 27, 31, 35, 40, 46, 52, 59, 67, 77, 87, 99, 113)
F32 = jnp.float32
BF16 = jnp.bfloat16
MESH = pl.DeviceIdType.MESH
LOCAL_VMEM = 32 << 20


def cost(gigaflops):
    return pl.CostEstimate(flops=int(gigaflops * 1e9), bytes_accessed=1 << 20, transcendentals=0)
NT = (((1,), (1,)), ((), ()))
TN = (((0,), (0,)), ((), ()))


def dot(a, b, dims=(((1,), (0,)), ((), ()))):
    return lax.dot_general(a, b, dims, preferred_element_type=F32)


def diagonal_buckets(diff):
    apart = np.abs(diff)
    coarse = 8 + sum((apart >= step).astype(np.int32) for step in ENC_STEPS)
    enc = np.where(apart < 8, apart, coarse) + 16 * (diff > 0)
    behind = np.maximum(-diff, 0)
    coarse = 16 + sum((behind >= step).astype(np.int32) for step in DEC_STEPS)
    dec = np.where(behind < 16, behind, coarse)
    return enc.astype(np.int32), dec.astype(np.int32)


def diagonals(bias_ref, head, length):
    row = jnp.broadcast_to(bias_ref[pl.ds(head, 1), :], (length, 2 * length))
    return pltpu.roll(row, 0, 1, stride=1, stride_axis=0)[:, :length]


def fill_masks(info, mask_ref):
    seqs, length, _ = mask_ref.shape
    row_id = lax.broadcasted_iota(jnp.int32, (length, length), 0)
    col_id = lax.broadcasted_iota(jnp.int32, (length, length), 1)
    reach = jnp.where(info[seqs] > 0, row_id, length)
    for seq in range(seqs):
        allowed = (col_id < info[seq]) & (col_id <= reach)
        mask_ref[seq] = jnp.where(allowed, 0.0, -1000000000.0)


def attend(info, bias_ref, q_ref, k_ref, v_ref, out_ref, log_ref, mask_ref):
    has_bias = bias_ref is not None
    seqs, length, _ = mask_ref.shape
    low = lax.broadcasted_iota(jnp.int32, (length, 128), 1) < 64
    fill_masks(info, mask_ref)

    @pl.loop(0, q_ref.shape[1] // 128, unroll=4)
    def _(pair):
        cols = pl.ds(pl.multiple_of(pair * 128, 128), 128)
        biases = [diagonals(bias_ref, 2 * pair + side, length) if has_bias else 0.0 for side in range(2)]
        for seq in range(seqs):
            rows = pl.ds(seq * length, length)
            q, k, v = q_ref[rows, cols] * 0.125, k_ref[rows, cols], v_ref[rows, cols]
            mixed, peaks = [], []
            for side in range(2):
                mine = low if side == 0 else jnp.logical_not(low)
                part = jnp.where(mine, q, jnp.zeros_like(q))
                scores = dot(part, k, NT) + (mask_ref[seq] + biases[side])
                peak = jnp.max(scores, axis=-1, keepdims=True)
                spread = jnp.exp(scores - peak).astype(BF16)
                mixed.append(dot(spread, jnp.where(mine, v, jnp.ones_like(v))))
                peaks.append(peak)
            total = pltpu.roll(jnp.where(low, mixed[1], mixed[0]), 64, 1)
            out_ref[rows, cols] = (jnp.where(low, mixed[0], mixed[1]) / total).astype(BF16)
            log_ref[rows, cols] = jnp.where(low, peaks[0], peaks[1]) + jnp.log(total)


def attend_back(info, bias_ref, q_ref, k_ref, v_ref, a_ref, log_ref, g_ref, dq_ref, dkv_ref, shift, diag_ref, mask_ref):
    has_bias = bias_ref is not None
    seqs, length, _ = mask_ref.shape
    width = q_ref.shape[1]
    low = lax.broadcasted_iota(jnp.int32, (length, 128), 1) < 64
    fill_masks(info, mask_ref)
    if has_bias:
        row_id = lax.broadcasted_iota(jnp.int32, (length, length), 0)
        col_id = lax.broadcasted_iota(jnp.int32, (length, length), 1)
        flip = (row_id + col_id == length - 1).astype(F32).astype(BF16)

    @pl.loop(0, width // 128, unroll=4)
    def _(pair):
        cols = pl.ds(pl.multiple_of(pair * 128, 128), 128)
        kcols = pl.ds(pl.multiple_of(shift + pair * 128, 128), 128)
        vcols = pl.ds(pl.multiple_of(shift + width + pair * 128, 128), 128)
        biases = [diagonals(bias_ref, 2 * pair + side, length) if has_bias else 0.0 for side in range(2)]
        sums = [0.0, 0.0]
        for seq in range(seqs):
            rows = pl.ds(seq * length, length)
            q, k, v, g = q_ref[rows, cols] * 0.125, k_ref[rows, cols], v_ref[rows, cols], g_ref[rows, cols]
            logs = log_ref[rows, cols]
            turned = pltpu.roll(logs, 64, 1)
            product = g.astype(F32) * a_ref[rows, cols].astype(F32)
            minus = (-pltpu.roll(product, 64, 1)).astype(BF16)
            scaled = k * 0.125
            dqs, dks, dvs = [], [], []
            for side in range(2):
                mine = low if side == 0 else jnp.logical_not(low)
                part = jnp.where(mine, q, jnp.zeros_like(q))
                scores = dot(part, k, NT) + (mask_ref[seq] + biases[side])
                probs = jnp.exp(scores - jnp.where(mine, logs, turned))
                dvs.append(dot(probs.astype(BF16), g, TN))
                centred = dot(jnp.where(mine, g, minus), jnp.where(mine, v, jnp.ones_like(v)), NT)
                dlow = (probs * centred).astype(BF16)
                dqs.append(dot(dlow, scaled))
                dks.append(dot(dlow, q, TN))
                if has_bias:
                    sums[side] = sums[side] + dlow.astype(F32)
            dq_ref[rows, cols] = jnp.where(low, dqs[0], dqs[1]).astype(BF16)
            dkv_ref[rows, kcols] = jnp.where(low, dks[0], dks[1]).astype(BF16)
            dkv_ref[rows, vcols] = jnp.where(low, dvs[0], dvs[1]).astype(BF16)
        if has_bias:
            for side in range(2):
                upside = dot(flip, sums[side].astype(BF16))
                wide = jnp.concatenate([upside, jnp.zeros((length, length), F32)], axis=1)
                turned = pltpu.roll(wide, 0, 1, stride=1, stride_axis=0)
                diag_ref[pl.ds(2 * pair + side, 1), :] = jnp.sum(turned, axis=0, keepdims=True)


def norm_parts(values, gain):
    scale = lax.rsqrt(jnp.mean(values * values, axis=-1, keepdims=True) + EPS)
    return values * scale * gain, scale


def norm_back(values, scale, gain, grad):
    unit = values * scale
    gain_grad = jnp.sum(grad * unit, axis=0)
    pushed = grad * gain
    back = scale * (pushed - unit * jnp.mean(pushed * unit, axis=-1, keepdims=True))
    return back, gain_grad


def gelu_parts(gate):
    c, a = 0.7978845608028654, 0.044715
    square = gate * gate
    u = 0.5 + 0.5 * jnp.tanh(gate * (c + c * a * square))
    slope = u * (1.0 + (gate * (2.0 * c + 6.0 * c * a * square)) * (1.0 - u))
    return gate * u, slope


def flipped(value, bit):
    step = 1 << bit
    return value + step * (1 - 2 * (value // step % 2))


def crossed(value, other):
    for bit in range(other.bit_length()):
        if other >> bit & 1:
            value = flipped(value, bit)
    return value


def greet(partners):
    barrier = pltpu.get_barrier_semaphore()
    for partner in partners:
        pl.semaphore_signal(barrier, inc=1, device_id=partner, device_id_type=MESH)
    pl.semaphore_wait(barrier, len(partners))


def remote(src, dst, out_sem, in_sem, device):
    return pltpu.make_async_remote_copy(
        src_ref=src,
        dst_ref=dst,
        send_sem=out_sem,
        recv_sem=in_sem,
        device_id=device,
        device_id_type=MESH,
    )


def tile_loop(count, step, body):
    @pl.loop(0, count // step)
    def _(i):
        body(pl.multiple_of(i * step, step), step)

    if count % step:
        body(count // step * step, count % step)


def groups_of(experts, block):
    size = 1
    while size * 2 * block <= 320 and size * 2 <= experts:
        size *= 2
    if experts <= 2 * size:
        half = max(size // 2, 1)
        return [(k, half) for k in range(0, experts, half)]
    return [(k, size) for k in range(0, experts, size)]


class Turn:
    def __init__(self, experts, block, there, home):
        self.me, self.dp = lax.axis_index("expert"), lax.axis_index("dp")
        self.experts, self.block = experts, block
        self.peer = {"dp": 1 - self.dp}
        self.groups = groups_of(experts, block)
        self.there_refs, self.home_refs = there, home

    def greet(self):
        greet([{"expert": crossed(self.me, k)} for k in range(1, self.experts)] + [self.peer])

    def there(self, k):
        src, dst, out_sems, in_sems = self.there_refs
        partner = crossed(self.me, k)
        return remote(src.at[partner], dst.at[self.me], out_sems.at[k], in_sems.at[k], {"expert": partner})

    def home(self, k):
        src, dst, out_sems, in_sems = self.home_refs
        partner = crossed(self.me, k)
        return remote(src.at[partner], dst.at[self.me], out_sems.at[k], in_sems.at[k], {"expert": partner})

    def arrive(self, first, size):
        for k in range(max(first, 1), first + size):
            self.there(k).wait_recv()

    def base(self, first, size):
        return crossed(self.me // size, first // size) * size

    def spans(self, first, size):
        base = self.base(first, size)
        rows = pl.ds(pl.multiple_of(base * self.block, size * self.block), size * self.block)
        return pl.ds(base, size), rows


def every_other(width, own, parity):
    row = lax.broadcasted_iota(jnp.int32, (width, width // 2), 0)
    col = lax.broadcasted_iota(jnp.int32, (width, width // 2), 1)
    return (row == (2 * (col // own) + parity) * own + col % own).astype(F32).astype(BF16)


class Lefts:
    def __init__(self, refs, out, scratch, width, experts):
        self.me, self.own, self.width = lax.axis_index("expert"), width // (2 * experts), width
        self.refs, self.out = refs, out
        self.held, self.stage, self.loaded, self.sent, self.came = scratch
        self.half = width // 2
        self.dp = lax.axis_index("dp")

    def fetch(self, i):
        return pltpu.make_async_copy(self.refs[i], self.held.at[i % 2], self.loaded.at[i])

    def copy(self, i):
        device = {"dp": 1 - self.dp} if i < 2 else {"expert": flipped(self.me, 0)}
        return remote(self.stage.at[i], self.out.at[i], self.sent.at[i], self.came.at[i], device)

    def load(self):
        for i in range(2):
            self.fetch(i).start()

    def send(self):
        for i in range(4):
            self.fetch(i).wait()
            slot = i % self.held.shape[0]
            if i < 2:
                cols = pl.ds(pl.multiple_of((1 - self.dp) * self.half, 128), self.half)
                self.stage[i] = self.held[slot, :, cols]
            else:
                picked = every_other(self.width, self.own, 1 - self.me % 2)
                self.stage[i] = dot(self.held[slot], picked).astype(BF16)
            self.copy(i).start()
            if i + 2 < 4:
                self.fetch(i + 2).start()

    def wait(self):
        for i in range(4):
            self.copy(i).wait()


def transpose_kernel_part(loads, tall, wide, wsem, tsem):
    copies = [pltpu.make_async_copy(src, dst, wsem.at[i]) for i, (src, dst, _) in enumerate(loads)]
    for copy in copies:
        copy.start()
    for i, (_, held, out) in enumerate(loads):
        slab = tall.shape[1]
        stages = [tall.at[i] if out.shape[1] == tall.shape[2] else wide.at[pl.ds(i * slab, slab)] for i in range(2)]
        steps = out.shape[0] // slab
        copies[i].wait()

        def put(t, slot, stages=stages, out=out, slab=slab):
            rows = pl.ds(pl.multiple_of(t * slab, slab), slab)
            return pltpu.make_async_copy(stages[slot], out.at[rows], tsem.at[slot])

        def step(pair, carry, stages=stages, held=held, put=put, slab=slab, steps=steps):
            for slot in range(2):
                t = 2 * pair + slot

                @pl.when(t < steps)
                def _(t=t, slot=slot):
                    @pl.when(pair > 0)
                    def _():
                        put(t - 2, slot).wait()

                    cols = pl.ds(pl.multiple_of(t * slab, slab), slab)
                    stages[slot][...] = jnp.transpose(held[:, cols])
                    put(t, slot).start()

            return carry

        lax.fori_loop(0, pl.cdiv(steps, 2), step, 0)
        for t in (steps - 2, steps - 1):
            put(t, t % 2).wait()


def expert_forward_kernel(turn, has_prev, *refs):
    send_ref, w_in, w_down = refs[:3]
    left_refs, refs = refs[3 + 10 * has_prev : 3 + 14 * has_prev], refs[3 + 14 * has_prev :]
    back_out, rows_out, slope_out, value_out, hidden_out, slope_peer_out, value_peer_out = refs[:7]
    wgt_out, wut_out, wdt_out = refs[7:10]
    left_out, refs = refs[10 : 10 + has_prev], refs[10 + has_prev :]
    wg, wu, wd, rows, back, made, rows_peer, slopes, values, hidden = refs[:10]
    slopes_peer, values_peer, tall = refs[10:13]
    wsem, s1, r1, s2, r2, sx, rx, osem, tsem = refs[13:22]
    experts, block, width = send_ref.shape
    ff = wd.shape[0]
    span = ff // 2
    lefts = Lefts(left_refs, left_out[0], (tall, *refs[22:]), width, experts) if has_prev else None

    @pl.when(lax.axis_index("half") != turn)
    def _():
        if lefts:
            lefts.load()
            greet([{"dp": 1 - lax.axis_index("dp")}, {"expert": flipped(lax.axis_index("expert"), 0)}])
            lefts.send()
        loads = ((w_in.at[0], wg, wgt_out), (w_in.at[1], wu, wut_out), (w_down, wd, wdt_out))
        transpose_kernel_part(loads, tall, slopes, wsem, tsem)
        if lefts:
            lefts.wait()

    @pl.when(lax.axis_index("half") == turn)
    def _():
        t = Turn(experts, block, (send_ref, rows, s1, r1), (made, back, s2, r2))
        t.greet()

        def rows_over(part):
            blocks, _ = t.spans(*t.groups[part])
            return remote(rows.at[blocks], rows_peer.at[blocks], sx.at[part], rx.at[part], t.peer)

        for k in range(1, experts):
            t.there(k).start()
        rows[t.me] = send_ref[t.me]
        loads = [
            pltpu.make_async_copy(src, dst, wsem.at[i])
            for i, (src, dst) in enumerate(((w_in.at[0], wg), (w_in.at[1], wu), (w_down, wd)))
        ]
        for load in loads:
            load.start()
        if lefts:
            lefts.load()
        for part, (first, size) in enumerate(t.groups):
            t.arrive(first, size)
            rows_over(part).start()
            blocks, span_rows = t.spans(first, size)
            if part == 0:
                loads[0].wait()
                loads[1].wait()

            def up_tile(start, count, blocks=blocks, span_rows=span_rows, size=size):
                x = rows[blocks].reshape(size * block, width)
                cols = pl.ds(start, count)
                value, slope = gelu_parts(dot(x, wg[:, cols]))
                up = dot(x, wu[:, cols])
                hidden[span_rows, cols] = (value * up).astype(BF16)
                values[span_rows, cols] = value.astype(BF16)
                slopes[span_rows, cols] = (up * slope).astype(BF16)

            tile_loop(ff, 512, up_tile)
            if part == 0:
                loads[2].wait()

            def down_tile(start, count, blocks=blocks, span_rows=span_rows, size=size):
                cols = pl.ds(start, count)
                y = dot(hidden[span_rows, :], wd[:, cols]).astype(BF16)
                made[blocks, :, cols] = y.reshape(size, block, count)

            tile_loop(width, 512, down_tile)
            for k in range(max(first, 1), first + size):
                t.home(k).start()
        back[t.me] = made[t.me]
        half_cols = pl.ds(pl.multiple_of(t.dp * span, 128), span)
        other_cols = pl.ds(pl.multiple_of((1 - t.dp) * span, 128), span)
        outs = [
            (slopes, slope_out),
            (values, value_out),
            (hidden.at[:, half_cols], hidden_out.at[0]),
            (rows, rows_out.at[0]),
        ]
        outs = [pltpu.make_async_copy(src, dst, osem.at[i]) for i, (src, dst) in enumerate(outs)]
        for out in outs:
            out.start()
        if lefts:
            lefts.send()

        for part in range(len(t.groups)):
            rows_over(part).wait_recv()

        def peer_tile(start, count):
            x = rows_peer[...].reshape(experts * block, width)
            here = pl.ds(start, count)
            cols = pl.ds(pl.multiple_of(t.dp * span + start, 128), count)
            value, slope = gelu_parts(dot(x, wg[:, cols]))
            up = dot(x, wu[:, cols])
            hidden[:, pl.ds(pl.multiple_of((1 - t.dp) * span + start, 128), count)] = (value * up).astype(BF16)
            values_peer[:, here] = value.astype(BF16)
            slopes_peer[:, here] = (up * slope).astype(BF16)

        tile_loop(span, 512, peer_tile)
        more = [
            (slopes_peer, slope_peer_out),
            (values_peer, value_peer_out),
            (hidden.at[:, other_cols], hidden_out.at[1]),
            (rows_peer, rows_out.at[1]),
        ]
        more = [pltpu.make_async_copy(src, dst, osem.at[4 + i]) for i, (src, dst) in enumerate(more)]
        for out in more:
            out.start()
        for k in range(1, experts):
            t.home(k).wait_recv()
        back_copy = pltpu.make_async_copy(back, back_out, osem.at[8])
        back_copy.start()
        for k in range(1, experts):
            t.there(k).wait_send()
            t.home(k).wait_send()
        for part in range(len(t.groups)):
            rows_over(part).wait_send()
        if lefts:
            lefts.wait()
        for out in [*outs, *more, back_copy]:
            out.wait()


def expert_backward_kernel(turn, has_prev, *refs):
    send_ref = refs[0]
    sources = refs[1:8]
    refs = refs[8 + 3 * has_prev :]
    back_out, mixed_out, grad_out = refs[:3]
    wdt, dgate, dup, wgt, wut, dgate_peer, dup_peer = refs[3:10]
    grads, back, made, grads_peer = refs[10:14]
    wsem, s1, r1, s2, r2, sx, rx, osem = refs[14:]
    experts, block, width = send_ref.shape
    ff = wdt.shape[1]
    span = ff // 2
    dp = lax.axis_index("dp")
    t = Turn(experts, block, (send_ref, grads, s1, r1), (made, back, s2, r2))

    @pl.when(lax.axis_index("half") == turn)
    def _():
        t.greet()

        def grads_over(part):
            blocks, _ = t.spans(*t.groups[part])
            return remote(grads.at[blocks], grads_peer.at[blocks], sx.at[part], rx.at[part], t.peer)

        for k in range(1, experts):
            t.there(k).start()
        grads[t.me] = send_ref[t.me]
        held = (wdt, dgate, dup, wgt, wut, dgate_peer, dup_peer)
        loads = [pltpu.make_async_copy(src, dst, wsem.at[i]) for i, (src, dst) in enumerate(zip(sources, held))]
        for load in loads:
            load.start()
        for load in loads[:3]:
            load.wait()
        for part, (first, size) in enumerate(t.groups):
            t.arrive(first, size)
            grads_over(part).start()
            blocks, span_rows = t.spans(first, size)

            def hidden_tile(start, count, blocks=blocks, span_rows=span_rows, size=size):
                dy = grads[blocks].reshape(size * block, width)
                cols = pl.ds(start, count)
                dhidden = dot(dy, wdt[:, cols])
                dgate[span_rows, cols] = (dhidden * dgate[span_rows, cols].astype(F32)).astype(BF16)
                dup[span_rows, cols] = (dhidden * dup[span_rows, cols].astype(F32)).astype(BF16)

            tile_loop(ff, 512, hidden_tile)
            if part == 0:
                loads[3].wait()
                loads[4].wait()

            def rows_tile(start, count, blocks=blocks, span_rows=span_rows, size=size):
                cols = pl.ds(start, count)
                dr = dot(dgate[span_rows, :], wgt[:, cols]) + dot(dup[span_rows, :], wut[:, cols])
                made[blocks, :, cols] = dr.astype(BF16).reshape(size, block, count)

            tile_loop(width, 512, rows_tile)
            for k in range(max(first, 1), first + size):
                t.home(k).start()
        back[t.me] = made[t.me]
        half_cols = pl.ds(pl.multiple_of(dp * span, 128), span)
        outs = [
            (dgate.at[:, half_cols], mixed_out.at[0, 0]),
            (dup.at[:, half_cols], mixed_out.at[1, 0]),
            (grads, grad_out.at[0]),
        ]
        outs = [pltpu.make_async_copy(src, dst, osem.at[i]) for i, (src, dst) in enumerate(outs)]
        for out in outs:
            out.start()

        for load in loads[5:]:
            load.wait()
        for part in range(len(t.groups)):
            grads_over(part).wait_recv()

        def peer_tile(start, count):
            dy = grads_peer[...].reshape(experts * block, width)
            here = pl.ds(start, count)
            dhidden = dot(dy, wdt[:, pl.ds(pl.multiple_of(dp * span + start, 128), count)])
            dgate_peer[:, here] = (dhidden * dgate_peer[:, here].astype(F32)).astype(BF16)
            dup_peer[:, here] = (dhidden * dup_peer[:, here].astype(F32)).astype(BF16)

        tile_loop(span, 512, peer_tile)
        more = [
            (dgate_peer, mixed_out.at[0, 1]),
            (dup_peer, mixed_out.at[1, 1]),
            (grads_peer, grad_out.at[1]),
        ]
        more = [pltpu.make_async_copy(src, dst, osem.at[3 + i]) for i, (src, dst) in enumerate(more)]
        for out in more:
            out.start()
        for k in range(1, experts):
            t.home(k).wait_recv()
        back_copy = pltpu.make_async_copy(back, back_out, osem.at[6])
        back_copy.start()
        for k in range(1, experts):
            t.there(k).wait_send()
            t.home(k).wait_send()
        for part in range(len(t.groups)):
            grads_over(part).wait_send()
        for out in [*outs, *more, back_copy]:
            out.wait()


def expert_call(kernel, number, turn, send, sources, prev, more, out_shape, scratch, name):
    vmem, hbm = pl.BlockSpec(memory_space=pltpu.VMEM), pl.BlockSpec(memory_space=pl.ANY)
    prev = list(prev or [])
    return pl.pallas_call(
        functools.partial(kernel, turn, bool(prev)),
        in_specs=[vmem] + [hbm] * (len(sources) + len(prev) + len(more)),
        out_specs=[hbm] * len(out_shape),
        out_shape=out_shape,
        input_output_aliases={1 + len(sources) + i: i for i in range(len(prev))},
        scratch_shapes=scratch,
        compiler_params=pltpu.CompilerParams(
            collective_id=number, has_side_effects=True, vmem_limit_bytes=60 << 20
        ),
        cost_estimate=cost(40),
        name=name,
    )(send, *sources, *prev, *more)


def moe_forward(send, w_in, w_down, turn, prev, lefts, slab):
    experts, block, width = send.shape
    ff = w_down.shape[0]
    total = experts * block
    parts = len(groups_of(experts, block))
    dma = pltpu.SemaphoreType.DMA
    scratch = [
        pltpu.VMEM((width, ff), BF16),
        pltpu.VMEM((width, ff), BF16),
        pltpu.VMEM((ff, width), BF16),
        *[pltpu.VMEM(send.shape, BF16)] * 4,
        *[pltpu.VMEM((total, ff), BF16)] * 3,
        *[pltpu.VMEM((total, ff // 2), BF16)] * 2,
        pltpu.VMEM((2, slab, width), BF16),
        dma((3,)),
        *[dma((experts,))] * 4,
        *[dma((parts,))] * 2,
        dma((9,)),
        dma((2,)),
    ]
    shapes = [
        send.shape,
        (2, *send.shape),
        (total, ff),
        (total, ff),
        (2, total, ff // 2),
        (total, ff // 2),
        (total, ff // 2),
        (ff, width),
        (ff, width),
        (width, ff),
    ]
    if lefts:
        rows = lefts[0].shape[0]
        shapes.append((4, rows, width // 2))
        scratch += [pltpu.VMEM((4, rows, width // 2), BF16), *[dma((4,))] * 3]
    out_shape = [jax.ShapeDtypeStruct(shape, BF16) for shape in shapes]
    return expert_call(
        expert_forward_kernel, 1 + turn, turn, send, [w_in, w_down], prev, lefts, out_shape, scratch, "moe_forward"
    )


def moe_backward(grad_send, saved, turn, prev):
    experts, block, width = grad_send.shape
    _, _, slope, value, _, slope_peer, value_peer, wgt, wut, wdt, _ = saved
    total, ff = slope.shape
    parts = len(groups_of(experts, block))
    dma = pltpu.SemaphoreType.DMA
    scratch = [
        pltpu.VMEM((width, ff), BF16),
        *[pltpu.VMEM((total, ff), BF16)] * 2,
        *[pltpu.VMEM((ff, width), BF16)] * 2,
        *[pltpu.VMEM((total, ff // 2), BF16)] * 2,
        *[pltpu.VMEM(grad_send.shape, BF16)] * 4,
        dma((7,)),
        *[dma((experts,))] * 4,
        *[dma((parts,))] * 2,
        dma((7,)),
    ]
    out_shape = [
        jax.ShapeDtypeStruct(grad_send.shape, BF16),
        jax.ShapeDtypeStruct((2, 2, total, ff // 2), BF16),
        jax.ShapeDtypeStruct((2, *grad_send.shape), BF16),
    ]
    return expert_call(
        expert_backward_kernel,
        3 + turn,
        turn,
        grad_send,
        [wdt, slope, value, wgt, wut, slope_peer, value_peer],
        prev,
        [],
        out_shape,
        scratch,
        "moe_backward",
    )


GATE, TOTAL, SCALE, ROUTE, FIRST = 0, 2, 3, 4, 8


class Loads:
    def __init__(self, pairs, sems):
        self.copies = [pltpu.make_async_copy(src, dst, sems.at[i]) for i, (src, dst) in enumerate(pairs)]

    def start(self):
        for copy in self.copies:
            copy.start()

    def wait(self, *which):
        for i in which:
            self.copies[i].wait()


def slots_kernel(experts, capacity, block, order_ref, spots_out, both_out, turned_out, both_turned_out, tally_out, route_out, route_rows):
    seqs, pairs = order_ref.shape
    top = spots_out.shape[1] // both_out.shape[1]
    length = pairs // top
    rows = seqs * length
    slots = spots_out.shape[0]
    expert_id = lax.broadcasted_iota(jnp.int32, (experts, pairs), 0)
    slot_id = lax.broadcasted_iota(jnp.int32, (slots, length), 0)
    row_id = lax.broadcasted_iota(jnp.int32, (pairs, pairs), 0)
    col_id = lax.broadcasted_iota(jnp.int32, (pairs, pairs), 1)
    earlier = (row_id < col_id).astype(F32).astype(BF16)
    route_rows[...] = jnp.zeros_like(route_rows)
    tally = jnp.zeros((experts, 128), F32)
    lane = lax.broadcasted_iota(jnp.int32, (experts, 128), 1)
    for seq in range(seqs):
        order = order_ref[seq : seq + 1, :]
        picked = (expert_id == order).astype(F32)
        place = jnp.sum(dot(picked.astype(BF16), earlier) * picked, axis=0, keepdims=True)
        kept = place < capacity
        target = jnp.where(kept, order * block + seq * capacity + place.astype(jnp.int32), -1)
        taken = jnp.sum(picked * kept.astype(F32), axis=1, keepdims=True)
        whole = jnp.sum(picked, axis=1, keepdims=True)
        tally = tally + jnp.where(lane == 0, taken, jnp.where(lane == 1, whole, 0.0))
        total = jnp.zeros((slots, length), F32)
        for k in range(top):
            part = pl.ds(k * length, length)
            hot = (slot_id == target[:, k * length : (k + 1) * length]).astype(F32)
            spots_out[:, pl.ds(k * rows + seq * length, length)] = hot.astype(BF16)
            total = total + hot
            route_rows[pl.ds(ROUTE + k, 1), pl.ds(seq * length, length)] = order_ref[
                pl.ds(seq, 1), part
            ].astype(F32)
        both_out[:, pl.ds(seq * length, length)] = total.astype(BF16)
    tally_out[...] = tally
    turned_out[...] = jnp.transpose(spots_out[...])
    both_turned_out[...] = jnp.transpose(both_out[...])
    route_out[...] = jnp.transpose(route_rows[...])


def find_slots(order, experts, capacity, block, top):
    seqs, pairs = order.shape
    rows = seqs * pairs // top
    slots = experts * block
    vmem = pl.BlockSpec(memory_space=pltpu.VMEM)
    return pl.pallas_call(
        functools.partial(slots_kernel, experts, capacity, block),
        in_specs=[vmem],
        out_specs=[vmem] * 6,
        out_shape=[
            jax.ShapeDtypeStruct((slots, top * rows), BF16),
            jax.ShapeDtypeStruct((slots, rows), BF16),
            jax.ShapeDtypeStruct((top * rows, slots), BF16),
            jax.ShapeDtypeStruct((rows, slots), BF16),
            jax.ShapeDtypeStruct((experts, 128), F32),
            jax.ShapeDtypeStruct((rows, 128), F32),
        ],
        scratch_shapes=[pltpu.VMEM((128, rows), F32)],
        compiler_params=pltpu.CompilerParams(vmem_limit_bytes=LOCAL_VMEM),
        cost_estimate=cost(1),
        name="find_slots",
    )(order)


def enter_kernel(cross, experts, count, info, gain_ref, router_ref, lanes_ref, lead_ref, *refs):
    held, refs = refs[:count], refs[count:]
    mixed_out, log_out, result_out, stats_out, send_out, low_ref, mask_ref = refs
    w_out, x, spots = held[count - 3 :]
    rows, width = x.shape
    step = min(512, width)
    if cross:
        q_ref, kv = held[:2]
        k_ref, v_ref = kv.at[:, pl.ds(0, width)], kv.at[:, pl.ds(width, width)]
    else:
        q_ref, k_ref, v_ref = (held[0].at[:, pl.ds(i * width, width)] for i in range(3))

    def work():
        attend(info, None if cross else lead_ref, q_ref, k_ref, v_ref, mixed_out, log_out, mask_ref)
        for start in range(0, width, step):
            cols = pl.ds(start, step)
            result_out[:, cols] = x[:, cols].astype(F32) + dot(mixed_out[...], w_out[:, cols])
        values = result_out[...]
        scale = lax.rsqrt(jnp.mean(values * values, axis=-1, keepdims=True) + EPS)
        normed = values * scale * gain_ref[...]
        low = normed.astype(BF16)
        low_ref[...] = low
        logits = dot(low, router_ref[...]) + dot((normed - low.astype(F32)).astype(BF16), router_ref[...])
        lane = lax.broadcasted_iota(jnp.int32, (rows, 128), 1)
        valid = (lane >= FIRST) & (lane < FIRST + experts)
        logits = jnp.where(valid, logits, -1e30)
        spread = jnp.where(valid, jnp.exp(logits - jnp.max(logits, axis=-1, keepdims=True)), 0.0)
        probs = spread / jnp.sum(spread, axis=-1, keepdims=True)
        routes = lanes_ref[...]
        chosen = [
            jnp.sum(
                jnp.where(lane == routes[:, ROUTE + k : ROUTE + k + 1].astype(jnp.int32) + FIRST, probs, 0.0),
                axis=-1,
                keepdims=True,
            )
            for k in range(2)
        ]
        total = chosen[0] + chosen[1]
        stats = probs + routes
        for at, column in ((GATE, chosen[0] / total), (GATE + 1, chosen[1] / total), (TOTAL, total), (SCALE, scale)):
            stats = jnp.where(lane == at, column, stats)
        stats_out[...] = stats
        for start in range(0, width, step):
            cols = pl.ds(start, step)
            send_out[:, cols] = dot(spots[...], low_ref[:, cols]).astype(BF16)

    if not cross:
        work()
        return
    decoder = lax.axis_index("half") == 1
    pl.when(decoder)(work)

    @pl.when(jnp.logical_not(decoder))
    def _():
        result_out[...] = x[...].astype(F32)
        stats_out[...] = lead_ref[...]


def enter(info, gain, router, lanes, lead, cross, sources, experts, length):
    rows, width = sources[-2].shape
    vmem = pl.BlockSpec(memory_space=pltpu.VMEM)
    count = len(sources)
    return pl.pallas_call(
        functools.partial(enter_kernel, cross, experts, count),
        in_specs=[pl.BlockSpec(memory_space=pltpu.SMEM)] + [vmem] * (4 + count),
        out_specs=[vmem] * 5,
        out_shape=[
            jax.ShapeDtypeStruct((rows, width), BF16),
            jax.ShapeDtypeStruct((rows, width), F32),
            jax.ShapeDtypeStruct((rows, width), F32),
            jax.ShapeDtypeStruct((rows, 128), F32),
            jax.ShapeDtypeStruct((sources[-1].shape[0], width), BF16),
        ],
        scratch_shapes=[
            pltpu.VMEM((rows, width), BF16),
            pltpu.VMEM((rows // length, length, length), F32),
        ],
        compiler_params=pltpu.CompilerParams(vmem_limit_bytes=LOCAL_VMEM),
        cost_estimate=cost(10),
        name="enter_cross" if cross else "enter_self",
    )(info, gain, router, lanes, lead, *sources)


def norm_back_rows(values, scale, gain, grad):
    unit = values * scale
    pushed = grad * gain
    back = scale * (pushed - unit * jnp.mean(pushed * unit, axis=-1, keepdims=True))
    return back, jnp.sum(grad * unit, axis=0, keepdims=True)


def leave_kernel(cross, experts, count, info, stats_ref, gain_ref, router_ref, *refs):
    bias_ref, refs = (None, refs) if cross else (refs[0], refs[1:])
    sources, refs = refs[:count], refs[count:]
    grad_out, branch_out, dgain_out, dlog_out, dq_out, last_out = refs[:6]
    held, (dmixed, mask_ref, sems) = refs[6 : 6 + count], refs[6 + count :]
    back, both, grad, results, x, w_out, a, log = held[:8]
    seqs, length, _ = mask_ref.shape
    width = x.shape[1]
    loads = Loads(zip(sources, held), sems)
    if cross:
        q_ref, kv = held[8:]
        k_ref, v_ref = kv.at[:, pl.ds(0, width)], kv.at[:, pl.ds(width, width)]
        dkv_out, shift, diag_out = last_out, 0, None
    else:
        qkv, ready = held[8:]
        q_ref, k_ref, v_ref = (qkv.at[:, pl.ds(i * width, width)] for i in range(3))
        dkv_out, shift, diag_out = dq_out, width, last_out

    def leave():
        loads.wait(0, 1, 2, 3, 4)
        dgain = jnp.zeros((1, width), F32)
        lane = lax.broadcasted_iota(jnp.int32, (length, 128), 1)
        for seq in range(seqs):
            rows = pl.ds(seq * length, length)
            stats = stats_ref[rows, :]
            gates = [stats[:, GATE + k : GATE + k + 1] for k in range(2)]
            hots = [
                (lane == stats[:, ROUTE + k : ROUTE + k + 1].astype(jnp.int32) + FIRST).astype(F32)
                for k in range(2)
            ]
            probs = jnp.where((lane >= FIRST) & (lane < FIRST + experts), stats, 0.0)
            g = grad[rows, :].astype(F32)
            dgates = [
                jnp.sum(g * results[k, rows, :].astype(F32), axis=-1, keepdims=True) for k in range(2)
            ]
            shared = dgates[0] * gates[0] + dgates[1] * gates[1]
            dprobs = sum((dgates[k] - shared) / stats[:, TOTAL : TOTAL + 1] * hots[k] for k in range(2))
            dlog = probs * (dprobs - jnp.sum(dprobs * probs, axis=-1, keepdims=True))
            dlog_out[rows, :] = dlog
            dnormed = dot(both[rows, :], back[...]) + dot(dlog.astype(BF16), router_ref[...], NT)
            dx, part = norm_back_rows(x[rows, :], stats[:, SCALE : SCALE + 1], gain_ref[...], dnormed)
            dgain = dgain + part
            grad_out[rows, :] = g + dx
        dgain_out[...] = jnp.broadcast_to(dgain, dgain_out.shape)

    def attention():
        loads.wait(5)
        branch_out[...] = grad_out[...].astype(BF16)
        step = min(512, width)
        for start in range(0, width, step):
            cols = pl.ds(start, step)
            dmixed[:, cols] = dot(branch_out[...], w_out[cols, :], NT).astype(BF16)
        loads.wait(*((6, 7, 8, 9) if cross else (6, 7, 8)))
        attend_back(
            info, bias_ref, q_ref, k_ref, v_ref, a, log, dmixed, dq_out, dkv_out, shift, diag_out, mask_ref
        )

    decoder = lax.axis_index("half") == 1
    if cross:

        @pl.when(decoder)
        def _():
            loads.start()
            leave()
            attention()

    else:
        loads.start()

        @pl.when(jnp.logical_not(decoder))
        def _():
            leave()
            loads.wait(9)

        @pl.when(decoder)
        def _():
            loads.wait(0, 1, 2, 3, 4, 9)
            grad_out[...] = ready[...]

        attention()


def leave(info, stats, gain, router, bias, sources, experts, length):
    cross = bias is None
    rows, width = sources[4].shape
    seqs = rows // length
    vmem, hbm = pl.BlockSpec(memory_space=pltpu.VMEM), pl.BlockSpec(memory_space=pl.ANY)
    lead = [] if cross else [bias]
    out_shape = [
        jax.ShapeDtypeStruct((rows, width), F32),
        jax.ShapeDtypeStruct((rows, width), BF16),
        jax.ShapeDtypeStruct((8, width), F32),
        jax.ShapeDtypeStruct((rows, 128), F32),
        jax.ShapeDtypeStruct((rows, width if cross else 3 * width), BF16),
        jax.ShapeDtypeStruct((rows, 2 * width), BF16) if cross else jax.ShapeDtypeStruct(bias.shape, F32),
    ]
    return pl.pallas_call(
        functools.partial(leave_kernel, cross, experts, len(sources)),
        in_specs=[pl.BlockSpec(memory_space=pltpu.SMEM)] + [vmem] * (3 + len(lead)) + [hbm] * len(sources),
        out_specs=[vmem] * 6,
        out_shape=out_shape,
        scratch_shapes=[
            *(pltpu.VMEM(a.shape, a.dtype) for a in sources),
            pltpu.VMEM((rows, width), BF16),
            pltpu.VMEM((seqs, length, length), F32),
            pltpu.SemaphoreType.DMA((len(sources),)),
        ],
        compiler_params=pltpu.CompilerParams(vmem_limit_bytes=56 << 20),
        cost_estimate=cost(16),
        name="leave_cross" if cross else "leave_self",
    )(info, stats, gain, router, *lead, *sources)


def memory_kernel(stats_ref, gain_ref, *refs):
    (dmemory, w, x, cotangent, spots), parts, refs = refs[:5], refs[5:7], refs[7:]
    grad_out, send_out, dgain_out, cross_out, dnormed, spread = refs
    rows, width = x.shape

    @pl.when(lax.axis_index("half") == 1)
    def _():
        for i, part in enumerate(parts):
            cross_out[:, pl.ds(i * width, width)] = part[...]

    @pl.when(lax.axis_index("half") == 0)
    def _():
        cross_out[...] = dmemory[...]
        step = min(512, width)
        for start in range(0, width, step):
            cols = pl.ds(start, step)
            dnormed[:, cols] = dot(dmemory[...], w[cols, :], NT)
        scale = lax.rsqrt(jnp.mean(x[...] * x[...], axis=-1, keepdims=True) + EPS)
        dx, dgain = norm_back_rows(x[...], scale, gain_ref[...], dnormed[...])
        dgain_out[...] = jnp.broadcast_to(dgain, dgain_out.shape)
        grad = cotangent[...].astype(F32) + dx
        grad_out[...] = grad
        for k in range(2):
            gate = stats_ref[:, GATE + k : GATE + k + 1]
            spread[pl.ds(k * rows, rows), :] = (gate * grad).astype(BF16)
        for start in range(0, width, step):
            cols = pl.ds(start, step)
            send_out[:, cols] = dot(spots[...], spread[:, cols]).astype(BF16)


def memory_gradient(stats, gain, sources, parts):
    rows, width = sources[2].shape
    vmem = pl.BlockSpec(memory_space=pltpu.VMEM)
    return pl.pallas_call(
        memory_kernel,
        in_specs=[vmem] * (2 + len(sources) + len(parts)),
        out_specs=[vmem] * 4,
        out_shape=[
            jax.ShapeDtypeStruct((rows, width), F32),
            jax.ShapeDtypeStruct((sources[4].shape[0], width), BF16),
            jax.ShapeDtypeStruct((8, width), F32),
            jax.ShapeDtypeStruct((rows, 2 * width), BF16),
        ],
        scratch_shapes=[
            pltpu.VMEM((rows, width), F32),
            pltpu.VMEM((2 * rows, width), BF16),
        ],
        compiler_params=pltpu.CompilerParams(vmem_limit_bytes=LOCAL_VMEM),
        cost_estimate=cost(4),
        name="memory_gradient",
    )(stats, gain, *sources, *parts)


def dense_kernel(stages, chunk, lag, *refs):
    sources, small_ref = refs[:11], refs[11]
    out_refs, small_out, small_in = refs[12:15], refs[15], refs[16]
    held, xt_ref, refs = refs[17:28], refs[28], refs[29:]
    x_refs, own_refs, peer_refs, xp = held[:4], held[4:7], held[7:10], held[10]
    sums, parts = refs[:stages], refs[stages : 2 * stages]
    odd_parts, ss, rs, sk, rk, sl = refs[2 * stages :]
    counts = [ref.shape[1] // chunk for ref in own_refs]
    starts = [sum(counts[:i]) for i in range(3)]
    chunks = sum(counts)
    per_cross = counts[2] // 2
    rows, half = xp.shape[1:]
    dp, me = lax.axis_index("dp"), lax.axis_index("expert")
    peer = {"dp": 1 - dp}
    partners = [flipped(me, k) for k in range(stages)]
    bits = [me // (1 << k) % 2 for k in range(stages)]
    load = [pltpu.make_async_copy(sources[i], held[i], sl.at[i]) for i in range(11)]
    for i in (10, 2, 3, 6, 9, 0, 4, 7, 1, 5, 8):
        load[i].start()
    greet([peer] + [{"expert": p} for p in partners])

    def send_small(step):
        src = small_ref if step == 0 else small_out.at[step - 1]
        device = peer if step == 0 else {"expert": partners[stages - step]}
        return remote(src, small_in.at[step], ss.at[step], rs.at[step], device)

    eighth = odd_parts.shape[1]

    def send_part(k, c, odd):
        if k == 0 and odd:
            src = sums[0].at[c, pl.ds((1 - dp) * eighth, eighth)]
            return remote(src, odd_parts.at[c - early], sk.at[0, c], rk.at[0, c], peer)
        other = 1 - bits[k]
        src = sums[0].at[c, :, :, other] if k == 0 else sums[k].at[c, :, other]
        return remote(src, parts[k].at[c], sk.at[k, c], rk.at[k, c], {"expert": partners[k]})

    def turn_x(g):
        load[g].wait()
        if g < 2:
            cols = pl.ds(pl.multiple_of(dp * half, half), half)
            own = x_refs[g][:, cols]
        else:
            own = dot(x_refs[g][...], every_other(2 * half, out_refs[0].shape[0], bits[0])).astype(BF16)
        xt_ref[g, :, :rows] = jnp.transpose(own)
        xt_ref[g, :, rows:] = jnp.transpose(xp[g])

    def small_step(j):
        send_small(j).wait_recv()
        own = small_ref[...] if j == 0 else small_out[j - 1]
        small_out[j] = own + small_in[j]
        if j < stages:
            send_small(j + 1).start()

    send_small(0).start()
    load[10].wait()
    last = counts[2]
    early = chunks - last
    per = chunks // last

    def produce(i, carry):
        c = jnp.where(lax.rem(i, per) == 0, early + i // per, i - i // per - 1)
        for g in range(3):

            @pl.when(c == starts[g])
            def _(g=g):
                load[4 + g].wait()
                load[7 + g].wait()
                for x in (g,) if g < 2 else (2, 3):
                    turn_x(x)

            @pl.when((c >= starts[g]) & (c < starts[g] + counts[g]))
            def _(g=g):
                at = c - starts[g]
                cols = pl.ds(pl.multiple_of(at * chunk, chunk), chunk)
                which = g if g < 2 else 2 + at // per_cross
                total = dot(xt_ref[which, :, :rows], own_refs[g][:, cols])
                total += dot(xt_ref[which, :, rows:], peer_refs[g][:, cols])
                sums[0][c] = total.astype(BF16).reshape(sums[0].shape[1:])
                send_part(0, c, g == 2).start()

        for j in range(2):

            @pl.when(i == 3 + 6 * j)
            def _(j=j):
                small_step(j)

        return carry

    lax.fori_loop(0, chunks, produce, 0)

    def advance(k, c, odd):
        send_part(k, c, odd).wait_recv()
        if k == 0 and odd:
            mine, other = sums[0][c, pl.ds(dp * eighth, eighth)], odd_parts[c - early]
        else:
            mine = sums[0][c, :, :, bits[0]] if k == 0 else sums[k][c, :, bits[k]]
            other = parts[k][c]
        total = mine.astype(F32) + other.astype(F32)
        if k + 1 < stages:
            sums[k + 1][c] = total.astype(BF16).reshape(sums[k + 1].shape[1:])
            send_part(k + 1, c, odd).start()
            return
        total = total.reshape(total.shape[-2:])
        for g in (2,) if odd else (0, 1):

            @pl.when((c >= starts[g]) & (c < starts[g] + counts[g]))
            def _(g=g):
                at = pl.multiple_of((c - starts[g]) * chunk, chunk)
                out_refs[g][:, pl.ds(at, chunk)] = total

    def reduce(i, carry):
        for k in range(stages):
            c = i - lag * k

            @pl.when((c >= 0) & (c < early))
            def _(k=k, c=c):
                advance(k, c, False)

        for k in range(stages):
            twice = i - 1 - 3 * k

            @pl.when((twice >= 0) & (lax.rem(twice, 2) == 0) & (twice < 2 * last))
            def _(k=k, twice=twice):
                advance(k, early + twice // 2, True)

        for j in range(2, stages + 1):

            @pl.when(i == 3 * j - 2)
            def _(j=j):
                small_step(j)

        return carry

    steps = max(early + lag * (stages - 1), 2 * last + 3 * (stages - 1), 3 * stages - 1)
    lax.fori_loop(0, steps, reduce, 0)

    def finish(c, carry, odd):
        for k in range(stages):
            send_part(k, c, odd).wait_send()
        return carry

    lax.fori_loop(0, early, functools.partial(finish, odd=False), 0)
    lax.fori_loop(early, chunks, functools.partial(finish, odd=True), 0)
    for j in range(stages + 1):
        send_small(j).wait_send()


def to_neighbour(array):
    count = lax.axis_size("expert")
    return lax.ppermute(array, "expert", [(i, i ^ 1) for i in range(count)])


def over_dp(array):
    return lax.ppermute(array, "dp", [(0, 1), (1, 0)])


def dense_gradients(lefts, lefts_peer, own, peer, small, experts):
    chunk = 512
    rows, width = lefts[0].shape
    half_rows = width // 2
    chunks = sum(y.shape[1] for y in own) // chunk
    stages = experts.bit_length() - 1
    keep = half_rows // experts
    vmem, hbm = pl.BlockSpec(memory_space=pltpu.VMEM), pl.BlockSpec(memory_space=pl.ANY)
    dma = pltpu.SemaphoreType.DMA
    sources = [*lefts, *own, *peer, lefts_peer]
    blocks = [(experts // 4, 2, 2)] + [(experts >> (k + 1), 2) for k in range(1, stages)]
    halved = [(experts // 4, 2)] + [(experts >> (k + 1),) for k in range(1, stages)]
    scratch = [pltpu.VMEM((stages + 1, *small.shape), F32)]
    scratch += [pltpu.VMEM(a.shape, BF16) for a in sources]
    scratch += [pltpu.VMEM((4, half_rows, 2 * rows), BF16)]
    scratch += [pltpu.VMEM((chunks, *b, keep, chunk), BF16) for b in blocks + halved]
    scratch += [pltpu.VMEM((own[2].shape[1] // chunk, experts // 8, 2, 2, keep, chunk), BF16)]
    scratch += [dma((stages + 1,)), dma((stages + 1,)), dma((stages, chunks)), dma((stages, chunks))]
    scratch += [dma((len(sources),))]
    *outs, sums = pl.pallas_call(
        functools.partial(dense_kernel, stages, chunk, 2),
        in_specs=[hbm] * len(sources) + [vmem],
        out_specs=[vmem] * 4,
        out_shape=[
            *(jax.ShapeDtypeStruct((keep, y.shape[1]), F32) for y in own),
            jax.ShapeDtypeStruct((stages + 1, *small.shape), F32),
        ],
        scratch_shapes=scratch,
        compiler_params=pltpu.CompilerParams(
            collective_id=0, has_side_effects=True, vmem_limit_bytes=56 << 20
        ),
        cost_estimate=cost(45),
        name="dense_gradients",
    )(*sources, small)
    return outs, sums[stages]


def product_kernel(x_ref, y_ref, out_ref):
    out_ref[...] = dot(x_ref[...], y_ref[...].reshape(y_ref.shape[-2:]), TN).reshape(out_ref.shape)


def expert_gradients(rows, mixed, hidden, grads):
    total, width = rows.shape
    span = hidden.shape[1]
    tile, wide = 256, min(512, width)
    params = pltpu.CompilerParams(vmem_limit_bytes=40 << 20)
    din = pl.pallas_call(
        product_kernel,
        grid=(2, width // wide),
        in_specs=[
            pl.BlockSpec((total, wide), lambda g, i: (0, i)),
            pl.BlockSpec((1, total, span), lambda g, i: (g, 0, 0)),
        ],
        out_specs=pl.BlockSpec((1, wide, span), lambda g, i: (g, i, 0)),
        out_shape=jax.ShapeDtypeStruct((2, width, span), F32),
        compiler_params=params,
        cost_estimate=cost(12),
        name="expert_in_gradient",
    )(rows, mixed)
    ddown = pl.pallas_call(
        product_kernel,
        grid=(pl.cdiv(span, tile),),
        in_specs=[
            pl.BlockSpec((total, tile), lambda i: (0, i)),
            pl.BlockSpec((total, width), lambda i: (0, 0)),
        ],
        out_specs=pl.BlockSpec((tile, width), lambda i: (i, 0)),
        out_shape=jax.ShapeDtypeStruct((span, width), F32),
        compiler_params=params,
        cost_estimate=cost(7),
        name="expert_out_gradient",
    )(hidden, grads)
    return din, ddown


def body(
    tokens,
    cotangent,
    lengths,
    routes,
    self_qkv,
    self_out,
    cross_weights,
    router,
    gains,
    bias_table,
    expert_in,
    expert_out,
):
    _, seqs, length, width = tokens.shape
    heads = H
    experts = router.shape[2]
    top = routes.shape[3]
    capacity = (5 * top * length + 4 * experts - 1) // (4 * experts)
    block_rows = -(-seqs * capacity // 16) * 16
    rows = seqs * length
    slots = experts * block_rows
    half_index = lax.axis_index("half")
    decoder = half_index == 1
    wqkv, wout, wcross, wrouter, gain = (
        self_qkv[0],
        self_out[0],
        cross_weights[0],
        router[0],
        gains[0],
    )
    w_in, w_down = expert_in[0, 0], expert_out[0, 0]

    column = np.arange(2 * length)
    entry = np.arange(BUCKETS * heads)
    hot, hot_back = (
        jnp.where(
            decoder,
            *(
                (entry[:, None] // heads == bucket[None, :]).astype(np.float32)
                for bucket in reversed(diagonal_buckets(diff))
            ),
        )
        for diff in (np.where(column < length, column, column - 2 * length), column - length + 1)
    )
    own_head = entry[None, :] % heads == np.arange(heads)[:, None]
    bias = lax.dot_general(
        jnp.where(own_head, bias_table, 0.0),
        hot,
        (((1,), (0,)), ((), ())),
        precision=lax.Precision.HIGHEST,
        preferred_element_type=F32,
    )
    own_lengths = jnp.where(decoder, lengths[1], lengths[0])
    self_info = jnp.concatenate([own_lengths, half_index[None]]).astype(jnp.int32)
    cross_info = jnp.concatenate([lengths[0], jnp.zeros((1,), jnp.int32)]).astype(jnp.int32)

    order = jnp.transpose(routes[0], (0, 2, 1)).reshape(seqs, top * length)
    spots, both_spots, stacked, both, tally, route_lanes = find_slots(order, experts, capacity, block_rows, top)
    tallies = jnp.concatenate([tally[:, 0], tally[:, 1] - tally[:, 0]])
    router_wide = jnp.pad(wrouter, ((0, 0), (FIRST, 128 - FIRST - experts)))

    def fetch(returned):
        flat = returned.reshape(slots, width)
        return dot(stacked, flat).astype(BF16).reshape(top, rows, width)

    def combine(values, stats, results):
        return values + sum(stats[:, GATE + k : GATE + k + 1] * results[k] for k in range(top))

    values = tokens[0].reshape(rows, width).astype(F32)
    normed, scale0 = norm_parts(values, gain[0])
    low0 = normed.astype(BF16)
    qkv = dot(low0, wqkv).astype(BF16)
    mixed0, log0, first, stats, send = enter(
        self_info,
        gain[1:2],
        router_wide,
        route_lanes,
        bias,
        False,
        [qkv, wout, tokens[0].reshape(rows, width), both_spots],
        experts,
        length,
    )

    send_shape = (experts, block_rows, width)
    saved = moe_forward(send.reshape(send_shape), w_in, w_down, 0, None, [], rows)
    final_enc = combine(first, stats, fetch(saved[0]))
    normed, scale_m = norm_parts(final_enc, gain[2])
    low_m = normed.astype(BF16)
    memory = dot(low_m, wcross).astype(BF16)
    names = ("half", "dp", "expert")
    forward_pairs, back_pairs = half_pairs(lax.axis_size("dp") * lax.axis_size("expert"))
    memory = lax.ppermute(memory, names, forward_pairs)

    normed, scale_c = norm_parts(first, gain[2])
    low_c = normed.astype(BF16)
    query = dot(low_c, wcross[:, :width]).astype(BF16)
    mixed_c, log_c, second, stats, send = enter(
        cross_info,
        gain[1:2],
        router_wide,
        route_lanes,
        stats,
        True,
        [query, memory, wcross[:, width:], first, both_spots],
        experts,
        length,
    )

    lefts = [low0, mixed0, jnp.where(decoder, low_c, low_m), jnp.where(decoder, mixed_c, low_m)]
    saved = moe_forward(send.reshape(send_shape), w_in, w_down, 1, saved, lefts, rows)
    results = fetch(saved[0])
    final = combine(second, stats, results)
    outputs = final.astype(BF16)

    grad_dec = cotangent[0].reshape(rows, width)
    spread = [(stats[:, GATE + k : GATE + k + 1] * grad_dec.astype(F32)).astype(BF16) for k in range(top)]
    grad_send = dot(spots, jnp.concatenate(spread)).astype(BF16)
    kept_from = moe_backward(grad_send.reshape(experts, block_rows, width), saved, 1, None)

    grad_second, dbranch_c, dgain_moe_dec, dlog_dec, dquery, dmemory = leave(
        cross_info,
        stats,
        gain[1:2],
        router_wide,
        None,
        [
            kept_from[0].reshape(slots, width),
            both,
            grad_dec,
            results,
            second,
            wcross[:, width:],
            mixed_c,
            log_c,
            query,
            memory,
        ],
        experts,
        length,
    )
    dmemory = lax.ppermute(dmemory, names, back_pairs)
    dnormed = dot(dquery, wcross[:, :width], NT)
    dvalues, dgain_c = norm_back(first, scale_c, gain[2], dnormed)
    grad_first_dec = grad_second + dvalues

    grad, grad_send, dgain_m, cross_grad = memory_gradient(
        stats, gain[2:3], [dmemory, wcross, final_enc, grad_dec, spots], [dquery, dbranch_c]
    )
    back, mixed_grads, all_grad = moe_backward(
        grad_send.reshape(experts, block_rows, width), saved, 0, kept_from
    )
    all_rows, hidden, lefts_peer = saved[1], saved[4], saved[10]
    grad_first, dbranch, dgain_moe, dlog, dqkv_rows, diag = leave(
        self_info,
        stats,
        gain[1:2],
        router_wide,
        bias,
        [
            back.reshape(slots, width),
            both,
            grad,
            results,
            second,
            wout,
            mixed0,
            log0,
            qkv,
            grad_first_dec,
        ],
        experts,
        length,
    )
    ff_half = hidden.shape[-1]
    din, ddown = expert_gradients(
        all_rows.reshape(-1, width),
        mixed_grads.reshape(2, -1, ff_half),
        hidden.reshape(-1, ff_half),
        all_grad.reshape(-1, width),
    )
    dlog = jnp.where(decoder, dlog_dec, dlog)[:, FIRST : FIRST + experts]
    dgain_moe = jnp.where(decoder, dgain_moe_dec[0], dgain_moe[0])
    drouter = lax.dot_general(
        second * stats[:, SCALE : SCALE + 1] * gain[1],
        dlog,
        TN,
        precision=lax.Precision.HIGHEST,
        preferred_element_type=F32,
    )
    dnormed = dot(dqkv_rows, wqkv, NT)
    dvalues, dgain_self = norm_back(values, scale0, gain[0], dnormed)
    d_tokens = (grad_first + dvalues).astype(BF16)
    by_entry = lax.dot_general(
        diag, hot_back, NT, precision=lax.Precision.HIGHEST, preferred_element_type=F32
    )
    dtable = jnp.sum(jnp.where(own_head, by_entry, 0.0), axis=0)

    own_grads = (dqkv_rows, dbranch, cross_grad)
    peer_grads = (over_dp(dqkv_rows), over_dp(dbranch), to_neighbour(cross_grad))
    places = 2 * experts
    own = width // places
    extra = jnp.concatenate([dtable.reshape(places, -1), tallies.reshape(places, 1)], axis=1)
    extra = jnp.pad(extra, ((0, 0), (0, -extra.shape[1] % own)))
    small = jnp.concatenate(
        [
            jnp.transpose(drouter),
            jnp.stack([dgain_self, dgain_moe, jnp.where(decoder, dgain_c, dgain_m[0])]),
            jnp.swapaxes(extra.reshape(places, -1, own), 0, 1).reshape(-1, width),
        ]
    )
    small = jnp.pad(small, ((0, -small.shape[0] % 8), (0, 0)))
    (dqkv, dout, dcross), small = dense_gradients(
        lefts, lefts_peer, own_grads, peer_grads, small, experts
    )
    place = lax.axis_index("dp") * experts + lax.axis_index("expert")
    mine = lax.dynamic_slice_in_dim(small, place * own, own, 1)
    tail = mine[experts + 3 :].reshape(-1)
    own_table = dtable.shape[0] // places
    d_table = tail[:own_table]
    counts = tail[own_table].astype(jnp.int32)

    return (
        outputs.reshape(1, seqs, length, width),
        d_tokens.reshape(1, seqs, length, width),
        dqkv[None],
        dout[None],
        dcross[None],
        jnp.transpose(mine[:experts])[None],
        mine[experts : experts + 3][None],
        d_table[None],
        din[None, None],
        ddown[None, None],
        counts.reshape(1, 1, 1),
    )


def half_pairs(count):
    return (
        [(i, count + i) for i in range(count)],
        [(count + i, i) for i in range(count)],
    )


def solution(mesh):
    placed = (
        P("half", ("dp", "expert"), None, None),
        P("half", ("dp", "expert"), None, None),
        P(None, ("dp", "expert")),
        P("half", ("dp", "expert"), None, None),
        P("half", None, None),
        P("half", None, None),
        P("half", None, None),
        P("half", None, None),
        P("half", None, None),
        P("half", None),
        P("half", "expert", None, None, None),
        P("half", "expert", None, None),
    )
    return jax.shard_map(
        body,
        mesh=mesh,
        in_specs=placed,
        out_specs=(
            P("half", ("dp", "expert"), None, None),
            P("half", ("dp", "expert"), None, None),
            P("half", ("dp", "expert"), None),
            P("half", ("dp", "expert"), None),
            P("half", ("dp", "expert"), None),
            P("half", ("dp", "expert"), None),
            P("half", None, ("dp", "expert")),
            P("half", ("dp", "expert")),
            P("half", "expert", None, None, "dp"),
            P("half", "expert", "dp", None),
            P("half", "dp", "expert"),
        ),
        check_vma=False,
    )
```
